32 devices in a mesh: gx: 4 (over z), gy: 8 (over y, x, core).
Axes of the slice: x: 2, y: 2, z: 4, core: 2. Of those that a mesh axis runs over, the one named last changes fastest.
Arguments:
- permeability: float32 [3, 128, 16384], P(None, 'gx', 'gy'), may hold values from 0.03 to 1000, as said below
Outputs:
- fine_pressure: float32 [128, 16384], P('gx', 'gy')
- twin_pressure: float32 [64, 4096], P('gx', 'gy')
The draws below stay inside these ranges and needn't reach their ends.
Inputs may be any that keep to these rules, and one draw needn't show every extreme that they name: `permeability`: positive conductivities; entry 0, 1, 2 of the first dimension is the conductivity along the grid's first, second, third dimension.
All inputs are finite; a program needn't handle non-finite values.
Results may differ from the reference program's by a relative error of at most 0.0003.
Values sent between devices are 32-bit elements; how exact they have to be, the bound alone decides.
No kernel may reach another device: no remote copies, remote signals or barrier semaphores. Data moves between devices by JAX's collectives and lax.ppermute only.
A program may use at most 192 MiB of HBM per device.

```python
import math
import jax
import jax.numpy as jnp
from jax import lax

EL = 32
ELZ = 16
MX = 4
MZ = 2
EZ = 2
PATCH_ITERS = 3
COARSE_ITERS = 2
NX = 128
NY = 512
NZ = 32


def draw_permeability(key, part):
    noise_key, phase_key, swing_key = jax.random.split(key, 3)
    place_rows = (jnp.arange(NX, dtype=jnp.float32) + 0.5) / NX
    place_cols = (jnp.arange(NY, dtype=jnp.float32) + 0.5) / NY
    phase = jax.random.uniform(phase_key, (NZ,), jnp.float32, 0.0, 2.0 * math.pi)
    swing = jax.random.uniform(swing_key, (NZ,), jnp.float32, 0.5, 2.5)
    across = 2.0 * math.pi * (jnp.arange(NY, dtype=jnp.float32) + 0.5) / 24.0
    meander = jnp.sin(2.0 * math.pi * jnp.arange(NX, dtype=jnp.float32) / 96.0)
    wave = across[None, :, None] + phase[None, None, :] + swing[None, None, :] * meander[:, None, None]
    channel = 3.0 * jax.nn.sigmoid(6.0 * (jnp.sin(wave) - 0.5))
    trend = math.log(3.0) * (place_rows[:, None, None] + place_cols[None, :, None])
    rough = jnp.clip(0.6 * jax.random.normal(noise_key, (3, NX, NY, NZ), jnp.float32), -1.5, 1.5)
    layered = jnp.array([0.0, 0.0, -1.6], jnp.float32)[:, None, None, None]
    values = jnp.exp(trend[None] + channel[None] + rough + layered)
    return values.reshape(3, NX, NY * NZ)


def setup_inputs(seed: int = 0) -> dict:
    key_list = jax.random.split(jax.random.key(seed), 2)
    return {
        "permeability": draw_permeability(jax.random.fold_in(key_list[1], 71), 0),
    }


def harmonic(first, second, spacing):
    return spacing * 2.0 * first * second / (first + second)


def face_weights(conduct, width, spacing):
    weight_rows = harmonic(conduct[0][..., :-width], conduct[0][..., width:], spacing)
    weight_cols = harmonic(conduct[1][..., :-1], conduct[1][..., 1:], spacing)
    column = jnp.arange(weight_cols.shape[-1], dtype=jnp.int32) % width
    weight_cols = jnp.where(column == width - 1, jnp.zeros_like(weight_cols), weight_cols)
    weight_depth = harmonic(conduct[2][:, :-1], conduct[2][:, 1:], spacing)
    return weight_rows, weight_cols, weight_depth


def apply_operator(field, weights, width):
    weight_rows, weight_cols, weight_depth = weights
    flux = weight_rows * (field[..., :-width] - field[..., width:])
    result = jnp.pad(flux, ((0, 0), (0, 0), (0, 0), (0, width))) - jnp.pad(flux, ((0, 0), (0, 0), (0, 0), (width, 0)))
    flux = weight_cols * (field[..., :-1] - field[..., 1:])
    result = result + jnp.pad(flux, ((0, 0), (0, 0), (0, 0), (0, 1))) - jnp.pad(flux, ((0, 0), (0, 0), (0, 0), (1, 0)))
    flux = weight_depth * (field[:, :, :-1] - field[:, :, 1:])
    result = result + jnp.pad(flux, ((0, 0), (0, 0), (0, 1), (0, 0))) - jnp.pad(flux, ((0, 0), (0, 0), (1, 0), (0, 0)))
    return result


def interior_mask(depth, rows, width):
    level = jnp.arange(depth, dtype=jnp.int32)[:, None]
    cell = jnp.arange(rows * width, dtype=jnp.int32)[None, :]
    row_index = cell // width
    line_index = cell % width
    inside = (level > 0) & (level < depth - 1) & (row_index > 0) & (row_index < rows - 1) & (line_index > 0) & (line_index < width - 1)
    return inside.astype(jnp.float32)


def shape_functions(depth, rows, width, edge, edge_depth, margin, margin_depth):
    cell = jnp.arange(rows * width, dtype=jnp.int32)
    place_rows = ((cell // width).astype(jnp.float32) - margin + 0.5) / edge
    place_cols = ((cell % width).astype(jnp.float32) - margin + 0.5) / edge
    place_depth = (jnp.arange(depth, dtype=jnp.int32).astype(jnp.float32) - margin_depth + 0.5) / edge_depth
    factors = []
    for basis in range(8):
        along_rows = place_rows if basis // 4 else 1.0 - place_rows
        along_cols = place_cols if (basis // 2) % 2 else 1.0 - place_cols
        along_depth = place_depth if basis % 2 else 1.0 - place_depth
        factors.append(along_depth[:, None] * (along_rows * along_cols)[None, :])
    return jnp.stack(factors)[:, None]


def patch_fields(block, edge_depth, margin_depth):
    depth = edge_depth + 2 * margin_depth
    count = (block.shape[3] - 2 * margin_depth) // edge_depth
    pieces = [block[:, :, :, index * edge_depth: index * edge_depth + depth] for index in range(count)]
    stacked = jnp.stack(pieces, axis=1)
    return jnp.transpose(stacked, (0, 1, 4, 2, 3)).reshape(3, count, depth, block.shape[1] * block.shape[2])


def solve_column(block, edge, edge_depth, margin, margin_depth, spacing):
    rows = block.shape[1]
    width = block.shape[2]
    depth = edge_depth + 2 * margin_depth
    conduct = patch_fields(block, edge_depth, margin_depth)
    count = conduct.shape[1]
    weights = face_weights(conduct, width, spacing)
    inside = interior_mask(depth, rows, width)
    start = shape_functions(depth, rows, width, edge, edge_depth, margin, margin_depth)
    residual = -inside * apply_operator(start, weights, width)
    direction = residual
    norm_now = jnp.sum(residual * residual, axis=(2, 3), keepdims=True)
    update = jnp.zeros_like(residual)
    for step in range(PATCH_ITERS):
        image = inside * apply_operator(direction, weights, width)
        alpha = norm_now / jnp.sum(direction * image, axis=(2, 3), keepdims=True)
        update = update + alpha * direction
        residual = residual - alpha * image
        norm_next = jnp.sum(residual * residual, axis=(2, 3), keepdims=True)
        direction = residual + (norm_next / norm_now) * direction
        norm_now = norm_next
    solution = start + update
    local = solution.reshape(8, count, depth, rows, width)[:, :, margin_depth:margin_depth + edge_depth, margin:margin + edge, margin:margin + edge]
    local = local.reshape(8, count, edge_depth, edge * edge)
    element_conduct = conduct.reshape(3, count, depth, rows, width)[:, :, margin_depth:margin_depth + edge_depth, margin:margin + edge, margin:margin + edge]
    element_conduct = element_conduct.reshape(3, count, edge_depth, edge * edge)
    inner_rows, inner_cols, inner_depth = face_weights(element_conduct, edge, spacing)
    jump = local[..., :-edge] - local[..., edge:]
    stiffness = jnp.einsum("aezn,bezn->eab", jump * inner_rows, jump, precision=lax.Precision.HIGHEST)
    jump = local[..., :-1] - local[..., 1:]
    stiffness = stiffness + jnp.einsum("aezn,bezn->eab", jump * inner_cols, jump, precision=lax.Precision.HIGHEST)
    jump = local[:, :, :-1] - local[:, :, 1:]
    stiffness = stiffness + jnp.einsum("aezn,bezn->eab", jump * inner_depth, jump, precision=lax.Precision.HIGHEST)
    return local, stiffness


def coarsen(block):
    comps, rows, width, depth = block.shape
    grouped = block.reshape(comps, rows // 2, 2, width // 2, 2, depth // 2, 2)
    return 0.125 * jnp.sum(grouped, axis=(2, 4, 6))


def corner_stack(corner_first, corner_rows, corner_cols, corner_both, count):
    table = [[corner_first, corner_cols], [corner_rows, corner_both]]
    values = []
    for basis in range(8):
        lift = basis % 2
        values.append(table[basis // 4][(basis // 2) % 2][..., lift:lift + count])
    return jnp.stack(values, axis=-1)


def spread(values, count):
    parts = [[None, None], [None, None]]
    for basis in range(8):
        lift = basis % 2
        widths = [(0, 0)] * (values.ndim - 2) + [(lift, 1 - lift)]
        padded = jnp.pad(values[..., basis], widths)
        first = basis // 4
        second = (basis // 2) % 2
        if parts[first][second] is None:
            parts[first][second] = padded
        else:
            parts[first][second] = parts[first][second] + padded
    return parts


def pressure_tile(local, weights, edge):
    combined = jnp.sum(jnp.transpose(weights)[:, :, None, None] * local, axis=0)
    count = combined.shape[0]
    depth = combined.shape[1]
    return jnp.transpose(combined.reshape(count, depth, edge, edge), (2, 3, 0, 1)).reshape(edge, edge, count * depth)


def coarse_global(stiffness, count):
    def operate(nodes):
        shifted_rows = jnp.roll(nodes, -1, 1)
        shifted_cols = jnp.roll(nodes, -1, 2)
        shifted_both = jnp.roll(shifted_rows, -1, 2)
        element = corner_stack(nodes, shifted_rows, shifted_cols, shifted_both, count)
        local = jnp.einsum("lijkab,lijkb->lijka", stiffness, element, precision=lax.Precision.HIGHEST)
        parts = spread(local, count)
        result = parts[0][0] + jnp.roll(parts[1][0], 1, 1) + jnp.roll(parts[0][1], 1, 2)
        return result + jnp.roll(jnp.roll(parts[1][1], 1, 1), 1, 2)

    def total(first, second):
        return jnp.sum(first * second, axis=(1, 2, 3), keepdims=True)

    level = jnp.arange(count + 1, dtype=jnp.int32)
    inside = ((level > 0) & (level < count)).astype(jnp.float32)
    boundary = jnp.broadcast_to((level == 0).astype(jnp.float32), stiffness.shape[:3] + (count + 1,))
    residual = -inside * operate(boundary)
    direction = residual
    update = jnp.zeros_like(residual)
    norm_now = total(residual, residual)
    for step in range(COARSE_ITERS):
        image = inside * operate(direction)
        alpha = norm_now / total(direction, image)
        update = update + alpha * direction
        residual = residual - alpha * image
        norm_next = total(residual, residual)
        direction = residual + (norm_next / norm_now) * direction
        norm_now = norm_next
    return boundary + update


def reference(permeability):
    field = permeability.reshape(3, NX, NY, NZ)
    extended = jnp.pad(field, ((0, 0), (0, 0), (0, 0), (MZ, MZ)), mode="edge")
    twin_extended = coarsen(extended)
    half_edge = EL // 2
    half_margin = MX // 2
    row_elems = NX // EL
    col_elems = NY // EL

    def blocks(index):
        first = index // col_elems
        second = index % col_elems
        fine_rows = (first * EL - MX + jnp.arange(EL + 2 * MX, dtype=jnp.int32)) % NX
        fine_cols = (second * EL - MX + jnp.arange(EL + 2 * MX, dtype=jnp.int32)) % NY
        twin_rows = (first * half_edge - half_margin + jnp.arange(half_edge + 2 * half_margin, dtype=jnp.int32)) % (NX // 2)
        twin_cols = (second * half_edge - half_margin + jnp.arange(half_edge + 2 * half_margin, dtype=jnp.int32)) % (NY // 2)
        fine_block = jnp.take(jnp.take(extended, fine_rows, axis=1), fine_cols, axis=2)
        twin_block = jnp.take(jnp.take(twin_extended, twin_rows, axis=1), twin_cols, axis=2)
        return fine_block, twin_block

    def column_stiffness(index):
        fine_block, twin_block = blocks(index)
        fine_stiff = solve_column(fine_block, EL, ELZ, MX, MZ, 1.0)[1]
        twin_stiff = solve_column(twin_block, half_edge, ELZ // 2, half_margin, MZ // 2, 2.0)[1]
        return jnp.stack([fine_stiff, twin_stiff])

    indices = jnp.arange(row_elems * col_elems, dtype=jnp.int32)
    totals = lax.map(column_stiffness, indices)
    stiffness = jnp.transpose(totals, (1, 0, 2, 3, 4)).reshape(2, row_elems, col_elems, EZ, 8, 8)
    nodes = coarse_global(stiffness, EZ)
    shifted_rows = jnp.roll(nodes, -1, 1)
    shifted_cols = jnp.roll(nodes, -1, 2)
    shifted_both = jnp.roll(shifted_rows, -1, 2)

    def column_pressure(index):
        first = index // col_elems
        second = index % col_elems
        weights = corner_stack(nodes[:, first, second], shifted_rows[:, first, second], shifted_cols[:, first, second], shifted_both[:, first, second], EZ)
        fine_block, twin_block = blocks(index)
        fine_local = solve_column(fine_block, EL, ELZ, MX, MZ, 1.0)[0]
        twin_local = solve_column(twin_block, half_edge, ELZ // 2, half_margin, MZ // 2, 2.0)[0]
        return pressure_tile(fine_local, weights[0], EL), pressure_tile(twin_local, weights[1], half_edge)

    fine_tiles, twin_tiles = lax.map(column_pressure, indices)
    fine_pressure = jnp.transpose(fine_tiles.reshape(row_elems, col_elems, EL, EL, NZ), (0, 2, 1, 3, 4)).reshape(NX, NY * NZ)
    twin_pressure = jnp.transpose(twin_tiles.reshape(row_elems, col_elems, half_edge, half_edge, NZ // 2), (0, 2, 1, 3, 4)).reshape(NX // 2, (NY // 2) * (NZ // 2))
    return (fine_pressure, twin_pressure)
```

```python
import functools
import typing

import jax
import jax.numpy as jnp
from jax import lax
from jax.experimental import pallas as pl
from jax.experimental.pallas import tpu as pltpu
from jax.sharding import PartitionSpec as P

EL = 32
ELZ = 16
MX = 4
MZ = 2
EZ = 2
LANES = 128
SUBS = 8
COLUMNS = 2
F32 = jnp.float32
BF16 = jnp.bfloat16


class Level(typing.NamedTuple):
    edge: int
    edz: int
    mx: int
    mz: int
    spacing: float
    step: int

    @property
    def width(self):
        return self.edge + 2 * self.mx

    @property
    def inner(self):
        return self.edz + 2 * self.mz - 2

    @property
    def seg(self):
        return -(-self.width // SUBS)

    @property
    def tiles(self):
        return self.seg * self.seg

    @property
    def planes(self):
        return EZ * self.edz + 2

    @property
    def blocks(self):
        return -(-3 * self.seg // 2) * 2

    def base(self, e):
        return e * self.edz + 2 - self.mz


FINE = Level(EL, ELZ, MX, MZ, 1.0, 1)
TWIN = Level(EL // 2, ELZ // 2, MX // 2, MZ // 2, 2.0, 2)
LEVELS = (FINE, TWIN)


def lane_iota(shape=(SUBS, LANES)):
    return lax.broadcasted_iota(jnp.int32, shape, len(shape) - 1)


def sub_iota(shape=(SUBS, LANES)):
    return lax.broadcasted_iota(jnp.int32, shape, len(shape) - 2)


def turn(value, shift, axis=1):
    return pltpu.roll(value, shift % value.shape[axis], axis)


def lane_parts():
    lane = lane_iota()
    return lane // 16, lane // 2 % 8, lane % 2


class Consts:
    def __init__(self, lv):
        basis, xo, _ = lane_parts()
        yo = sub_iota()
        ax, ay, az = basis // 4, basis // 2 % 2, basis % 2
        self.lv = lv
        s = lv.seg
        self.az = az
        self.fx, self.fy, self.mask = [], [], {}
        self.inx, self.iny, self.facex, self.facey = [], [], [], []
        for i in range(s):
            x = xo * s + i
            y = yo * s + i
            px = (x.astype(F32) - lv.mx + 0.5) / lv.edge
            py = (y.astype(F32) - lv.mx + 0.5) / lv.edge
            self.fx.append(jnp.where(ax == 1, px, 1.0 - px))
            self.fy.append(jnp.where(ay == 1, py, 1.0 - py))
            xs = [s * o + i for o in range(SUBS)]

            def ranged(value, low, high):
                if all(low <= v <= high for v in xs):
                    return None
                return ((value >= low) & (value <= high)).astype(F32)

            self.inx.append((ranged(x, 1, lv.width - 2), ranged(x, lv.mx, lv.mx + lv.edge - 1)))
            self.iny.append((ranged(y, 1, lv.width - 2), ranged(y, lv.mx, lv.mx + lv.edge - 1)))
            cut = (lv.mx - 1, lv.mx + lv.edge - 1)
            self.facex.append(((x != cut[0]) & (x != cut[1])).astype(F32) if any(v in cut for v in xs) else None)
            self.facey.append(((y != cut[0]) & (y != cut[1])).astype(F32) if any(v in cut for v in xs) else None)
        self.sx = jnp.where(ax == 1, -1.0 / lv.edge, 1.0 / lv.edge).astype(F32)
        self.sy = jnp.where(ay == 1, -1.0 / lv.edge, 1.0 / lv.edge).astype(F32)
        self.sz = jnp.where(az == 1, -1.0 / lv.edz, 1.0 / lv.edz).astype(F32)

    def fz(self, plane):
        place = (jnp.asarray(plane, jnp.int32).astype(F32) - self.lv.mz + 0.5) / self.lv.edz
        return jnp.where(self.az == 1, place, 1.0 - place)

    def masked(self, value, i, j, kind):
        for table, index in ((self.inx, i), (self.iny, j)):
            factor = table[index][kind]
            if factor is not None:
                value = value * factor
        return value


def tree(values):
    values = list(values)
    while len(values) > 1:
        values = [a + b for a, b in zip(values[::2], values[1::2])] + (
            [values[-1]] if len(values) % 2 else []
        )
    return values[0]


def xor_lane(value, bit):
    return jnp.where(lane_iota(value.shape) // bit % 2 == 1, turn(value, bit), turn(value, -bit))


def problem_sum(value):
    for shift in (4, 2, 1):
        value = value + turn(value, shift, 0)
    for bit in (2, 4, 8):
        value = value + xor_lane(value, bit)
    return value


def spread_weights(lv, k_ref, ws_ref, hi_ref, lo_ref, w_ref):
    s = lv.seg
    wide = (SUBS, 2 * LANES)
    pos = lane_iota(wide) % LANES
    yo = sub_iota(wide)
    first = pos < 40
    second = (pos >= 40) & (pos < 80)
    edge_x = first & (pos >= (lv.width - 1) * lv.step)

    def plane(z, _):
        cells = [k_ref[z, i] for i in range(s)]
        for i in range(s):
            k = cells[i]
            nbx = turn(k, -lv.step)
            nby = cells[i + 1] if i < s - 1 else turn(cells[0], -1, 0)
            nbz = k_ref[z + 1, i]
            nb = jnp.where(first, nbx, jnp.where(second, nby, nbz))
            w = (2.0 * lv.spacing) * k * nb / (k + nb)
            bad = edge_x | (second & (yo * s + i >= lv.width - 1))
            ws_ref[z * s + i] = jnp.where(bad, 0.0, w)
        return 0

    lax.fori_loop(0, lv.planes, plane, 0)
    rows = lv.planes * s * SUBS
    full = ws_ref[...].reshape(rows, 2 * LANES)
    high = full.astype(BF16)
    hi_ref[...] = high
    lo_ref[...] = (full - high.astype(F32)).astype(BF16)
    shape = (2 * LANES, 2 * LANES)
    row = lax.broadcasted_iota(jnp.int32, shape, 0)
    lane = lax.broadcasted_iota(jnp.int32, shape, 1)
    xo = lane // 2 % 8
    upper = lane // LANES
    source = (lane % 2) * LANES + lv.step * s * xo

    def block(n, _):
        number = 2 * n + upper
        comp = number // s
        i = number - comp * s
        hit = (row == source + comp * 40 + lv.step * i) & (xo * s + i < lv.width)
        pick = hit.astype(F32).astype(BF16)
        out = jnp.dot(hi_ref[...], pick, preferred_element_type=F32)
        out = out + jnp.dot(lo_ref[...], pick, preferred_element_type=F32)
        w_ref[2 * n] = out[:, :LANES].reshape(lv.planes * s, SUBS, LANES)
        w_ref[2 * n + 1] = out[:, LANES:].reshape(lv.planes * s, SUBS, LANES)
        return 0

    lax.fori_loop(0, lv.blocks // 2, block, 0)


def load_weights(lv, w_ref, pz):
    s = lv.seg

    def get(m, i, j, plane=None):
        return w_ref[m * s + i, (pz if plane is None else plane) * s + j]

    return get


def start_residual(lv, cs, e, w_ref, d_ref):
    s = lv.seg

    def body(z, acc):
        pz = lv.base(e) + z
        below = jnp.maximum(pz - 1, 0)
        get = load_weights(lv, w_ref, pz)
        gz = cs.fz(z + 1)
        along_x = [cs.sx * gz * cs.fy[j] for j in range(s)]
        along_y = [cs.sy * gz * cs.fx[i] for i in range(s)]
        squares = []
        flux_y = {}
        for i in range(s):
            for j in range(s):
                flux_y[i, j] = get(1, i, j) * along_y[i]
        for j in range(s):
            flux_x = [get(0, i, j) * along_x[j] for i in range(s)]
            for i in range(s):
                prev_x = flux_x[i - 1] if i else turn(flux_x[s - 1], 2)
                prev_y = flux_y[i, j - 1] if j else turn(flux_y[i, s - 1], 1, 0)
                along_z = cs.sz * cs.fx[i] * cs.fy[j]
                value = (prev_x - flux_x[i]) + (prev_y - flux_y[i, j])
                value = value + along_z * (get(2, i, j, below) - get(2, i, j))
                value = cs.masked(value, i, j, 0)
                d_ref[z, i * s + j] = value
                squares.append(value * value)
        return acc + tree(squares)

    return lax.fori_loop(0, lv.inner, body, jnp.zeros((SUBS, LANES), F32))


def apply(lv, cs, e, w_ref, d_ref, q_ref, fz_ref, fresh):
    s = lv.seg
    keep = q_ref is not None

    def plane(z):
        return [fresh(z, k) for k in range(lv.tiles)]

    first = plane(0)
    below = max(lv.base(e) - 1, 0)
    get = load_weights(lv, w_ref, below)
    acc = jnp.zeros((SUBS, LANES), F32)
    for i in range(s):
        for j in range(s):
            flux = -get(2, i, j) * first[i * s + j]
            if keep:
                fz_ref[i * s + j] = flux
            else:
                acc = acc - flux * first[i * s + j]

    def body(z, acc):
        get = load_weights(lv, w_ref, lv.base(e) + z)
        terms = []
        u = [d_ref[z, k] for k in range(lv.tiles)]
        flux_y = {}
        for i in range(s):
            for j in range(s):
                after = u[i * s + j + 1] if j < s - 1 else turn(u[i * s], -1, 0)
                jump = u[i * s + j] - after
                flux_y[i, j] = get(1, i, j) * jump
                if not keep:
                    terms.append(flux_y[i, j] * jump)
        for j in range(s):
            flux_x = []
            for i in range(s):
                after = u[(i + 1) * s + j] if i < s - 1 else turn(u[j], -2)
                jump = u[i * s + j] - after
                flux_x.append(get(0, i, j) * jump)
                if not keep:
                    terms.append(flux_x[i] * jump)
            for i in range(s):
                k = i * s + j
                jump = u[k] - fresh(z + 1, k)
                flux = get(2, i, j) * jump
                if keep:
                    prev_x = flux_x[i - 1] if i else turn(flux_x[s - 1], 2)
                    prev_y = flux_y[i, j - 1] if j else turn(flux_y[i, s - 1], 1, 0)
                    value = (flux_x[i] - prev_x) + (flux_y[i, j] - prev_y) + (flux - fz_ref[k])
                    fz_ref[k] = flux
                    value = cs.masked(value, i, j, 0)
                    q_ref[z, k] = value
                    terms.append(u[k] * value)
                else:
                    terms.append(flux * jump)
        return acc + tree(terms)

    return lax.fori_loop(0, lv.inner, body, acc)


def reduce_residual(lv, source_ref, q_ref, r_ref, alpha):
    def body(z, acc):
        squares = []
        for k in range(lv.tiles):
            value = source_ref[z, k] - alpha * q_ref[z, k]
            r_ref[z, k] = value
            squares.append(value * value)
        return acc + tree(squares)

    return lax.fori_loop(0, lv.inner, body, jnp.zeros((SUBS, LANES), F32))


def finish(lv, cs, e, w_ref, d_refs, alphas, phi_ref, fz_ref):
    s = lv.seg
    even = (cs.az == 0).astype(F32)
    zero = jnp.zeros((SUBS, LANES), F32)

    def fresh(z, i, j):
        k = i * s + j
        inner = z + lv.mz - 1
        value = cs.fx[i] * cs.fy[j] * cs.fz(z + lv.mz)
        for alpha, d_ref in zip(alphas, d_refs):
            value = value + alpha * d_ref[inner, k]
        value = cs.masked(value, i, j, 1)
        phi_ref[e * lv.edz + z, k] = value
        return value

    for i in range(s):
        for j in range(s):
            fresh(0, i, j)
            fz_ref[i * s + j] = zero

    def body(z, accs):
        get = load_weights(lv, w_ref, lv.base(e) + lv.mz - 1 + z)
        after_z = jnp.minimum(z + 1, lv.edz - 1)
        u = [phi_ref[e * lv.edz + z, k] for k in range(lv.tiles)]
        sums = [[] for _ in accs]
        flux_y = {}
        for i in range(s):
            for j in range(s):
                after = u[i * s + j + 1] if j < s - 1 else turn(u[i * s], -1, 0)
                flux = get(1, i, j) * (u[i * s + j] - after)
                flux_y[i, j] = flux if cs.facey[j] is None else flux * cs.facey[j]
        for j in range(s):
            flux_x = []
            for i in range(s):
                after = u[(i + 1) * s + j] if i < s - 1 else turn(u[j], -2)
                flux = get(0, i, j) * (u[i * s + j] - after)
                flux_x.append(flux if cs.facex[i] is None else flux * cs.facex[i])
            for i in range(s):
                k = i * s + j
                flux = get(2, i, j) * (u[k] - fresh(after_z, i, j))
                prev_x = flux_x[i - 1] if i else turn(flux_x[s - 1], 2)
                prev_y = flux_y[i, j - 1] if j else turn(flux_y[i, s - 1], 1, 0)
                value = (flux_x[i] - prev_x) + (flux_y[i, j] - prev_y) + (flux - fz_ref[k])
                fz_ref[k] = flux
                sums[0].append(value * u[k])
                sums[1].append(value * turn(u[k], -32))
                sums[2].append(value * turn(u[k], 64))
                if e == 0:
                    low = u[k] * even
                    low = low + turn(low, 32)
                    low = low + turn(low, 64)
                    sums[3].append(value * turn(low, 16))
        return tuple(acc + tree(part) for acc, part in zip(accs, sums))

    count = 4 if e == 0 else 3
    return lax.fori_loop(0, lv.edz, body, (zero,) * count)


def solve_kernel(
    center, x_low, x_high, y_low, y_high, corner_ll, corner_lh, corner_hl, corner_hh,
    phi_fine, phi_twin, message,
    flat, rows, pairs, twin_rows,
    kf, kt, wsf, wst, hif, hit, lof, lot, wf, wt,
    fine_fields, twin_fields, fzf, fzt,
):
    lanes = center.shape[2]
    rim = y_low.shape[2]
    nx = center.shape[1]
    top = MX + nx
    for m in range(3):
        off = m * (nx + 2 * MX)
        flat[off : off + MX, :rim] = corner_ll[m]
        flat[off : off + MX, rim : rim + lanes] = x_low[m]
        flat[off : off + MX, rim + lanes :] = corner_lh[m]
        flat[off + MX : off + top, :rim] = y_low[m]
        flat[off + MX : off + top, rim : rim + lanes] = center[m]
        flat[off + MX : off + top, rim + lanes :] = y_high[m]
        flat[off + top : off + top + MX, :rim] = corner_hl[m]
        flat[off + top : off + top + MX, rim : rim + lanes] = x_high[m]
        flat[off + top : off + top + MX, rim + lanes :] = corner_hh[m]
    used = 3 * (nx + 2 * MX)
    flat[used:, :] = jnp.ones((LANES - used, flat.shape[1]), F32)
    for t in range(flat.shape[1] // LANES):
        rows[t * LANES : (t + 1) * LANES, :] = flat[:, t * LANES : (t + 1) * LANES].T

    nz = EZ * ELZ
    def coarse(y, _):
        start = pl.multiple_of(y * 2 * nz, 2 * nz)
        both = rows[pl.ds(start, nz), :] + rows[pl.ds(start + nz, nz), :]
        both = both + turn(both, -1)
        pairs[...] = both
        middle = 0.125 * (pairs[pl.ds(0, nz // 2, stride=2), :] + pairs[pl.ds(1, nz // 2, stride=2), :])
        to = pl.multiple_of(y * nz, nz)
        twin_rows[pl.ds(to, 8), :] = jnp.broadcast_to(0.25 * both[0:1], (8, LANES))
        twin_rows[pl.ds(to + 8, nz // 2), :] = middle
        twin_rows[pl.ds(to + 8 + nz // 2, 8), :] = jnp.broadcast_to(0.25 * both[nz - 1 : nz], (8, LANES))
        return 0

    twin_y = rows.shape[0] // nz // 2
    lax.fori_loop(0, twin_y, coarse, 0)
    twin_rows[twin_y * nz :, :] = jnp.ones((twin_rows.shape[0] - twin_y * nz, LANES), F32)

    def gather_fine(z, _):
        cell = jnp.clip(z - 1, 0, nz - 1)
        for i in range(FINE.seg):
            for c in range(COLUMNS):
                start = (EL * c + i) * nz + cell
                kf[z, i, :, c * LANES : (c + 1) * LANES] = rows[pl.ds(start, SUBS, stride=FINE.seg * nz), :]
        return 0

    lax.fori_loop(0, FINE.planes + 1, gather_fine, 0)

    def gather_twin(z, _):
        cell = jnp.minimum(z, TWIN.planes - 1) + 7
        for i in range(TWIN.seg):
            for c in range(COLUMNS):
                start = (TWIN.edge * c + i) * nz + cell
                kt[z, i, :, c * LANES : (c + 1) * LANES] = twin_rows[pl.ds(start, SUBS, stride=TWIN.seg * nz), :]
        return 0

    lax.fori_loop(0, TWIN.planes + 1, gather_twin, 0)

    spread_weights(FINE, kf, wsf, hif, lof, wf)
    spread_weights(TWIN, kt, wst, hit, lot, wt)

    consts = [Consts(lv) for lv in LEVELS]
    w_refs = (wf, wt)
    fields = (fine_fields, twin_fields)
    fz_refs = (fzf, fzt)
    phis = (phi_fine, phi_twin)
    cases = [(n, e) for n in range(2) for e in range(EZ)]

    def field(n, e, which):
        return fields[n].at[e * 5 + which]

    for n, e in cases:
        for which in range(5):
            for k in range(LEVELS[n].tiles):
                field(n, e, which)[LEVELS[n].inner, k] = jnp.zeros((SUBS, LANES), F32)

    rr = [problem_sum(v) for v in [start_residual(LEVELS[n], consts[n], e, w_refs[n], field(n, e, 0)) for n, e in cases]]
    alphas = [[] for _ in cases]
    betas = [None] * len(cases)
    for step in range(3):
        dots = []
        for p, (n, e) in enumerate(cases):
            d_ref = field(n, e, step)
            if step == 0:
                def fresh(z, k, d_ref=d_ref):
                    return d_ref[z, k]
            else:
                def fresh(z, k, d_ref=d_ref, old=field(n, e, step - 1), r=field(n, e, 4), beta=betas[p]):
                    value = r[z, k] + beta * old[z, k]
                    d_ref[z, k] = value
                    return value
            q_ref = field(n, e, 3) if step < 2 else None
            dots.append(apply(LEVELS[n], consts[n], e, w_refs[n], d_ref, q_ref, fz_refs[n], fresh))
        dots = [problem_sum(v) for v in dots]
        for p in range(len(cases)):
            alphas[p].append(rr[p] / dots[p])
        if step < 2:
            new = []
            for p, (n, e) in enumerate(cases):
                source = field(n, e, 0) if step == 0 else field(n, e, 4)
                new.append(reduce_residual(LEVELS[n], source, field(n, e, 3), field(n, e, 4), alphas[p][step]))
            new = [problem_sum(v) for v in new]
            betas = [a / b for a, b in zip(new, rr)]
            rr = new

    totals = []
    for p, (n, e) in enumerate(cases):
        d_refs = [field(n, e, which) for which in range(3)]
        totals.append(finish(LEVELS[n], consts[n], e, w_refs[n], d_refs, alphas[p], phis[n], fz_refs[n]))
    totals = [[problem_sum(v) for v in part] for part in totals]
    basis, xo, _ = lane_parts()
    packed = []
    for n in range(2):
        low, high = totals[2 * n], totals[2 * n + 1]
        parts = [turn(low[q], -16) + high[q] for q in range(3)] + [turn(low[3], -16)]
        slots = jnp.where(xo == 0, parts[0], jnp.where(xo == 1, parts[1], jnp.where(xo == 2, parts[2], parts[3])))
        packed.append(slots)
    message[...] = jnp.where(basis % 2 == 0, packed[0], turn(packed[1], 16))


def coarse_nodes(gathered, gy_count, me):
    total_rows = gathered.shape[0]
    shape = gathered.shape
    lane = lane_iota(shape)
    row = sub_iota(shape)
    corner = lane // 32
    column = lane % 2
    last = row % gy_count == gy_count - 1
    start = row % gy_count == 0
    one = gathered
    two = turn(gathered, -2)
    four = turn(gathered, -4)
    rhs = turn(gathered, -6)
    two_back = turn(two, 32)

    def next_x(u):
        return turn(u, -gy_count, 0)

    def prev_x(u):
        return turn(u, gy_count, 0)

    def next_y(u):
        ahead = jnp.where(last, turn(u, gy_count - 1, 0), turn(u, -1, 0))
        return jnp.where(column == 0, turn(u, -1), turn(ahead, 1))

    def prev_y(u):
        behind = jnp.where(start, turn(u, 1 - gy_count, 0), turn(u, 1, 0))
        return jnp.where(column == 1, turn(u, 1), turn(behind, -1))

    def by_corner(a, b, c, d):
        return jnp.where(corner == 0, a, jnp.where(corner == 1, b, jnp.where(corner == 2, c, d)))

    def corners(u):
        ux = next_x(u)
        return by_corner(u, next_y(u), ux, next_y(ux))

    def assemble(v):
        vx = prev_x(v)
        w = by_corner(v, prev_y(v), vx, prev_y(vx))
        w = w + turn(w, 64)
        return w + turn(w, 32)

    def operate(u):
        c = corners(u)
        return assemble(one * c + two * turn(c, -32) + two_back * turn(c, 32) + four * turn(c, 64))

    def total(a, b):
        v = a * b
        v = tree([v[r : r + SUBS] for r in range(0, total_rows, SUBS)])
        for shift in (4, 2, 1):
            v = v + turn(v, shift, 0)
        v = v + xor_lane(v, 1)
        return v[0:1]

    residual = -assemble(rhs)
    direction = residual
    update = jnp.zeros_like(residual)
    now = total(residual, residual)
    for step in range(2):
        image = operate(direction)
        alpha = now / total(direction, image)
        update = update + alpha * direction
        if step == 0:
            residual = residual - alpha * image
            new = total(residual, residual)
            direction = residual + new / now * direction
            now = new
    mine = jnp.where(row == me, corners(update), 0.0)
    mine = jnp.sum(mine, axis=0, keepdims=True)
    mine = jnp.broadcast_to(mine, (SUBS, LANES))
    mine = jnp.where(lane_iota() // 2 % 8 == 0, mine, 0.0)
    for shift in (2, 4, 8):
        mine = mine + turn(mine, shift)
    return mine


def pressure(lv, phi_ref, scales, o_ref, t_ref, out_ref):
    s = lv.seg
    basis, _, _ = lane_parts()
    low4 = basis < 4
    low2 = basis // 2 % 2 == 0
    low1 = basis % 2 == 0
    nz = EZ * lv.edz

    def pair4(a, b):
        if b is None:
            return a + turn(a, 64)
        return jnp.where(low4, a, b) + turn(jnp.where(low4, b, a), 64)

    def fold(value, low, bit):
        return jnp.where(low, turn(value, -bit), turn(value, bit))

    def pair(a, b, low, bit):
        if b is None:
            return a + fold(a, low, bit)
        return jnp.where(low, a, b) + fold(jnp.where(low, b, a), low, bit)

    for e in range(EZ):
        def body(z, _, e=e):
            plane = e * lv.edz + z
            for j in range(s):
                v = [phi_ref[plane, i * s + j] * scales[e] for i in range(s)]
                v = v + [None] * (6 - s)
                t = [pair4(v[0], v[1]), pair4(v[2], v[3]), None if v[4] is None else pair4(v[4], v[5])]
                q = pair(t[0], t[1], low2, 32)
                q4 = None if t[2] is None else pair(t[2], None, low2, 32)
                o_ref[pl.ds(pl.multiple_of((plane * s + j) * SUBS, SUBS), SUBS), :] = pair(q, q4, low1, 16)
            return 0

        lax.fori_loop(0, lv.edz, body, 0)
    slots = (0, 4, 2, 6, 1)
    per = LANES // nz
    tiles = lv.edge // per
    for t in range(tiles):
        parts = []
        for n in range(per):
            y = lv.mx + t * per + n
            parts.append(o_ref[pl.ds(y % s * SUBS + y // s, nz, stride=s * SUBS), :])
        t_ref[t] = jnp.concatenate(parts, axis=0).T
        for c in range(COLUMNS):
            at = (c * tiles + t) * LANES
            for x in range(lv.edge):
                xo, i = divmod(x + lv.mx, s)
                out_ref[x : x + 1, at : at + LANES] = t_ref[t, pl.ds(slots[i] * 16 + xo * 2 + c, 1), :]


def pressure_kernel(gy_count, me_ref, gathered, phi_fine, phi_twin, fine_out, twin_out, of, ot, tf, tt):
    mine = coarse_nodes(gathered[...], gy_count, me_ref[0])
    even = lane_iota() // 16 % 2 == 0
    up = turn(mine, 16)
    down = turn(mine, -16)
    fine_scales = [jnp.where(even, 1.0, up), jnp.where(even, mine, 0.0)]
    twin_scales = [jnp.where(even, 1.0, mine), jnp.where(even, down, 0.0)]
    pressure(FINE, phi_fine, fine_scales, of, tf, fine_out)
    pressure(TWIN, phi_twin, twin_scales, ot, tt, twin_out)


def vmem(shape, dtype=F32):
    return pltpu.VMEM(shape, dtype)


def shards(permeability):
    nz = EZ * ELZ
    rows = permeability.shape[1]
    lanes = permeability.shape[2]
    assert rows == EL and lanes == COLUMNS * EL * nz
    rim = MX * nz
    gx, gy = lax.axis_size("gx"), lax.axis_size("gy")

    def sent(value, dx, dy):
        pairs = [
            (i * gy + j, (i + dx) % gx * gy + (j + dy) % gy) for i in range(gx) for j in range(gy)
        ]
        return lax.ppermute(value, ("gx", "gy"), pairs)

    first_x, last_x = permeability[:, :MX], permeability[:, rows - MX :]
    first_y, last_y = permeability[:, :, :rim], permeability[:, :, lanes - rim :]
    halos = [
        sent(last_x, 1, 0),
        sent(first_x, -1, 0),
        sent(last_y, 0, 1),
        sent(first_y, 0, -1),
        sent(last_x[:, :, lanes - rim :], 1, 1),
        sent(last_x[:, :, :rim], 1, -1),
        sent(first_x[:, :, lanes - rim :], -1, 1),
        sent(first_x[:, :, :rim], -1, -1),
    ]
    flat_lanes = lanes + 2 * rim
    scratch = [
        vmem((LANES, flat_lanes)),
        vmem((flat_lanes, LANES)),
        vmem((nz, LANES)),
        vmem((SUBS * (TWIN.seg + 2) * nz, LANES)),
    ]
    for make in (
        lambda lv: vmem((lv.planes + 1, lv.seg, SUBS, 2 * LANES)),
        lambda lv: vmem((lv.planes * lv.seg, SUBS, 2 * LANES)),
        lambda lv: vmem((lv.planes * lv.seg * SUBS, 2 * LANES), BF16),
        lambda lv: vmem((lv.planes * lv.seg * SUBS, 2 * LANES), BF16),
        lambda lv: vmem((lv.blocks, lv.planes * lv.seg, SUBS, LANES)),
        lambda lv: vmem((EZ * 5, lv.inner + 1, lv.tiles, SUBS, LANES)),
        lambda lv: vmem((lv.tiles, SUBS, LANES)),
    ):
        scratch += [make(FINE), make(TWIN)]
    full = pl.BlockSpec(memory_space=pltpu.VMEM)
    phi_shapes = [
        jax.ShapeDtypeStruct((EZ * lv.edz, lv.tiles, SUBS, LANES), F32) for lv in LEVELS
    ]
    phi_fine, phi_twin, message = pl.pallas_call(
        solve_kernel,
        out_shape=phi_shapes + [jax.ShapeDtypeStruct((SUBS, LANES), F32)],
        in_specs=[full] * 9,
        out_specs=[full] * 3,
        scratch_shapes=scratch,
        compiler_params=pltpu.CompilerParams(vmem_limit_bytes=56 * 1024 * 1024),
        name="solve",
    )(permeability, *halos)
    gathered = lax.all_gather(message[:1], ("gx", "gy"), axis=0, tiled=True)
    me = (lax.axis_index("gx") * gy + lax.axis_index("gy")).astype(jnp.int32).reshape(1)
    outs = [
        jax.ShapeDtypeStruct((lv.edge, COLUMNS * lv.edge * EZ * lv.edz), F32) for lv in LEVELS
    ]
    scratch = [vmem((EZ * lv.edz * lv.seg * SUBS, LANES)) for lv in LEVELS]
    scratch += [vmem((lv.edge * EZ * lv.edz // LANES, LANES, LANES)) for lv in LEVELS]
    return tuple(
        pl.pallas_call(
            functools.partial(pressure_kernel, gy),
            out_shape=outs,
            in_specs=[pl.BlockSpec(memory_space=pltpu.SMEM)] + [full] * 3,
            out_specs=[full] * 2,
            scratch_shapes=scratch,
            compiler_params=pltpu.CompilerParams(vmem_limit_bytes=40 * 1024 * 1024),
            name="pressure",
        )(me, gathered, phi_fine, phi_twin)
    )


def solution(mesh):
    return jax.shard_map(
        shards,
        mesh=mesh,
        in_specs=(P(None, "gx", "gy"),),
        out_specs=(P("gx", "gy"), P("gx", "gy")),
        check_vma=False,
    )
```

```python
import functools
import typing

import jax
import jax.numpy as jnp
from jax import lax
from jax.experimental import pallas as pl
from jax.experimental.pallas import tpu as pltpu
from jax.sharding import PartitionSpec as P

EL = 32
ELZ = 16
MX = 4
MZ = 2
EZ = 2
LANES = 128
SUBS = 8
COLUMNS = 2
F32 = jnp.float32
BF16 = jnp.bfloat16


class Level(typing.NamedTuple):
    edge: int
    edz: int
    mx: int
    mz: int
    spacing: float
    step: int

    @property
    def width(self):
        return self.edge + 2 * self.mx

    @property
    def inner(self):
        return self.edz + 2 * self.mz - 2

    @property
    def seg(self):
        return -(-self.width // SUBS)

    @property
    def tiles(self):
        return self.seg * self.seg

    @property
    def planes(self):
        return EZ * self.edz + 2

    @property
    def blocks(self):
        return -(-3 * self.seg // 2) * 2

    def base(self, e):
        return e * self.edz + 2 - self.mz


FINE = Level(EL, ELZ, MX, MZ, 1.0, 1)
TWIN = Level(EL // 2, ELZ // 2, MX // 2, MZ // 2, 2.0, 2)
LEVELS = (FINE, TWIN)


def lane_iota(shape=(SUBS, LANES)):
    return lax.broadcasted_iota(jnp.int32, shape, len(shape) - 1)


def sub_iota(shape=(SUBS, LANES)):
    return lax.broadcasted_iota(jnp.int32, shape, len(shape) - 2)


def turn(value, shift, axis=1):
    return pltpu.roll(value, shift % value.shape[axis], axis)


def lane_parts():
    lane = lane_iota()
    return lane // 16, lane // 2 % 8, lane % 2


class Consts:
    def __init__(self, lv):
        basis, xo, _ = lane_parts()
        yo = sub_iota()
        ax, ay, az = basis // 4, basis // 2 % 2, basis % 2
        self.lv = lv
        s = lv.seg
        self.az = az
        self.fx, self.fy, self.mask = [], [], {}
        self.inx, self.iny, self.facex, self.facey = [], [], [], []
        for i in range(s):
            x = xo * s + i
            y = yo * s + i
            px = (x.astype(F32) - lv.mx + 0.5) / lv.edge
            py = (y.astype(F32) - lv.mx + 0.5) / lv.edge
            self.fx.append(jnp.where(ax == 1, px, 1.0 - px))
            self.fy.append(jnp.where(ay == 1, py, 1.0 - py))
            xs = [s * o + i for o in range(SUBS)]

            def ranged(value, low, high):
                if all(low <= v <= high for v in xs):
                    return None
                return ((value >= low) & (value <= high)).astype(F32)

            self.inx.append((ranged(x, 1, lv.width - 2), ranged(x, lv.mx, lv.mx + lv.edge - 1)))
            self.iny.append((ranged(y, 1, lv.width - 2), ranged(y, lv.mx, lv.mx + lv.edge - 1)))
            cut = (lv.mx - 1, lv.mx + lv.edge - 1)
            self.facex.append(((x != cut[0]) & (x != cut[1])).astype(F32) if any(v in cut for v in xs) else None)
            self.facey.append(((y != cut[0]) & (y != cut[1])).astype(F32) if any(v in cut for v in xs) else None)
        self.sx = jnp.where(ax == 1, -1.0 / lv.edge, 1.0 / lv.edge).astype(F32)
        self.sy = jnp.where(ay == 1, -1.0 / lv.edge, 1.0 / lv.edge).astype(F32)
        self.sz = jnp.where(az == 1, -1.0 / lv.edz, 1.0 / lv.edz).astype(F32)

    def fz(self, plane):
        place = (jnp.asarray(plane, jnp.int32).astype(F32) - self.lv.mz + 0.5) / self.lv.edz
        return jnp.where(self.az == 1, place, 1.0 - place)

    def masked(self, value, i, j, kind):
        for table, index in ((self.inx, i), (self.iny, j)):
            factor = table[index][kind]
            if factor is not None:
                value = value * factor
        return value


def tree(values):
    values = list(values)
    while len(values) > 1:
        values = [a + b for a, b in zip(values[::2], values[1::2])] + (
            [values[-1]] if len(values) % 2 else []
        )
    return values[0]


def xor_lane(value, bit):
    return jnp.where(lane_iota(value.shape) // bit % 2 == 1, turn(value, bit), turn(value, -bit))


def problem_sum(value):
    for shift in (4, 2, 1):
        value = value + turn(value, shift, 0)
    for bit in (2, 4, 8):
        value = value + xor_lane(value, bit)
    return value


def spread_weights(lv, k_ref, ws_ref, hi_ref, lo_ref, w_ref):
    s = lv.seg
    wide = (SUBS, 2 * LANES)
    pos = lane_iota(wide) % LANES
    yo = sub_iota(wide)
    first = pos < 40
    second = (pos >= 40) & (pos < 80)
    edge_x = first & (pos >= (lv.width - 1) * lv.step)

    def plane(z, _):
        cells = [k_ref[z, i] for i in range(s)]
        for i in range(s):
            k = cells[i]
            nbx = turn(k, -lv.step)
            nby = cells[i + 1] if i < s - 1 else turn(cells[0], -1, 0)
            nbz = k_ref[z + 1, i]
            nb = jnp.where(first, nbx, jnp.where(second, nby, nbz))
            w = (2.0 * lv.spacing) * k * nb / (k + nb)
            bad = edge_x | (second & (yo * s + i >= lv.width - 1))
            ws_ref[z * s + i] = jnp.where(bad, 0.0, w)
        return 0

    lax.fori_loop(0, lv.planes, plane, 0)
    rows = lv.planes * s * SUBS
    full = ws_ref[...].reshape(rows, 2 * LANES)
    high = full.astype(BF16)
    hi_ref[...] = high
    lo_ref[...] = (full - high.astype(F32)).astype(BF16)
    shape = (2 * LANES, 2 * LANES)
    row = lax.broadcasted_iota(jnp.int32, shape, 0)
    lane = lax.broadcasted_iota(jnp.int32, shape, 1)
    xo = lane // 2 % 8
    upper = lane // LANES
    source = (lane % 2) * LANES + lv.step * s * xo

    def block(n, _):
        number = 2 * n + upper
        comp = number // s
        i = number - comp * s
        hit = (row == source + comp * 40 + lv.step * i) & (xo * s + i < lv.width)
        pick = hit.astype(F32).astype(BF16)
        out = jnp.dot(hi_ref[...], pick, preferred_element_type=F32)
        out = out + jnp.dot(lo_ref[...], pick, preferred_element_type=F32)
        w_ref[2 * n] = out[:, :LANES].reshape(lv.planes * s, SUBS, LANES)
        w_ref[2 * n + 1] = out[:, LANES:].reshape(lv.planes * s, SUBS, LANES)
        return 0

    lax.fori_loop(0, lv.blocks // 2, block, 0)


def load_weights(lv, w_ref, pz):
    s = lv.seg

    def get(m, i, j, plane=None):
        return w_ref[m * s + i, (pz if plane is None else plane) * s + j]

    return get


def start_residual(lv, cs, e, w_ref, d_ref):
    s = lv.seg

    def body(z, acc):
        pz = lv.base(e) + z
        below = jnp.maximum(pz - 1, 0)
        get = load_weights(lv, w_ref, pz)
        gz = cs.fz(z + 1)
        along_x = [cs.sx * gz * cs.fy[j] for j in range(s)]
        along_y = [cs.sy * gz * cs.fx[i] for i in range(s)]
        squares = []
        flux_y = {}
        for i in range(s):
            for j in range(s):
                flux_y[i, j] = get(1, i, j) * along_y[i]
        for j in range(s):
            flux_x = [get(0, i, j) * along_x[j] for i in range(s)]
            for i in range(s):
                prev_x = flux_x[i - 1] if i else turn(flux_x[s - 1], 2)
                prev_y = flux_y[i, j - 1] if j else turn(flux_y[i, s - 1], 1, 0)
                along_z = cs.sz * cs.fx[i] * cs.fy[j]
                value = (prev_x - flux_x[i]) + (prev_y - flux_y[i, j])
                value = value + along_z * (get(2, i, j, below) - get(2, i, j))
                value = cs.masked(value, i, j, 0)
                d_ref[z, i * s + j] = value
                squares.append(value * value)
        return acc + tree(squares)

    return lax.fori_loop(0, lv.inner, body, jnp.zeros((SUBS, LANES), F32))


def apply(lv, cs, e, w_ref, d_ref, q_ref, fz_ref, fresh):
    s = lv.seg
    keep = q_ref is not None

    def plane(z):
        return [fresh(z, k) for k in range(lv.tiles)]

    first = plane(0)
    below = max(lv.base(e) - 1, 0)
    get = load_weights(lv, w_ref, below)
    acc = jnp.zeros((SUBS, LANES), F32)
    for i in range(s):
        for j in range(s):
            flux = -get(2, i, j) * first[i * s + j]
            if keep:
                fz_ref[i * s + j] = flux
            else:
                acc = acc - flux * first[i * s + j]

    def body(z, acc):
        get = load_weights(lv, w_ref, lv.base(e) + z)
        terms = []
        u = [d_ref[z, k] for k in range(lv.tiles)]
        flux_y = {}
        for i in range(s):
            for j in range(s):
                after = u[i * s + j + 1] if j < s - 1 else turn(u[i * s], -1, 0)
                jump = u[i * s + j] - after
                flux_y[i, j] = get(1, i, j) * jump
                if not keep:
                    terms.append(flux_y[i, j] * jump)
        for j in range(s):
            flux_x = []
            for i in range(s):
                after = u[(i + 1) * s + j] if i < s - 1 else turn(u[j], -2)
                jump = u[i * s + j] - after
                flux_x.append(get(0, i, j) * jump)
                if not keep:
                    terms.append(flux_x[i] * jump)
            for i in range(s):
                k = i * s + j
                jump = u[k] - fresh(z + 1, k)
                flux = get(2, i, j) * jump
                if keep:
                    prev_x = flux_x[i - 1] if i else turn(flux_x[s - 1], 2)
                    prev_y = flux_y[i, j - 1] if j else turn(flux_y[i, s - 1], 1, 0)
                    value = (flux_x[i] - prev_x) + (flux_y[i, j] - prev_y) + (flux - fz_ref[k])
                    fz_ref[k] = flux
                    value = cs.masked(value, i, j, 0)
                    q_ref[z, k] = value
                    terms.append(u[k] * value)
                else:
                    terms.append(flux * jump)
        return acc + tree(terms)

    return lax.fori_loop(0, lv.inner, body, acc)


def reduce_residual(lv, source_ref, q_ref, r_ref, alpha):
    def body(z, acc):
        squares = []
        for k in range(lv.tiles):
            value = source_ref[z, k] - alpha * q_ref[z, k]
            r_ref[z, k] = value
            squares.append(value * value)
        return acc + tree(squares)

    return lax.fori_loop(0, lv.inner, body, jnp.zeros((SUBS, LANES), F32))


def finish(lv, cs, e, w_ref, d_refs, alphas, phi_ref, fz_ref):
    s = lv.seg
    even = (cs.az == 0).astype(F32)
    zero = jnp.zeros((SUBS, LANES), F32)

    def fresh(z, i, j):
        k = i * s + j
        inner = z + lv.mz - 1
        value = cs.fx[i] * cs.fy[j] * cs.fz(z + lv.mz)
        for alpha, d_ref in zip(alphas, d_refs):
            value = value + alpha * d_ref[inner, k]
        value = cs.masked(value, i, j, 1)
        phi_ref[e * lv.edz + z, k] = value
        return value

    for i in range(s):
        for j in range(s):
            fresh(0, i, j)
            fz_ref[i * s + j] = zero

    def body(z, accs):
        get = load_weights(lv, w_ref, lv.base(e) + lv.mz - 1 + z)
        after_z = jnp.minimum(z + 1, lv.edz - 1)
        u = [phi_ref[e * lv.edz + z, k] for k in range(lv.tiles)]
        sums = [[] for _ in accs]
        flux_y = {}
        for i in range(s):
            for j in range(s):
                after = u[i * s + j + 1] if j < s - 1 else turn(u[i * s], -1, 0)
                flux = get(1, i, j) * (u[i * s + j] - after)
                flux_y[i, j] = flux if cs.facey[j] is None else flux * cs.facey[j]
        for j in range(s):
            flux_x = []
            for i in range(s):
                after = u[(i + 1) * s + j] if i < s - 1 else turn(u[j], -2)
                flux = get(0, i, j) * (u[i * s + j] - after)
                flux_x.append(flux if cs.facex[i] is None else flux * cs.facex[i])
            for i in range(s):
                k = i * s + j
                flux = get(2, i, j) * (u[k] - fresh(after_z, i, j))
                prev_x = flux_x[i - 1] if i else turn(flux_x[s - 1], 2)
                prev_y = flux_y[i, j - 1] if j else turn(flux_y[i, s - 1], 1, 0)
                value = (flux_x[i] - prev_x) + (flux_y[i, j] - prev_y) + (flux - fz_ref[k])
                fz_ref[k] = flux
                sums[0].append(value * u[k])
                sums[1].append(value * turn(u[k], -32))
                sums[2].append(value * turn(u[k], 64))
                if e == 0:
                    low = u[k] * even
                    low = low + turn(low, 32)
                    low = low + turn(low, 64)
                    sums[3].append(value * turn(low, 16))
        return tuple(acc + tree(part) for acc, part in zip(accs, sums))

    count = 4 if e == 0 else 3
    return lax.fori_loop(0, lv.edz, body, (zero,) * count)


def solve_kernel(
    center, x_low, x_high, y_low, y_high,
    phi_fine, phi_twin, message,
    flat, rows, pairs, twin_rows,
    kf, kt, wsf, wst, hif, hit, lof, lot, wf, wt,
    fine_fields, twin_fields, fzf, fzt,
):
    lanes = center.shape[2]
    rim = y_low.shape[2]
    nx = center.shape[1]
    top = MX + nx
    for m in range(3):
        off = m * (nx + 2 * MX)
        flat[off : off + top + MX, :rim] = y_low[m]
        flat[off : off + MX, rim : rim + lanes] = x_low[m]
        flat[off + MX : off + top, rim : rim + lanes] = center[m]
        flat[off + top : off + top + MX, rim : rim + lanes] = x_high[m]
        flat[off : off + top + MX, rim + lanes :] = y_high[m]
    used = 3 * (nx + 2 * MX)
    flat[used:, :] = jnp.ones((LANES - used, flat.shape[1]), F32)
    for t in range(flat.shape[1] // LANES):
        rows[t * LANES : (t + 1) * LANES, :] = flat[:, t * LANES : (t + 1) * LANES].T

    nz = EZ * ELZ
    def coarse(y, _):
        start = pl.multiple_of(y * 2 * nz, 2 * nz)
        both = rows[pl.ds(start, nz), :] + rows[pl.ds(start + nz, nz), :]
        both = both + turn(both, -1)
        pairs[...] = both
        middle = 0.125 * (pairs[pl.ds(0, nz // 2, stride=2), :] + pairs[pl.ds(1, nz // 2, stride=2), :])
        to = pl.multiple_of(y * nz, nz)
        twin_rows[pl.ds(to, 8), :] = jnp.broadcast_to(0.25 * both[0:1], (8, LANES))
        twin_rows[pl.ds(to + 8, nz // 2), :] = middle
        twin_rows[pl.ds(to + 8 + nz // 2, 8), :] = jnp.broadcast_to(0.25 * both[nz - 1 : nz], (8, LANES))
        return 0

    twin_y = rows.shape[0] // nz // 2
    lax.fori_loop(0, twin_y, coarse, 0)
    twin_rows[twin_y * nz :, :] = jnp.ones((twin_rows.shape[0] - twin_y * nz, LANES), F32)

    def gather_fine(z, _):
        cell = jnp.clip(z - 1, 0, nz - 1)
        for i in range(FINE.seg):
            for c in range(COLUMNS):
                start = (EL * c + i) * nz + cell
                kf[z, i, :, c * LANES : (c + 1) * LANES] = rows[pl.ds(start, SUBS, stride=FINE.seg * nz), :]
        return 0

    lax.fori_loop(0, FINE.planes + 1, gather_fine, 0)

    def gather_twin(z, _):
        cell = jnp.minimum(z, TWIN.planes - 1) + 7
        for i in range(TWIN.seg):
            for c in range(COLUMNS):
                start = (TWIN.edge * c + i) * nz + cell
                kt[z, i, :, c * LANES : (c + 1) * LANES] = twin_rows[pl.ds(start, SUBS, stride=TWIN.seg * nz), :]
        return 0

    lax.fori_loop(0, TWIN.planes + 1, gather_twin, 0)

    spread_weights(FINE, kf, wsf, hif, lof, wf)
    spread_weights(TWIN, kt, wst, hit, lot, wt)

    consts = [Consts(lv) for lv in LEVELS]
    w_refs = (wf, wt)
    fields = (fine_fields, twin_fields)
    fz_refs = (fzf, fzt)
    phis = (phi_fine, phi_twin)
    cases = [(n, e) for n in range(2) for e in range(EZ)]

    def field(n, e, which):
        return fields[n].at[e * 5 + which]

    for n, e in cases:
        for which in range(5):
            for k in range(LEVELS[n].tiles):
                field(n, e, which)[LEVELS[n].inner, k] = jnp.zeros((SUBS, LANES), F32)

    rr = [problem_sum(v) for v in [start_residual(LEVELS[n], consts[n], e, w_refs[n], field(n, e, 0)) for n, e in cases]]
    alphas = [[] for _ in cases]
    betas = [None] * len(cases)
    for step in range(3):
        dots = []
        for p, (n, e) in enumerate(cases):
            d_ref = field(n, e, step)
            if step == 0:
                def fresh(z, k, d_ref=d_ref):
                    return d_ref[z, k]
            else:
                def fresh(z, k, d_ref=d_ref, old=field(n, e, step - 1), r=field(n, e, 4), beta=betas[p]):
                    value = r[z, k] + beta * old[z, k]
                    d_ref[z, k] = value
                    return value
            q_ref = field(n, e, 3) if step < 2 else None
            dots.append(apply(LEVELS[n], consts[n], e, w_refs[n], d_ref, q_ref, fz_refs[n], fresh))
        dots = [problem_sum(v) for v in dots]
        for p in range(len(cases)):
            alphas[p].append(rr[p] / dots[p])
        if step < 2:
            new = []
            for p, (n, e) in enumerate(cases):
                source = field(n, e, 0) if step == 0 else field(n, e, 4)
                new.append(reduce_residual(LEVELS[n], source, field(n, e, 3), field(n, e, 4), alphas[p][step]))
            new = [problem_sum(v) for v in new]
            betas = [a / b for a, b in zip(new, rr)]
            rr = new

    totals = []
    for p, (n, e) in enumerate(cases):
        d_refs = [field(n, e, which) for which in range(3)]
        totals.append(finish(LEVELS[n], consts[n], e, w_refs[n], d_refs, alphas[p], phis[n], fz_refs[n]))
    totals = [[problem_sum(v) for v in part] for part in totals]
    basis, xo, _ = lane_parts()
    packed = []
    for n in range(2):
        low, high = totals[2 * n], totals[2 * n + 1]
        parts = [turn(low[q], -16) + high[q] for q in range(3)] + [turn(low[3], -16)]
        slots = jnp.where(xo == 0, parts[0], jnp.where(xo == 1, parts[1], jnp.where(xo == 2, parts[2], parts[3])))
        packed.append(slots)
    row = jnp.where(basis % 2 == 0, packed[0], turn(packed[1], 16))
    for r in range(0, message.shape[0], SUBS):
        message[r : r + SUBS, :] = row


def coarse_nodes(gathered, gy_count, me):
    total_rows = gathered.shape[0]
    shape = gathered.shape
    lane = lane_iota(shape)
    row = sub_iota(shape)
    corner = lane // 32
    column = lane % 2
    last = row % gy_count == gy_count - 1
    start = row % gy_count == 0
    one = gathered
    two = turn(gathered, -2)
    four = turn(gathered, -4)
    rhs = turn(gathered, -6)
    two_back = turn(two, 32)

    def next_x(u):
        return turn(u, -gy_count, 0)

    def prev_x(u):
        return turn(u, gy_count, 0)

    def next_y(u):
        ahead = jnp.where(last, turn(u, gy_count - 1, 0), turn(u, -1, 0))
        return jnp.where(column == 0, turn(u, -1), turn(ahead, 1))

    def prev_y(u):
        behind = jnp.where(start, turn(u, 1 - gy_count, 0), turn(u, 1, 0))
        return jnp.where(column == 1, turn(u, 1), turn(behind, -1))

    def by_corner(a, b, c, d):
        return jnp.where(corner == 0, a, jnp.where(corner == 1, b, jnp.where(corner == 2, c, d)))

    def corners(u):
        ux = next_x(u)
        return by_corner(u, next_y(u), ux, next_y(ux))

    def assemble(v):
        vx = prev_x(v)
        w = by_corner(v, prev_y(v), vx, prev_y(vx))
        w = w + turn(w, 64)
        return w + turn(w, 32)

    def operate(u):
        c = corners(u)
        return assemble(one * c + two * turn(c, -32) + two_back * turn(c, 32) + four * turn(c, 64))

    def total(a, b):
        v = a * b
        v = tree([v[r : r + SUBS] for r in range(0, total_rows, SUBS)])
        for shift in (4, 2, 1):
            v = v + turn(v, shift, 0)
        v = v + xor_lane(v, 1)
        return v[0:1]

    residual = -assemble(rhs)
    direction = residual
    update = jnp.zeros_like(residual)
    now = total(residual, residual)
    for step in range(2):
        image = operate(direction)
        alpha = now / total(direction, image)
        update = update + alpha * direction
        if step == 0:
            residual = residual - alpha * image
            new = total(residual, residual)
            direction = residual + new / now * direction
            now = new
    mine = jnp.where(row == me, corners(update), 0.0)
    mine = jnp.sum(mine, axis=0, keepdims=True)
    mine = jnp.broadcast_to(mine, (SUBS, LANES))
    mine = jnp.where(lane_iota() // 2 % 8 == 0, mine, 0.0)
    for shift in (2, 4, 8):
        mine = mine + turn(mine, shift)
    return mine


def pressure(lv, phi_ref, scales, o_ref, t_ref, out_ref):
    s = lv.seg
    basis, _, _ = lane_parts()
    low4 = basis < 4
    low2 = basis // 2 % 2 == 0
    low1 = basis % 2 == 0
    nz = EZ * lv.edz

    def pair4(a, b):
        if b is None:
            return a + turn(a, 64)
        return jnp.where(low4, a, b) + turn(jnp.where(low4, b, a), 64)

    def fold(value, low, bit):
        return jnp.where(low, turn(value, -bit), turn(value, bit))

    def pair(a, b, low, bit):
        if b is None:
            return a + fold(a, low, bit)
        return jnp.where(low, a, b) + fold(jnp.where(low, b, a), low, bit)

    for e in range(EZ):
        def body(z, _, e=e):
            plane = e * lv.edz + z
            for j in range(s):
                v = [phi_ref[plane, i * s + j] * scales[e] for i in range(s)]
                v = v + [None] * (6 - s)
                t = [pair4(v[0], v[1]), pair4(v[2], v[3]), None if v[4] is None else pair4(v[4], v[5])]
                q = pair(t[0], t[1], low2, 32)
                q4 = None if t[2] is None else pair(t[2], None, low2, 32)
                o_ref[pl.ds(pl.multiple_of((plane * s + j) * SUBS, SUBS), SUBS), :] = pair(q, q4, low1, 16)
            return 0

        lax.fori_loop(0, lv.edz, body, 0)
    slots = (0, 4, 2, 6, 1)
    per = LANES // nz
    tiles = lv.edge // per
    for t in range(tiles):
        parts = []
        for n in range(per):
            y = lv.mx + t * per + n
            parts.append(o_ref[pl.ds(y % s * SUBS + y // s, nz, stride=s * SUBS), :])
        t_ref[t] = jnp.concatenate(parts, axis=0).T
        for c in range(COLUMNS):
            at = (c * tiles + t) * LANES
            for x in range(lv.edge):
                xo, i = divmod(x + lv.mx, s)
                out_ref[x : x + 1, at : at + LANES] = t_ref[t, pl.ds(slots[i] * 16 + xo * 2 + c, 1), :]


def pressure_kernel(gy_count, me_ref, gathered, phi_fine, phi_twin, fine_out, twin_out, of, ot, tf, tt):
    mine = coarse_nodes(gathered[...], gy_count, me_ref[0])
    even = lane_iota() // 16 % 2 == 0
    up = turn(mine, 16)
    down = turn(mine, -16)
    fine_scales = [jnp.where(even, 1.0, up), jnp.where(even, mine, 0.0)]
    twin_scales = [jnp.where(even, 1.0, mine), jnp.where(even, down, 0.0)]
    pressure(FINE, phi_fine, fine_scales, of, tf, fine_out)
    pressure(TWIN, phi_twin, twin_scales, ot, tt, twin_out)


def vmem(shape, dtype=F32):
    return pltpu.VMEM(shape, dtype)


def shards(permeability):
    nz = EZ * ELZ
    rows = permeability.shape[1]
    lanes = permeability.shape[2]
    assert rows == EL and lanes == COLUMNS * EL * nz
    rim = MX * nz
    gx, gy = lax.axis_size("gx"), lax.axis_size("gy")

    def sent(value, axis, shift):
        count = lax.axis_size(axis)
        return lax.ppermute(value, axis, [(i, (i + shift) % count) for i in range(count)])

    x_low = sent(permeability[:, rows - MX :], "gx", 1)
    x_high = sent(permeability[:, :MX], "gx", -1)

    def strip(part):
        return jnp.concatenate([x_low[:, :, part], permeability[:, :, part], x_high[:, :, part]], axis=1)

    y_low = sent(strip(slice(lanes - rim, lanes)), "gy", 1)
    y_high = sent(strip(slice(0, rim)), "gy", -1)
    halos = [x_low, x_high, y_low, y_high]
    flat_lanes = lanes + 2 * rim
    scratch = [
        vmem((LANES, flat_lanes)),
        vmem((flat_lanes, LANES)),
        vmem((nz, LANES)),
        vmem((SUBS * (TWIN.seg + 2) * nz, LANES)),
    ]
    for make in (
        lambda lv: vmem((lv.planes + 1, lv.seg, SUBS, 2 * LANES)),
        lambda lv: vmem((lv.planes * lv.seg, SUBS, 2 * LANES)),
        lambda lv: vmem((lv.planes * lv.seg * SUBS, 2 * LANES), BF16),
        lambda lv: vmem((lv.planes * lv.seg * SUBS, 2 * LANES), BF16),
        lambda lv: vmem((lv.blocks, lv.planes * lv.seg, SUBS, LANES)),
        lambda lv: vmem((EZ * 5, lv.inner + 1, lv.tiles, SUBS, LANES)),
        lambda lv: vmem((lv.tiles, SUBS, LANES)),
    ):
        scratch += [make(FINE), make(TWIN)]
    full = pl.BlockSpec(memory_space=pltpu.VMEM)
    phi_shapes = [
        jax.ShapeDtypeStruct((EZ * lv.edz, lv.tiles, SUBS, LANES), F32) for lv in LEVELS
    ]
    phi_fine, phi_twin, message = pl.pallas_call(
        solve_kernel,
        out_shape=phi_shapes + [jax.ShapeDtypeStruct((gx * gy, LANES), F32)],
        in_specs=[full] * 5,
        out_specs=[full] * 3,
        scratch_shapes=scratch,
        compiler_params=pltpu.CompilerParams(vmem_limit_bytes=56 * 1024 * 1024),
        name="solve",
    )(permeability, *halos)
    gathered = lax.all_to_all(message, ("gx", "gy"), 0, 0, tiled=True)
    me = (lax.axis_index("gx") * gy + lax.axis_index("gy")).astype(jnp.int32).reshape(1)
    outs = [
        jax.ShapeDtypeStruct((lv.edge, COLUMNS * lv.edge * EZ * lv.edz), F32) for lv in LEVELS
    ]
    scratch = [vmem((EZ * lv.edz * lv.seg * SUBS, LANES)) for lv in LEVELS]
    scratch += [vmem((lv.edge * EZ * lv.edz // LANES, LANES, LANES)) for lv in LEVELS]
    return tuple(
        pl.pallas_call(
            functools.partial(pressure_kernel, gy),
            out_shape=outs,
            in_specs=[pl.BlockSpec(memory_space=pltpu.SMEM)] + [full] * 3,
            out_specs=[full] * 2,
            scratch_shapes=scratch,
            compiler_params=pltpu.CompilerParams(vmem_limit_bytes=40 * 1024 * 1024),
            name="pressure",
        )(me, gathered, phi_fine, phi_twin)
    )


def solution(mesh):
    return jax.shard_map(
        shards,
        mesh=mesh,
        in_specs=(P(None, "gx", "gy"),),
        out_specs=(P("gx", "gy"), P("gx", "gy")),
        check_vma=False,
    )
```

```python
import functools
import typing

import jax
import jax.numpy as jnp
from jax import lax
from jax.experimental import pallas as pl
from jax.experimental.pallas import tpu as pltpu
from jax.sharding import PartitionSpec as P

EL = 32
ELZ = 16
MX = 4
MZ = 2
EZ = 2
LANES = 128
SUBS = 8
COLUMNS = 2
F32 = jnp.float32
BF16 = jnp.bfloat16


class Level(typing.NamedTuple):
    edge: int
    edz: int
    mx: int
    mz: int
    spacing: float
    step: int

    @property
    def width(self):
        return self.edge + 2 * self.mx

    @property
    def inner(self):
        return self.edz + 2 * self.mz - 2

    @property
    def seg(self):
        return -(-self.width // SUBS)

    @property
    def tiles(self):
        return self.seg * self.seg

    @property
    def planes(self):
        return EZ * self.edz + 2

    @property
    def blocks(self):
        return -(-3 * self.seg // 2) * 2

    def base(self, e):
        return e * self.edz + 2 - self.mz


FINE = Level(EL, ELZ, MX, MZ, 1.0, 1)
TWIN = Level(EL // 2, ELZ // 2, MX // 2, MZ // 2, 2.0, 2)
LEVELS = (FINE, TWIN)


def lane_iota(shape=(SUBS, LANES)):
    return lax.broadcasted_iota(jnp.int32, shape, len(shape) - 1)


def sub_iota(shape=(SUBS, LANES)):
    return lax.broadcasted_iota(jnp.int32, shape, len(shape) - 2)


def turn(value, shift, axis=1):
    return pltpu.roll(value, shift % value.shape[axis], axis)


def lane_parts():
    lane = lane_iota()
    return lane // 16, lane % 8, lane // 8 % 2


class Consts:
    def __init__(self, lv):
        basis, xo, _ = lane_parts()
        yo = sub_iota()
        ax, ay, az = basis // 4, basis // 2 % 2, basis % 2
        self.lv = lv
        s = lv.seg
        self.az = az
        self.fx, self.fy, self.mask = [], [], {}
        self.inx, self.iny, self.facex, self.facey = [], [], [], []
        for i in range(s):
            x = xo * s + i
            y = yo * s + i
            px = (x.astype(F32) - lv.mx + 0.5) / lv.edge
            py = (y.astype(F32) - lv.mx + 0.5) / lv.edge
            self.fx.append(jnp.where(ax == 1, px, 1.0 - px))
            self.fy.append(jnp.where(ay == 1, py, 1.0 - py))
            xs = [s * o + i for o in range(SUBS)]

            def ranged(value, low, high):
                if all(low <= v <= high for v in xs):
                    return None
                return ((value >= low) & (value <= high)).astype(F32)

            self.inx.append((ranged(x, 1, lv.width - 2), ranged(x, lv.mx, lv.mx + lv.edge - 1)))
            self.iny.append((ranged(y, 1, lv.width - 2), ranged(y, lv.mx, lv.mx + lv.edge - 1)))
            cut = (lv.mx - 1, lv.mx + lv.edge - 1)
            self.facex.append(((x != cut[0]) & (x != cut[1])).astype(F32) if any(v in cut for v in xs) else None)
            self.facey.append(((y != cut[0]) & (y != cut[1])).astype(F32) if any(v in cut for v in xs) else None)
        self.sx = jnp.where(ax == 1, -1.0 / lv.edge, 1.0 / lv.edge).astype(F32)
        self.sy = jnp.where(ay == 1, -1.0 / lv.edge, 1.0 / lv.edge).astype(F32)
        self.sz = jnp.where(az == 1, -1.0 / lv.edz, 1.0 / lv.edz).astype(F32)

    def fz(self, plane):
        place = (jnp.asarray(plane, jnp.int32).astype(F32) - self.lv.mz + 0.5) / self.lv.edz
        return jnp.where(self.az == 1, place, 1.0 - place)

    def masked(self, value, i, j, kind):
        for table, index in ((self.inx, i), (self.iny, j)):
            factor = table[index][kind]
            if factor is not None:
                value = value * factor
        return value


def tree(values):
    values = list(values)
    while len(values) > 1:
        values = [a + b for a, b in zip(values[::2], values[1::2])] + (
            [values[-1]] if len(values) % 2 else []
        )
    return values[0]


def xor_lane(value, bit):
    return jnp.where(lane_iota(value.shape) // bit % 2 == 1, turn(value, bit), turn(value, -bit))


def problem_sum(value):
    for shift in (4, 2, 1):
        value = value + turn(value, shift, 0)
    for bit in (1, 2, 4):
        value = value + xor_lane(value, bit)
    return value


def spread_weights(lv, k_ref, lhs_refs, w_refs):
    s = lv.seg
    wide = (SUBS, LANES)
    pos = lane_iota(wide)
    yo = sub_iota(wide)
    first = pos < 40
    third = pos >= 80
    second = (pos >= 40) & (pos < 80)
    edge_x = first & (pos >= (lv.width - 1) * lv.step)

    def one(z, i, c):
        part = slice(c * LANES, (c + 1) * LANES)
        k = k_ref[z, i, :, part]
        nbx = turn(k, -lv.step)
        nby = k_ref[z, i + 1, :, part] if i < s - 1 else turn(k_ref[z, 0, :, part], -1, 0)
        nbz = k_ref[z + 1, i, :, part]
        nb = jnp.where(first, nbx, jnp.where(second, nby, nbz))
        w = (2.0 * lv.spacing) * k * nb / (k + nb)
        bad = edge_x | (second & (yo * s + i >= lv.width - 1))
        w = jnp.where(bad, 0.0, w)
        high = w.astype(BF16).astype(F32)
        low = w - high
        near, wrap = turn(low, 40), turn(low, 48)
        return (
            jnp.where(first, high, near),
            jnp.where(third, near, high),
            jnp.where(third, high, wrap),
        )

    def planes(t, _):
        units = [(2 * t + n, i) for n in range(2) for i in range(s)]
        for p in range(s):
            for c in range(COLUMNS):
                up, down = one(*units[2 * p], c), one(*units[2 * p + 1], c)
                for m in range(3):
                    both = jnp.concatenate([up[m], down[m]], axis=0).astype(BF16)
                    lhs_refs[m][t * s + p, :, c * LANES : (c + 1) * LANES] = both
        return 0

    lax.fori_loop(0, lv.planes // 2, planes, 0)
    rows = lv.planes * s * SUBS
    shape = (2 * LANES, 2 * LANES)
    row = lax.broadcasted_iota(jnp.int32, shape, 0)
    lane = lax.broadcasted_iota(jnp.int32, (1, 2 * LANES), 1)
    xo = lane % 8
    upper = lane // LANES
    for q in range(-(-s // 2)):
        x = xo * s + 2 * q + upper
        for m in range(3):
            source = lane // 8 % 2 * LANES + lv.step * x
            valid = (x < lv.width) & (2 * q + upper < s)
            high = jnp.where(valid, source + m * 40, -1)
            low = jnp.where(valid, source + (m + 1) % 3 * 40, -1)
            pick = ((row == high) | (row == low)).astype(F32).astype(BF16)
            lhs = lhs_refs[m][...].reshape(rows, 2 * LANES)
            out = jnp.dot(lhs, pick, preferred_element_type=F32)
            for half in range(min(2, s - 2 * q)):
                part = out[:, half * LANES : (half + 1) * LANES]
                w_refs[m][2 * q + half] = part.reshape(lv.planes * s, SUBS, LANES)


class Case:
    def __init__(self, lv, cs, e, w_refs, fields, fz_ref):
        self.lv, self.cs, self.e, self.w_refs = lv, cs, e, w_refs
        self.d, self.q, self.r, self.fz = fields[:3], fields[3], fields[4], fz_ref

    def weights(self, plane):
        s = self.lv.seg
        return lambda m, i, j: self.w_refs[m][i, plane * s + j]


def looped(cases, count, group, begin, step):
    zero = jnp.zeros((SUBS, LANES), F32)
    counts = [begin(case) for case in cases]
    start = tuple(zero for n in counts for _ in range(n))

    def body(t, sums):
        sums = list(sums)
        at = 0
        for case, n in zip(cases, counts):
            got = step(case, t * group)
            for k in range(n):
                sums[at + k] = sums[at + k] + got[k]
            at += n
        return tuple(sums)

    if count == group:
        sums = body(0, start)
    else:
        sums = lax.fori_loop(0, count // group, body, start)
    out, at = [], 0
    for n in counts:
        out.append(sums[at : at + n])
        at += n
    return out


def start_residual(cases, group):
    lv, cs, s = cases[0].lv, cases[0].cs, cases[0].lv.seg

    def step(case, z0):
        total = []
        for z in [z0 + n for n in range(group)]:
            pz = lv.base(case.e) + z
            get = case.weights(pz)
            below = case.weights(jnp.maximum(pz - 1, 0))
            gz = cs.fz(z + 1)
            along_x = [cs.sx * gz * cs.fy[j] for j in range(s)]
            along_y = [cs.sy * gz * cs.fx[i] for i in range(s)]
            last = [get(1, i, s - 1) * along_y[i] for i in range(s)]
            before = [turn(v, 1, 0) for v in last]
            for j in range(s):
                flux_y = last if j == s - 1 else [get(1, i, j) * along_y[i] for i in range(s)]
                flux_x = [get(0, i, j) * along_x[j] for i in range(s)]
                squares = []
                for i in range(s):
                    prev_x = flux_x[i - 1] if i else turn(flux_x[s - 1], 1)
                    along_z = cs.sz * cs.fx[i] * cs.fy[j]
                    value = (prev_x - flux_x[i]) + (before[i] - flux_y[i])
                    value = value + along_z * (below(2, i, j) - get(2, i, j))
                    value = cs.masked(value, i, j, 0)
                    case.d[0][z, i * s + j] = value
                    squares.append(value * value)
                total.append(tree(squares))
                before = flux_y
        return [tree(total)]

    return [part[0] for part in looped(cases, lv.inner, group, lambda case: 1, step)]


def fluxes(case, get, u, j, last):
    s = case.lv.seg
    jump_y = []
    for i in range(s):
        after = u[i * s + j + 1] if j < s - 1 else turn(u[i * s], -1, 0)
        jump_y.append(u[i * s + j] - after)
    flux_y = last if last is not None else [get(1, i, j) * jump_y[i] for i in range(s)]
    jump_x = []
    for i in range(s):
        after = u[(i + 1) * s + j] if i < s - 1 else turn(u[j], -1)
        jump_x.append(u[i * s + j] - after)
    flux_x = [get(0, i, j) * jump_x[i] for i in range(s)]
    return flux_x, flux_y, jump_x, jump_y


def last_row(case, get, u):
    s = case.lv.seg
    return [get(1, i, s - 1) * (u[i * s + s - 1] - turn(u[i * s], -1, 0)) for i in range(s)]


def apply(cases, group, number, betas):
    lv, cs, s = cases[0].lv, cases[0].cs, cases[0].lv.seg
    keep = number < 2

    def fresh(case, z, k):
        if number == 0:
            return case.d[0][z, k]
        value = case.r[z, k] + betas[case.e] * case.d[number - 1][z, k]
        case.d[number][z, k] = value
        return value

    firsts = []
    for case in cases:
        get = case.weights(max(lv.base(case.e) - 1, 0))
        terms = []
        for k in range(lv.tiles):
            value = fresh(case, 0, k)
            flux = -get(2, k // s, k % s) * value
            if keep:
                case.fz[k] = flux
            else:
                terms.append(-flux * value)
        firsts.append(tree(terms) if terms else 0.0)

    def step(case, z0):
        total = []
        u = [case.d[number][z0, k] for k in range(lv.tiles)]
        flux_z = [case.fz[k] for k in range(lv.tiles)] if keep else None
        for z in [z0 + n for n in range(group)]:
            get = case.weights(lv.base(case.e) + z)
            after = [None] * lv.tiles
            if keep:
                last = last_row(case, get, u)
                before = [turn(v, 1, 0) for v in last]
            for j in range(s):
                flux_x, flux_y, jump_x, jump_y = fluxes(case, get, u, j, last if keep and j == s - 1 else None)
                terms = []
                for i in range(s):
                    k = i * s + j
                    after[k] = fresh(case, z + 1, k)
                    jump = u[k] - after[k]
                    flux = get(2, i, j) * jump
                    if keep:
                        prev_x = flux_x[i - 1] if i else turn(flux_x[s - 1], 1)
                        value = (flux_x[i] - prev_x) + (flux_y[i] - before[i]) + (flux - flux_z[k])
                        flux_z[k] = flux
                        value = cs.masked(value, i, j, 0)
                        case.q[z, k] = value
                        terms.append(u[k] * value)
                    else:
                        terms.append((flux * jump + flux_x[i] * jump_x[i]) + flux_y[i] * jump_y[i])
                before = flux_y
                total.append(tree(terms))
            u = after
        if keep:
            for k in range(lv.tiles):
                case.fz[k] = flux_z[k]
        return [tree(total)]

    sums = looped(cases, lv.inner, group, lambda case: 1, step)
    return [part[0] + first for part, first in zip(sums, firsts)]


def reduce_residual(cases, group, number, alphas):
    lv = cases[0].lv

    def step(case, z0):
        total = []
        source = case.d[0] if number == 0 else case.r
        for z in [z0 + n for n in range(group)]:
            squares = []
            for k in range(lv.tiles):
                value = source[z, k] - alphas[case.e] * case.q[z, k]
                case.r[z, k] = value
                squares.append(value * value)
            total.append(tree(squares))
        return [tree(total)]

    return [part[0] for part in looped(cases, lv.inner, group, lambda case: 1, step)]


def finish(cases, group, alphas, phi_ref):
    lv, cs, s = cases[0].lv, cases[0].cs, cases[0].lv.seg
    even = (cs.az == 0).astype(F32)
    zero = jnp.zeros((SUBS, LANES), F32)

    def place(case, z, k):
        return pl.ds(pl.multiple_of(((case.e * lv.edz + z) * lv.tiles + k) * SUBS, SUBS), SUBS)

    def fresh(case, z, i, j, gz):
        k = i * s + j
        inner = z + lv.mz - 1
        value = cs.fx[i] * cs.fy[j] * gz
        for alpha, d_ref in zip(alphas[case.e], case.d):
            value = value + alpha * d_ref[inner, k]
        value = cs.masked(value, i, j, 1)
        phi_ref[place(case, z, k), :] = value
        return value

    for case in cases:
        gz = cs.fz(lv.mz)
        for i in range(s):
            for j in range(s):
                fresh(case, 0, i, j, gz)
                case.fz[i * s + j] = zero

    def step(case, z0):
        sums = [[] for _ in range(4 if case.e == 0 else 3)]
        u = [phi_ref[place(case, z0, k), :] for k in range(lv.tiles)]
        flux_z = [case.fz[k] for k in range(lv.tiles)]
        for z in [z0 + n for n in range(group)]:
            get = case.weights(lv.base(case.e) + lv.mz - 1 + z)
            up = jnp.minimum(z + 1, lv.edz - 1)
            gz = cs.fz(up + lv.mz)
            after = [None] * lv.tiles

            def cut(values, table):
                return [v if f is None else v * f for v, f in zip(values, table)]

            last = cut(last_row(case, get, u), [cs.facey[s - 1]] * s)
            before = [turn(v, 1, 0) for v in last]
            for j in range(s):
                flux_x, flux_y, _, _ = fluxes(case, get, u, j, last if j == s - 1 else None)
                flux_x = cut(flux_x, cs.facex)
                if j < s - 1:
                    flux_y = cut(flux_y, [cs.facey[j]] * s)
                parts = [[] for _ in sums]
                for i in range(s):
                    k = i * s + j
                    after[k] = fresh(case, up, i, j, gz)
                    flux = get(2, i, j) * (u[k] - after[k])
                    prev_x = flux_x[i - 1] if i else turn(flux_x[s - 1], 1)
                    value = (flux_x[i] - prev_x) + (flux_y[i] - before[i]) + (flux - flux_z[k])
                    flux_z[k] = flux
                    parts[0].append(value * u[k])
                    parts[1].append(value * turn(u[k], -32))
                    parts[2].append(value * turn(u[k], 64))
                    if case.e == 0:
                        low = u[k] * even
                        low = low + turn(low, 32)
                        low = low + turn(low, 64)
                        parts[3].append(value * turn(low, 16))
                for total, part in zip(sums, parts):
                    total.append(tree(part))
                before = flux_y
            u = after
        for k in range(lv.tiles):
            case.fz[k] = flux_z[k]
        return [tree(total) for total in sums]

    return looped(cases, lv.edz, group, lambda case: 4 if case.e == 0 else 3, step)


GROUPS = {FINE: 2, TWIN: 8}


def solve_kernel(
    center, x_low, x_high, y_low, y_high,
    phi_fine, phi_twin, message,
    flat, rows, pairs, twin_rows, *refs,
):
    lanes = center.shape[2]
    rim = (flat.shape[1] - lanes) // 2
    nx = center.shape[1]
    top = MX + nx
    for m in range(3):
        off = m * (nx + 2 * MX)
        flat[off : off + top + MX, :rim] = y_low[m]
        flat[off : off + MX, rim : rim + lanes] = x_low[m]
        flat[off + MX : off + top, rim : rim + lanes] = center[m]
        flat[off + top : off + top + MX, rim : rim + lanes] = x_high[m]
        flat[off : off + top + MX, rim + lanes :] = y_high[m]
    used = 3 * (nx + 2 * MX)
    flat[used:, :] = jnp.ones((LANES - used, flat.shape[1]), F32)
    for t in range(flat.shape[1] // LANES):
        rows[t * LANES : (t + 1) * LANES, :] = flat[:, t * LANES : (t + 1) * LANES].T

    nz = EZ * ELZ
    twin_y = rows.shape[0] // nz // 2
    for y in range(twin_y):
        both = rows[2 * y * nz : (2 * y + 1) * nz, :] + rows[(2 * y + 1) * nz : (2 * y + 2) * nz, :]
        both = both + turn(both, -1)
        at = y * nz
        pairs[at : at + nz, :] = both
        twin_rows[at : at + 8, :] = jnp.broadcast_to(0.25 * both[0:1], (8, LANES))
        twin_rows[at + 8 + nz // 2 : at + nz, :] = jnp.broadcast_to(0.25 * both[nz - 1 : nz], (8, LANES))
    for y in range(twin_y):
        at = y * nz
        middle = pairs[pl.ds(at, nz // 2, stride=2), :] + pairs[pl.ds(at + 1, nz // 2, stride=2), :]
        twin_rows[at + 8 : at + 8 + nz // 2, :] = 0.125 * middle
    twin_rows[twin_y * nz :, :] = jnp.ones((twin_rows.shape[0] - twin_y * nz, LANES), F32)

    refs = list(refs)

    def take(count):
        got = refs[:count]
        del refs[:count]
        return got

    groups = []
    for lv, source in zip(LEVELS, (rows, twin_rows)):
        (k_ref,) = take(1)
        lhs_refs, w_refs = take(3), take(3)
        for z in range(lv.planes + 1):
            cell = min(max(z - 1, 0), nz - 1) if lv is FINE else min(z, lv.planes - 1) + 7
            for i in range(lv.seg):
                for c in range(COLUMNS):
                    start = (lv.edge * c + i) * nz + cell
                    k_ref[z, i, :, c * LANES : (c + 1) * LANES] = source[pl.ds(start, SUBS, stride=lv.seg * nz), :]
        spread_weights(lv, k_ref, lhs_refs, w_refs)
        cs = Consts(lv)
        cases = []
        for e in range(EZ):
            fields = take(5)
            (fz_ref,) = take(1)
            case = Case(lv, cs, e, w_refs, fields, fz_ref)
            for k in range(lv.tiles):
                case.d[0][lv.inner, k] = jnp.zeros((SUBS, LANES), F32)
                case.r[lv.inner, k] = jnp.zeros((SUBS, LANES), F32)
            cases.append(case)
        groups.append(cases)

    def both_levels(work):
        sums = [work(n, cases, GROUPS[cases[0].lv]) for n, cases in enumerate(groups)]
        return [[problem_sum(v) for v in part] for part in sums]

    rr = both_levels(lambda n, cases, group: start_residual(cases, group))
    alphas = [[[] for _ in range(EZ)] for _ in LEVELS]
    betas = [None] * len(LEVELS)
    for step in range(3):
        dots = both_levels(lambda n, cases, group: apply(cases, group, step, betas[n]))
        now = [[a / b for a, b in zip(rr[n], dots[n])] for n in range(len(LEVELS))]
        for n in range(len(LEVELS)):
            for e in range(EZ):
                alphas[n][e].append(now[n][e])
        if step < 2:
            new = both_levels(lambda n, cases, group: reduce_residual(cases, group, step, now[n]))
            betas = [[a / b for a, b in zip(new[n], rr[n])] for n in range(len(LEVELS))]
            rr = new

    phis = (phi_fine, phi_twin)
    totals = [finish(cases, GROUPS[cases[0].lv], alphas[n], phis[n]) for n, cases in enumerate(groups)]
    totals = [[[problem_sum(v) for v in part] for part in level] for level in totals]
    basis, xo, _ = lane_parts()
    packed = []
    for low, high in totals:
        parts = [turn(low[q], -16) + high[q] for q in range(3)] + [turn(low[3], -16)]
        packed.append(
            jnp.where(xo == 0, parts[0], jnp.where(xo == 1, parts[1], jnp.where(xo == 2, parts[2], parts[3])))
        )
    row = jnp.where(basis % 2 == 0, packed[0], turn(packed[1], 16))
    for r in range(0, message.shape[0], SUBS):
        message[r : r + SUBS, :] = row


def coarse_nodes(gathered, gy_count, me):
    total_rows = gathered.shape[0]
    shape = gathered.shape
    lane = lane_iota(shape)
    row = sub_iota(shape)
    corner = lane // 32
    column = lane // 8 % 2
    last = row % gy_count == gy_count - 1
    start = row % gy_count == 0
    one = gathered
    two = turn(gathered, -1)
    four = turn(gathered, -2)
    rhs = turn(gathered, -3)
    two_back = turn(two, 32)

    def next_x(u):
        return turn(u, -gy_count, 0)

    def prev_x(u):
        return turn(u, gy_count, 0)

    def next_y(u):
        ahead = jnp.where(last, turn(u, gy_count - 1, 0), turn(u, -1, 0))
        return jnp.where(column == 0, turn(u, -8), turn(ahead, 8))

    def prev_y(u):
        behind = jnp.where(start, turn(u, 1 - gy_count, 0), turn(u, 1, 0))
        return jnp.where(column == 1, turn(u, 8), turn(behind, -8))

    def by_corner(a, b, c, d):
        return jnp.where(corner == 0, a, jnp.where(corner == 1, b, jnp.where(corner == 2, c, d)))

    def corners(u):
        ux = next_x(u)
        return by_corner(u, next_y(u), ux, next_y(ux))

    def assemble(v):
        vx = prev_x(v)
        w = by_corner(v, prev_y(v), vx, prev_y(vx))
        w = w + turn(w, 64)
        return w + turn(w, 32)

    def operate(u):
        c = corners(u)
        return assemble(one * c + two * turn(c, -32) + two_back * turn(c, 32) + four * turn(c, 64))

    def total(a, b):
        v = a * b
        v = tree([v[r : r + SUBS] for r in range(0, total_rows, SUBS)])
        for shift in (4, 2, 1):
            v = v + turn(v, shift, 0)
        v = v + xor_lane(v, 8)
        return v[0:1]

    residual = -assemble(rhs)
    direction = residual
    update = jnp.zeros_like(residual)
    now = total(residual, residual)
    for step in range(2):
        image = operate(direction)
        alpha = now / total(direction, image)
        update = update + alpha * direction
        if step == 0:
            residual = residual - alpha * image
            new = total(residual, residual)
            direction = residual + new / now * direction
            now = new
    mine = jnp.where(row == me, corners(update), 0.0)
    mine = jnp.sum(mine, axis=0, keepdims=True)
    return jnp.broadcast_to(mine, (SUBS, LANES))


def turn_kernel(phi_fine, phi_twin, fine_out, twin_out):
    for lv, phi_ref, out_ref in ((FINE, phi_fine, fine_out), (TWIN, phi_twin, twin_out)):
        s = lv.seg
        nz = EZ * lv.edz
        per = LANES // nz
        tiles = lv.edge // per
        for i in range(s):
            for t in range(tiles):
                parts = []
                for n in range(per):
                    y = lv.mx + t * per + n
                    start = (i * s + y % s) * SUBS + y // s
                    parts.append(phi_ref[pl.ds(start, nz, stride=lv.tiles * SUBS), :])
                out_ref[i * tiles + t] = jnp.concatenate(parts, axis=0).T


def pressure_kernel(gy_count, me_ref, gathered, fine_turned, twin_turned, fine_out, twin_out, fine_all, twin_all):
    mine = coarse_nodes(gathered[...], gy_count, me_ref[0])
    for n, (lv, turned, out_ref, all_ref) in enumerate(
        ((FINE, fine_turned, fine_out, fine_all), (TWIN, twin_turned, twin_out, twin_all))
    ):
        s = lv.seg
        nz = EZ * lv.edz
        tiles = lv.edge * nz // LANES
        lower = lane_iota() % nz < lv.edz
        scales = {}
        for c in range(COLUMNS):
            for p in range(4):
                at = p * 32 + n * 16 + c * 8
                node = jnp.broadcast_to(mine[:, at : at + 1], (SUBS, LANES))
                scales[2 * p, c] = jnp.where(lower, 1.0, node)
                scales[2 * p + 1, c] = jnp.where(lower, node, 0.0)
        for c in range(COLUMNS):
            for t in range(tiles):
                at = (c * tiles + t) * LANES
                for i in range(s):
                    value = tree(
                        [turned[i * tiles + t, a * 16 + c * 8 : a * 16 + c * 8 + 8, :] * scales[a, c] for a in range(8)]
                    )
                    all_ref[c * tiles + t, pl.ds(i, SUBS, stride=s), :] = value
                out_ref[:, at : at + LANES] = all_ref[c * tiles + t, lv.mx : lv.mx + lv.edge, :]


def vmem(shape, dtype=F32):
    return pltpu.VMEM(shape, dtype)


def shards(permeability):
    nz = EZ * ELZ
    rows = permeability.shape[1]
    lanes = permeability.shape[2]
    assert rows == EL and lanes == COLUMNS * EL * nz
    rim = MX * nz
    gx, gy = lax.axis_size("gx"), lax.axis_size("gy")

    def sent(value, axis, shift):
        count = lax.axis_size(axis)
        return lax.ppermute(value, axis, [(i, (i + shift) % count) for i in range(count)])

    x_low = sent(permeability[:, rows - MX :], "gx", 1)
    x_high = sent(permeability[:, :MX], "gx", -1)

    def strip(part):
        return jnp.concatenate([x_low[:, :, part], permeability[:, :, part], x_high[:, :, part]], axis=1)

    y_low = sent(strip(slice(lanes - rim, lanes)), "gy", 1)
    y_high = sent(strip(slice(0, rim)), "gy", -1)
    halos = [x_low, x_high, y_low, y_high]
    flat_lanes = lanes + 2 * rim
    scratch = [
        vmem((LANES, flat_lanes)),
        vmem((flat_lanes, LANES)),
        vmem((flat_lanes // 2, LANES)),
        vmem((SUBS * (TWIN.seg + 2) * nz, LANES)),
    ]
    for lv in LEVELS:
        scratch.append(vmem((lv.planes + 1, lv.seg, SUBS, 2 * LANES)))
        scratch += [vmem((lv.planes * lv.seg // 2, 2 * SUBS, 2 * LANES), BF16)] * 3
        scratch += [vmem((lv.seg, lv.planes * lv.seg, SUBS, LANES))] * 3
        for e in range(EZ):
            scratch += [vmem((lv.inner + 1, lv.tiles, SUBS, LANES))] * 5
            scratch.append(vmem((lv.tiles, SUBS, LANES)))
    full = pl.BlockSpec(memory_space=pltpu.VMEM)
    phi_shapes = [
        jax.ShapeDtypeStruct((EZ * lv.edz * lv.tiles * SUBS, LANES), F32) for lv in LEVELS
    ]
    phi_fine, phi_twin, message = pl.pallas_call(
        solve_kernel,
        out_shape=phi_shapes + [jax.ShapeDtypeStruct((gx * gy, LANES), F32)],
        in_specs=[full] * 5,
        out_specs=[full] * 3,
        scratch_shapes=scratch,
        compiler_params=pltpu.CompilerParams(vmem_limit_bytes=52 * 1024 * 1024),
        name="solve",
    )(permeability, *halos)
    gathered = lax.all_to_all(message, ("gx", "gy"), 0, 0, tiled=True)
    turned = pl.pallas_call(
        turn_kernel,
        out_shape=[
            jax.ShapeDtypeStruct((lv.seg * lv.edge * EZ * lv.edz // LANES, LANES, LANES), F32) for lv in LEVELS
        ],
        in_specs=[full] * 2,
        out_specs=[full] * 2,
        compiler_params=pltpu.CompilerParams(vmem_limit_bytes=16 * 1024 * 1024),
        cost_estimate=pl.CostEstimate(flops=4000000, bytes_accessed=8000000, transcendentals=0),
        name="turned",
    )(phi_fine, phi_twin)
    me = (lax.axis_index("gx") * gy + lax.axis_index("gy")).astype(jnp.int32).reshape(1)
    return tuple(
        pl.pallas_call(
            functools.partial(pressure_kernel, gy),
            out_shape=[
                jax.ShapeDtypeStruct((lv.edge, COLUMNS * lv.edge * EZ * lv.edz), F32) for lv in LEVELS
            ],
            in_specs=[pl.BlockSpec(memory_space=pltpu.SMEM)] + [full] * 3,
            out_specs=[full] * 2,
            scratch_shapes=[vmem((COLUMNS * lv.edge * EZ * lv.edz // LANES, SUBS * lv.seg, LANES)) for lv in LEVELS],
            compiler_params=pltpu.CompilerParams(vmem_limit_bytes=16 * 1024 * 1024),
            name="pressure",
        )(me, gathered, *turned)
    )


def solution(mesh):
    return jax.shard_map(
        shards,
        mesh=mesh,
        in_specs=(P(None, "gx", "gy"),),
        out_specs=(P("gx", "gy"), P("gx", "gy")),
        check_vma=False,
    )
```

```python
import functools
import typing

import jax
import jax.numpy as jnp
from jax import lax
from jax.experimental import pallas as pl
from jax.experimental.pallas import tpu as pltpu
from jax.sharding import PartitionSpec as P

EL = 32
ELZ = 16
MX = 4
MZ = 2
EZ = 2
LANES = 128
SUBS = 8
COLUMNS = 2
F32 = jnp.float32
BF16 = jnp.bfloat16


class Level(typing.NamedTuple):
    edge: int
    edz: int
    mx: int
    mz: int
    spacing: float
    step: int

    @property
    def width(self):
        return self.edge + 2 * self.mx

    @property
    def inner(self):
        return self.edz + 2 * self.mz - 2

    @property
    def seg(self):
        return -(-self.width // SUBS)

    @property
    def tiles(self):
        return self.seg * self.seg

    @property
    def levels(self):
        return EZ * self.edz + 2

    @property
    def planes(self):
        return -(-(self.inner + 1) // 2) * 2


FINE = Level(EL, ELZ, MX, MZ, 1.0, 1)
TWIN = Level(EL // 2, ELZ // 2, MX // 2, MZ // 2, 2.0, 2)
LEVELS = (FINE, TWIN)


def lane_iota(shape=(SUBS, LANES)):
    return lax.broadcasted_iota(jnp.int32, shape, len(shape) - 1)


def sub_iota(shape=(SUBS, LANES)):
    return lax.broadcasted_iota(jnp.int32, shape, len(shape) - 2)


def turn(value, shift, axis=1):
    return pltpu.roll(value, shift % value.shape[axis], axis)


def lane_parts():
    lane = lane_iota()
    return lane // 32, lane // 16 % 2, lane // 8 % 2, lane % 8


class Consts:
    def __init__(self, lv):
        corner, _, _, xo = lane_parts()
        yo = sub_iota()
        ax, ay = corner // 2, corner % 2
        self.lv = lv
        s = lv.seg
        self.fx, self.fy = [], []
        self.inx, self.iny, self.facex, self.facey = [], [], [], []
        for i in range(s):
            x = xo * s + i
            y = yo * s + i
            px = (x.astype(F32) - lv.mx + 0.5) / lv.edge
            py = (y.astype(F32) - lv.mx + 0.5) / lv.edge
            self.fx.append(jnp.where(ax == 1, px, 1.0 - px))
            self.fy.append(jnp.where(ay == 1, py, 1.0 - py))
            xs = [s * o + i for o in range(SUBS)]

            def ranged(value, low, high):
                if all(low <= v <= high for v in xs):
                    return None
                return ((value >= low) & (value <= high)).astype(F32)

            self.inx.append((ranged(x, 1, lv.width - 2), ranged(x, lv.mx, lv.mx + lv.edge - 1)))
            self.iny.append((ranged(y, 1, lv.width - 2), ranged(y, lv.mx, lv.mx + lv.edge - 1)))
            cut = (lv.mx - 1, lv.mx + lv.edge - 1)
            self.facex.append(((x != cut[0]) & (x != cut[1])).astype(F32) if any(v in cut for v in xs) else None)
            self.facey.append(((y != cut[0]) & (y != cut[1])).astype(F32) if any(v in cut for v in xs) else None)
        sx = jnp.where(ax == 1, -1.0 / lv.edge, 1.0 / lv.edge).astype(F32)
        sy = jnp.where(ay == 1, -1.0 / lv.edge, 1.0 / lv.edge).astype(F32)
        self.along_x = [sx * f for f in self.fy]
        self.along_y = [sy * f for f in self.fx]

    def fz(self, plane):
        place = (jnp.asarray(plane, jnp.int32).astype(F32) - self.lv.mz + 0.5) / self.lv.edz
        return 1.0 - place, place

    def masked(self, value, i, j, kind):
        for table, index in ((self.inx, i), (self.iny, j)):
            factor = table[index][kind]
            if factor is not None:
                value = value * factor
        return value


def tree(values):
    values = list(values)
    while len(values) > 1:
        values = [a + b for a, b in zip(values[::2], values[1::2])] + (
            [values[-1]] if len(values) % 2 else []
        )
    return values[0]


def xor_lane(value, bit):
    return jnp.where(lane_iota(value.shape) // bit % 2 == 1, turn(value, bit), turn(value, -bit))


def problem_sum(value):
    for shift in (4, 2, 1):
        value = value + turn(value, shift, 0)
    for bit in (1, 2, 4):
        value = value + xor_lane(value, bit)
    return value


def spread_weights(lv, k_ref, high_refs, low_refs, w_refs):
    s = lv.seg
    wide = (SUBS, LANES)
    pos = lane_iota(wide)
    yo = sub_iota(wide)
    first = pos < 40
    third = pos >= 80
    second = (pos >= 40) & (pos < 80)
    edge_x = first & (pos >= (lv.width - 1) * lv.step)

    def one(z, i, c):
        part = slice(c * LANES, (c + 1) * LANES)
        k = k_ref[z, i, :, part]
        nbx = turn(k, -lv.step)
        nby = k_ref[z, i + 1, :, part] if i < s - 1 else turn(k_ref[z, 0, :, part], -1, 0)
        nbz = k_ref[z + 1, i, :, part]
        nb = jnp.where(first, nbx, jnp.where(second, nby, nbz))
        w = (2.0 * lv.spacing) * k * nb / (k + nb)
        bad = edge_x | (second & (yo * s + i >= lv.width - 1))
        return jnp.where(bad, 0.0, w)

    def planes(t, _):
        units = [(2 * t + n, i) for n in range(2) for i in range(s)]
        for e in range(EZ):
            made = []
            for plane, i in units:
                z = jnp.clip(e * lv.edz + plane + 1 - lv.mz, 0, lv.levels - 1)
                w0, w1 = one(z, i, 0), one(z, i, 1)
                near, wrap = turn(w1, 40), turn(w1, 48)
                made.append((jnp.where(first, w0, near), jnp.where(third, near, w0), jnp.where(third, w0, wrap)))
            for p in range(s):
                for m in range(3):
                    both = jnp.concatenate([made[2 * p][m], made[2 * p + 1][m]], axis=0)
                    high = both.astype(BF16)
                    part = slice(e * LANES, (e + 1) * LANES)
                    high_refs[m][t * s + p, :, part] = high
                    low_refs[m][t * s + p, :, part] = (both - high.astype(F32)).astype(BF16)
        return 0

    lax.fori_loop(0, lv.planes // 2, planes, 0)
    rows = lv.planes * s * SUBS
    row = lax.broadcasted_iota(jnp.int32, (2 * LANES, 2 * LANES), 0)
    lane = lax.broadcasted_iota(jnp.int32, (1, 2 * LANES), 1)
    upper = lane // LANES
    for q in range(-(-s // 2)):
        x = lane % 8 * s + 2 * q + upper
        valid = (x < lv.width) & (2 * q + upper < s)
        for m in range(3):
            segment = jnp.where(lane // 8 % 2 == 0, m, (m + 1) % 3)
            source = jnp.where(valid, lane // 16 % 2 * LANES + segment * 40 + lv.step * x, -1)
            pick = (row == source).astype(F32).astype(BF16)
            out = jnp.dot(high_refs[m][...].reshape(rows, 2 * LANES), pick, preferred_element_type=F32)
            out = out + jnp.dot(low_refs[m][...].reshape(rows, 2 * LANES), pick, preferred_element_type=F32)
            for half in range(min(2, s - 2 * q)):
                part = out[:, half * LANES : (half + 1) * LANES]
                w_refs[m][2 * q + half] = part.reshape(lv.planes * s, SUBS, LANES)


class Case:
    def __init__(self, lv, w_refs, fields, planes):
        self.lv, self.cs, self.w_refs = lv, Consts(lv), w_refs
        self.d, self.q, self.r = fields[:3], fields[3], fields[4]
        self.fz, self.chosen, self.total = planes

    def weights(self, plane):
        s = self.lv.seg
        return lambda m, i, j: self.w_refs[m][i, plane * s + j]


HALVES = (0, 1)


def looped(count, group, sums, step):
    def body(t, sums):
        return tuple(a + b for a, b in zip(sums, step(t * group)))

    start = tuple(jnp.zeros((SUBS, LANES), F32) for _ in range(sums))
    return list(lax.fori_loop(0, count // group, body, start))


def start_residual(case, group):
    lv, cs, s = case.lv, case.cs, case.lv.seg

    def step(z0):
        total = [[], []]
        for z in [z0 + n for n in range(group)]:
            get, below = case.weights(z + 1), case.weights(z)
            gz = cs.fz(z + 1)
            last = [get(1, i, s - 1) * cs.along_y[i] for i in range(s)]
            before = [turn(v, 1, 0) for v in last]
            for j in range(s):
                flux_y = last if j == s - 1 else [get(1, i, j) * cs.along_y[i] for i in range(s)]
                flux_x = [get(0, i, j) * cs.along_x[j] for i in range(s)]
                squares = [[], []]
                for i in range(s):
                    k = i * s + j
                    prev_x = flux_x[i - 1] if i else turn(flux_x[s - 1], 1)
                    flat = (prev_x - flux_x[i]) + (before[i] - flux_y[i])
                    flat = cs.masked(flat, i, j, 0)
                    tall = (cs.fx[i] * cs.fy[j]) * (1.0 / lv.edz) * (below(2, i, j) - get(2, i, j))
                    tall = cs.masked(tall, i, j, 0)
                    for h, value in enumerate((flat * gz[0] + tall, flat * gz[1] - tall)):
                        case.d[0][z, h * lv.tiles + k] = value
                        squares[h].append(value * value)
                for h in HALVES:
                    total[h].append(tree(squares[h]))
                before = flux_y
        return [tree(t) for t in total]

    return looped(lv.inner, group, 2, step)


def row_jumps(u, s, j):
    jump_x = [u[i * s + j] - (u[(i + 1) * s + j] if i < s - 1 else turn(u[j], -1)) for i in range(s)]
    jump_y = [u[i * s + j] - (u[i * s + j + 1] if j < s - 1 else turn(u[i * s], -1, 0)) for i in range(s)]
    return jump_x, jump_y


def apply(case, group, number, betas):
    lv, cs, s = case.lv, case.cs, case.lv.seg
    keep = number < 2
    n = lv.tiles

    def fresh(z, h, k):
        at = h * n + k
        if number == 0:
            return case.d[0][z, at]
        value = case.r[z, at] + betas[h] * case.d[number - 1][z, at]
        case.d[number][z, at] = value
        return value

    firsts = []
    get = case.weights(0)
    for h in HALVES:
        terms = []
        for k in range(n):
            value = fresh(0, h, k)
            flux = -get(2, k // s, k % s) * value
            if keep:
                case.fz[h * n + k] = flux
            else:
                terms.append(-flux * value)
        firsts.append(tree(terms) if terms else 0.0)

    def step(z0):
        total = [[], []]
        u = [[case.d[number][z0, h * n + k] for k in range(n)] for h in HALVES]
        flux_z = [[case.fz[h * n + k] for k in range(n)] for h in HALVES] if keep else None
        for z in [z0 + t for t in range(group)]:
            get = case.weights(z + 1)
            after = [[None] * n for _ in HALVES]
            if keep:
                wy = [get(1, i, s - 1) for i in range(s)]
                last = [[wy[i] * (u[h][i * s + s - 1] - turn(u[h][i * s], -1, 0)) for i in range(s)] for h in HALVES]
                before = [[turn(v, 1, 0) for v in last[h]] for h in HALVES]
            for j in range(s):
                wx = [get(0, i, j) for i in range(s)]
                wy = [get(1, i, j) for i in range(s)]
                wz = [get(2, i, j) for i in range(s)]
                for h in HALVES:
                    jump_x, jump_y = row_jumps(u[h], s, j)
                    flux_x = [w * v for w, v in zip(wx, jump_x)]
                    flux_y = last[h] if keep and j == s - 1 else [w * v for w, v in zip(wy, jump_y)]
                    terms = []
                    for i in range(s):
                        k = i * s + j
                        after[h][k] = fresh(z + 1, h, k)
                        jump = u[h][k] - after[h][k]
                        flux = wz[i] * jump
                        if keep:
                            prev_x = flux_x[i - 1] if i else turn(flux_x[s - 1], 1)
                            value = (flux_x[i] - prev_x) + (flux_y[i] - before[h][i]) + (flux - flux_z[h][k])
                            flux_z[h][k] = flux
                            value = cs.masked(value, i, j, 0)
                            case.q[z, h * n + k] = value
                            terms.append(u[h][k] * value)
                        else:
                            terms.append((flux * jump + flux_x[i] * jump_x[i]) + flux_y[i] * jump_y[i])
                    total[h].append(tree(terms))
                    if keep:
                        before[h] = flux_y
            u = after
        if keep:
            for h in HALVES:
                for k in range(n):
                    case.fz[h * n + k] = flux_z[h][k]
        return [tree(t) for t in total]

    return [a + b for a, b in zip(looped(lv.inner, group, 2, step), firsts)]


def reduce_residual(case, group, number, alphas):
    lv = case.lv

    def step(z0):
        total = [[], []]
        source = case.d[0] if number == 0 else case.r
        for z in [z0 + n for n in range(group)]:
            for h in HALVES:
                squares = []
                for k in range(lv.tiles):
                    at = h * lv.tiles + k
                    value = source[z, at] - alphas[h] * case.q[z, at]
                    case.r[z, at] = value
                    squares.append(value * value)
                total[h].append(tree(squares))
        return [tree(t) for t in total]

    return looped(lv.inner, group, 2, step)


def finish(case, group, alphas, phi_ref):
    lv, cs, s = case.lv, case.cs, case.lv.seg
    n = lv.tiles
    lower = lane_parts()[1] == 0

    def fresh(z, i, j, gz):
        k = i * s + j
        inner = z + lv.mz - 1
        both = cs.fx[i] * cs.fy[j]
        values = []
        for h in HALVES:
            value = both * gz[h]
            for alpha, d_ref in zip(alphas[h], case.d):
                value = value + alpha * d_ref[inner, h * n + k]
            value = cs.masked(value, i, j, 1)
            at = pl.multiple_of(((z * 2 + h) * n + k) * SUBS, SUBS)
            phi_ref[pl.ds(at, SUBS), :] = value
            values.append(value)
        total = values[0] + turn(values[0], 32)
        return jnp.where(lower, values[1], values[0]), total + turn(total, 64)

    gz = cs.fz(lv.mz)
    for i in range(s):
        for j in range(s):
            k = i * s + j
            case.chosen[k], case.total[k] = fresh(0, i, j, gz)
            case.fz[k] = jnp.zeros((SUBS, LANES), F32)

    def cut(values, table):
        return [v if f is None else v * f for v, f in zip(values, table)]

    def step(z0):
        sums = [[] for _ in range(4)]
        u = [case.chosen[k] for k in range(n)]
        low = [case.total[k] for k in range(n)]
        flux_z = [case.fz[k] for k in range(n)]
        for z in [z0 + t for t in range(group)]:
            get = case.weights(z + lv.mz)
            up = jnp.minimum(z + 1, lv.edz - 1)
            gz = cs.fz(up + lv.mz)
            after, after_low = [None] * n, [None] * n
            last = [get(1, i, s - 1) * (u[i * s + s - 1] - turn(u[i * s], -1, 0)) for i in range(s)]
            last = cut(last, [cs.facey[s - 1]] * s)
            before = [turn(v, 1, 0) for v in last]
            for j in range(s):
                jump_x, jump_y = row_jumps(u, s, j)
                flux_x = cut([get(0, i, j) * jump_x[i] for i in range(s)], cs.facex)
                flux_y = last
                if j < s - 1:
                    flux_y = cut([get(1, i, j) * jump_y[i] for i in range(s)], [cs.facey[j]] * s)
                parts = [[] for _ in sums]
                for i in range(s):
                    k = i * s + j
                    after[k], after_low[k] = fresh(up, i, j, gz)
                    flux = get(2, i, j) * (u[k] - after[k])
                    prev_x = flux_x[i - 1] if i else turn(flux_x[s - 1], 1)
                    value = (flux_x[i] - prev_x) + (flux_y[i] - before[i]) + (flux - flux_z[k])
                    flux_z[k] = flux
                    parts[0].append(value * u[k])
                    parts[1].append(value * turn(u[k], -32))
                    parts[2].append(value * turn(u[k], 64))
                    parts[3].append(value * low[k])
                for total, part in zip(sums, parts):
                    total.append(tree(part))
                before = flux_y
            u, low = after, after_low
        for k in range(n):
            case.fz[k], case.chosen[k], case.total[k] = flux_z[k], u[k], low[k]
        return [tree(total) for total in sums]

    return looped(lv.edz, group, 4, step)


GROUPS = {FINE: 1, TWIN: 4}


def solve_kernel(
    center, x_low, x_high, y_low, y_high,
    phi_fine, phi_twin, message,
    flat, rows, pairs, twin_rows, *refs,
):
    lanes = center.shape[2]
    rim = (flat.shape[1] - lanes) // 2
    nx = center.shape[1]
    top = MX + nx
    for m in range(3):
        off = m * (nx + 2 * MX)
        flat[off : off + top + MX, :rim] = y_low[m]
        flat[off : off + MX, rim : rim + lanes] = x_low[m]
        flat[off + MX : off + top, rim : rim + lanes] = center[m]
        flat[off + top : off + top + MX, rim : rim + lanes] = x_high[m]
        flat[off : off + top + MX, rim + lanes :] = y_high[m]
    used = 3 * (nx + 2 * MX)
    flat[used:, :] = jnp.ones((LANES - used, flat.shape[1]), F32)
    for t in range(flat.shape[1] // LANES):
        rows[t * LANES : (t + 1) * LANES, :] = flat[:, t * LANES : (t + 1) * LANES].T

    nz = EZ * ELZ
    twin_y = rows.shape[0] // nz // 2
    for y in range(twin_y):
        both = rows[2 * y * nz : (2 * y + 1) * nz, :] + rows[(2 * y + 1) * nz : (2 * y + 2) * nz, :]
        both = both + turn(both, -1)
        at = y * nz
        pairs[at : at + nz, :] = both
        twin_rows[at : at + 8, :] = jnp.broadcast_to(0.25 * both[0:1], (8, LANES))
        twin_rows[at + 8 + nz // 2 : at + nz, :] = jnp.broadcast_to(0.25 * both[nz - 1 : nz], (8, LANES))
    for y in range(twin_y):
        at = y * nz
        middle = pairs[pl.ds(at, nz // 2, stride=2), :] + pairs[pl.ds(at + 1, nz // 2, stride=2), :]
        twin_rows[at + 8 : at + 8 + nz // 2, :] = 0.125 * middle
    twin_rows[twin_y * nz :, :] = jnp.ones((twin_rows.shape[0] - twin_y * nz, LANES), F32)

    refs = list(refs)

    def take(count):
        got = refs[:count]
        del refs[:count]
        return got

    cases = []
    for lv, source in zip(LEVELS, (rows, twin_rows)):
        (k_ref,) = take(1)
        high_refs, low_refs, w_refs = take(3), take(3), take(3)
        for z in range(lv.levels + 1):
            cell = min(max(z - 1, 0), nz - 1) if lv is FINE else min(z, lv.levels - 1) + 7
            for i in range(lv.seg):
                for c in range(COLUMNS):
                    start = (lv.edge * c + i) * nz + cell
                    k_ref[z, i, :, c * LANES : (c + 1) * LANES] = source[pl.ds(start, SUBS, stride=lv.seg * nz), :]
        spread_weights(lv, k_ref, high_refs, low_refs, w_refs)
        case = Case(lv, w_refs, take(5), take(3))
        for k in range(2 * lv.tiles):
            case.d[0][lv.inner, k] = jnp.zeros((SUBS, LANES), F32)
            case.r[lv.inner, k] = jnp.zeros((SUBS, LANES), F32)
        cases.append(case)

    def both_levels(work):
        sums = [work(n, case, GROUPS[case.lv]) for n, case in enumerate(cases)]
        return [[problem_sum(v) for v in part] for part in sums]

    rr = both_levels(lambda n, case, group: start_residual(case, group))
    alphas = [[[], []] for _ in LEVELS]
    betas = [None] * len(LEVELS)
    for step in range(3):
        dots = both_levels(lambda n, case, group: apply(case, group, step, betas[n]))
        now = [[a / b for a, b in zip(rr[n], dots[n])] for n in range(len(LEVELS))]
        for n in range(len(LEVELS)):
            for h in HALVES:
                alphas[n][h].append(now[n][h])
        if step < 2:
            new = both_levels(lambda n, case, group: reduce_residual(case, group, step, now[n]))
            betas = [[a / b for a, b in zip(new[n], rr[n])] for n in range(len(LEVELS))]
            rr = new

    phis = (phi_fine, phi_twin)
    totals = both_levels(lambda n, case, group: finish(case, group, alphas[n], phis[n]))
    _, element, _, slot = lane_parts()
    packed = []
    for level in totals:
        parts = [v + xor_lane(v, 16) for v in level[:3]]
        parts.append(jnp.where(element == 0, level[3], turn(level[3], 16)))
        packed.append(
            jnp.where(slot == 0, parts[0], jnp.where(slot == 1, parts[1], jnp.where(slot == 2, parts[2], parts[3])))
        )
    row = jnp.where(element == 0, packed[0], packed[1])
    for r in range(0, message.shape[0], SUBS):
        message[r : r + SUBS, :] = row


def coarse_nodes(gathered, gy_count, me):
    total_rows = gathered.shape[0]
    shape = gathered.shape
    lane = lane_iota(shape)
    row = sub_iota(shape)
    corner = lane // 32
    column = lane // 8 % 2
    last = row % gy_count == gy_count - 1
    start = row % gy_count == 0
    one = gathered
    two = turn(gathered, -1)
    four = turn(gathered, -2)
    rhs = turn(gathered, -3)
    two_back = turn(two, 32)

    def next_x(u):
        return turn(u, -gy_count, 0)

    def prev_x(u):
        return turn(u, gy_count, 0)

    def next_y(u):
        ahead = jnp.where(last, turn(u, gy_count - 1, 0), turn(u, -1, 0))
        return jnp.where(column == 0, turn(u, -8), turn(ahead, 8))

    def prev_y(u):
        behind = jnp.where(start, turn(u, 1 - gy_count, 0), turn(u, 1, 0))
        return jnp.where(column == 1, turn(u, 8), turn(behind, -8))

    def by_corner(a, b, c, d):
        return jnp.where(corner == 0, a, jnp.where(corner == 1, b, jnp.where(corner == 2, c, d)))

    def corners(u):
        ux = next_x(u)
        return by_corner(u, next_y(u), ux, next_y(ux))

    def assemble(v):
        vx = prev_x(v)
        w = by_corner(v, prev_y(v), vx, prev_y(vx))
        w = w + turn(w, 64)
        return w + turn(w, 32)

    def operate(u):
        c = corners(u)
        return assemble(one * c + two * turn(c, -32) + two_back * turn(c, 32) + four * turn(c, 64))

    def total(a, b):
        v = a * b
        v = tree([v[r : r + SUBS] for r in range(0, total_rows, SUBS)])
        for shift in (4, 2, 1):
            v = v + turn(v, shift, 0)
        v = v + xor_lane(v, 8)
        return v[0:1]

    residual = -assemble(rhs)
    direction = residual
    update = jnp.zeros_like(residual)
    now = total(residual, residual)
    for step in range(2):
        image = operate(direction)
        alpha = now / total(direction, image)
        update = update + alpha * direction
        if step == 0:
            residual = residual - alpha * image
            new = total(residual, residual)
            direction = residual + new / now * direction
            now = new
    mine = jnp.where(row == me, corners(update), 0.0)
    mine = jnp.sum(mine, axis=0, keepdims=True)
    return jnp.broadcast_to(mine, (SUBS, LANES))


def turn_kernel(phi_fine, phi_twin, fine_out, twin_out):
    for lv, phi_ref, out_ref in ((FINE, phi_fine, fine_out), (TWIN, phi_twin, twin_out)):
        s = lv.seg
        nz = EZ * lv.edz
        per = LANES // nz
        tiles = lv.edge // per
        for i in range(s):
            for t in range(tiles):
                parts = []
                for n in range(per):
                    y = lv.mx + t * per + n
                    start = (i * s + y % s) * SUBS + y // s
                    halves = [
                        phi_ref[pl.ds(h * lv.tiles * SUBS + start, lv.edz, stride=2 * lv.tiles * SUBS), :]
                        for h in range(2)
                    ]
                    lower = lane_iota(halves[0].shape) // 16 % 2 == 0
                    parts.append(jnp.where(lower, halves[0], turn(halves[1], 16)))
                    parts.append(jnp.where(lower, turn(halves[0], -16), halves[1]))
                out_ref[i * tiles + t] = jnp.concatenate(parts, axis=0).T


def pressure_kernel(gy_count, me_ref, gathered, fine_turned, twin_turned, fine_out, twin_out, fine_all, twin_all):
    mine = coarse_nodes(gathered[...], gy_count, me_ref[0])
    for n, (lv, turned, out_ref, all_ref) in enumerate(
        ((FINE, fine_turned, fine_out, fine_all), (TWIN, twin_turned, twin_out, twin_all))
    ):
        s = lv.seg
        nz = EZ * lv.edz
        tiles = lv.edge * nz // LANES
        lower = lane_iota() % nz < lv.edz
        scales = {}
        for c in range(COLUMNS):
            for p in range(4):
                at = p * 32 + n * 16 + c * 8
                node = jnp.broadcast_to(mine[:, at : at + 1], (SUBS, LANES))
                scales[2 * p, c] = jnp.where(lower, 1.0, node)
                scales[2 * p + 1, c] = jnp.where(lower, node, 0.0)
        for c in range(COLUMNS):
            for t in range(tiles):
                at = (c * tiles + t) * LANES
                for i in range(s):
                    value = tree(
                        [turned[i * tiles + t, a * 16 + c * 8 : a * 16 + c * 8 + 8, :] * scales[a, c] for a in range(8)]
                    )
                    all_ref[c * tiles + t, pl.ds(i, SUBS, stride=s), :] = value
                out_ref[:, at : at + LANES] = all_ref[c * tiles + t, lv.mx : lv.mx + lv.edge, :]


def vmem(shape, dtype=F32):
    return pltpu.VMEM(shape, dtype)


def shards(permeability):
    nz = EZ * ELZ
    rows = permeability.shape[1]
    lanes = permeability.shape[2]
    assert rows == EL and lanes == COLUMNS * EL * nz
    rim = MX * nz
    gx, gy = lax.axis_size("gx"), lax.axis_size("gy")

    def sent(value, axis, shift):
        count = lax.axis_size(axis)
        return lax.ppermute(value, axis, [(i, (i + shift) % count) for i in range(count)])

    x_low = sent(permeability[:, rows - MX :], "gx", 1)
    x_high = sent(permeability[:, :MX], "gx", -1)

    def strip(part):
        return jnp.concatenate([x_low[:, :, part], permeability[:, :, part], x_high[:, :, part]], axis=1)

    y_low = sent(strip(slice(lanes - rim, lanes)), "gy", 1)
    y_high = sent(strip(slice(0, rim)), "gy", -1)
    halos = [x_low, x_high, y_low, y_high]
    flat_lanes = lanes + 2 * rim
    scratch = [
        vmem((LANES, flat_lanes)),
        vmem((flat_lanes, LANES)),
        vmem((flat_lanes // 2, LANES)),
        vmem((SUBS * (TWIN.seg + 2) * nz, LANES)),
    ]
    for lv in LEVELS:
        scratch.append(vmem((lv.levels + 1, lv.seg, SUBS, 2 * LANES)))
        scratch += [vmem((lv.planes * lv.seg // 2, 2 * SUBS, 2 * LANES), BF16)] * 6
        scratch += [vmem((lv.seg, lv.planes * lv.seg, SUBS, LANES))] * 3
        scratch += [vmem((lv.inner + 1, 2 * lv.tiles, SUBS, LANES))] * 5
        scratch.append(vmem((2 * lv.tiles, SUBS, LANES)))
        scratch += [vmem((lv.tiles, SUBS, LANES))] * 2
    full = pl.BlockSpec(memory_space=pltpu.VMEM)
    phi_shapes = [
        jax.ShapeDtypeStruct((EZ * lv.edz * lv.tiles * SUBS, LANES), F32) for lv in LEVELS
    ]
    phi_fine, phi_twin, message = pl.pallas_call(
        solve_kernel,
        out_shape=phi_shapes + [jax.ShapeDtypeStruct((gx * gy, LANES), F32)],
        in_specs=[full] * 5,
        out_specs=[full] * 3,
        scratch_shapes=scratch,
        compiler_params=pltpu.CompilerParams(vmem_limit_bytes=44 * 1024 * 1024),
        name="solve",
    )(permeability, *halos)
    gathered = lax.all_to_all(message, ("gx", "gy"), 0, 0, tiled=True)
    turned = pl.pallas_call(
        turn_kernel,
        out_shape=[
            jax.ShapeDtypeStruct((lv.seg * lv.edge * EZ * lv.edz // LANES, LANES, LANES), F32) for lv in LEVELS
        ],
        in_specs=[full] * 2,
        out_specs=[full] * 2,
        compiler_params=pltpu.CompilerParams(vmem_limit_bytes=16 * 1024 * 1024),
        cost_estimate=pl.CostEstimate(flops=4000000, bytes_accessed=8000000, transcendentals=0),
        name="turned",
    )(phi_fine, phi_twin)
    me = (lax.axis_index("gx") * gy + lax.axis_index("gy")).astype(jnp.int32).reshape(1)
    return tuple(
        pl.pallas_call(
            functools.partial(pressure_kernel, gy),
            out_shape=[
                jax.ShapeDtypeStruct((lv.edge, COLUMNS * lv.edge * EZ * lv.edz), F32) for lv in LEVELS
            ],
            in_specs=[pl.BlockSpec(memory_space=pltpu.SMEM)] + [full] * 3,
            out_specs=[full] * 2,
            scratch_shapes=[vmem((COLUMNS * lv.edge * EZ * lv.edz // LANES, SUBS * lv.seg, LANES)) for lv in LEVELS],
            compiler_params=pltpu.CompilerParams(vmem_limit_bytes=16 * 1024 * 1024),
            name="pressure",
        )(me, gathered, *turned)
    )


def solution(mesh):
    return jax.shard_map(
        shards,
        mesh=mesh,
        in_specs=(P(None, "gx", "gy"),),
        out_specs=(P("gx", "gy"), P("gx", "gy")),
        check_vma=False,
    )
```

```python
import functools
import typing

import jax
import jax.numpy as jnp
from jax import lax
from jax.experimental import pallas as pl
from jax.experimental.pallas import tpu as pltpu
from jax.sharding import PartitionSpec as P

EL = 32
ELZ = 16
MX = 4
MZ = 2
EZ = 2
LANES = 128
SUBS = 8
COLUMNS = 2
F32 = jnp.float32
BF16 = jnp.bfloat16


class Level(typing.NamedTuple):
    edge: int
    edz: int
    mx: int
    mz: int
    spacing: float
    step: int

    @property
    def width(self):
        return self.edge + 2 * self.mx

    @property
    def inner(self):
        return self.edz + 2 * self.mz - 2

    @property
    def seg(self):
        return -(-self.width // SUBS)

    @property
    def tiles(self):
        return self.seg * self.seg

    @property
    def levels(self):
        return EZ * self.edz + 2

    @property
    def planes(self):
        return -(-(self.inner + 1) // 2) * 2


FINE = Level(EL, ELZ, MX, MZ, 1.0, 1)
TWIN = Level(EL // 2, ELZ // 2, MX // 2, MZ // 2, 2.0, 2)
LEVELS = (FINE, TWIN)


def lane_iota(shape=(SUBS, LANES)):
    return lax.broadcasted_iota(jnp.int32, shape, len(shape) - 1)


def sub_iota(shape=(SUBS, LANES)):
    return lax.broadcasted_iota(jnp.int32, shape, len(shape) - 2)


def turn(value, shift, axis=1):
    return pltpu.roll(value, shift % value.shape[axis], axis)


def lane_parts():
    lane = lane_iota()
    return lane // 32, lane // 16 % 2, lane // 8 % 2, lane % 8


class Consts:
    def __init__(self, lv):
        corner, _, _, xo = lane_parts()
        yo = sub_iota()
        ax, ay = corner // 2, corner % 2
        self.lv = lv
        s = lv.seg
        self.fx, self.fy = [], []
        self.inx, self.iny, self.facex, self.facey = [], [], [], []
        for i in range(s):
            x = xo * s + i
            y = yo * s + i
            px = (x.astype(F32) - lv.mx + 0.5) / lv.edge
            py = (y.astype(F32) - lv.mx + 0.5) / lv.edge
            self.fx.append(jnp.where(ax == 1, px, 1.0 - px))
            self.fy.append(jnp.where(ay == 1, py, 1.0 - py))
            xs = [s * o + i for o in range(SUBS)]

            def ranged(value, low, high):
                if all(low <= v <= high for v in xs):
                    return None
                return ((value >= low) & (value <= high)).astype(F32)

            self.inx.append((ranged(x, 1, lv.width - 2), ranged(x, lv.mx, lv.mx + lv.edge - 1)))
            self.iny.append((ranged(y, 1, lv.width - 2), ranged(y, lv.mx, lv.mx + lv.edge - 1)))
            cut = (lv.mx - 1, lv.mx + lv.edge - 1)
            self.facex.append(((x != cut[0]) & (x != cut[1])).astype(F32) if any(v in cut for v in xs) else None)
            self.facey.append(((y != cut[0]) & (y != cut[1])).astype(F32) if any(v in cut for v in xs) else None)
        sx = jnp.where(ax == 1, -1.0 / lv.edge, 1.0 / lv.edge).astype(F32)
        sy = jnp.where(ay == 1, -1.0 / lv.edge, 1.0 / lv.edge).astype(F32)
        self.along_x = [sx * f for f in self.fy]
        self.along_y = [sy * f for f in self.fx]

    def fz(self, plane):
        place = (jnp.asarray(plane, jnp.int32).astype(F32) - self.lv.mz + 0.5) / self.lv.edz
        return 1.0 - place, place

    def masked(self, value, i, j, kind):
        for table, index in ((self.inx, i), (self.iny, j)):
            factor = table[index][kind]
            if factor is not None:
                value = value * factor
        return value


def tree(values):
    values = list(values)
    while len(values) > 1:
        values = [a + b for a, b in zip(values[::2], values[1::2])] + (
            [values[-1]] if len(values) % 2 else []
        )
    return values[0]


def xor_lane(value, bit):
    return jnp.where(lane_iota(value.shape) // bit % 2 == 1, turn(value, bit), turn(value, -bit))


def problem_sum(value):
    for shift in (4, 2, 1):
        value = value + turn(value, shift, 0)
    for bit in (1, 2, 4):
        value = value + xor_lane(value, bit)
    return value


def spread_weights(lv, k_ref, high_refs, low_refs, w_refs):
    s = lv.seg
    wide = (SUBS, LANES)
    pos = lane_iota(wide)
    yo = sub_iota(wide)
    first = pos < 40
    third = pos >= 80
    second = (pos >= 40) & (pos < 80)
    edge_x = first & (pos >= (lv.width - 1) * lv.step)

    def one(z, i, c):
        part = slice(c * LANES, (c + 1) * LANES)
        k = k_ref[z, i, :, part]
        nbx = turn(k, -lv.step)
        nby = k_ref[z, i + 1, :, part] if i < s - 1 else turn(k_ref[z, 0, :, part], -1, 0)
        nbz = k_ref[z + 1, i, :, part]
        nb = jnp.where(first, nbx, jnp.where(second, nby, nbz))
        w = (2.0 * lv.spacing) * k * nb / (k + nb)
        bad = edge_x | (second & (yo * s + i >= lv.width - 1))
        return jnp.where(bad, 0.0, w)

    def planes(t, _):
        units = [(2 * t + n, i) for n in range(2) for i in range(s)]
        for e in range(EZ):
            made = []
            for plane, i in units:
                z = jnp.clip(e * lv.edz + plane + 1 - lv.mz, 0, lv.levels - 1)
                w0, w1 = one(z, i, 0), one(z, i, 1)
                near, wrap = turn(w1, 40), turn(w1, 48)
                made.append((jnp.where(first, w0, near), jnp.where(third, near, w0), jnp.where(third, w0, wrap)))
            for p in range(s):
                for m in range(3):
                    both = jnp.concatenate([made[2 * p][m], made[2 * p + 1][m]], axis=0)
                    high = both.astype(BF16)
                    part = slice(e * LANES, (e + 1) * LANES)
                    high_refs[m][t * s + p, :, part] = high
                    low_refs[m][t * s + p, :, part] = (both - high.astype(F32)).astype(BF16)
        return 0

    lax.fori_loop(0, lv.planes // 2, planes, 0)
    rows = lv.planes * s * SUBS
    row = lax.broadcasted_iota(jnp.int32, (2 * LANES, 2 * LANES), 0)
    lane = lax.broadcasted_iota(jnp.int32, (1, 2 * LANES), 1)
    upper = lane // LANES
    for q in range(-(-s // 2)):
        x = lane % 8 * s + 2 * q + upper
        valid = (x < lv.width) & (2 * q + upper < s)
        for m in range(3):
            segment = jnp.where(lane // 8 % 2 == 0, m, (m + 1) % 3)
            source = jnp.where(valid, lane // 16 % 2 * LANES + segment * 40 + lv.step * x, -1)
            pick = (row == source).astype(F32).astype(BF16)
            out = jnp.dot(high_refs[m][...].reshape(rows, 2 * LANES), pick, preferred_element_type=F32)
            out = out + jnp.dot(low_refs[m][...].reshape(rows, 2 * LANES), pick, preferred_element_type=F32)
            for half in range(min(2, s - 2 * q)):
                part = out[:, half * LANES : (half + 1) * LANES]
                w_refs[m][2 * q + half] = part.reshape(lv.planes * s, SUBS, LANES)


class Case:
    def __init__(self, lv, w_refs, fields, planes):
        self.lv, self.cs, self.w_refs = lv, Consts(lv), w_refs
        self.d, self.q, self.r = fields[:3], fields[3], fields[4]
        self.fz, self.chosen, self.total = planes

    def weights(self, plane):
        s = self.lv.seg
        return lambda m, i, j: self.w_refs[m][i, plane * s + j]


HALVES = (0, 1)


def phi_rows(lv):
    return EZ * lv.edz * lv.tiles * SUBS


def turned_tiles(lv):
    return lv.edge * EZ * lv.edz // LANES


def looped(count, group, sums, step):
    def body(t, sums):
        return tuple(a + b for a, b in zip(sums, step(t * group)))

    start = tuple(jnp.zeros((SUBS, LANES), F32) for _ in range(sums))
    return list(lax.fori_loop(0, count // group, body, start))


def start_residual(case, group):
    lv, cs, s = case.lv, case.cs, case.lv.seg

    def step(z0):
        total = [[], []]
        for z in [z0 + n for n in range(group)]:
            get, below = case.weights(z + 1), case.weights(z)
            gz = cs.fz(z + 1)
            last = [get(1, i, s - 1) * cs.along_y[i] for i in range(s)]
            before = [turn(v, 1, 0) for v in last]
            for j in range(s):
                flux_y = last if j == s - 1 else [get(1, i, j) * cs.along_y[i] for i in range(s)]
                flux_x = [get(0, i, j) * cs.along_x[j] for i in range(s)]
                squares = [[], []]
                for i in range(s):
                    k = i * s + j
                    prev_x = flux_x[i - 1] if i else turn(flux_x[s - 1], 1)
                    flat = (prev_x - flux_x[i]) + (before[i] - flux_y[i])
                    flat = cs.masked(flat, i, j, 0)
                    tall = (cs.fx[i] * cs.fy[j]) * (1.0 / lv.edz) * (below(2, i, j) - get(2, i, j))
                    tall = cs.masked(tall, i, j, 0)
                    for h, value in enumerate((flat * gz[0] + tall, flat * gz[1] - tall)):
                        case.d[0][z, h * lv.tiles + k] = value
                        squares[h].append(value * value)
                for h in HALVES:
                    total[h].append(tree(squares[h]))
                before = flux_y
        return [tree(t) for t in total]

    return looped(lv.inner, group, 2, step)


def row_jumps(u, s, j):
    jump_x = [u[i * s + j] - (u[(i + 1) * s + j] if i < s - 1 else turn(u[j], -1)) for i in range(s)]
    jump_y = [u[i * s + j] - (u[i * s + j + 1] if j < s - 1 else turn(u[i * s], -1, 0)) for i in range(s)]
    return jump_x, jump_y


def apply(case, group, number, betas):
    lv, cs, s = case.lv, case.cs, case.lv.seg
    keep = number < 2
    n = lv.tiles

    def fresh(z, h, k):
        at = h * n + k
        if number == 0:
            return case.d[0][z, at]
        value = case.r[z, at] + betas[h] * case.d[number - 1][z, at]
        case.d[number][z, at] = value
        return value

    firsts = []
    get = case.weights(0)
    for h in HALVES:
        terms = []
        for k in range(n):
            value = fresh(0, h, k)
            flux = -get(2, k // s, k % s) * value
            if keep:
                case.fz[h * n + k] = flux
            else:
                terms.append(-flux * value)
        firsts.append(tree(terms) if terms else 0.0)

    def step(z0):
        total = [[], []]
        u = [[case.d[number][z0, h * n + k] for k in range(n)] for h in HALVES]
        flux_z = [[case.fz[h * n + k] for k in range(n)] for h in HALVES] if keep else None
        for z in [z0 + t for t in range(group)]:
            get = case.weights(z + 1)
            after = [[None] * n for _ in HALVES]
            if keep:
                wy = [get(1, i, s - 1) for i in range(s)]
                last = [[wy[i] * (u[h][i * s + s - 1] - turn(u[h][i * s], -1, 0)) for i in range(s)] for h in HALVES]
                before = [[turn(v, 1, 0) for v in last[h]] for h in HALVES]
            for j in range(s):
                wx = [get(0, i, j) for i in range(s)]
                wy = [get(1, i, j) for i in range(s)]
                wz = [get(2, i, j) for i in range(s)]
                for h in HALVES:
                    jump_x, jump_y = row_jumps(u[h], s, j)
                    flux_x = [w * v for w, v in zip(wx, jump_x)]
                    flux_y = last[h] if keep and j == s - 1 else [w * v for w, v in zip(wy, jump_y)]
                    terms = []
                    for i in range(s):
                        k = i * s + j
                        after[h][k] = fresh(z + 1, h, k)
                        jump = u[h][k] - after[h][k]
                        flux = wz[i] * jump
                        if keep:
                            prev_x = flux_x[i - 1] if i else turn(flux_x[s - 1], 1)
                            value = (flux_x[i] - prev_x) + (flux_y[i] - before[h][i]) + (flux - flux_z[h][k])
                            flux_z[h][k] = flux
                            value = cs.masked(value, i, j, 0)
                            case.q[z, h * n + k] = value
                            terms.append(u[h][k] * value)
                        else:
                            terms.append((flux * jump + flux_x[i] * jump_x[i]) + flux_y[i] * jump_y[i])
                    total[h].append(tree(terms))
                    if keep:
                        before[h] = flux_y
            u = after
        if keep:
            for h in HALVES:
                for k in range(n):
                    case.fz[h * n + k] = flux_z[h][k]
        return [tree(t) for t in total]

    return [a + b for a, b in zip(looped(lv.inner, group, 2, step), firsts)]


def reduce_residual(case, group, number, alphas):
    lv = case.lv

    def step(z0):
        total = [[], []]
        source = case.d[0] if number == 0 else case.r
        for z in [z0 + n for n in range(group)]:
            for h in HALVES:
                squares = []
                for k in range(lv.tiles):
                    at = h * lv.tiles + k
                    value = source[z, at] - alphas[h] * case.q[z, at]
                    case.r[z, at] = value
                    squares.append(value * value)
                total[h].append(tree(squares))
        return [tree(t) for t in total]

    return looped(lv.inner, group, 2, step)


def finish(case, group, alphas, phi_ref):
    lv, cs, s = case.lv, case.cs, case.lv.seg
    n = lv.tiles
    lower = lane_parts()[1] == 0

    def fresh(z, i, j, gz):
        k = i * s + j
        inner = z + lv.mz - 1
        both = cs.fx[i] * cs.fy[j]
        values = []
        for h in HALVES:
            value = both * gz[h]
            for alpha, d_ref in zip(alphas[h], case.d):
                value = value + alpha * d_ref[inner, h * n + k]
            value = cs.masked(value, i, j, 1)
            at = pl.multiple_of(((z * 2 + h) * n + k) * SUBS, SUBS)
            phi_ref[pl.ds(at, SUBS), :] = value
            values.append(value)
        total = values[0] + turn(values[0], 32)
        return jnp.where(lower, values[1], values[0]), total + turn(total, 64)

    gz = cs.fz(lv.mz)
    for i in range(s):
        for j in range(s):
            k = i * s + j
            case.chosen[k], case.total[k] = fresh(0, i, j, gz)
            case.fz[k] = jnp.zeros((SUBS, LANES), F32)

    def cut(values, table):
        return [v if f is None else v * f for v, f in zip(values, table)]

    def step(z0):
        sums = [[] for _ in range(4)]
        u = [case.chosen[k] for k in range(n)]
        low = [case.total[k] for k in range(n)]
        flux_z = [case.fz[k] for k in range(n)]
        for z in [z0 + t for t in range(group)]:
            get = case.weights(z + lv.mz)
            up = jnp.minimum(z + 1, lv.edz - 1)
            gz = cs.fz(up + lv.mz)
            after, after_low = [None] * n, [None] * n
            last = [get(1, i, s - 1) * (u[i * s + s - 1] - turn(u[i * s], -1, 0)) for i in range(s)]
            last = cut(last, [cs.facey[s - 1]] * s)
            before = [turn(v, 1, 0) for v in last]
            for j in range(s):
                jump_x, jump_y = row_jumps(u, s, j)
                flux_x = cut([get(0, i, j) * jump_x[i] for i in range(s)], cs.facex)
                flux_y = last
                if j < s - 1:
                    flux_y = cut([get(1, i, j) * jump_y[i] for i in range(s)], [cs.facey[j]] * s)
                parts = [[] for _ in sums]
                for i in range(s):
                    k = i * s + j
                    after[k], after_low[k] = fresh(up, i, j, gz)
                    flux = get(2, i, j) * (u[k] - after[k])
                    prev_x = flux_x[i - 1] if i else turn(flux_x[s - 1], 1)
                    value = (flux_x[i] - prev_x) + (flux_y[i] - before[i]) + (flux - flux_z[k])
                    flux_z[k] = flux
                    parts[0].append(value * u[k])
                    parts[1].append(value * turn(u[k], -32))
                    parts[2].append(value * turn(u[k], 64))
                    parts[3].append(value * low[k])
                for total, part in zip(sums, parts):
                    total.append(tree(part))
                before = flux_y
            u, low = after, after_low
        for k in range(n):
            case.fz[k], case.chosen[k], case.total[k] = flux_z[k], u[k], low[k]
        return [tree(total) for total in sums]

    return looped(lv.edz, group, 4, step)


GROUPS = {FINE: 2, TWIN: 8}


def solve_kernel(
    center, x_low, x_high, y_low, y_high,
    phi, message,
    flat, rows, pairs, twin_rows, *refs,
):
    lanes = center.shape[2]
    rim = (flat.shape[1] - lanes) // 2
    nx = center.shape[1]
    top = MX + nx
    for m in range(3):
        off = m * (nx + 2 * MX)
        flat[off : off + top + MX, :rim] = y_low[m]
        flat[off : off + MX, rim : rim + lanes] = x_low[m]
        flat[off + MX : off + top, rim : rim + lanes] = center[m]
        flat[off + top : off + top + MX, rim : rim + lanes] = x_high[m]
        flat[off : off + top + MX, rim + lanes :] = y_high[m]
    used = 3 * (nx + 2 * MX)
    flat[used:, :] = jnp.ones((LANES - used, flat.shape[1]), F32)
    for t in range(flat.shape[1] // LANES):
        rows[t * LANES : (t + 1) * LANES, :] = flat[:, t * LANES : (t + 1) * LANES].T

    nz = EZ * ELZ
    twin_y = rows.shape[0] // nz // 2
    for y in range(twin_y):
        both = rows[2 * y * nz : (2 * y + 1) * nz, :] + rows[(2 * y + 1) * nz : (2 * y + 2) * nz, :]
        both = both + turn(both, -1)
        at = y * nz
        pairs[at : at + nz, :] = both
        twin_rows[at : at + 8, :] = jnp.broadcast_to(0.25 * both[0:1], (8, LANES))
        twin_rows[at + 8 + nz // 2 : at + nz, :] = jnp.broadcast_to(0.25 * both[nz - 1 : nz], (8, LANES))
    for y in range(twin_y):
        at = y * nz
        middle = pairs[pl.ds(at, nz // 2, stride=2), :] + pairs[pl.ds(at + 1, nz // 2, stride=2), :]
        twin_rows[at + 8 : at + 8 + nz // 2, :] = 0.125 * middle
    twin_rows[twin_y * nz :, :] = jnp.ones((twin_rows.shape[0] - twin_y * nz, LANES), F32)

    refs = list(refs)

    def take(count):
        got = refs[:count]
        del refs[:count]
        return got

    cases = []
    for lv, source in zip(LEVELS, (rows, twin_rows)):
        (k_ref,) = take(1)
        high_refs, low_refs, w_refs = take(3), take(3), take(3)
        for z in range(lv.levels + 1):
            cell = min(max(z - 1, 0), nz - 1) if lv is FINE else min(z, lv.levels - 1) + 7
            for i in range(lv.seg):
                for c in range(COLUMNS):
                    start = (lv.edge * c + i) * nz + cell
                    k_ref[z, i, :, c * LANES : (c + 1) * LANES] = source[pl.ds(start, SUBS, stride=lv.seg * nz), :]
        spread_weights(lv, k_ref, high_refs, low_refs, w_refs)
        case = Case(lv, w_refs, take(5), take(3))
        for k in range(2 * lv.tiles):
            case.d[0][lv.inner, k] = jnp.zeros((SUBS, LANES), F32)
            case.r[lv.inner, k] = jnp.zeros((SUBS, LANES), F32)
        cases.append(case)

    def both_levels(work):
        sums = [work(n, case, GROUPS[case.lv]) for n, case in enumerate(cases)]
        return [[problem_sum(v) for v in part] for part in sums]

    rr = both_levels(lambda n, case, group: start_residual(case, group))
    alphas = [[[], []] for _ in LEVELS]
    betas = [None] * len(LEVELS)
    for step in range(3):
        dots = both_levels(lambda n, case, group: apply(case, group, step, betas[n]))
        now = [[a / b for a, b in zip(rr[n], dots[n])] for n in range(len(LEVELS))]
        for n in range(len(LEVELS)):
            for h in HALVES:
                alphas[n][h].append(now[n][h])
        if step < 2:
            new = both_levels(lambda n, case, group: reduce_residual(case, group, step, now[n]))
            betas = [[a / b for a, b in zip(new[n], rr[n])] for n in range(len(LEVELS))]
            rr = new

    split = phi.shape[0] - phi_rows(TWIN)
    phis = (phi.at[pl.ds(0, split)], phi.at[pl.ds(split, phi_rows(TWIN))])
    totals = both_levels(lambda n, case, group: finish(case, group, alphas[n], phis[n]))
    _, element, _, slot = lane_parts()
    packed = []
    for level in totals:
        parts = [v + xor_lane(v, 16) for v in level[:3]]
        parts.append(jnp.where(element == 0, level[3], turn(level[3], 16)))
        packed.append(
            jnp.where(slot == 0, parts[0], jnp.where(slot == 1, parts[1], jnp.where(slot == 2, parts[2], parts[3])))
        )
    row = jnp.where(element == 0, packed[0], packed[1])
    for r in range(0, message.shape[0], SUBS):
        message[r : r + SUBS, :] = row


def coarse_nodes(gathered, gy_count, me):
    total_rows = gathered.shape[0]
    shape = gathered.shape
    lane = lane_iota(shape)
    row = sub_iota(shape)
    corner = lane // 32
    column = lane // 8 % 2
    last = row % gy_count == gy_count - 1
    start = row % gy_count == 0
    one = gathered
    two = turn(gathered, -1)
    four = turn(gathered, -2)
    rhs = turn(gathered, -3)
    two_back = turn(two, 32)

    def next_x(u):
        return turn(u, -gy_count, 0)

    def prev_x(u):
        return turn(u, gy_count, 0)

    def next_y(u):
        ahead = jnp.where(last, turn(u, gy_count - 1, 0), turn(u, -1, 0))
        return jnp.where(column == 0, turn(u, -8), turn(ahead, 8))

    def prev_y(u):
        behind = jnp.where(start, turn(u, 1 - gy_count, 0), turn(u, 1, 0))
        return jnp.where(column == 1, turn(u, 8), turn(behind, -8))

    def by_corner(a, b, c, d):
        return jnp.where(corner == 0, a, jnp.where(corner == 1, b, jnp.where(corner == 2, c, d)))

    def corners(u):
        ux = next_x(u)
        return by_corner(u, next_y(u), ux, next_y(ux))

    def assemble(v):
        vx = prev_x(v)
        w = by_corner(v, prev_y(v), vx, prev_y(vx))
        w = w + turn(w, 64)
        return w + turn(w, 32)

    def operate(u):
        c = corners(u)
        return assemble(one * c + two * turn(c, -32) + two_back * turn(c, 32) + four * turn(c, 64))

    def total(a, b):
        v = a * b
        v = tree([v[r : r + SUBS] for r in range(0, total_rows, SUBS)])
        for shift in (4, 2, 1):
            v = v + turn(v, shift, 0)
        v = v + xor_lane(v, 8)
        return v[0:1]

    residual = -assemble(rhs)
    direction = residual
    update = jnp.zeros_like(residual)
    now = total(residual, residual)
    for step in range(2):
        image = operate(direction)
        alpha = now / total(direction, image)
        update = update + alpha * direction
        if step == 0:
            residual = residual - alpha * image
            new = total(residual, residual)
            direction = residual + new / now * direction
            now = new
    mine = jnp.where(row == me, corners(update), 0.0)
    mine = jnp.sum(mine, axis=0, keepdims=True)
    return jnp.broadcast_to(mine, (SUBS, LANES))


def turn_kernel(phi, out_ref, work, sem):
    start_row, number = 0, 0
    copies = []
    for lv in LEVELS:
        s = lv.seg
        nz = EZ * lv.edz
        per = LANES // nz
        for i in range(s):
            for t in range(turned_tiles(lv)):
                parts = []
                for n in range(per):
                    y = lv.mx + t * per + n
                    start = start_row + (i * s + y % s) * SUBS + y // s
                    halves = [
                        phi[pl.ds(h * lv.tiles * SUBS + start, lv.edz, stride=2 * lv.tiles * SUBS), :]
                        for h in range(2)
                    ]
                    lower = lane_iota(halves[0].shape) // 16 % 2 == 0
                    parts.append(jnp.where(lower, halves[0], turn(halves[1], 16)))
                    parts.append(jnp.where(lower, turn(halves[0], -16), halves[1]))
                work[number] = jnp.concatenate(parts, axis=0).T
                number += 1
            done = number - turned_tiles(lv)
            copies.append(
                pltpu.make_async_copy(
                    work.at[pl.ds(done, turned_tiles(lv))], out_ref.at[pl.ds(done, turned_tiles(lv))], sem.at[len(copies)]
                )
            )
            copies[-1].start()
        start_row += phi_rows(lv)
    for copy in copies:
        copy.wait()


def pressure_kernel(gy_count, me_ref, gathered, source, fine_out, twin_out, turned, fine_all, twin_all, sem):
    fetch = pltpu.make_async_copy(source, turned, sem)
    fetch.start()
    mine = coarse_nodes(gathered[...], gy_count, me_ref[0])
    fetch.wait()
    first = 0
    for n, (lv, out_ref, all_ref) in enumerate(((FINE, fine_out, fine_all), (TWIN, twin_out, twin_all))):
        s = lv.seg
        nz = EZ * lv.edz
        tiles = turned_tiles(lv)
        lower = lane_iota() % nz < lv.edz
        scales = {}
        for c in range(COLUMNS):
            for p in range(4):
                at = p * 32 + n * 16 + c * 8
                node = jnp.broadcast_to(mine[:, at : at + 1], (SUBS, LANES))
                scales[2 * p, c] = jnp.where(lower, 1.0, node)
                scales[2 * p + 1, c] = jnp.where(lower, node, 0.0)
        for c in range(COLUMNS):
            for t in range(tiles):
                at = (c * tiles + t) * LANES
                for i in range(s):
                    value = tree(
                        [turned[first + i * tiles + t, a * 16 + c * 8 : a * 16 + c * 8 + 8, :] * scales[a, c] for a in range(8)]
                    )
                    all_ref[c * tiles + t, pl.ds(i, SUBS, stride=s), :] = value
                out_ref[:, at : at + LANES] = all_ref[c * tiles + t, lv.mx : lv.mx + lv.edge, :]
        first += s * tiles


def vmem(shape, dtype=F32):
    return pltpu.VMEM(shape, dtype)


def shards(permeability):
    nz = EZ * ELZ
    rows = permeability.shape[1]
    lanes = permeability.shape[2]
    assert rows == EL and lanes == COLUMNS * EL * nz
    rim = MX * nz
    gx, gy = lax.axis_size("gx"), lax.axis_size("gy")

    def sent(value, axis, shift):
        count = lax.axis_size(axis)
        return lax.ppermute(value, axis, [(i, (i + shift) % count) for i in range(count)])

    x_low = sent(permeability[:, rows - MX :], "gx", 1)
    x_high = sent(permeability[:, :MX], "gx", -1)

    def strip(part):
        return jnp.concatenate([x_low[:, :, part], permeability[:, :, part], x_high[:, :, part]], axis=1)

    y_low = sent(strip(slice(lanes - rim, lanes)), "gy", 1)
    y_high = sent(strip(slice(0, rim)), "gy", -1)
    halos = [x_low, x_high, y_low, y_high]
    flat_lanes = lanes + 2 * rim
    scratch = [
        vmem((LANES, flat_lanes)),
        vmem((flat_lanes, LANES)),
        vmem((flat_lanes // 2, LANES)),
        vmem((SUBS * (TWIN.seg + 2) * nz, LANES)),
    ]
    for lv in LEVELS:
        scratch.append(vmem((lv.levels + 1, lv.seg, SUBS, 2 * LANES)))
        scratch += [vmem((lv.planes * lv.seg // 2, 2 * SUBS, 2 * LANES), BF16)] * 6
        scratch += [vmem((lv.seg, lv.planes * lv.seg, SUBS, LANES))] * 3
        scratch += [vmem((lv.inner + 1, 2 * lv.tiles, SUBS, LANES))] * 5
        scratch.append(vmem((2 * lv.tiles, SUBS, LANES)))
        scratch += [vmem((lv.tiles, SUBS, LANES))] * 2
    full = pl.BlockSpec(memory_space=pltpu.VMEM)
    phi, message = pl.pallas_call(
        solve_kernel,
        out_shape=[
            jax.ShapeDtypeStruct((sum(phi_rows(lv) for lv in LEVELS), LANES), F32),
            jax.ShapeDtypeStruct((gx * gy, LANES), F32),
        ],
        in_specs=[full] * 5,
        out_specs=[full] * 2,
        scratch_shapes=scratch,
        compiler_params=pltpu.CompilerParams(vmem_limit_bytes=44 * 1024 * 1024),
        name="solve",
    )(permeability, *halos)
    gathered = lax.all_to_all(message, ("gx", "gy"), 0, 0, tiled=True)
    tiles = sum(lv.seg * turned_tiles(lv) for lv in LEVELS)
    turned = pl.pallas_call(
        turn_kernel,
        out_shape=jax.ShapeDtypeStruct((tiles, LANES, LANES), F32),
        in_specs=[full],
        out_specs=pl.BlockSpec(memory_space=pltpu.HBM),
        scratch_shapes=[
            vmem((tiles, LANES, LANES)),
            pltpu.SemaphoreType.DMA((sum(lv.seg for lv in LEVELS),)),
        ],
        compiler_params=pltpu.CompilerParams(vmem_limit_bytes=16 * 1024 * 1024),
        cost_estimate=pl.CostEstimate(flops=4000000, bytes_accessed=8000000, transcendentals=0),
        name="turned",
    )(phi)
    me = (lax.axis_index("gx") * gy + lax.axis_index("gy")).astype(jnp.int32).reshape(1)
    return tuple(
        pl.pallas_call(
            functools.partial(pressure_kernel, gy),
            out_shape=[
                jax.ShapeDtypeStruct((lv.edge, COLUMNS * lv.edge * EZ * lv.edz), F32) for lv in LEVELS
            ],
            in_specs=[pl.BlockSpec(memory_space=pltpu.SMEM), full, pl.BlockSpec(memory_space=pltpu.HBM)],
            out_specs=[full] * 2,
            scratch_shapes=[vmem((tiles, LANES, LANES))]
            + [vmem((COLUMNS * turned_tiles(lv), SUBS * lv.seg, LANES)) for lv in LEVELS]
            + [pltpu.SemaphoreType.DMA],
            compiler_params=pltpu.CompilerParams(vmem_limit_bytes=16 * 1024 * 1024),
            name="pressure",
        )(me, gathered, turned)
    )


def solution(mesh):
    return jax.shard_map(
        shards,
        mesh=mesh,
        in_specs=(P(None, "gx", "gy"),),
        out_specs=(P("gx", "gy"), P("gx", "gy")),
        check_vma=False,
    )
```

```python
import functools
import typing

import jax
import jax.numpy as jnp
from jax import lax
from jax.experimental import pallas as pl
from jax.experimental.pallas import tpu as pltpu
from jax.sharding import PartitionSpec as P

EL = 32
ELZ = 16
MX = 4
MZ = 2
EZ = 2
LANES = 128
SUBS = 8
COLUMNS = 2
F32 = jnp.float32
BF16 = jnp.bfloat16


class Level(typing.NamedTuple):
    edge: int
    edz: int
    mx: int
    mz: int
    spacing: float
    step: int

    @property
    def width(self):
        return self.edge + 2 * self.mx

    @property
    def inner(self):
        return self.edz + 2 * self.mz - 2

    @property
    def seg(self):
        return -(-self.width // SUBS)

    @property
    def tiles(self):
        return self.seg * self.seg

    @property
    def levels(self):
        return EZ * self.edz + 2

    @property
    def planes(self):
        return -(-(self.inner + 1) // 2) * 2


FINE = Level(EL, ELZ, MX, MZ, 1.0, 1)
TWIN = Level(EL // 2, ELZ // 2, MX // 2, MZ // 2, 2.0, 2)
LEVELS = (FINE, TWIN)


def lane_iota(shape=(SUBS, LANES)):
    return lax.broadcasted_iota(jnp.int32, shape, len(shape) - 1)


def sub_iota(shape=(SUBS, LANES)):
    return lax.broadcasted_iota(jnp.int32, shape, len(shape) - 2)


def turn(value, shift, axis=1):
    return pltpu.roll(value, shift % value.shape[axis], axis)


def lane_parts():
    lane = lane_iota()
    return lane // 32, lane // 16 % 2, lane // 8 % 2, lane % 8


class Consts:
    def __init__(self, lv):
        corner, _, _, xo = lane_parts()
        yo = sub_iota()
        ax, ay = corner // 2, corner % 2
        self.lv = lv
        s = lv.seg
        self.fx, self.fy = [], []
        self.inx, self.iny, self.facex, self.facey = [], [], [], []
        for i in range(s):
            x = xo * s + i
            y = yo * s + i
            px = (x.astype(F32) - lv.mx + 0.5) / lv.edge
            py = (y.astype(F32) - lv.mx + 0.5) / lv.edge
            self.fx.append(jnp.where(ax == 1, px, 1.0 - px))
            self.fy.append(jnp.where(ay == 1, py, 1.0 - py))
            xs = [s * o + i for o in range(SUBS)]

            def ranged(value, low, high):
                if all(low <= v <= high for v in xs):
                    return None
                return ((value >= low) & (value <= high)).astype(F32)

            self.inx.append((ranged(x, 1, lv.width - 2), ranged(x, lv.mx, lv.mx + lv.edge - 1)))
            self.iny.append((ranged(y, 1, lv.width - 2), ranged(y, lv.mx, lv.mx + lv.edge - 1)))
            cut = (lv.mx - 1, lv.mx + lv.edge - 1)
            self.facex.append(((x != cut[0]) & (x != cut[1])).astype(F32) if any(v in cut for v in xs) else None)
            self.facey.append(((y != cut[0]) & (y != cut[1])).astype(F32) if any(v in cut for v in xs) else None)
        sx = jnp.where(ax == 1, -1.0 / lv.edge, 1.0 / lv.edge).astype(F32)
        sy = jnp.where(ay == 1, -1.0 / lv.edge, 1.0 / lv.edge).astype(F32)
        self.along_x = [sx * f for f in self.fy]
        self.along_y = [sy * f for f in self.fx]

    def fz(self, plane):
        place = (jnp.asarray(plane, jnp.int32).astype(F32) - self.lv.mz + 0.5) / self.lv.edz
        return 1.0 - place, place

    def masked(self, value, i, j, kind):
        for table, index in ((self.inx, i), (self.iny, j)):
            factor = table[index][kind]
            if factor is not None:
                value = value * factor
        return value


def tree(values):
    values = list(values)
    while len(values) > 1:
        values = [a + b for a, b in zip(values[::2], values[1::2])] + (
            [values[-1]] if len(values) % 2 else []
        )
    return values[0]


def xor_lane(value, bit):
    return jnp.where(lane_iota(value.shape) // bit % 2 == 1, turn(value, bit), turn(value, -bit))


def problem_sum(value):
    for shift in (4, 2, 1):
        value = value + turn(value, shift, 0)
    for bit in (1, 2, 4):
        value = value + xor_lane(value, bit)
    return value


def spread_weights(lv, k_ref, high_refs, low_refs, w_refs):
    s = lv.seg
    wide = (SUBS, LANES)
    pos = lane_iota(wide)
    yo = sub_iota(wide)
    first = pos < 40
    third = pos >= 80
    second = (pos >= 40) & (pos < 80)
    edge_x = first & (pos >= (lv.width - 1) * lv.step)

    def one(z, i, c):
        part = slice(c * LANES, (c + 1) * LANES)
        k = k_ref[z, i, :, part]
        nbx = turn(k, -lv.step)
        nby = k_ref[z, i + 1, :, part] if i < s - 1 else turn(k_ref[z, 0, :, part], -1, 0)
        nbz = k_ref[z + 1, i, :, part]
        nb = jnp.where(first, nbx, jnp.where(second, nby, nbz))
        w = (2.0 * lv.spacing) * k * nb / (k + nb)
        bad = edge_x | (second & (yo * s + i >= lv.width - 1))
        return jnp.where(bad, 0.0, w)

    def planes(t, _):
        units = [(2 * t + n, i) for n in range(2) for i in range(s)]
        for e in range(EZ):
            made = []
            for plane, i in units:
                z = jnp.clip(e * lv.edz + plane + 1 - lv.mz, 0, lv.levels - 1)
                w0, w1 = one(z, i, 0), one(z, i, 1)
                near, wrap = turn(w1, 40), turn(w1, 48)
                made.append((jnp.where(first, w0, near), jnp.where(third, near, w0), jnp.where(third, w0, wrap)))
            for p in range(s):
                for m in range(3):
                    both = jnp.concatenate([made[2 * p][m], made[2 * p + 1][m]], axis=0)
                    high = both.astype(BF16)
                    part = slice(e * LANES, (e + 1) * LANES)
                    high_refs[m][t * s + p, :, part] = high
                    low_refs[m][t * s + p, :, part] = (both - high.astype(F32)).astype(BF16)
        return 0

    lax.fori_loop(0, lv.planes // 2, planes, 0)
    rows = lv.planes * s * SUBS
    row = lax.broadcasted_iota(jnp.int32, (2 * LANES, 2 * LANES), 0)
    lane = lax.broadcasted_iota(jnp.int32, (1, 2 * LANES), 1)
    upper = lane // LANES
    for q in range(-(-s // 2)):
        x = lane % 8 * s + 2 * q + upper
        valid = (x < lv.width) & (2 * q + upper < s)
        for m in range(3):
            segment = jnp.where(lane // 8 % 2 == 0, m, (m + 1) % 3)
            source = jnp.where(valid, lane // 16 % 2 * LANES + segment * 40 + lv.step * x, -1)
            pick = (row == source).astype(F32).astype(BF16)
            out = jnp.dot(high_refs[m][...].reshape(rows, 2 * LANES), pick, preferred_element_type=F32)
            out = out + jnp.dot(low_refs[m][...].reshape(rows, 2 * LANES), pick, preferred_element_type=F32)
            for half in range(min(2, s - 2 * q)):
                part = out[:, half * LANES : (half + 1) * LANES]
                w_refs[m][2 * q + half] = part.reshape(lv.planes * s, SUBS, LANES)


class Case:
    def __init__(self, lv, w_refs, fields, planes):
        self.lv, self.cs, self.w_refs = lv, Consts(lv), w_refs
        self.d, self.q, self.r = fields[:3], fields[3], fields[4]
        self.fz, self.chosen, self.total = planes

    def weights(self, plane):
        s = self.lv.seg
        return lambda m, i, j: self.w_refs[m][i, plane * s + j]


HALVES = (0, 1)


def phi_rows(lv):
    return EZ * lv.edz * lv.tiles * SUBS


def turned_tiles(lv):
    return lv.edge * EZ * lv.edz // LANES


def looped(count, group, sums, step):
    def body(t, sums):
        return tuple(a + b for a, b in zip(sums, step(t * group)))

    start = tuple(jnp.zeros((SUBS, LANES), F32) for _ in range(sums))
    return list(lax.fori_loop(0, count // group, body, start))


def start_residual(case, group):
    lv, cs, s = case.lv, case.cs, case.lv.seg

    def step(z0):
        total = [[], []]
        for z in [z0 + n for n in range(group)]:
            get, below = case.weights(z + 1), case.weights(z)
            gz = cs.fz(z + 1)
            last = [get(1, i, s - 1) * cs.along_y[i] for i in range(s)]
            before = [turn(v, 1, 0) for v in last]
            for j in range(s):
                flux_y = last if j == s - 1 else [get(1, i, j) * cs.along_y[i] for i in range(s)]
                flux_x = [get(0, i, j) * cs.along_x[j] for i in range(s)]
                squares = [[], []]
                for i in range(s):
                    k = i * s + j
                    prev_x = flux_x[i - 1] if i else turn(flux_x[s - 1], 1)
                    flat = (prev_x - flux_x[i]) + (before[i] - flux_y[i])
                    flat = cs.masked(flat, i, j, 0)
                    tall = (cs.fx[i] * cs.fy[j]) * (1.0 / lv.edz) * (below(2, i, j) - get(2, i, j))
                    tall = cs.masked(tall, i, j, 0)
                    for h, value in enumerate((flat * gz[0] + tall, flat * gz[1] - tall)):
                        case.d[0][z, h * lv.tiles + k] = value
                        squares[h].append(value * value)
                for h in HALVES:
                    total[h].append(tree(squares[h]))
                before = flux_y
        return [tree(t) for t in total]

    return looped(lv.inner, group, 2, step)


def row_jumps(u, s, j):
    jump_x = [u[i * s + j] - (u[(i + 1) * s + j] if i < s - 1 else turn(u[j], -1)) for i in range(s)]
    jump_y = [u[i * s + j] - (u[i * s + j + 1] if j < s - 1 else turn(u[i * s], -1, 0)) for i in range(s)]
    return jump_x, jump_y


def apply(case, group, number, betas):
    lv, cs, s = case.lv, case.cs, case.lv.seg
    keep = number < 2
    n = lv.tiles

    def fresh(z, h, k):
        at = h * n + k
        if number == 0:
            return case.d[0][z, at]
        value = case.r[z, at] + betas[h] * case.d[number - 1][z, at]
        case.d[number][z, at] = value
        return value

    firsts = []
    get = case.weights(0)
    for h in HALVES:
        terms = []
        for k in range(n):
            value = fresh(0, h, k)
            flux = -get(2, k // s, k % s) * value
            if keep:
                case.fz[h * n + k] = flux
            else:
                terms.append(-flux * value)
        firsts.append(tree(terms) if terms else 0.0)

    def step(z0):
        total = [[], []]
        u = [[case.d[number][z0, h * n + k] for k in range(n)] for h in HALVES]
        flux_z = [[case.fz[h * n + k] for k in range(n)] for h in HALVES] if keep else None
        for z in [z0 + t for t in range(group)]:
            get = case.weights(z + 1)
            after = [[None] * n for _ in HALVES]
            if keep:
                wy = [get(1, i, s - 1) for i in range(s)]
                last = [[wy[i] * (u[h][i * s + s - 1] - turn(u[h][i * s], -1, 0)) for i in range(s)] for h in HALVES]
                before = [[turn(v, 1, 0) for v in last[h]] for h in HALVES]
            for j in range(s):
                wx = [get(0, i, j) for i in range(s)]
                wy = [get(1, i, j) for i in range(s)]
                wz = [get(2, i, j) for i in range(s)]
                for h in HALVES:
                    jump_x, jump_y = row_jumps(u[h], s, j)
                    flux_x = [w * v for w, v in zip(wx, jump_x)]
                    flux_y = last[h] if keep and j == s - 1 else [w * v for w, v in zip(wy, jump_y)]
                    terms = []
                    for i in range(s):
                        k = i * s + j
                        after[h][k] = fresh(z + 1, h, k)
                        jump = u[h][k] - after[h][k]
                        flux = wz[i] * jump
                        if keep:
                            prev_x = flux_x[i - 1] if i else turn(flux_x[s - 1], 1)
                            value = (flux_x[i] - prev_x) + (flux_y[i] - before[h][i]) + (flux - flux_z[h][k])
                            flux_z[h][k] = flux
                            value = cs.masked(value, i, j, 0)
                            case.q[z, h * n + k] = value
                            terms.append(u[h][k] * value)
                        else:
                            terms.append((flux * jump + flux_x[i] * jump_x[i]) + flux_y[i] * jump_y[i])
                    total[h].append(tree(terms))
                    if keep:
                        before[h] = flux_y
            u = after
        if keep:
            for h in HALVES:
                for k in range(n):
                    case.fz[h * n + k] = flux_z[h][k]
        return [tree(t) for t in total]

    return [a + b for a, b in zip(looped(lv.inner, group, 2, step), firsts)]


def reduce_residual(case, group, number, alphas):
    lv = case.lv

    def step(z0):
        total = [[], []]
        source = case.d[0] if number == 0 else case.r
        for z in [z0 + n for n in range(group)]:
            for h in HALVES:
                squares = []
                for k in range(lv.tiles):
                    at = h * lv.tiles + k
                    value = source[z, at] - alphas[h] * case.q[z, at]
                    case.r[z, at] = value
                    squares.append(value * value)
                total[h].append(tree(squares))
        return [tree(t) for t in total]

    return looped(lv.inner, group, 2, step)


def finish(case, group, alphas, phi_ref):
    lv, cs, s = case.lv, case.cs, case.lv.seg
    n = lv.tiles
    lower = lane_parts()[1] == 0

    def fresh(z, i, j, gz):
        k = i * s + j
        inner = z + lv.mz - 1
        both = cs.fx[i] * cs.fy[j]
        values = []
        for h in HALVES:
            value = both * gz[h]
            for alpha, d_ref in zip(alphas[h], case.d):
                value = value + alpha * d_ref[inner, h * n + k]
            value = cs.masked(value, i, j, 1)
            at = pl.multiple_of(((z * 2 + h) * n + k) * SUBS, SUBS)
            phi_ref[pl.ds(at, SUBS), :] = value
            values.append(value)
        total = values[0] + turn(values[0], 32)
        return jnp.where(lower, values[1], values[0]), total + turn(total, 64)

    gz = cs.fz(lv.mz)
    for i in range(s):
        for j in range(s):
            k = i * s + j
            case.chosen[k], case.total[k] = fresh(0, i, j, gz)
            case.fz[k] = jnp.zeros((SUBS, LANES), F32)

    def cut(values, table):
        return [v if f is None else v * f for v, f in zip(values, table)]

    def step(z0):
        sums = [[] for _ in range(4)]
        u = [case.chosen[k] for k in range(n)]
        low = [case.total[k] for k in range(n)]
        flux_z = [case.fz[k] for k in range(n)]
        for z in [z0 + t for t in range(group)]:
            get = case.weights(z + lv.mz)
            up = jnp.minimum(z + 1, lv.edz - 1)
            gz = cs.fz(up + lv.mz)
            after, after_low = [None] * n, [None] * n
            last = [get(1, i, s - 1) * (u[i * s + s - 1] - turn(u[i * s], -1, 0)) for i in range(s)]
            last = cut(last, [cs.facey[s - 1]] * s)
            before = [turn(v, 1, 0) for v in last]
            for j in range(s):
                jump_x, jump_y = row_jumps(u, s, j)
                flux_x = cut([get(0, i, j) * jump_x[i] for i in range(s)], cs.facex)
                flux_y = last
                if j < s - 1:
                    flux_y = cut([get(1, i, j) * jump_y[i] for i in range(s)], [cs.facey[j]] * s)
                parts = [[] for _ in sums]
                for i in range(s):
                    k = i * s + j
                    after[k], after_low[k] = fresh(up, i, j, gz)
                    flux = get(2, i, j) * (u[k] - after[k])
                    prev_x = flux_x[i - 1] if i else turn(flux_x[s - 1], 1)
                    value = (flux_x[i] - prev_x) + (flux_y[i] - before[i]) + (flux - flux_z[k])
                    flux_z[k] = flux
                    parts[0].append(value * u[k])
                    parts[1].append(value * turn(u[k], -32))
                    parts[2].append(value * turn(u[k], 64))
                    parts[3].append(value * low[k])
                for total, part in zip(sums, parts):
                    total.append(tree(part))
                before = flux_y
            u, low = after, after_low
        for k in range(n):
            case.fz[k], case.chosen[k], case.total[k] = flux_z[k], u[k], low[k]
        return [tree(total) for total in sums]

    return looped(lv.edz, group, 4, step)


GROUPS = {FINE: 1, TWIN: 2}


def solve_kernel(
    center, x_low, x_high, y_low, y_high,
    phi, message,
    flat, rows, pairs, twin_rows, *refs,
):
    lanes = center.shape[2]
    rim = (flat.shape[1] - lanes) // 2
    nx = center.shape[1]
    top = MX + nx
    for m in range(3):
        off = m * (nx + 2 * MX)
        flat[off : off + top + MX, :rim] = y_low[m]
        flat[off : off + MX, rim : rim + lanes] = x_low[m]
        flat[off + MX : off + top, rim : rim + lanes] = center[m]
        flat[off + top : off + top + MX, rim : rim + lanes] = x_high[m]
        flat[off : off + top + MX, rim + lanes :] = y_high[m]
    used = 3 * (nx + 2 * MX)
    flat[used:, :] = jnp.ones((LANES - used, flat.shape[1]), F32)
    for t in range(flat.shape[1] // LANES):
        rows[t * LANES : (t + 1) * LANES, :] = flat[:, t * LANES : (t + 1) * LANES].T

    nz = EZ * ELZ
    twin_y = rows.shape[0] // nz // 2
    for y in range(twin_y):
        both = rows[2 * y * nz : (2 * y + 1) * nz, :] + rows[(2 * y + 1) * nz : (2 * y + 2) * nz, :]
        both = both + turn(both, -1)
        at = y * nz
        pairs[at : at + nz, :] = both
        twin_rows[at : at + 8, :] = jnp.broadcast_to(0.25 * both[0:1], (8, LANES))
        twin_rows[at + 8 + nz // 2 : at + nz, :] = jnp.broadcast_to(0.25 * both[nz - 1 : nz], (8, LANES))
    for y in range(twin_y):
        at = y * nz
        middle = pairs[pl.ds(at, nz // 2, stride=2), :] + pairs[pl.ds(at + 1, nz // 2, stride=2), :]
        twin_rows[at + 8 : at + 8 + nz // 2, :] = 0.125 * middle
    twin_rows[twin_y * nz :, :] = jnp.ones((twin_rows.shape[0] - twin_y * nz, LANES), F32)

    refs = list(refs)

    def take(count):
        got = refs[:count]
        del refs[:count]
        return got

    cases = []
    for lv, source in zip(LEVELS, (rows, twin_rows)):
        (k_ref,) = take(1)
        high_refs, low_refs, w_refs = take(3), take(3), take(3)
        for z in range(lv.levels + 1):
            cell = min(max(z - 1, 0), nz - 1) if lv is FINE else min(z, lv.levels - 1) + 7
            for i in range(lv.seg):
                for c in range(COLUMNS):
                    start = (lv.edge * c + i) * nz + cell
                    k_ref[z, i, :, c * LANES : (c + 1) * LANES] = source[pl.ds(start, SUBS, stride=lv.seg * nz), :]
        spread_weights(lv, k_ref, high_refs, low_refs, w_refs)
        case = Case(lv, w_refs, take(5), take(3))
        for k in range(2 * lv.tiles):
            case.d[0][lv.inner, k] = jnp.zeros((SUBS, LANES), F32)
            case.r[lv.inner, k] = jnp.zeros((SUBS, LANES), F32)
        cases.append(case)

    def both_levels(work):
        sums = [work(n, case, GROUPS[case.lv]) for n, case in enumerate(cases)]
        return [[problem_sum(v) for v in part] for part in sums]

    rr = both_levels(lambda n, case, group: start_residual(case, group))
    alphas = [[[], []] for _ in LEVELS]
    betas = [None] * len(LEVELS)
    for step in range(3):
        dots = both_levels(lambda n, case, group: apply(case, group, step, betas[n]))
        now = [[a / b for a, b in zip(rr[n], dots[n])] for n in range(len(LEVELS))]
        for n in range(len(LEVELS)):
            for h in HALVES:
                alphas[n][h].append(now[n][h])
        if step < 2:
            new = both_levels(lambda n, case, group: reduce_residual(case, group, step, now[n]))
            betas = [[a / b for a, b in zip(new[n], rr[n])] for n in range(len(LEVELS))]
            rr = new

    split = phi.shape[0] - phi_rows(TWIN)
    phis = (phi.at[pl.ds(0, split)], phi.at[pl.ds(split, phi_rows(TWIN))])
    totals = both_levels(lambda n, case, group: finish(case, group, alphas[n], phis[n]))
    _, element, _, slot = lane_parts()
    packed = []
    for level in totals:
        parts = [v + xor_lane(v, 16) for v in level[:3]]
        parts.append(jnp.where(element == 0, level[3], turn(level[3], 16)))
        packed.append(
            jnp.where(slot == 0, parts[0], jnp.where(slot == 1, parts[1], jnp.where(slot == 2, parts[2], parts[3])))
        )
    row = jnp.where(element == 0, packed[0], packed[1])
    for r in range(0, message.shape[0], SUBS):
        message[r : r + SUBS, :] = row


def coarse_nodes(gathered, gy_count, me):
    total_rows = gathered.shape[0]
    shape = gathered.shape
    lane = lane_iota(shape)
    row = sub_iota(shape)
    corner = lane // 32
    column = lane // 8 % 2
    last = row % gy_count == gy_count - 1
    start = row % gy_count == 0
    one = gathered
    two = turn(gathered, -1)
    four = turn(gathered, -2)
    rhs = turn(gathered, -3)
    two_back = turn(two, 32)

    def next_x(u):
        return turn(u, -gy_count, 0)

    def prev_x(u):
        return turn(u, gy_count, 0)

    def next_y(u):
        ahead = jnp.where(last, turn(u, gy_count - 1, 0), turn(u, -1, 0))
        return jnp.where(column == 0, turn(u, -8), turn(ahead, 8))

    def prev_y(u):
        behind = jnp.where(start, turn(u, 1 - gy_count, 0), turn(u, 1, 0))
        return jnp.where(column == 1, turn(u, 8), turn(behind, -8))

    def by_corner(a, b, c, d):
        return jnp.where(corner == 0, a, jnp.where(corner == 1, b, jnp.where(corner == 2, c, d)))

    def corners(u):
        ux = next_x(u)
        return by_corner(u, next_y(u), ux, next_y(ux))

    def assemble(v):
        vx = prev_x(v)
        w = by_corner(v, prev_y(v), vx, prev_y(vx))
        w = w + turn(w, 64)
        return w + turn(w, 32)

    def operate(u):
        c = corners(u)
        return assemble(one * c + two * turn(c, -32) + two_back * turn(c, 32) + four * turn(c, 64))

    def total(a, b):
        v = a * b
        v = tree([v[r : r + SUBS] for r in range(0, total_rows, SUBS)])
        for shift in (4, 2, 1):
            v = v + turn(v, shift, 0)
        v = v + xor_lane(v, 8)
        return v[0:1]

    residual = -assemble(rhs)
    direction = residual
    update = jnp.zeros_like(residual)
    now = total(residual, residual)
    for step in range(2):
        image = operate(direction)
        alpha = now / total(direction, image)
        update = update + alpha * direction
        if step == 0:
            residual = residual - alpha * image
            new = total(residual, residual)
            direction = residual + new / now * direction
            now = new
    mine = jnp.where(row == me, corners(update), 0.0)
    mine = jnp.sum(mine, axis=0, keepdims=True)
    return jnp.broadcast_to(mine, (SUBS, LANES))


def turn_kernel(phi, out_ref):
    start_row, number = 0, 0
    for lv in LEVELS:
        s = lv.seg
        nz = EZ * lv.edz
        per = LANES // nz
        for i in range(s):
            for t in range(turned_tiles(lv)):
                parts = []
                for n in range(per):
                    y = lv.mx + t * per + n
                    start = start_row + (i * s + y % s) * SUBS + y // s
                    halves = [
                        phi[pl.ds(h * lv.tiles * SUBS + start, lv.edz, stride=2 * lv.tiles * SUBS), :]
                        for h in range(2)
                    ]
                    lower = lane_iota(halves[0].shape) // 16 % 2 == 0
                    parts.append(jnp.where(lower, halves[0], turn(halves[1], 16)))
                    parts.append(jnp.where(lower, turn(halves[0], -16), halves[1]))
                out_ref[number] = jnp.concatenate(parts, axis=0).T
                number += 1
        start_row += phi_rows(lv)


def pressure_kernel(gy_count, me_ref, gathered, turned, fine_out, twin_out, fine_all, twin_all):
    mine = coarse_nodes(gathered[...], gy_count, me_ref[0])
    first = 0
    for n, (lv, out_ref, all_ref) in enumerate(((FINE, fine_out, fine_all), (TWIN, twin_out, twin_all))):
        s = lv.seg
        nz = EZ * lv.edz
        tiles = turned_tiles(lv)
        lower = lane_iota() % nz < lv.edz
        scales = {}
        for c in range(COLUMNS):
            for p in range(4):
                at = p * 32 + n * 16 + c * 8
                node = jnp.broadcast_to(mine[:, at : at + 1], (SUBS, LANES))
                scales[2 * p, c] = jnp.where(lower, 1.0, node)
                scales[2 * p + 1, c] = jnp.where(lower, node, 0.0)
        for c in range(COLUMNS):
            for t in range(tiles):
                at = (c * tiles + t) * LANES
                for i in range(s):
                    value = tree(
                        [turned[first + i * tiles + t, a * 16 + c * 8 : a * 16 + c * 8 + 8, :] * scales[a, c] for a in range(8)]
                    )
                    all_ref[c * tiles + t, pl.ds(i, SUBS, stride=s), :] = value
                out_ref[:, at : at + LANES] = all_ref[c * tiles + t, lv.mx : lv.mx + lv.edge, :]
        first += s * tiles


def vmem(shape, dtype=F32):
    return pltpu.VMEM(shape, dtype)


def shards(permeability):
    nz = EZ * ELZ
    rows = permeability.shape[1]
    lanes = permeability.shape[2]
    assert rows == EL and lanes == COLUMNS * EL * nz
    rim = MX * nz
    gx, gy = lax.axis_size("gx"), lax.axis_size("gy")

    def sent(value, axis, shift):
        count = lax.axis_size(axis)
        return lax.ppermute(value, axis, [(i, (i + shift) % count) for i in range(count)])

    x_low = sent(permeability[:, rows - MX :], "gx", 1)
    x_high = sent(permeability[:, :MX], "gx", -1)

    def strip(part):
        return jnp.concatenate([x_low[:, :, part], permeability[:, :, part], x_high[:, :, part]], axis=1)

    y_low = sent(strip(slice(lanes - rim, lanes)), "gy", 1)
    y_high = sent(strip(slice(0, rim)), "gy", -1)
    halos = [x_low, x_high, y_low, y_high]
    flat_lanes = lanes + 2 * rim
    scratch = [
        vmem((LANES, flat_lanes)),
        vmem((flat_lanes, LANES)),
        vmem((flat_lanes // 2, LANES)),
        vmem((SUBS * (TWIN.seg + 2) * nz, LANES)),
    ]
    for lv in LEVELS:
        scratch.append(vmem((lv.levels + 1, lv.seg, SUBS, 2 * LANES)))
        scratch += [vmem((lv.planes * lv.seg // 2, 2 * SUBS, 2 * LANES), BF16)] * 6
        scratch += [vmem((lv.seg, lv.planes * lv.seg, SUBS, LANES))] * 3
        scratch += [vmem((lv.inner + 1, 2 * lv.tiles, SUBS, LANES))] * 5
        scratch.append(vmem((2 * lv.tiles, SUBS, LANES)))
        scratch += [vmem((lv.tiles, SUBS, LANES))] * 2
    full = pl.BlockSpec(memory_space=pltpu.VMEM)
    phi, message = pl.pallas_call(
        solve_kernel,
        out_shape=[
            vmem((sum(phi_rows(lv) for lv in LEVELS), LANES)),
            jax.ShapeDtypeStruct((gx * gy, LANES), F32),
        ],
        in_specs=[full] * 5,
        out_specs=[full] * 2,
        scratch_shapes=scratch,
        compiler_params=pltpu.CompilerParams(vmem_limit_bytes=44 * 1024 * 1024),
        name="solve",
    )(permeability, *halos)
    gathered = lax.all_to_all(message, ("gx", "gy"), 0, 0, tiled=True)
    tiles = sum(lv.seg * turned_tiles(lv) for lv in LEVELS)
    turned = pl.pallas_call(
        turn_kernel,
        out_shape=vmem((tiles, LANES, LANES)),
        in_specs=[full],
        out_specs=full,
        compiler_params=pltpu.CompilerParams(vmem_limit_bytes=16 * 1024 * 1024),
        cost_estimate=pl.CostEstimate(flops=4000000, bytes_accessed=8000000, transcendentals=0),
        name="turned",
    )(phi)
    me = (lax.axis_index("gx") * gy + lax.axis_index("gy")).astype(jnp.int32).reshape(1)
    return tuple(
        pl.pallas_call(
            functools.partial(pressure_kernel, gy),
            out_shape=[
                jax.ShapeDtypeStruct((lv.edge, COLUMNS * lv.edge * EZ * lv.edz), F32) for lv in LEVELS
            ],
            in_specs=[pl.BlockSpec(memory_space=pltpu.SMEM), full, full],
            out_specs=[full] * 2,
            scratch_shapes=[vmem((COLUMNS * turned_tiles(lv), SUBS * lv.seg, LANES)) for lv in LEVELS],
            compiler_params=pltpu.CompilerParams(vmem_limit_bytes=16 * 1024 * 1024),
            name="pressure",
        )(me, gathered, turned)
    )


def solution(mesh):
    return jax.shard_map(
        shards,
        mesh=mesh,
        in_specs=(P(None, "gx", "gy"),),
        out_specs=(P("gx", "gy"), P("gx", "gy")),
        check_vma=False,
    )
```

```python
import functools
import typing

import jax
import jax.numpy as jnp
from jax import lax
from jax.experimental import pallas as pl
from jax.experimental.pallas import tpu as pltpu
from jax.sharding import PartitionSpec as P

EL = 32
ELZ = 16
MX = 4
MZ = 2
EZ = 2
LANES = 128
SUBS = 8
COLUMNS = 2
F32 = jnp.float32
BF16 = jnp.bfloat16


class Level(typing.NamedTuple):
    edge: int
    edz: int
    mx: int
    mz: int
    spacing: float
    step: int

    @property
    def width(self):
        return self.edge + 2 * self.mx

    @property
    def inner(self):
        return self.edz + 2 * self.mz - 2

    @property
    def seg(self):
        return -(-self.width // SUBS)

    @property
    def tiles(self):
        return self.seg * self.seg

    @property
    def levels(self):
        return EZ * self.edz + 2

    @property
    def planes(self):
        return -(-(self.inner + 1) // 2) * 2


FINE = Level(EL, ELZ, MX, MZ, 1.0, 1)
TWIN = Level(EL // 2, ELZ // 2, MX // 2, MZ // 2, 2.0, 2)
LEVELS = (FINE, TWIN)


def lane_iota(shape=(SUBS, LANES)):
    return lax.broadcasted_iota(jnp.int32, shape, len(shape) - 1)


def sub_iota(shape=(SUBS, LANES)):
    return lax.broadcasted_iota(jnp.int32, shape, len(shape) - 2)


def turn(value, shift, axis=1):
    return pltpu.roll(value, shift % value.shape[axis], axis)


def lane_parts():
    lane = lane_iota()
    return lane // 32, lane // 16 % 2, lane // 8 % 2, lane % 8


class Consts:
    def __init__(self, lv):
        corner, _, _, xo = lane_parts()
        yo = sub_iota()
        ax, ay = corner // 2, corner % 2
        self.lv = lv
        s = lv.seg
        self.fx, self.fy = [], []
        self.inx, self.iny, self.facex, self.facey = [], [], [], []
        for i in range(s):
            x = xo * s + i
            y = yo * s + i
            px = (x.astype(F32) - lv.mx + 0.5) / lv.edge
            py = (y.astype(F32) - lv.mx + 0.5) / lv.edge
            self.fx.append(jnp.where(ax == 1, px, 1.0 - px))
            self.fy.append(jnp.where(ay == 1, py, 1.0 - py))
            xs = [s * o + i for o in range(SUBS)]

            def ranged(value, low, high):
                if all(low <= v <= high for v in xs):
                    return None
                return ((value >= low) & (value <= high)).astype(F32)

            self.inx.append((ranged(x, 1, lv.width - 2), ranged(x, lv.mx, lv.mx + lv.edge - 1)))
            self.iny.append((ranged(y, 1, lv.width - 2), ranged(y, lv.mx, lv.mx + lv.edge - 1)))
            cut = (lv.mx - 1, lv.mx + lv.edge - 1)
            self.facex.append(((x != cut[0]) & (x != cut[1])).astype(F32) if any(v in cut for v in xs) else None)
            self.facey.append(((y != cut[0]) & (y != cut[1])).astype(F32) if any(v in cut for v in xs) else None)
        sx = jnp.where(ax == 1, -1.0 / lv.edge, 1.0 / lv.edge).astype(F32)
        sy = jnp.where(ay == 1, -1.0 / lv.edge, 1.0 / lv.edge).astype(F32)
        self.along_x = [sx * f for f in self.fy]
        self.along_y = [sy * f for f in self.fx]

    def fz(self, plane):
        place = (jnp.asarray(plane, jnp.int32).astype(F32) - self.lv.mz + 0.5) / self.lv.edz
        return 1.0 - place, place

    def masked(self, value, i, j, kind):
        for table, index in ((self.inx, i), (self.iny, j)):
            factor = table[index][kind]
            if factor is not None:
                value = value * factor
        return value


def tree(values):
    values = list(values)
    while len(values) > 1:
        values = [a + b for a, b in zip(values[::2], values[1::2])] + (
            [values[-1]] if len(values) % 2 else []
        )
    return values[0]


def xor_lane(value, bit):
    return jnp.where(lane_iota(value.shape) // bit % 2 == 1, turn(value, bit), turn(value, -bit))


def problem_sum(value):
    for shift in (4, 2, 1):
        value = value + turn(value, shift, 0)
    for bit in (1, 2, 4):
        value = value + xor_lane(value, bit)
    return value


def spread_weights(lv, k_ref, high_refs, low_refs, w_refs):
    s = lv.seg
    wide = (SUBS, LANES)
    pos = lane_iota(wide)
    yo = sub_iota(wide)
    first = pos < 40
    third = pos >= 80
    second = (pos >= 40) & (pos < 80)
    edge_x = first & (pos >= (lv.width - 1) * lv.step)

    def one(z, i, c):
        part = slice(c * LANES, (c + 1) * LANES)
        k = k_ref[z, i, :, part]
        nbx = turn(k, -lv.step)
        nby = k_ref[z, i + 1, :, part] if i < s - 1 else turn(k_ref[z, 0, :, part], -1, 0)
        nbz = k_ref[z + 1, i, :, part]
        nb = jnp.where(first, nbx, jnp.where(second, nby, nbz))
        w = (2.0 * lv.spacing) * k * nb / (k + nb)
        bad = edge_x | (second & (yo * s + i >= lv.width - 1))
        return jnp.where(bad, 0.0, w)

    def planes(t, _):
        units = [(2 * t + n, i) for n in range(2) for i in range(s)]
        for e in range(EZ):
            made = []
            for plane, i in units:
                z = jnp.clip(e * lv.edz + plane + 1 - lv.mz, 0, lv.levels - 1)
                w0, w1 = one(z, i, 0), one(z, i, 1)
                near, wrap = turn(w1, 40), turn(w1, 48)
                made.append((jnp.where(first, w0, near), jnp.where(third, near, w0), jnp.where(third, w0, wrap)))
            for p in range(s):
                for m in range(3):
                    both = jnp.concatenate([made[2 * p][m], made[2 * p + 1][m]], axis=0)
                    high = both.astype(BF16)
                    part = slice(e * LANES, (e + 1) * LANES)
                    high_refs[m][t * s + p, :, part] = high
                    low_refs[m][t * s + p, :, part] = (both - high.astype(F32)).astype(BF16)
        return 0

    lax.fori_loop(0, lv.planes // 2, planes, 0)
    rows = lv.planes * s * SUBS
    row = lax.broadcasted_iota(jnp.int32, (2 * LANES, 2 * LANES), 0)
    lane = lax.broadcasted_iota(jnp.int32, (1, 2 * LANES), 1)
    upper = lane // LANES
    for q in range(-(-s // 2)):
        x = lane % 8 * s + 2 * q + upper
        valid = (x < lv.width) & (2 * q + upper < s)
        for m in range(3):
            segment = jnp.where(lane // 8 % 2 == 0, m, (m + 1) % 3)
            source = jnp.where(valid, lane // 16 % 2 * LANES + segment * 40 + lv.step * x, -1)
            pick = (row == source).astype(F32).astype(BF16)
            out = jnp.dot(high_refs[m][...].reshape(rows, 2 * LANES), pick, preferred_element_type=F32)
            out = out + jnp.dot(low_refs[m][...].reshape(rows, 2 * LANES), pick, preferred_element_type=F32)
            for half in range(min(2, s - 2 * q)):
                part = out[:, half * LANES : (half + 1) * LANES]
                w_refs[m][2 * q + half] = part.reshape(lv.planes * s, SUBS, LANES)


class Case:
    def __init__(self, lv, w_refs, fields, planes):
        self.lv, self.cs, self.w_refs = lv, Consts(lv), w_refs
        self.d, self.q, self.r = fields[:3], fields[3], fields[4]
        self.fz, self.chosen, self.total = planes

    def weights(self, plane):
        s = self.lv.seg
        return lambda m, i, j: self.w_refs[m][i, plane * s + j]


HALVES = (0, 1)


def phi_rows(lv):
    return lv.edz * (lv.tiles + lv.seg) * SUBS


def turned_tiles(lv):
    return lv.edge * EZ * lv.edz // LANES


def looped(count, group, sums, step):
    def body(t, sums):
        return tuple(a + b for a, b in zip(sums, step(t * group)))

    start = tuple(jnp.zeros((SUBS, LANES), F32) for _ in range(sums))
    return list(lax.fori_loop(0, count // group, body, start))


def start_residual(case, group):
    lv, cs, s = case.lv, case.cs, case.lv.seg

    def step(z0):
        total = [[], []]
        for z in [z0 + n for n in range(group)]:
            get, below = case.weights(z + 1), case.weights(z)
            gz = cs.fz(z + 1)
            last = [get(1, i, s - 1) * cs.along_y[i] for i in range(s)]
            before = [turn(v, 1, 0) for v in last]
            for j in range(s):
                flux_y = last if j == s - 1 else [get(1, i, j) * cs.along_y[i] for i in range(s)]
                flux_x = [get(0, i, j) * cs.along_x[j] for i in range(s)]
                squares = [[], []]
                for i in range(s):
                    k = i * s + j
                    prev_x = flux_x[i - 1] if i else turn(flux_x[s - 1], 1)
                    flat = (prev_x - flux_x[i]) + (before[i] - flux_y[i])
                    flat = cs.masked(flat, i, j, 0)
                    tall = (cs.fx[i] * cs.fy[j]) * (1.0 / lv.edz) * (below(2, i, j) - get(2, i, j))
                    tall = cs.masked(tall, i, j, 0)
                    for h, value in enumerate((flat * gz[0] + tall, flat * gz[1] - tall)):
                        case.d[0][z, h * lv.tiles + k] = value
                        squares[h].append(value * value)
                for h in HALVES:
                    total[h].append(tree(squares[h]))
                before = flux_y
        return [tree(t) for t in total]

    return looped(lv.inner, group, 2, step)


def row_jumps(u, s, j):
    jump_x = [u[i * s + j] - (u[(i + 1) * s + j] if i < s - 1 else turn(u[j], -1)) for i in range(s)]
    jump_y = [u[i * s + j] - (u[i * s + j + 1] if j < s - 1 else turn(u[i * s], -1, 0)) for i in range(s)]
    return jump_x, jump_y


def apply(case, group, number, betas):
    lv, cs, s = case.lv, case.cs, case.lv.seg
    keep = number < 2
    n = lv.tiles

    def fresh(z, h, k):
        at = h * n + k
        if number == 0:
            return case.d[0][z, at]
        value = case.r[z, at] + betas[h] * case.d[number - 1][z, at]
        case.d[number][z, at] = value
        return value

    firsts = []
    get = case.weights(0)
    for h in HALVES:
        terms = []
        for k in range(n):
            value = fresh(0, h, k)
            flux = -get(2, k // s, k % s) * value
            if keep:
                case.fz[h * n + k] = flux
            else:
                terms.append(-flux * value)
        firsts.append(tree(terms) if terms else 0.0)

    def step(z0):
        total = [[], []]
        u = [[case.d[number][z0, h * n + k] for k in range(n)] for h in HALVES]
        flux_z = [[case.fz[h * n + k] for k in range(n)] for h in HALVES] if keep else None
        for z in [z0 + t for t in range(group)]:
            get = case.weights(z + 1)
            after = [[None] * n for _ in HALVES]
            if keep:
                wy = [get(1, i, s - 1) for i in range(s)]
                last = [[wy[i] * (u[h][i * s + s - 1] - turn(u[h][i * s], -1, 0)) for i in range(s)] for h in HALVES]
                before = [[turn(v, 1, 0) for v in last[h]] for h in HALVES]
            for j in range(s):
                wx = [get(0, i, j) for i in range(s)]
                wy = [get(1, i, j) for i in range(s)]
                wz = [get(2, i, j) for i in range(s)]
                for h in HALVES:
                    jump_x, jump_y = row_jumps(u[h], s, j)
                    flux_x = [w * v for w, v in zip(wx, jump_x)]
                    flux_y = last[h] if keep and j == s - 1 else [w * v for w, v in zip(wy, jump_y)]
                    terms = []
                    for i in range(s):
                        k = i * s + j
                        after[h][k] = fresh(z + 1, h, k)
                        jump = u[h][k] - after[h][k]
                        flux = wz[i] * jump
                        if keep:
                            prev_x = flux_x[i - 1] if i else turn(flux_x[s - 1], 1)
                            value = (flux_x[i] - prev_x) + (flux_y[i] - before[h][i]) + (flux - flux_z[h][k])
                            flux_z[h][k] = flux
                            value = cs.masked(value, i, j, 0)
                            case.q[z, h * n + k] = value
                            terms.append(u[h][k] * value)
                        else:
                            terms.append((flux * jump + flux_x[i] * jump_x[i]) + flux_y[i] * jump_y[i])
                    total[h].append(tree(terms))
                    if keep:
                        before[h] = flux_y
            u = after
        if keep:
            for h in HALVES:
                for k in range(n):
                    case.fz[h * n + k] = flux_z[h][k]
        return [tree(t) for t in total]

    return [a + b for a, b in zip(looped(lv.inner, group, 2, step), firsts)]


def reduce_residual(case, group, number, alphas):
    lv = case.lv

    def step(z0):
        total = [[], []]
        source = case.d[0] if number == 0 else case.r
        for z in [z0 + n for n in range(group)]:
            for h in HALVES:
                squares = []
                for k in range(lv.tiles):
                    at = h * lv.tiles + k
                    value = source[z, at] - alphas[h] * case.q[z, at]
                    case.r[z, at] = value
                    squares.append(value * value)
                total[h].append(tree(squares))
        return [tree(t) for t in total]

    return looped(lv.inner, group, 2, step)


def finish(case, group, alphas, phi_ref):
    lv, cs, s = case.lv, case.cs, case.lv.seg
    n = lv.tiles
    corner, element, _, _ = lane_parts()
    lower = element == 0

    def fresh(z, i, j, gz):
        k = i * s + j
        inner = z + lv.mz - 1
        both = cs.fx[i] * cs.fy[j]
        values = []
        for h in HALVES:
            value = both * gz[h]
            for alpha, d_ref in zip(alphas[h], case.d):
                value = value + alpha * d_ref[inner, h * n + k]
            value = cs.masked(value, i, j, 1)
            values.append(value)
        total = values[0] + turn(values[0], 32)
        chosen = jnp.where(lower, values[1], values[0])
        at = pl.multiple_of((z * n + k) * SUBS, SUBS)
        phi_ref[pl.ds(at, SUBS), :] = chosen
        return chosen, total + turn(total, 64)

    def pack(z, j, totals):
        packed = totals[0]
        for i in range(1, min(s, 4)):
            packed = jnp.where(corner == i, totals[i], packed)
        if s > 4:
            packed = jnp.where(lower, packed, turn(totals[4], 16))
        at = pl.multiple_of((lv.edz * n + z * s + j) * SUBS, SUBS)
        phi_ref[pl.ds(at, SUBS), :] = packed

    gz = cs.fz(lv.mz)
    for i in range(s):
        for j in range(s):
            k = i * s + j
            case.chosen[k], case.total[k] = fresh(0, i, j, gz)
            case.fz[k] = jnp.zeros((SUBS, LANES), F32)
    for j in range(s):
        pack(0, j, [case.total[i * s + j] for i in range(s)])

    def cut(values, table):
        return [v if f is None else v * f for v, f in zip(values, table)]

    def step(z0):
        sums = [[] for _ in range(4)]
        u = [case.chosen[k] for k in range(n)]
        low = [case.total[k] for k in range(n)]
        flux_z = [case.fz[k] for k in range(n)]
        for z in [z0 + t for t in range(group)]:
            get = case.weights(z + lv.mz)
            up = jnp.minimum(z + 1, lv.edz - 1)
            gz = cs.fz(up + lv.mz)
            after, after_low = [None] * n, [None] * n
            last = [get(1, i, s - 1) * (u[i * s + s - 1] - turn(u[i * s], -1, 0)) for i in range(s)]
            last = cut(last, [cs.facey[s - 1]] * s)
            before = [turn(v, 1, 0) for v in last]
            for j in range(s):
                jump_x, jump_y = row_jumps(u, s, j)
                flux_x = cut([get(0, i, j) * jump_x[i] for i in range(s)], cs.facex)
                flux_y = last
                if j < s - 1:
                    flux_y = cut([get(1, i, j) * jump_y[i] for i in range(s)], [cs.facey[j]] * s)
                parts = [[] for _ in sums]
                for i in range(s):
                    k = i * s + j
                    after[k], after_low[k] = fresh(up, i, j, gz)
                    flux = get(2, i, j) * (u[k] - after[k])
                    prev_x = flux_x[i - 1] if i else turn(flux_x[s - 1], 1)
                    value = (flux_x[i] - prev_x) + (flux_y[i] - before[i]) + (flux - flux_z[k])
                    flux_z[k] = flux
                    parts[0].append(value * u[k])
                    parts[1].append(value * turn(u[k], -32))
                    parts[2].append(value * turn(u[k], 64))
                    parts[3].append(value * low[k])
                pack(up, j, [after_low[i * s + j] for i in range(s)])
                for total, part in zip(sums, parts):
                    total.append(tree(part))
                before = flux_y
            u, low = after, after_low
        for k in range(n):
            case.fz[k], case.chosen[k], case.total[k] = flux_z[k], u[k], low[k]
        return [tree(total) for total in sums]

    return looped(lv.edz, group, 4, step)


GROUPS = {FINE: 1, TWIN: 8}


def place_kernel(center, out_ref):
    nx = center.shape[1]
    out_ref[...] = jnp.ones(out_ref.shape, F32)
    for m in range(3):
        off = m * (nx + 2 * MX) + MX
        out_ref[off : off + nx, :] = center[m]


def solve_kernel(
    inside, x_low, x_high, y_low, y_high,
    phi, message,
    flat, sides, rows, pairs, twin_rows, *refs,
):
    lanes = inside.shape[1]
    rim = y_low.shape[2]
    wide = y_low.shape[1]
    for m in range(3):
        off = m * wide
        flat[off : off + MX, :] = x_low[m]
        flat[off + wide - MX : off + wide, :] = x_high[m]
        sides[off : off + wide, :rim] = y_low[m]
        sides[off : off + wide, rim:] = y_high[m]
    sides[3 * wide :, :] = jnp.ones((LANES - 3 * wide, sides.shape[1]), F32)
    row = sub_iota((LANES, LANES))
    place = row % wide
    outer = (row < 3 * wide) & ((place < MX) | (place >= wide - MX))
    for t in range(rim // LANES):
        low, high = slice(t * LANES, (t + 1) * LANES), slice(rim + t * LANES, rim + (t + 1) * LANES)
        rows[low, :] = sides[:, low].T
        rows[lanes + rim + t * LANES : lanes + rim + (t + 1) * LANES, :] = sides[:, high].T
    for t in range(lanes // LANES):
        part = slice(t * LANES, (t + 1) * LANES)
        rows[rim + t * LANES : rim + (t + 1) * LANES, :] = jnp.where(outer, flat[:, part], inside[:, part]).T

    nz = EZ * ELZ
    twin_y = rows.shape[0] // nz // 2
    for y in range(twin_y):
        both = rows[2 * y * nz : (2 * y + 1) * nz, :] + rows[(2 * y + 1) * nz : (2 * y + 2) * nz, :]
        both = both + turn(both, -1)
        at = y * nz
        pairs[at : at + nz, :] = both
        twin_rows[at : at + 8, :] = jnp.broadcast_to(0.25 * both[0:1], (8, LANES))
        twin_rows[at + 8 + nz // 2 : at + nz, :] = jnp.broadcast_to(0.25 * both[nz - 1 : nz], (8, LANES))
    for y in range(twin_y):
        at = y * nz
        middle = pairs[pl.ds(at, nz // 2, stride=2), :] + pairs[pl.ds(at + 1, nz // 2, stride=2), :]
        twin_rows[at + 8 : at + 8 + nz // 2, :] = 0.125 * middle
    twin_rows[twin_y * nz :, :] = jnp.ones((twin_rows.shape[0] - twin_y * nz, LANES), F32)

    refs = list(refs)

    def take(count):
        got = refs[:count]
        del refs[:count]
        return got

    cases = []
    for lv, source in zip(LEVELS, (rows, twin_rows)):
        (k_ref,) = take(1)
        high_refs, low_refs, w_refs = take(3), take(3), take(3)
        for z in range(lv.levels + 1):
            cell = min(max(z - 1, 0), nz - 1) if lv is FINE else min(z, lv.levels - 1) + 7
            for i in range(lv.seg):
                for c in range(COLUMNS):
                    start = (lv.edge * c + i) * nz + cell
                    k_ref[z, i, :, c * LANES : (c + 1) * LANES] = source[pl.ds(start, SUBS, stride=lv.seg * nz), :]
        spread_weights(lv, k_ref, high_refs, low_refs, w_refs)
        case = Case(lv, w_refs, take(5), take(3))
        for k in range(2 * lv.tiles):
            case.d[0][lv.inner, k] = jnp.zeros((SUBS, LANES), F32)
            case.r[lv.inner, k] = jnp.zeros((SUBS, LANES), F32)
        cases.append(case)

    def both_levels(work):
        sums = [work(n, case, GROUPS[case.lv]) for n, case in enumerate(cases)]
        return [[problem_sum(v) for v in part] for part in sums]

    rr = both_levels(lambda n, case, group: start_residual(case, group))
    alphas = [[[], []] for _ in LEVELS]
    betas = [None] * len(LEVELS)
    for step in range(3):
        dots = both_levels(lambda n, case, group: apply(case, group, step, betas[n]))
        now = [[a / b for a, b in zip(rr[n], dots[n])] for n in range(len(LEVELS))]
        for n in range(len(LEVELS)):
            for h in HALVES:
                alphas[n][h].append(now[n][h])
        if step < 2:
            new = both_levels(lambda n, case, group: reduce_residual(case, group, step, now[n]))
            betas = [[a / b for a, b in zip(new[n], rr[n])] for n in range(len(LEVELS))]
            rr = new

    split = phi.shape[0] - phi_rows(TWIN)
    phis = (phi.at[pl.ds(0, split)], phi.at[pl.ds(split, phi_rows(TWIN))])
    totals = both_levels(lambda n, case, group: finish(case, group, alphas[n], phis[n]))
    _, element, _, slot = lane_parts()
    packed = []
    for level in totals:
        parts = [v + xor_lane(v, 16) for v in level[:3]]
        parts.append(jnp.where(element == 0, level[3], turn(level[3], 16)))
        packed.append(
            jnp.where(slot == 0, parts[0], jnp.where(slot == 1, parts[1], jnp.where(slot == 2, parts[2], parts[3])))
        )
    row = jnp.where(element == 0, packed[0], packed[1])
    for r in range(0, message.shape[0], SUBS):
        message[r : r + SUBS, :] = row


def coarse_nodes(gathered, gy_count, me):
    total_rows = gathered.shape[0]
    shape = gathered.shape
    lane = lane_iota(shape)
    row = sub_iota(shape)
    corner = lane // 32
    column = lane // 8 % 2
    last = row % gy_count == gy_count - 1
    start = row % gy_count == 0
    one = gathered
    two = turn(gathered, -1)
    four = turn(gathered, -2)
    rhs = turn(gathered, -3)
    two_back = turn(two, 32)

    def next_x(u):
        return turn(u, -gy_count, 0)

    def prev_x(u):
        return turn(u, gy_count, 0)

    def next_y(u):
        ahead = jnp.where(last, turn(u, gy_count - 1, 0), turn(u, -1, 0))
        return jnp.where(column == 0, turn(u, -8), turn(ahead, 8))

    def prev_y(u):
        behind = jnp.where(start, turn(u, 1 - gy_count, 0), turn(u, 1, 0))
        return jnp.where(column == 1, turn(u, 8), turn(behind, -8))

    def by_corner(a, b, c, d):
        return jnp.where(corner == 0, a, jnp.where(corner == 1, b, jnp.where(corner == 2, c, d)))

    def corners(u):
        ux = next_x(u)
        return by_corner(u, next_y(u), ux, next_y(ux))

    def assemble(v):
        vx = prev_x(v)
        w = by_corner(v, prev_y(v), vx, prev_y(vx))
        w = w + turn(w, 64)
        return w + turn(w, 32)

    def operate(u):
        c = corners(u)
        return assemble(one * c + two * turn(c, -32) + two_back * turn(c, 32) + four * turn(c, 64))

    def total(a, b):
        v = a * b
        v = tree([v[r : r + SUBS] for r in range(0, total_rows, SUBS)])
        for shift in (4, 2, 1):
            v = v + turn(v, shift, 0)
        v = v + xor_lane(v, 8)
        return v[0:1]

    residual = -assemble(rhs)
    direction = residual
    update = jnp.zeros_like(residual)
    now = total(residual, residual)
    for step in range(2):
        image = operate(direction)
        alpha = now / total(direction, image)
        update = update + alpha * direction
        if step == 0:
            residual = residual - alpha * image
            new = total(residual, residual)
            direction = residual + new / now * direction
            now = new
    mine = jnp.where(row == me, corners(update), 0.0)
    mine = jnp.sum(mine, axis=0, keepdims=True)
    return jnp.broadcast_to(mine, (SUBS, LANES))


def turn_kernel(phi, out_ref):
    start_row, number = 0, 0
    for lv in LEVELS:
        s = lv.seg
        nz = EZ * lv.edz
        per = LANES // nz
        sums_row = start_row + lv.edz * lv.tiles * SUBS
        for i in range(s):
            for t in range(turned_tiles(lv)):
                parts = []
                for n in range(per):
                    yo, j = divmod(lv.mx + t * per + n, s)
                    chosen = phi[pl.ds(start_row + (i * s + j) * SUBS + yo, lv.edz, stride=lv.tiles * SUBS), :]
                    total = phi[pl.ds(sums_row + j * SUBS + yo, lv.edz, stride=s * SUBS), :]
                    lower = lane_iota(chosen.shape) // 16 % 2 == 0
                    parts.append(jnp.where(lower, chosen, turn(total, 16) if i < 4 else total))
                    parts.append(jnp.where(lower, turn(chosen, -16), 0.0))
                out_ref[number] = jnp.concatenate(parts, axis=0).T
                number += 1
        start_row += phi_rows(lv)


def pressure_kernel(gy_count, me_ref, gathered, turned, fine_out, twin_out, fine_all, twin_all):
    mine = coarse_nodes(gathered[...], gy_count, me_ref[0])
    first = 0
    for n, (lv, out_ref, all_ref) in enumerate(((FINE, fine_out, fine_all), (TWIN, twin_out, twin_all))):
        s = lv.seg
        tiles = turned_tiles(lv)
        nodes = {}
        for c in range(COLUMNS):
            for p in range(4):
                at = p * 32 + n * 16 + c * 8
                nodes[p, c] = jnp.broadcast_to(mine[:, at : at + 1], (SUBS, LANES))
        for c in range(COLUMNS):
            for t in range(tiles):
                at = (c * tiles + t) * LANES
                for i in range(s):
                    def part(group):
                        return turned[first + i * tiles + t, group * 16 + c * 8 : group * 16 + c * 8 + 8, :]

                    value = tree([part(2 * p) * nodes[p, c] for p in range(4)]) + part(2 * (i % 4) + 1)
                    all_ref[c * tiles + t, pl.ds(i, SUBS, stride=s), :] = value
                out_ref[:, at : at + LANES] = all_ref[c * tiles + t, lv.mx : lv.mx + lv.edge, :]
        first += s * tiles


def vmem(shape, dtype=F32):
    return pltpu.VMEM(shape, dtype)


def shards(permeability):
    nz = EZ * ELZ
    rows = permeability.shape[1]
    lanes = permeability.shape[2]
    assert rows == EL and lanes == COLUMNS * EL * nz
    rim = MX * nz
    gx, gy = lax.axis_size("gx"), lax.axis_size("gy")

    def sent(value, axis, shift):
        count = lax.axis_size(axis)
        return lax.ppermute(value, axis, [(i, (i + shift) % count) for i in range(count)])

    x_low = sent(permeability[:, rows - MX :], "gx", 1)
    x_high = sent(permeability[:, :MX], "gx", -1)

    def strip(part):
        return jnp.concatenate([x_low[:, :, part], permeability[:, :, part], x_high[:, :, part]], axis=1)

    y_low = sent(strip(slice(lanes - rim, lanes)), "gy", 1)
    y_high = sent(strip(slice(0, rim)), "gy", -1)
    halos = [x_low, x_high, y_low, y_high]
    flat_lanes = lanes + 2 * rim
    scratch = [
        vmem((LANES, lanes)),
        vmem((LANES, 2 * rim)),
        vmem((flat_lanes, LANES)),
        vmem((flat_lanes // 2, LANES)),
        vmem((SUBS * (TWIN.seg + 2) * nz, LANES)),
    ]
    for lv in LEVELS:
        scratch.append(vmem((lv.levels + 1, lv.seg, SUBS, 2 * LANES)))
        scratch += [vmem((lv.planes * lv.seg // 2, 2 * SUBS, 2 * LANES), BF16)] * 6
        scratch += [vmem((lv.seg, lv.planes * lv.seg, SUBS, LANES))] * 3
        scratch += [vmem((lv.inner + 1, 2 * lv.tiles, SUBS, LANES))] * 5
        scratch.append(vmem((2 * lv.tiles, SUBS, LANES)))
        scratch += [vmem((lv.tiles, SUBS, LANES))] * 2
    full = pl.BlockSpec(memory_space=pltpu.VMEM)
    inside = pl.pallas_call(
        place_kernel,
        out_shape=vmem((LANES, lanes)),
        in_specs=[full],
        out_specs=full,
        compiler_params=pltpu.CompilerParams(vmem_limit_bytes=8 * 1024 * 1024),
        cost_estimate=pl.CostEstimate(flops=1000000, bytes_accessed=4000000, transcendentals=0),
        name="place",
    )(permeability)
    phi, message = pl.pallas_call(
        solve_kernel,
        out_shape=[
            vmem((sum(phi_rows(lv) for lv in LEVELS), LANES)),
            jax.ShapeDtypeStruct((gx * gy, LANES), F32),
        ],
        in_specs=[full] * 5,
        out_specs=[full] * 2,
        scratch_shapes=scratch,
        compiler_params=pltpu.CompilerParams(vmem_limit_bytes=44 * 1024 * 1024),
        name="solve",
    )(inside, *halos)
    gathered = lax.all_to_all(message, ("gx", "gy"), 0, 0, tiled=True)
    tiles = sum(lv.seg * turned_tiles(lv) for lv in LEVELS)
    turned = pl.pallas_call(
        turn_kernel,
        out_shape=vmem((tiles, LANES, LANES)),
        in_specs=[full],
        out_specs=full,
        compiler_params=pltpu.CompilerParams(vmem_limit_bytes=16 * 1024 * 1024),
        cost_estimate=pl.CostEstimate(flops=4000000, bytes_accessed=8000000, transcendentals=0),
        name="turned",
    )(phi)
    me = (lax.axis_index("gx") * gy + lax.axis_index("gy")).astype(jnp.int32).reshape(1)
    return tuple(
        pl.pallas_call(
            functools.partial(pressure_kernel, gy),
            out_shape=[
                jax.ShapeDtypeStruct((lv.edge, COLUMNS * lv.edge * EZ * lv.edz), F32) for lv in LEVELS
            ],
            in_specs=[pl.BlockSpec(memory_space=pltpu.SMEM), full, full],
            out_specs=[full] * 2,
            scratch_shapes=[vmem((COLUMNS * turned_tiles(lv), SUBS * lv.seg, LANES)) for lv in LEVELS],
            compiler_params=pltpu.CompilerParams(vmem_limit_bytes=16 * 1024 * 1024),
            name="pressure",
        )(me, gathered, turned)
    )


def solution(mesh):
    return jax.shard_map(
        shards,
        mesh=mesh,
        in_specs=(P(None, "gx", "gy"),),
        out_specs=(P("gx", "gy"), P("gx", "gy")),
        check_vma=False,
    )
```

```python
import functools
import typing

import jax
import jax.numpy as jnp
from jax import lax
from jax.experimental import pallas as pl
from jax.experimental.pallas import tpu as pltpu
from jax.sharding import PartitionSpec as P

EL = 32
ELZ = 16
MX = 4
MZ = 2
EZ = 2
LANES = 128
SUBS = 8
COLUMNS = 2
F32 = jnp.float32


class Level(typing.NamedTuple):
    edge: int
    edz: int
    mx: int
    mz: int
    spacing: float
    step: int

    @property
    def width(self):
        return self.edge + 2 * self.mx

    @property
    def inner(self):
        return self.edz + 2 * self.mz - 2

    @property
    def seg(self):
        return -(-self.width // SUBS)

    @property
    def tiles(self):
        return self.seg * self.seg

    @property
    def levels(self):
        return EZ * self.edz + 2

    @property
    def planes(self):
        return self.inner + 1


FINE = Level(EL, ELZ, MX, MZ, 1.0, 1)
TWIN = Level(EL // 2, ELZ // 2, MX // 2, MZ // 2, 2.0, 2)
LEVELS = (FINE, TWIN)


def lane_iota(shape=(SUBS, LANES)):
    return lax.broadcasted_iota(jnp.int32, shape, len(shape) - 1)


def sub_iota(shape=(SUBS, LANES)):
    return lax.broadcasted_iota(jnp.int32, shape, len(shape) - 2)


def turn(value, shift, axis=1):
    return pltpu.roll(value, shift % value.shape[axis], axis)


def lane_parts():
    lane = lane_iota()
    return lane // 32, lane // 16 % 2, lane // 8 % 2, lane % 8


class Consts:
    def __init__(self, lv):
        corner, _, _, xo = lane_parts()
        yo = sub_iota()
        ax, ay = corner // 2, corner % 2
        self.lv = lv
        s = lv.seg
        self.fx, self.fy = [], []
        self.inx, self.iny, self.facex, self.facey = [], [], [], []
        for i in range(s):
            x = xo * s + i
            y = yo * s + i
            px = (x.astype(F32) - lv.mx + 0.5) / lv.edge
            py = (y.astype(F32) - lv.mx + 0.5) / lv.edge
            self.fx.append(jnp.where(ax == 1, px, 1.0 - px))
            self.fy.append(jnp.where(ay == 1, py, 1.0 - py))
            xs = [s * o + i for o in range(SUBS)]

            def ranged(value, low, high):
                if all(low <= v <= high for v in xs):
                    return None
                return ((value >= low) & (value <= high)).astype(F32)

            self.inx.append((ranged(x, 1, lv.width - 2), ranged(x, lv.mx, lv.mx + lv.edge - 1)))
            self.iny.append((ranged(y, 1, lv.width - 2), ranged(y, lv.mx, lv.mx + lv.edge - 1)))
            cut = (lv.mx - 1, lv.mx + lv.edge - 1)
            self.facex.append(((x != cut[0]) & (x != cut[1])).astype(F32) if any(v in cut for v in xs) else None)
            self.facey.append(((y != cut[0]) & (y != cut[1])).astype(F32) if any(v in cut for v in xs) else None)
        sx = jnp.where(ax == 1, -1.0 / lv.edge, 1.0 / lv.edge).astype(F32)
        sy = jnp.where(ay == 1, -1.0 / lv.edge, 1.0 / lv.edge).astype(F32)
        self.along_x = [sx * f for f in self.fy]
        self.along_y = [sy * f for f in self.fx]

    def fz(self, plane):
        place = (jnp.asarray(plane, jnp.int32).astype(F32) - self.lv.mz + 0.5) / self.lv.edz
        return 1.0 - place, place

    def masked(self, value, i, j, kind):
        for table, index in ((self.inx, i), (self.iny, j)):
            factor = table[index][kind]
            if factor is not None:
                value = value * factor
        return value


def tree(values):
    values = list(values)
    while len(values) > 1:
        values = [a + b for a, b in zip(values[::2], values[1::2])] + (
            [values[-1]] if len(values) % 2 else []
        )
    return values[0]


def xor_lane(value, bit):
    return jnp.where(lane_iota(value.shape) // bit % 2 == 1, turn(value, bit), turn(value, -bit))


def problem_sum(value):
    for shift in (4, 2, 1):
        value = value + turn(value, shift, 0)
    for bit in (1, 2, 4):
        value = value + xor_lane(value, bit)
    return value


def spread_weights(lv, k_ref, w_refs):
    s = lv.seg
    lane = lane_iota()
    group = lane // 8
    yo = sub_iota()
    first = group < s
    second = (group >= s) & (group < 2 * s)
    turned_x = group % s == s - 1
    edge_x = first & (lane % 8 * s + group >= lv.width - 1)
    quarter = [group % 4 == n for n in range(4)]
    block = [group // 4 == n for n in range(4)]

    def choose(masks, values):
        return jnp.where(masks[0], values[0], jnp.where(masks[1], values[1], jnp.where(masks[2], values[2], values[3])))

    def one(z, j, c):
        part = slice(c * LANES, (c + 1) * LANES)
        k = k_ref[z, j, :, part]
        nbx = jnp.where(turned_x, turn(k, 8 * (s - 1) - 1), turn(k, -8))
        nby = k_ref[z, j + 1, :, part] if j < s - 1 else turn(k_ref[z, 0, :, part], -1, 0)
        nbz = k_ref[z + 1, j, :, part]
        nb = jnp.where(first, nbx, jnp.where(second, nby, nbz))
        w = (2.0 * lv.spacing) * k * nb / (k + nb)
        return jnp.where(edge_x | (second & (yo * s + j >= lv.width - 1)), 0.0, w)

    def plane(number, _):
        for j in range(s):
            parts = []
            for e in range(EZ):
                z = jnp.clip(e * lv.edz + number + 1 - lv.mz, 0, lv.levels - 1)
                for c in range(COLUMNS):
                    parts.append(turn(one(z, j, c), 8 * len(parts)))
            for low in range(4):
                mixed = choose([quarter[(low + t) % 4] for t in range(4)], parts)
                mixed = turn(mixed, -8 * low) if low else mixed
                shifted = [mixed] + [turn(mixed, 32 * t) for t in range(1, 4)]
                for w in range(4):
                    target = low + 4 * w
                    if target < 3 * s:
                        value = choose([block[(w + t) % 4] for t in range(4)], shifted)
                        w_refs[target // s][target % s, number * s + j] = value
        return 0

    lax.fori_loop(0, lv.inner + 1, plane, 0)


class Case:
    def __init__(self, lv, w_refs, fields, planes):
        self.lv, self.cs, self.w_refs = lv, Consts(lv), w_refs
        self.d, self.q, self.r = fields[:3], fields[3], fields[4]
        self.fz, self.chosen, self.total = planes

    def weights(self, plane):
        s = self.lv.seg
        return lambda m, i, j: self.w_refs[m][i, plane * s + j]


HALVES = (0, 1)


def plane_rows(lv):
    return (lv.tiles + lv.seg) * SUBS


def phi_rows(lv):
    return lv.edz * plane_rows(lv)


def turned_tiles(lv):
    return lv.edge * EZ * lv.edz // LANES


def looped(count, group, sums, step):
    def body(t, sums):
        return tuple(a + b for a, b in zip(sums, step(t * group)))

    start = tuple(jnp.zeros((SUBS, LANES), F32) for _ in range(sums))
    return list(lax.fori_loop(0, count // group, body, start))


def start_residual(case, group):
    lv, cs, s = case.lv, case.cs, case.lv.seg

    def step(z0):
        total = [[], []]
        for z in [z0 + n for n in range(group)]:
            get, below = case.weights(z + 1), case.weights(z)
            gz = cs.fz(z + 1)
            last = [get(1, i, s - 1) * cs.along_y[i] for i in range(s)]
            before = [turn(v, 1, 0) for v in last]
            for j in range(s):
                flux_y = last if j == s - 1 else [get(1, i, j) * cs.along_y[i] for i in range(s)]
                flux_x = [get(0, i, j) * cs.along_x[j] for i in range(s)]
                squares = [[], []]
                for i in range(s):
                    k = i * s + j
                    prev_x = flux_x[i - 1] if i else turn(flux_x[s - 1], 1)
                    flat = (prev_x - flux_x[i]) + (before[i] - flux_y[i])
                    flat = cs.masked(flat, i, j, 0)
                    tall = (cs.fx[i] * cs.fy[j]) * (1.0 / lv.edz) * (below(2, i, j) - get(2, i, j))
                    tall = cs.masked(tall, i, j, 0)
                    for h, value in enumerate((flat * gz[0] + tall, flat * gz[1] - tall)):
                        case.d[0][z, h * lv.tiles + k] = value
                        squares[h].append(value * value)
                for h in HALVES:
                    total[h].append(tree(squares[h]))
                before = flux_y
        return [tree(t) for t in total]

    return looped(lv.inner, group, 2, step)


def row_jumps(u, s, j):
    jump_x = [u[i * s + j] - (u[(i + 1) * s + j] if i < s - 1 else turn(u[j], -1)) for i in range(s)]
    jump_y = [u[i * s + j] - (u[i * s + j + 1] if j < s - 1 else turn(u[i * s], -1, 0)) for i in range(s)]
    return jump_x, jump_y


def apply(case, group, number, betas):
    lv, cs, s = case.lv, case.cs, case.lv.seg
    keep = number < 2
    n = lv.tiles

    def fresh(z, h, k):
        at = h * n + k
        if number == 0:
            return case.d[0][z, at]
        value = case.r[z, at] + betas[h] * case.d[number - 1][z, at]
        case.d[number][z, at] = value
        return value

    firsts = []
    get = case.weights(0)
    for h in HALVES:
        terms = []
        for k in range(n):
            value = fresh(0, h, k)
            flux = -get(2, k // s, k % s) * value
            if keep:
                case.fz[h * n + k] = flux
            else:
                terms.append(-flux * value)
        firsts.append(tree(terms) if terms else 0.0)

    def step(z0):
        total = [[], []]
        u = [[case.d[number][z0, h * n + k] for k in range(n)] for h in HALVES]
        flux_z = [[case.fz[h * n + k] for k in range(n)] for h in HALVES] if keep else None
        for z in [z0 + t for t in range(group)]:
            get = case.weights(z + 1)
            after = [[None] * n for _ in HALVES]
            if keep:
                wy = [get(1, i, s - 1) for i in range(s)]
                last = [[wy[i] * (u[h][i * s + s - 1] - turn(u[h][i * s], -1, 0)) for i in range(s)] for h in HALVES]
                before = [[turn(v, 1, 0) for v in last[h]] for h in HALVES]
            for j in range(s):
                wx = [get(0, i, j) for i in range(s)]
                wy = [get(1, i, j) for i in range(s)]
                wz = [get(2, i, j) for i in range(s)]
                for h in HALVES:
                    jump_x, jump_y = row_jumps(u[h], s, j)
                    flux_x = [w * v for w, v in zip(wx, jump_x)]
                    flux_y = last[h] if keep and j == s - 1 else [w * v for w, v in zip(wy, jump_y)]
                    terms = []
                    for i in range(s):
                        k = i * s + j
                        after[h][k] = fresh(z + 1, h, k)
                        jump = u[h][k] - after[h][k]
                        flux = wz[i] * jump
                        if keep:
                            prev_x = flux_x[i - 1] if i else turn(flux_x[s - 1], 1)
                            value = (flux_x[i] - prev_x) + (flux_y[i] - before[h][i]) + (flux - flux_z[h][k])
                            flux_z[h][k] = flux
                            value = cs.masked(value, i, j, 0)
                            case.q[z, h * n + k] = value
                            terms.append(u[h][k] * value)
                        else:
                            terms.append((flux * jump + flux_x[i] * jump_x[i]) + flux_y[i] * jump_y[i])
                    total[h].append(tree(terms))
                    if keep:
                        before[h] = flux_y
            u = after
        if keep:
            for h in HALVES:
                for k in range(n):
                    case.fz[h * n + k] = flux_z[h][k]
        return [tree(t) for t in total]

    return [a + b for a, b in zip(looped(lv.inner, group, 2, step), firsts)]


def reduce_residual(case, group, number, alphas):
    lv = case.lv

    def step(z0):
        total = [[], []]
        source = case.d[0] if number == 0 else case.r
        for z in [z0 + n for n in range(group)]:
            for h in HALVES:
                squares = []
                for k in range(lv.tiles):
                    at = h * lv.tiles + k
                    value = source[z, at] - alphas[h] * case.q[z, at]
                    case.r[z, at] = value
                    squares.append(value * value)
                total[h].append(tree(squares))
        return [tree(t) for t in total]

    return looped(lv.inner, group, 2, step)


def finish(case, group, alphas, phi_ref, send):
    lv, cs, s = case.lv, case.cs, case.lv.seg
    n = lv.tiles
    corner, element, _, _ = lane_parts()
    lower = element == 0

    def fresh(z, i, j, gz):
        k = i * s + j
        inner = z + lv.mz - 1
        both = cs.fx[i] * cs.fy[j]
        values = []
        for h in HALVES:
            value = both * gz[h]
            for alpha, d_ref in zip(alphas[h], case.d):
                value = value + alpha * d_ref[inner, h * n + k]
            value = cs.masked(value, i, j, 1)
            values.append(value)
        total = values[0] + turn(values[0], 32)
        chosen = jnp.where(lower, values[1], values[0])
        at = pl.multiple_of(z * plane_rows(lv) + k * SUBS, SUBS)
        phi_ref[pl.ds(at, SUBS), :] = chosen
        return chosen, total + turn(total, 64)

    def pack(z, j, totals):
        packed = totals[0]
        for i in range(1, min(s, 4)):
            packed = jnp.where(corner == i, totals[i], packed)
        if s > 4:
            packed = jnp.where(lower, packed, turn(totals[4], 16))
        at = pl.multiple_of(z * plane_rows(lv) + (n + j) * SUBS, SUBS)
        phi_ref[pl.ds(at, SUBS), :] = packed

    gz = cs.fz(lv.mz)
    for i in range(s):
        for j in range(s):
            k = i * s + j
            case.chosen[k], case.total[k] = fresh(0, i, j, gz)
            case.fz[k] = jnp.zeros((SUBS, LANES), F32)
    for j in range(s):
        pack(0, j, [case.total[i * s + j] for i in range(s)])

    def cut(values, table):
        return [v if f is None else v * f for v, f in zip(values, table)]

    def step(z0):
        sums = [[] for _ in range(4)]
        u = [case.chosen[k] for k in range(n)]
        low = [case.total[k] for k in range(n)]
        flux_z = [case.fz[k] for k in range(n)]
        for z in [z0 + t for t in range(group)]:
            get = case.weights(z + lv.mz)
            up = jnp.minimum(z + 1, lv.edz - 1)
            gz = cs.fz(up + lv.mz)
            after, after_low = [None] * n, [None] * n
            last = [get(1, i, s - 1) * (u[i * s + s - 1] - turn(u[i * s], -1, 0)) for i in range(s)]
            last = cut(last, [cs.facey[s - 1]] * s)
            before = [turn(v, 1, 0) for v in last]
            for j in range(s):
                jump_x, jump_y = row_jumps(u, s, j)
                flux_x = cut([get(0, i, j) * jump_x[i] for i in range(s)], cs.facex)
                flux_y = last
                if j < s - 1:
                    flux_y = cut([get(1, i, j) * jump_y[i] for i in range(s)], [cs.facey[j]] * s)
                parts = [[] for _ in sums]
                for i in range(s):
                    k = i * s + j
                    after[k], after_low[k] = fresh(up, i, j, gz)
                    flux = get(2, i, j) * (u[k] - after[k])
                    prev_x = flux_x[i - 1] if i else turn(flux_x[s - 1], 1)
                    value = (flux_x[i] - prev_x) + (flux_y[i] - before[i]) + (flux - flux_z[k])
                    flux_z[k] = flux
                    parts[0].append(value * u[k])
                    parts[1].append(value * turn(u[k], -32))
                    parts[2].append(value * turn(u[k], 64))
                    parts[3].append(value * low[k])
                pack(up, j, [after_low[i * s + j] for i in range(s)])
                for total, part in zip(sums, parts):
                    total.append(tree(part))
                before = flux_y
            u, low = after, after_low
        for k in range(n):
            case.fz[k], case.chosen[k], case.total[k] = flux_z[k], u[k], low[k]
        for z in [z0 + t for t in range(group)]:
            send(z).start()
        return [tree(total) for total in sums]

    return looped(lv.edz, group, 4, step)


GROUPS = {FINE: 1, TWIN: 8}


def place_kernel(center, out_ref):
    nx = center.shape[1]
    out_ref[...] = jnp.ones(out_ref.shape, F32)
    for m in range(3):
        off = m * (nx + 2 * MX) + MX
        out_ref[off : off + nx, :] = center[m]


def solve_kernel(
    inside, x_low, x_high, y_low, y_high,
    phi, message,
    flat, rows, twin_pairs, pairs, twin_rows, *refs,
):
    lanes = inside.shape[1]
    rim = y_low.shape[2]
    wide = y_low.shape[1]
    edge_tiles, inner_tiles = rim // LANES, lanes // LANES
    used = 3 * wide
    row = sub_iota((LANES, LANES))
    outer = (row < used) & ((row % wide < MX) | (row % wide >= wide - MX))
    for t in range(2 * edge_tiles + inner_tiles):
        if edge_tiles <= t < edge_tiles + inner_tiles:
            part = slice((t - edge_tiles) * LANES, (t - edge_tiles + 1) * LANES)
            for m in range(3):
                flat[t, m * wide : m * wide + MX, :] = x_low[m, :, part]
                flat[t, (m + 1) * wide - MX : (m + 1) * wide, :] = x_high[m, :, part]
            flat[t] = jnp.where(outer, flat[t], inside[:, part])
        else:
            source = y_low if t < edge_tiles else y_high
            at = t if t < edge_tiles else t - edge_tiles - inner_tiles
            for m in range(3):
                flat[t, m * wide : (m + 1) * wide, :] = source[m, :, at * LANES : (at + 1) * LANES]
            flat[t, used:, :] = jnp.ones((LANES - used, LANES), F32)

    def ordered(lv, t):
        parts = []
        for m in range(3):
            for i in range(lv.seg):
                some = [
                    flat[t, pl.ds(m * wide + lv.step * i + n, SUBS, stride=lv.step * lv.seg), :]
                    for n in range(lv.step)
                ]
                parts.append(tree(some))
        parts.append(jnp.ones((LANES - len(parts) * SUBS, LANES), F32))
        return jnp.concatenate(parts, axis=0)

    for t in range(flat.shape[0]):
        part = slice(t * LANES, (t + 1) * LANES)
        rows[part, :] = ordered(FINE, t).T
        twin_pairs[part, :] = ordered(TWIN, t).T

    nz = EZ * ELZ
    twin_y = rows.shape[0] // nz // 2
    for y in range(twin_y):
        at = y * nz
        both = twin_pairs[2 * at : 2 * at + nz, :] + twin_pairs[2 * at + nz : 2 * at + 2 * nz, :]
        pairs[at : at + nz, :] = both
        twin_rows[at : at + 8, :] = jnp.broadcast_to(0.25 * both[0:1], (8, LANES))
        twin_rows[at + 8 + nz // 2 : at + nz, :] = jnp.broadcast_to(0.25 * both[nz - 1 : nz], (8, LANES))
    for y in range(twin_y):
        at = y * nz
        middle = pairs[pl.ds(at, nz // 2, stride=2), :] + pairs[pl.ds(at + 1, nz // 2, stride=2), :]
        twin_rows[at + 8 : at + 8 + nz // 2, :] = 0.125 * middle
    twin_rows[twin_y * nz :, :] = jnp.ones((twin_rows.shape[0] - twin_y * nz, LANES), F32)

    refs = list(refs)

    def take(count):
        got = refs[:count]
        del refs[:count]
        return got

    cases = []
    for lv, source in zip(LEVELS, (rows, twin_rows)):
        (k_ref,) = take(1)
        w_refs = take(3)
        for z in range(lv.levels + 1):
            cell = min(max(z - 1, 0), nz - 1) if lv is FINE else min(z, lv.levels - 1) + 7
            for i in range(lv.seg):
                for c in range(COLUMNS):
                    start = (lv.edge * c + i) * nz + cell
                    k_ref[z, i, :, c * LANES : (c + 1) * LANES] = source[pl.ds(start, SUBS, stride=lv.seg * nz), :]
        spread_weights(lv, k_ref, w_refs)
        case = Case(lv, w_refs, take(5), take(3))
        for k in range(2 * lv.tiles):
            case.d[0][lv.inner, k] = jnp.zeros((SUBS, LANES), F32)
            case.r[lv.inner, k] = jnp.zeros((SUBS, LANES), F32)
        cases.append(case)

    def both_levels(work):
        sums = [work(n, case, GROUPS[case.lv]) for n, case in enumerate(cases)]
        return [[problem_sum(v) for v in part] for part in sums]

    rr = both_levels(lambda n, case, group: start_residual(case, group))
    alphas = [[[], []] for _ in LEVELS]
    betas = [None] * len(LEVELS)
    for step in range(3):
        dots = both_levels(lambda n, case, group: apply(case, group, step, betas[n]))
        now = [[a / b for a, b in zip(rr[n], dots[n])] for n in range(len(LEVELS))]
        for n in range(len(LEVELS)):
            for h in HALVES:
                alphas[n][h].append(now[n][h])
        if step < 2:
            new = both_levels(lambda n, case, group: reduce_residual(case, group, step, now[n]))
            betas = [[a / b for a, b in zip(new[n], rr[n])] for n in range(len(LEVELS))]
            rr = new

    phis, sems = take(2), take(2)

    def send(n, z):
        lv = LEVELS[n]
        size = plane_rows(lv)
        first = sum(phi_rows(v) for v in LEVELS[:n])
        return pltpu.make_async_copy(
            phis[n].at[pl.ds(pl.multiple_of(z * size, SUBS), size)],
            phi.at[pl.ds(pl.multiple_of(first + z * size, SUBS), size)],
            sems[n].at[z],
        )

    totals = both_levels(lambda n, case, group: finish(case, group, alphas[n], phis[n], functools.partial(send, n)))
    _, element, _, slot = lane_parts()
    packed = []
    for level in totals:
        parts = [v + xor_lane(v, 16) for v in level[:3]]
        parts.append(jnp.where(element == 0, level[3], turn(level[3], 16)))
        packed.append(
            jnp.where(slot == 0, parts[0], jnp.where(slot == 1, parts[1], jnp.where(slot == 2, parts[2], parts[3])))
        )
    row = jnp.where(element == 0, packed[0], packed[1])
    for r in range(0, message.shape[0], SUBS):
        message[r : r + SUBS, :] = row
    for n, lv in enumerate(LEVELS):
        for z in range(lv.edz):
            send(n, z).wait()


def coarse_nodes(gathered, gy_count, me):
    total_rows = gathered.shape[0]
    shape = gathered.shape
    lane = lane_iota(shape)
    row = sub_iota(shape)
    corner = lane // 32
    column = lane // 8 % 2
    last = row % gy_count == gy_count - 1
    start = row % gy_count == 0
    one = gathered
    two = turn(gathered, -1)
    four = turn(gathered, -2)
    rhs = turn(gathered, -3)
    two_back = turn(two, 32)

    def next_x(u):
        return turn(u, -gy_count, 0)

    def prev_x(u):
        return turn(u, gy_count, 0)

    def next_y(u):
        ahead = jnp.where(last, turn(u, gy_count - 1, 0), turn(u, -1, 0))
        return jnp.where(column == 0, turn(u, -8), turn(ahead, 8))

    def prev_y(u):
        behind = jnp.where(start, turn(u, 1 - gy_count, 0), turn(u, 1, 0))
        return jnp.where(column == 1, turn(u, 8), turn(behind, -8))

    def by_corner(a, b, c, d):
        return jnp.where(corner == 0, a, jnp.where(corner == 1, b, jnp.where(corner == 2, c, d)))

    def corners(u):
        ux = next_x(u)
        return by_corner(u, next_y(u), ux, next_y(ux))

    def assemble(v):
        vx = prev_x(v)
        w = by_corner(v, prev_y(v), vx, prev_y(vx))
        w = w + turn(w, 64)
        return w + turn(w, 32)

    def operate(u):
        c = corners(u)
        return assemble(one * c + two * turn(c, -32) + two_back * turn(c, 32) + four * turn(c, 64))

    def total(a, b):
        v = a * b
        v = tree([v[r : r + SUBS] for r in range(0, total_rows, SUBS)])
        for shift in (4, 2, 1):
            v = v + turn(v, shift, 0)
        v = v + xor_lane(v, 8)
        return v[0:1]

    residual = -assemble(rhs)
    direction = residual
    update = jnp.zeros_like(residual)
    now = total(residual, residual)
    for step in range(2):
        image = operate(direction)
        alpha = now / total(direction, image)
        update = update + alpha * direction
        if step == 0:
            residual = residual - alpha * image
            new = total(residual, residual)
            direction = residual + new / now * direction
            now = new
    mine = jnp.where(row == me, corners(update), 0.0)
    mine = jnp.sum(mine, axis=0, keepdims=True)
    return jnp.broadcast_to(mine, (SUBS, LANES))


def turn_kernel(phi, out_ref):
    start_row, number = 0, 0
    for lv in LEVELS:
        s = lv.seg
        nz = EZ * lv.edz
        per = LANES // nz
        sums_row = start_row + lv.tiles * SUBS
        for i in range(s):
            for t in range(turned_tiles(lv)):
                parts = []
                for n in range(per):
                    yo, j = divmod(lv.mx + t * per + n, s)
                    chosen = phi[pl.ds(start_row + (i * s + j) * SUBS + yo, lv.edz, stride=plane_rows(lv)), :]
                    total = phi[pl.ds(sums_row + j * SUBS + yo, lv.edz, stride=plane_rows(lv)), :]
                    lower = lane_iota(chosen.shape) // 16 % 2 == 0
                    parts.append(jnp.where(lower, chosen, turn(total, 16) if i < 4 else total))
                    parts.append(jnp.where(lower, turn(chosen, -16), 0.0))
                out_ref[number] = jnp.concatenate(parts, axis=0).T
                number += 1
        start_row += phi_rows(lv)


def pressure_kernel(gy_count, me_ref, gathered, turned, fine_out, twin_out, fine_all, twin_all):
    mine = coarse_nodes(gathered[...], gy_count, me_ref[0])
    first = 0
    for n, (lv, out_ref, all_ref) in enumerate(((FINE, fine_out, fine_all), (TWIN, twin_out, twin_all))):
        s = lv.seg
        tiles = turned_tiles(lv)
        nodes = {}
        for c in range(COLUMNS):
            for p in range(4):
                at = p * 32 + n * 16 + c * 8
                nodes[p, c] = jnp.broadcast_to(mine[:, at : at + 1], (SUBS, LANES))
        for c in range(COLUMNS):
            for t in range(tiles):
                at = (c * tiles + t) * LANES
                for i in range(s):
                    def part(group):
                        return turned[first + i * tiles + t, group * 16 + c * 8 : group * 16 + c * 8 + 8, :]

                    value = tree([part(2 * p) * nodes[p, c] for p in range(4)]) + part(2 * (i % 4) + 1)
                    all_ref[c * tiles + t, pl.ds(i, SUBS, stride=s), :] = value
                out_ref[:, at : at + LANES] = all_ref[c * tiles + t, lv.mx : lv.mx + lv.edge, :]
        first += s * tiles


def vmem(shape, dtype=F32):
    return pltpu.VMEM(shape, dtype)


def shards(permeability):
    nz = EZ * ELZ
    rows = permeability.shape[1]
    lanes = permeability.shape[2]
    assert rows == EL and lanes == COLUMNS * EL * nz
    rim = MX * nz
    gx, gy = lax.axis_size("gx"), lax.axis_size("gy")

    def sent(value, axis, shift):
        count = lax.axis_size(axis)
        return lax.ppermute(value, axis, [(i, (i + shift) % count) for i in range(count)])

    x_low = sent(permeability[:, rows - MX :], "gx", 1)
    x_high = sent(permeability[:, :MX], "gx", -1)

    def strip(part):
        return jnp.concatenate([x_low[:, :, part], permeability[:, :, part], x_high[:, :, part]], axis=1)

    y_low = sent(strip(slice(lanes - rim, lanes)), "gy", 1)
    y_high = sent(strip(slice(0, rim)), "gy", -1)
    halos = [x_low, x_high, y_low, y_high]
    flat_lanes = lanes + 2 * rim
    scratch = [
        vmem((flat_lanes // LANES, LANES, LANES)),
        vmem((flat_lanes, LANES)),
        vmem((flat_lanes, LANES)),
        vmem((flat_lanes // 2, LANES)),
        vmem((SUBS * (TWIN.seg + 2) * nz, LANES)),
    ]
    for lv in LEVELS:
        scratch.append(vmem((lv.levels + 1, lv.seg, SUBS, 2 * LANES)))
        scratch += [vmem((lv.seg, lv.planes * lv.seg, SUBS, LANES))] * 3
        scratch += [vmem((lv.inner + 1, 2 * lv.tiles, SUBS, LANES))] * 5
        scratch.append(vmem((2 * lv.tiles, SUBS, LANES)))
        scratch += [vmem((lv.tiles, SUBS, LANES))] * 2
    scratch += [vmem((phi_rows(lv), LANES)) for lv in LEVELS]
    scratch += [pltpu.SemaphoreType.DMA((lv.edz,)) for lv in LEVELS]
    full = pl.BlockSpec(memory_space=pltpu.VMEM)
    inside = pl.pallas_call(
        place_kernel,
        out_shape=vmem((LANES, lanes)),
        in_specs=[full],
        out_specs=full,
        compiler_params=pltpu.CompilerParams(vmem_limit_bytes=8 * 1024 * 1024),
        cost_estimate=pl.CostEstimate(flops=1000000, bytes_accessed=4000000, transcendentals=0),
        name="place",
    )(permeability)
    phi, message = pl.pallas_call(
        solve_kernel,
        out_shape=[
            pltpu.HBM((sum(phi_rows(lv) for lv in LEVELS), LANES), F32),
            jax.ShapeDtypeStruct((gx * gy, LANES), F32),
        ],
        in_specs=[full] * 5,
        out_specs=[pl.BlockSpec(memory_space=pltpu.HBM), full],
        scratch_shapes=scratch,
        compiler_params=pltpu.CompilerParams(vmem_limit_bytes=44 * 1024 * 1024),
        name="solve",
    )(inside, *halos)
    gathered = lax.all_to_all(message, ("gx", "gy"), 0, 0, tiled=True)
    tiles = sum(lv.seg * turned_tiles(lv) for lv in LEVELS)
    turned = pl.pallas_call(
        turn_kernel,
        out_shape=vmem((tiles, LANES, LANES)),
        in_specs=[full],
        out_specs=full,
        compiler_params=pltpu.CompilerParams(vmem_limit_bytes=16 * 1024 * 1024),
        cost_estimate=pl.CostEstimate(flops=4000000, bytes_accessed=8000000, transcendentals=0),
        name="turned",
    )(phi)
    me = (lax.axis_index("gx") * gy + lax.axis_index("gy")).astype(jnp.int32).reshape(1)
    return tuple(
        pl.pallas_call(
            functools.partial(pressure_kernel, gy),
            out_shape=[
                jax.ShapeDtypeStruct((lv.edge, COLUMNS * lv.edge * EZ * lv.edz), F32) for lv in LEVELS
            ],
            in_specs=[pl.BlockSpec(memory_space=pltpu.SMEM), full, full],
            out_specs=[full] * 2,
            scratch_shapes=[vmem((COLUMNS * turned_tiles(lv), SUBS * lv.seg, LANES)) for lv in LEVELS],
            compiler_params=pltpu.CompilerParams(vmem_limit_bytes=16 * 1024 * 1024),
            name="pressure",
        )(me, gathered, turned)
    )


def solution(mesh):
    return jax.shard_map(
        shards,
        mesh=mesh,
        in_specs=(P(None, "gx", "gy"),),
        out_specs=(P("gx", "gy"), P("gx", "gy")),
        check_vma=False,
    )
```

```python
import functools
import typing

import jax
import jax.numpy as jnp
from jax import lax
from jax.experimental import pallas as pl
from jax.experimental.pallas import tpu as pltpu
from jax.sharding import PartitionSpec as P

EL = 32
ELZ = 16
MX = 4
MZ = 2
EZ = 2
LANES = 128
SUBS = 8
COLUMNS = 2
F32 = jnp.float32
BF16 = jnp.bfloat16


class Level(typing.NamedTuple):
    edge: int
    edz: int
    mx: int
    mz: int
    spacing: float
    step: int

    @property
    def width(self):
        return self.edge + 2 * self.mx

    @property
    def inner(self):
        return self.edz + 2 * self.mz - 2

    @property
    def seg(self):
        return -(-self.width // SUBS)

    @property
    def tiles(self):
        return self.seg * self.seg

    @property
    def levels(self):
        return EZ * self.edz + 2

    @property
    def planes(self):
        return -(-(self.inner + 1) // 2) * 2


FINE = Level(EL, ELZ, MX, MZ, 1.0, 1)
TWIN = Level(EL // 2, ELZ // 2, MX // 2, MZ // 2, 2.0, 2)
LEVELS = (FINE, TWIN)


def lane_iota(shape=(SUBS, LANES)):
    return lax.broadcasted_iota(jnp.int32, shape, len(shape) - 1)


def sub_iota(shape=(SUBS, LANES)):
    return lax.broadcasted_iota(jnp.int32, shape, len(shape) - 2)


def turn(value, shift, axis=1):
    return pltpu.roll(value, shift % value.shape[axis], axis)


def lane_parts():
    lane = lane_iota()
    return lane // 32, lane // 16 % 2, lane // 8 % 2, lane % 8


class Consts:
    def __init__(self, lv):
        corner, _, _, xo = lane_parts()
        yo = sub_iota()
        ax, ay = corner // 2, corner % 2
        self.lv = lv
        s = lv.seg
        self.fx, self.fy = [], []
        self.inx, self.iny, self.facex, self.facey = [], [], [], []
        for i in range(s):
            x = xo * s + i
            y = yo * s + i
            px = (x.astype(F32) - lv.mx + 0.5) / lv.edge
            py = (y.astype(F32) - lv.mx + 0.5) / lv.edge
            self.fx.append(jnp.where(ax == 1, px, 1.0 - px))
            self.fy.append(jnp.where(ay == 1, py, 1.0 - py))
            xs = [s * o + i for o in range(SUBS)]

            def ranged(value, low, high):
                if all(low <= v <= high for v in xs):
                    return None
                return ((value >= low) & (value <= high)).astype(F32)

            self.inx.append((ranged(x, 1, lv.width - 2), ranged(x, lv.mx, lv.mx + lv.edge - 1)))
            self.iny.append((ranged(y, 1, lv.width - 2), ranged(y, lv.mx, lv.mx + lv.edge - 1)))
            cut = (lv.mx - 1, lv.mx + lv.edge - 1)
            self.facex.append(((x != cut[0]) & (x != cut[1])).astype(F32) if any(v in cut for v in xs) else None)
            self.facey.append(((y != cut[0]) & (y != cut[1])).astype(F32) if any(v in cut for v in xs) else None)
        sx = jnp.where(ax == 1, -1.0 / lv.edge, 1.0 / lv.edge).astype(F32)
        sy = jnp.where(ay == 1, -1.0 / lv.edge, 1.0 / lv.edge).astype(F32)
        self.along_x = [sx * f for f in self.fy]
        self.along_y = [sy * f for f in self.fx]

    def fz(self, plane):
        place = (jnp.asarray(plane, jnp.int32).astype(F32) - self.lv.mz + 0.5) / self.lv.edz
        return 1.0 - place, place

    def masked(self, value, i, j, kind):
        for table, index in ((self.inx, i), (self.iny, j)):
            factor = table[index][kind]
            if factor is not None:
                value = value * factor
        return value


def tree(values):
    values = list(values)
    while len(values) > 1:
        values = [a + b for a, b in zip(values[::2], values[1::2])] + (
            [values[-1]] if len(values) % 2 else []
        )
    return values[0]


def xor_lane(value, bit):
    return jnp.where(lane_iota(value.shape) // bit % 2 == 1, turn(value, bit), turn(value, -bit))


def problem_sum(value):
    for shift in (4, 2, 1):
        value = value + turn(value, shift, 0)
    for bit in (1, 2, 4):
        value = value + xor_lane(value, bit)
    return value


def spread_weights(lv, k_ref, high_refs, low_refs, w_refs):
    s = lv.seg
    wide = (SUBS, LANES)
    pos = lane_iota(wide)
    yo = sub_iota(wide)
    first = pos < 40
    third = pos >= 80
    second = (pos >= 40) & (pos < 80)
    edge_x = first & (pos >= (lv.width - 1) * lv.step)

    def one(z, i, c):
        part = slice(c * LANES, (c + 1) * LANES)
        k = k_ref[z, i, :, part]
        nbx = turn(k, -lv.step)
        nby = k_ref[z, i + 1, :, part] if i < s - 1 else turn(k_ref[z, 0, :, part], -1, 0)
        nbz = k_ref[z + 1, i, :, part]
        nb = jnp.where(first, nbx, jnp.where(second, nby, nbz))
        w = (2.0 * lv.spacing) * k * nb / (k + nb)
        bad = edge_x | (second & (yo * s + i >= lv.width - 1))
        return jnp.where(bad, 0.0, w)

    def planes(t, _):
        units = [(2 * t + n, i) for n in range(2) for i in range(s)]
        for e in range(EZ):
            made = []
            for plane, i in units:
                z = jnp.clip(e * lv.edz + plane + 1 - lv.mz, 0, lv.levels - 1)
                w0, w1 = one(z, i, 0), one(z, i, 1)
                near, wrap = turn(w1, 40), turn(w1, 48)
                made.append((jnp.where(first, w0, near), jnp.where(third, near, w0), jnp.where(third, w0, wrap)))
            for p in range(s):
                for m in range(3):
                    both = jnp.concatenate([made[2 * p][m], made[2 * p + 1][m]], axis=0)
                    high = both.astype(BF16)
                    part = slice(e * LANES, (e + 1) * LANES)
                    high_refs[m][t * s + p, :, part] = high
                    low_refs[m][t * s + p, :, part] = (both - high.astype(F32)).astype(BF16)
        return 0

    lax.fori_loop(0, lv.planes // 2, planes, 0)
    rows = lv.planes * s * SUBS
    row = lax.broadcasted_iota(jnp.int32, (2 * LANES, 2 * LANES), 0)
    lane = lax.broadcasted_iota(jnp.int32, (1, 2 * LANES), 1)
    upper = lane // LANES
    for q in range(-(-s // 2)):
        x = lane % 8 * s + 2 * q + upper
        valid = (x < lv.width) & (2 * q + upper < s)
        for m in range(3):
            segment = jnp.where(lane // 8 % 2 == 0, m, (m + 1) % 3)
            source = jnp.where(valid, lane // 16 % 2 * LANES + segment * 40 + lv.step * x, -1)
            pick = (row == source).astype(F32).astype(BF16)
            out = jnp.dot(high_refs[m][...].reshape(rows, 2 * LANES), pick, preferred_element_type=F32)
            out = out + jnp.dot(low_refs[m][...].reshape(rows, 2 * LANES), pick, preferred_element_type=F32)
            for half in range(min(2, s - 2 * q)):
                part = out[:, half * LANES : (half + 1) * LANES]
                w_refs[m][2 * q + half] = part.reshape(lv.planes * s, SUBS, LANES)


class Case:
    def __init__(self, lv, w_refs, fields, planes):
        self.lv, self.cs, self.w_refs = lv, Consts(lv), w_refs
        self.d, self.q, self.r = fields[:3], fields[3], fields[4]
        (self.fz,) = planes

    def weights(self, plane):
        s = self.lv.seg
        return lambda m, i, j: self.w_refs[m][i, plane * s + j]


HALVES = (0, 1)
CHUNK = 640


def plane_rows(lv):
    return lv.tiles * SUBS


def field_rows(lv):
    return lv.edz * plane_rows(lv)


def padded_rows(lv):
    return -(-field_rows(lv) // CHUNK) * CHUNK


def turned_tiles(lv):
    return lv.edge * EZ * lv.edz // LANES


def looped(count, group, sums, step):
    def body(t, sums):
        return tuple(a + b for a, b in zip(sums, step(t * group)))

    start = tuple(jnp.zeros((SUBS, LANES), F32) for _ in range(sums))
    return list(lax.fori_loop(0, count // group, body, start))


def start_residual(case, group):
    lv, cs, s = case.lv, case.cs, case.lv.seg

    def step(z0):
        total = [[], []]
        for z in [z0 + n for n in range(group)]:
            get, below = case.weights(z + 1), case.weights(z)
            gz = cs.fz(z + 1)
            last = [get(1, i, s - 1) * cs.along_y[i] for i in range(s)]
            before = [turn(v, 1, 0) for v in last]
            for j in range(s):
                flux_y = last if j == s - 1 else [get(1, i, j) * cs.along_y[i] for i in range(s)]
                flux_x = [get(0, i, j) * cs.along_x[j] for i in range(s)]
                squares = [[], []]
                for i in range(s):
                    k = i * s + j
                    prev_x = flux_x[i - 1] if i else turn(flux_x[s - 1], 1)
                    flat = (prev_x - flux_x[i]) + (before[i] - flux_y[i])
                    flat = cs.masked(flat, i, j, 0)
                    tall = (cs.fx[i] * cs.fy[j]) * (1.0 / lv.edz) * (below(2, i, j) - get(2, i, j))
                    tall = cs.masked(tall, i, j, 0)
                    for h, value in enumerate((flat * gz[0] + tall, flat * gz[1] - tall)):
                        case.d[0][z, h * lv.tiles + k] = value
                        squares[h].append(value * value)
                for h in HALVES:
                    total[h].append(tree(squares[h]))
                before = flux_y
        return [tree(t) for t in total]

    return looped(lv.inner, group, 2, step)


def row_jumps(u, s, j):
    jump_x = [u[i * s + j] - (u[(i + 1) * s + j] if i < s - 1 else turn(u[j], -1)) for i in range(s)]
    jump_y = [u[i * s + j] - (u[i * s + j + 1] if j < s - 1 else turn(u[i * s], -1, 0)) for i in range(s)]
    return jump_x, jump_y


def apply(case, group, number, betas):
    lv, cs, s = case.lv, case.cs, case.lv.seg
    keep = number < 2
    n = lv.tiles

    def fresh(z, h, k):
        at = h * n + k
        if number == 0:
            return case.d[0][z, at]
        value = case.r[z, at] + betas[h] * case.d[number - 1][z, at]
        case.d[number][z, at] = value
        return value

    firsts = []
    get = case.weights(0)
    for h in HALVES:
        terms = []
        for k in range(n):
            value = fresh(0, h, k)
            flux = -get(2, k // s, k % s) * value
            if keep:
                case.fz[h * n + k] = flux
            else:
                terms.append(-flux * value)
        firsts.append(tree(terms) if terms else 0.0)

    def step(z0):
        total = [[], []]
        u = [[case.d[number][z0, h * n + k] for k in range(n)] for h in HALVES]
        flux_z = [[case.fz[h * n + k] for k in range(n)] for h in HALVES] if keep else None
        for z in [z0 + t for t in range(group)]:
            get = case.weights(z + 1)
            after = [[None] * n for _ in HALVES]
            if keep:
                wy = [get(1, i, s - 1) for i in range(s)]
                last = [[wy[i] * (u[h][i * s + s - 1] - turn(u[h][i * s], -1, 0)) for i in range(s)] for h in HALVES]
                before = [[turn(v, 1, 0) for v in last[h]] for h in HALVES]
            for j in range(s):
                wx = [get(0, i, j) for i in range(s)]
                wy = [get(1, i, j) for i in range(s)]
                wz = [get(2, i, j) for i in range(s)]
                for h in HALVES:
                    jump_x, jump_y = row_jumps(u[h], s, j)
                    flux_x = [w * v for w, v in zip(wx, jump_x)]
                    flux_y = last[h] if keep and j == s - 1 else [w * v for w, v in zip(wy, jump_y)]
                    terms = []
                    for i in range(s):
                        k = i * s + j
                        after[h][k] = fresh(z + 1, h, k)
                        jump = u[h][k] - after[h][k]
                        flux = wz[i] * jump
                        if keep:
                            prev_x = flux_x[i - 1] if i else turn(flux_x[s - 1], 1)
                            value = (flux_x[i] - prev_x) + (flux_y[i] - before[h][i]) + (flux - flux_z[h][k])
                            flux_z[h][k] = flux
                            value = cs.masked(value, i, j, 0)
                            case.q[z, h * n + k] = value
                            terms.append(u[h][k] * value)
                        else:
                            terms.append((flux * jump + flux_x[i] * jump_x[i]) + flux_y[i] * jump_y[i])
                    total[h].append(tree(terms))
                    if keep:
                        before[h] = flux_y
            u = after
        if keep:
            for h in HALVES:
                for k in range(n):
                    case.fz[h * n + k] = flux_z[h][k]
        return [tree(t) for t in total]

    return [a + b for a, b in zip(looped(lv.inner, group, 2, step), firsts)]


def reduce_residual(case, group, number, alphas):
    lv = case.lv

    def step(z0):
        total = [[], []]
        source = case.d[0] if number == 0 else case.r
        for z in [z0 + n for n in range(group)]:
            for h in HALVES:
                squares = []
                for k in range(lv.tiles):
                    at = h * lv.tiles + k
                    value = source[z, at] - alphas[h] * case.q[z, at]
                    case.r[z, at] = value
                    squares.append(value * value)
                total[h].append(tree(squares))
        return [tree(t) for t in total]

    return looped(lv.inner, group, 2, step)


def finish(case, group, alphas, refs, send):
    lv, cs, s = case.lv, case.cs, case.lv.seg
    n = lv.tiles
    f_ref, p_ref, y_ref = refs
    lower = lane_parts()[1] == 0

    def at(z, k):
        return pl.ds(pl.multiple_of(z * plane_rows(lv) + k * SUBS, SUBS), SUBS)

    def fresh(z, i, j, gz):
        k = i * s + j
        inner = z + lv.mz - 1
        both = cs.fx[i] * cs.fy[j]
        values = []
        for h in HALVES:
            value = both * gz[h]
            for alpha, d_ref in zip(alphas[h], case.d):
                value = value + alpha * d_ref[inner, h * n + k]
            values.append(cs.masked(value, i, j, 1))
        chosen = jnp.where(lower, values[1], values[0])
        f_ref[at(z, k), :] = chosen
        p_ref[at(z, k), :] = values[0]
        return chosen

    gz = cs.fz(lv.mz)
    for i in range(s):
        for j in range(s):
            fresh(0, i, j, gz)
            case.fz[i * s + j] = jnp.zeros((SUBS, LANES), F32)
    rest = padded_rows(lv) - field_rows(lv)
    if rest:
        for ref in refs:
            ref[field_rows(lv) :, :] = jnp.zeros((rest, LANES), F32)

    def cut(values, table):
        return [v if f is None else v * f for v, f in zip(values, table)]

    def body(t, _):
        z0 = t * group
        u = [f_ref[at(z0, k), :] for k in range(n)]
        flux_z = [case.fz[k] for k in range(n)]
        for z in [z0 + m for m in range(group)]:
            get = case.weights(z + lv.mz)
            up = jnp.minimum(z + 1, lv.edz - 1)
            gz = cs.fz(up + lv.mz)
            after = [None] * n
            last = [get(1, i, s - 1) * (u[i * s + s - 1] - turn(u[i * s], -1, 0)) for i in range(s)]
            last = cut(last, [cs.facey[s - 1]] * s)
            before = [turn(v, 1, 0) for v in last]
            for j in range(s):
                jump_x, jump_y = row_jumps(u, s, j)
                flux_x = cut([get(0, i, j) * jump_x[i] for i in range(s)], cs.facex)
                flux_y = last
                if j < s - 1:
                    flux_y = cut([get(1, i, j) * jump_y[i] for i in range(s)], [cs.facey[j]] * s)
                for i in range(s):
                    k = i * s + j
                    after[k] = fresh(up, i, j, gz)
                    flux = get(2, i, j) * (u[k] - after[k])
                    prev_x = flux_x[i - 1] if i else turn(flux_x[s - 1], 1)
                    y_ref[at(z, k), :] = (flux_x[i] - prev_x) + (flux_y[i] - before[i]) + (flux - flux_z[k])
                    flux_z[k] = flux
                before = flux_y
            u = after
        for k in range(n):
            case.fz[k] = flux_z[k]
        for z in [z0 + m for m in range(group)]:
            for h in HALVES:
                send(h, z).start()
        return 0

    lax.fori_loop(0, lv.edz // group, body, 0)
    pairs = jnp.zeros((2 * LANES, LANES), F32)
    for start in range(0, padded_rows(lv), CHUNK):
        part = slice(start, start + CHUNK)
        left = jnp.concatenate([f_ref[part, :].T, p_ref[part, :].T], axis=0)
        right = y_ref[part, :]
        left_high, right_high = left.astype(BF16), right.astype(BF16)
        left_low = (left - left_high.astype(F32)).astype(BF16)
        right_low = (right - right_high.astype(F32)).astype(BF16)
        for a, b in ((left_high, right_high), (left_low, right_high), (left_high, right_low)):
            pairs = pairs + jnp.dot(a, b, preferred_element_type=F32)
    shape = (LANES, LANES)
    row, lane = sub_iota(shape), lane_iota(shape)
    sums = [jnp.where(row == (lane + 32 * k) % LANES, pairs[:LANES], 0.0) for k in range(3)]
    sums.append(jnp.where(row % 32 == lane % 32, pairs[LANES:], 0.0))
    out = []
    for value in sums:
        value = tree([value[r : r + SUBS] for r in range(0, LANES, SUBS)])
        out.append(value)
    return out


GROUPS = {FINE: 1, TWIN: 8}


def place_kernel(center, out_ref):
    nx = center.shape[1]
    out_ref[...] = jnp.ones(out_ref.shape, F32)
    for m in range(3):
        off = m * (nx + 2 * MX) + MX
        out_ref[off : off + nx, :] = center[m]


def solve_kernel(
    inside, x_low, x_high, y_low, y_high,
    phi, message,
    flat, sides, rows, pairs, twin_rows, *refs,
):
    lanes = inside.shape[1]
    rim = y_low.shape[2]
    wide = y_low.shape[1]
    for m in range(3):
        off = m * wide
        flat[off : off + MX, :] = x_low[m]
        flat[off + wide - MX : off + wide, :] = x_high[m]
        sides[off : off + wide, :rim] = y_low[m]
        sides[off : off + wide, rim:] = y_high[m]
    sides[3 * wide :, :] = jnp.ones((LANES - 3 * wide, sides.shape[1]), F32)
    row = sub_iota((LANES, LANES))
    place = row % wide
    outer = (row < 3 * wide) & ((place < MX) | (place >= wide - MX))
    for t in range(rim // LANES):
        low, high = slice(t * LANES, (t + 1) * LANES), slice(rim + t * LANES, rim + (t + 1) * LANES)
        rows[low, :] = sides[:, low].T
        rows[lanes + rim + t * LANES : lanes + rim + (t + 1) * LANES, :] = sides[:, high].T
    for t in range(lanes // LANES):
        part = slice(t * LANES, (t + 1) * LANES)
        rows[rim + t * LANES : rim + (t + 1) * LANES, :] = jnp.where(outer, flat[:, part], inside[:, part]).T

    nz = EZ * ELZ
    twin_y = rows.shape[0] // nz // 2
    for y in range(twin_y):
        both = rows[2 * y * nz : (2 * y + 1) * nz, :] + rows[(2 * y + 1) * nz : (2 * y + 2) * nz, :]
        both = both + turn(both, -1)
        at = y * nz
        pairs[at : at + nz, :] = both
        twin_rows[at : at + 8, :] = jnp.broadcast_to(0.25 * both[0:1], (8, LANES))
        twin_rows[at + 8 + nz // 2 : at + nz, :] = jnp.broadcast_to(0.25 * both[nz - 1 : nz], (8, LANES))
    for y in range(twin_y):
        at = y * nz
        middle = pairs[pl.ds(at, nz // 2, stride=2), :] + pairs[pl.ds(at + 1, nz // 2, stride=2), :]
        twin_rows[at + 8 : at + 8 + nz // 2, :] = 0.125 * middle
    twin_rows[twin_y * nz :, :] = jnp.ones((twin_rows.shape[0] - twin_y * nz, LANES), F32)

    refs = list(refs)

    def take(count):
        got = refs[:count]
        del refs[:count]
        return got

    cases = []
    for lv, source in zip(LEVELS, (rows, twin_rows)):
        (k_ref,) = take(1)
        high_refs, low_refs, w_refs = take(3), take(3), take(3)
        for z in range(lv.levels + 1):
            cell = min(max(z - 1, 0), nz - 1) if lv is FINE else min(z, lv.levels - 1) + 7
            for i in range(lv.seg):
                for c in range(COLUMNS):
                    start = (lv.edge * c + i) * nz + cell
                    k_ref[z, i, :, c * LANES : (c + 1) * LANES] = source[pl.ds(start, SUBS, stride=lv.seg * nz), :]
        spread_weights(lv, k_ref, high_refs, low_refs, w_refs)
        case = Case(lv, w_refs, take(5), take(1))
        for k in range(2 * lv.tiles):
            case.d[0][lv.inner, k] = jnp.zeros((SUBS, LANES), F32)
            case.r[lv.inner, k] = jnp.zeros((SUBS, LANES), F32)
        cases.append(case)

    def both_levels(work):
        sums = [work(n, case, GROUPS[case.lv]) for n, case in enumerate(cases)]
        return [[problem_sum(v) for v in part] for part in sums]

    rr = both_levels(lambda n, case, group: start_residual(case, group))
    alphas = [[[], []] for _ in LEVELS]
    betas = [None] * len(LEVELS)
    for step in range(3):
        dots = both_levels(lambda n, case, group: apply(case, group, step, betas[n]))
        now = [[a / b for a, b in zip(rr[n], dots[n])] for n in range(len(LEVELS))]
        for n in range(len(LEVELS)):
            for h in HALVES:
                alphas[n][h].append(now[n][h])
        if step < 2:
            new = both_levels(lambda n, case, group: reduce_residual(case, group, step, now[n]))
            betas = [[a / b for a, b in zip(new[n], rr[n])] for n in range(len(LEVELS))]
            rr = new

    results = [take(3), take(3)]
    sems = take(2)

    def send(n, h, z):
        lv = LEVELS[n]
        size = plane_rows(lv)
        first = sum(2 * field_rows(v) for v in LEVELS[:n]) + h * field_rows(lv)
        return pltpu.make_async_copy(
            results[n][h].at[pl.ds(pl.multiple_of(z * size, SUBS), size)],
            phi.at[pl.ds(pl.multiple_of(first + z * size, SUBS), size)],
            sems[n].at[h * lv.edz + z],
        )

    totals = both_levels(
        lambda n, case, group: finish(case, group, alphas[n], results[n], functools.partial(send, n))
    )
    _, element, _, slot = lane_parts()
    packed = []
    for level in totals:
        parts = [v + xor_lane(v, 16) for v in level[:3]]
        parts.append(jnp.where(element == 0, level[3], turn(level[3], 16)))
        packed.append(
            jnp.where(slot == 0, parts[0], jnp.where(slot == 1, parts[1], jnp.where(slot == 2, parts[2], parts[3])))
        )
    row = jnp.where(element == 0, packed[0], packed[1])
    for r in range(0, message.shape[0], SUBS):
        message[r : r + SUBS, :] = row
    for n, lv in enumerate(LEVELS):
        for h in HALVES:
            for z in range(lv.edz):
                send(n, h, z).wait()


def coarse_nodes(gathered, gy_count, me):
    total_rows = gathered.shape[0]
    shape = gathered.shape
    lane = lane_iota(shape)
    row = sub_iota(shape)
    corner = lane // 32
    column = lane // 8 % 2
    last = row % gy_count == gy_count - 1
    start = row % gy_count == 0
    one = gathered
    two = turn(gathered, -1)
    four = turn(gathered, -2)
    rhs = turn(gathered, -3)
    two_back = turn(two, 32)

    def next_x(u):
        return turn(u, -gy_count, 0)

    def prev_x(u):
        return turn(u, gy_count, 0)

    def next_y(u):
        ahead = jnp.where(last, turn(u, gy_count - 1, 0), turn(u, -1, 0))
        return jnp.where(column == 0, turn(u, -8), turn(ahead, 8))

    def prev_y(u):
        behind = jnp.where(start, turn(u, 1 - gy_count, 0), turn(u, 1, 0))
        return jnp.where(column == 1, turn(u, 8), turn(behind, -8))

    def by_corner(a, b, c, d):
        return jnp.where(corner == 0, a, jnp.where(corner == 1, b, jnp.where(corner == 2, c, d)))

    def corners(u):
        ux = next_x(u)
        return by_corner(u, next_y(u), ux, next_y(ux))

    def assemble(v):
        vx = prev_x(v)
        w = by_corner(v, prev_y(v), vx, prev_y(vx))
        w = w + turn(w, 64)
        return w + turn(w, 32)

    def operate(u):
        c = corners(u)
        return assemble(one * c + two * turn(c, -32) + two_back * turn(c, 32) + four * turn(c, 64))

    def total(a, b):
        v = a * b
        v = tree([v[r : r + SUBS] for r in range(0, total_rows, SUBS)])
        for shift in (4, 2, 1):
            v = v + turn(v, shift, 0)
        v = v + xor_lane(v, 8)
        return v[0:1]

    residual = -assemble(rhs)
    direction = residual
    update = jnp.zeros_like(residual)
    now = total(residual, residual)
    for step in range(2):
        image = operate(direction)
        alpha = now / total(direction, image)
        update = update + alpha * direction
        if step == 0:
            residual = residual - alpha * image
            new = total(residual, residual)
            direction = residual + new / now * direction
            now = new
    mine = jnp.where(row == me, corners(update), 0.0)
    mine = jnp.sum(mine, axis=0, keepdims=True)
    return jnp.broadcast_to(mine, (SUBS, LANES))


def turn_kernel(phi, out_ref):
    start_row, number = 0, 0
    for lv in LEVELS:
        s = lv.seg
        nz = EZ * lv.edz
        per = LANES // nz
        for i in range(s):
            for t in range(turned_tiles(lv)):
                parts = []
                for n in range(per):
                    yo, j = divmod(lv.mx + t * per + n, s)
                    start = start_row + (i * s + j) * SUBS + yo
                    chosen, bottom = [
                        phi[pl.ds(start + h * field_rows(lv), lv.edz, stride=plane_rows(lv)), :] for h in HALVES
                    ]
                    lower = lane_iota(chosen.shape) // 16 % 2 == 0
                    parts.append(jnp.where(lower, chosen, turn(bottom, 16)))
                    parts.append(jnp.where(lower, turn(chosen, -16), 0.0))
                out_ref[number] = jnp.concatenate(parts, axis=0).T
                number += 1
        start_row += 2 * field_rows(lv)


def pressure_kernel(gy_count, me_ref, gathered, turned, fine_out, twin_out, fine_all, twin_all):
    mine = coarse_nodes(gathered[...], gy_count, me_ref[0])
    first = 0
    for n, (lv, out_ref, all_ref) in enumerate(((FINE, fine_out, fine_all), (TWIN, twin_out, twin_all))):
        s = lv.seg
        tiles = turned_tiles(lv)
        nodes = {}
        for c in range(COLUMNS):
            for p in range(4):
                at = p * 32 + n * 16 + c * 8
                nodes[p, c] = jnp.broadcast_to(mine[:, at : at + 1], (SUBS, LANES))
        for c in range(COLUMNS):
            for t in range(tiles):
                at = (c * tiles + t) * LANES
                for i in range(s):
                    def part(group):
                        return turned[first + i * tiles + t, group * 16 + c * 8 : group * 16 + c * 8 + 8, :]

                    value = tree([part(2 * p) * nodes[p, c] + part(2 * p + 1) for p in range(4)])
                    all_ref[c * tiles + t, pl.ds(i, SUBS, stride=s), :] = value
                out_ref[:, at : at + LANES] = all_ref[c * tiles + t, lv.mx : lv.mx + lv.edge, :]
        first += s * tiles


def vmem(shape, dtype=F32):
    return pltpu.VMEM(shape, dtype)


def shards(permeability):
    nz = EZ * ELZ
    rows = permeability.shape[1]
    lanes = permeability.shape[2]
    assert rows == EL and lanes == COLUMNS * EL * nz
    rim = MX * nz
    gx, gy = lax.axis_size("gx"), lax.axis_size("gy")

    def sent(value, axis, shift):
        count = lax.axis_size(axis)
        return lax.ppermute(value, axis, [(i, (i + shift) % count) for i in range(count)])

    x_low = sent(permeability[:, rows - MX :], "gx", 1)
    x_high = sent(permeability[:, :MX], "gx", -1)

    def strip(part):
        return jnp.concatenate([x_low[:, :, part], permeability[:, :, part], x_high[:, :, part]], axis=1)

    y_low = sent(strip(slice(lanes - rim, lanes)), "gy", 1)
    y_high = sent(strip(slice(0, rim)), "gy", -1)
    halos = [x_low, x_high, y_low, y_high]
    flat_lanes = lanes + 2 * rim
    scratch = [
        vmem((LANES, lanes)),
        vmem((LANES, 2 * rim)),
        vmem((flat_lanes, LANES)),
        vmem((flat_lanes // 2, LANES)),
        vmem((SUBS * (TWIN.seg + 2) * nz, LANES)),
    ]
    for lv in LEVELS:
        scratch.append(vmem((lv.levels + 1, lv.seg, SUBS, 2 * LANES)))
        scratch += [vmem((lv.planes * lv.seg // 2, 2 * SUBS, 2 * LANES), BF16)] * 6
        scratch += [vmem((lv.seg, lv.planes * lv.seg, SUBS, LANES))] * 3
        scratch += [vmem((lv.inner + 1, 2 * lv.tiles, SUBS, LANES))] * 5
        scratch.append(vmem((2 * lv.tiles, SUBS, LANES)))
    for lv in LEVELS:
        scratch += [vmem((padded_rows(lv), LANES))] * 3
    scratch += [pltpu.SemaphoreType.DMA((2 * lv.edz,)) for lv in LEVELS]
    full = pl.BlockSpec(memory_space=pltpu.VMEM)
    inside = pl.pallas_call(
        place_kernel,
        out_shape=vmem((LANES, lanes)),
        in_specs=[full],
        out_specs=full,
        compiler_params=pltpu.CompilerParams(vmem_limit_bytes=8 * 1024 * 1024),
        cost_estimate=pl.CostEstimate(flops=1000000, bytes_accessed=4000000, transcendentals=0),
        name="place",
    )(permeability)
    phi, message = pl.pallas_call(
        solve_kernel,
        out_shape=[
            pltpu.HBM((sum(2 * field_rows(lv) for lv in LEVELS), LANES), F32),
            jax.ShapeDtypeStruct((gx * gy, LANES), F32),
        ],
        in_specs=[full] * 5,
        out_specs=[pl.BlockSpec(memory_space=pltpu.HBM), full],
        scratch_shapes=scratch,
        compiler_params=pltpu.CompilerParams(vmem_limit_bytes=50 * 1024 * 1024),
        name="solve",
    )(inside, *halos)
    gathered = lax.all_to_all(message, ("gx", "gy"), 0, 0, tiled=True)
    tiles = sum(lv.seg * turned_tiles(lv) for lv in LEVELS)
    turned = pl.pallas_call(
        turn_kernel,
        out_shape=vmem((tiles, LANES, LANES)),
        in_specs=[full],
        out_specs=full,
        compiler_params=pltpu.CompilerParams(vmem_limit_bytes=16 * 1024 * 1024),
        cost_estimate=pl.CostEstimate(flops=4000000, bytes_accessed=8000000, transcendentals=0),
        name="turned",
    )(phi)
    me = (lax.axis_index("gx") * gy + lax.axis_index("gy")).astype(jnp.int32).reshape(1)
    return tuple(
        pl.pallas_call(
            functools.partial(pressure_kernel, gy),
            out_shape=[
                jax.ShapeDtypeStruct((lv.edge, COLUMNS * lv.edge * EZ * lv.edz), F32) for lv in LEVELS
            ],
            in_specs=[pl.BlockSpec(memory_space=pltpu.SMEM), full, full],
            out_specs=[full] * 2,
            scratch_shapes=[vmem((COLUMNS * turned_tiles(lv), SUBS * lv.seg, LANES)) for lv in LEVELS],
            compiler_params=pltpu.CompilerParams(vmem_limit_bytes=16 * 1024 * 1024),
            name="pressure",
        )(me, gathered, turned)
    )


def solution(mesh):
    return jax.shard_map(
        shards,
        mesh=mesh,
        in_specs=(P(None, "gx", "gy"),),
        out_specs=(P("gx", "gy"), P("gx", "gy")),
        check_vma=False,
    )
```

```python
import functools
import typing

import jax
import jax.numpy as jnp
from jax import lax
from jax.experimental import pallas as pl
from jax.experimental.pallas import tpu as pltpu
from jax.sharding import PartitionSpec as P

EL = 32
ELZ = 16
MX = 4
MZ = 2
EZ = 2
LANES = 128
SUBS = 8
COLUMNS = 2
F32 = jnp.float32
BF16 = jnp.bfloat16


class Level(typing.NamedTuple):
    edge: int
    edz: int
    mx: int
    mz: int
    spacing: float
    step: int

    @property
    def width(self):
        return self.edge + 2 * self.mx

    @property
    def inner(self):
        return self.edz + 2 * self.mz - 2

    @property
    def seg(self):
        return -(-self.width // SUBS)

    @property
    def tiles(self):
        return self.seg * self.seg

    @property
    def levels(self):
        return EZ * self.edz + 2

    @property
    def planes(self):
        return -(-(self.inner + 1) // 2) * 2


FINE = Level(EL, ELZ, MX, MZ, 1.0, 1)
TWIN = Level(EL // 2, ELZ // 2, MX // 2, MZ // 2, 2.0, 2)
LEVELS = (FINE, TWIN)


def lane_iota(shape=(SUBS, LANES)):
    return lax.broadcasted_iota(jnp.int32, shape, len(shape) - 1)


def sub_iota(shape=(SUBS, LANES)):
    return lax.broadcasted_iota(jnp.int32, shape, len(shape) - 2)


def turn(value, shift, axis=1):
    return pltpu.roll(value, shift % value.shape[axis], axis)


def lane_parts():
    lane = lane_iota()
    return lane // 32, lane // 16 % 2, lane // 8 % 2, lane % 8


class Consts:
    def __init__(self, lv):
        corner, _, _, xo = lane_parts()
        yo = sub_iota()
        ax, ay = corner // 2, corner % 2
        self.lv = lv
        s = lv.seg
        self.fx, self.fy = [], []
        self.inx, self.iny, self.facex, self.facey = [], [], [], []
        for i in range(s):
            x = xo * s + i
            y = yo * s + i
            px = (x.astype(F32) - lv.mx + 0.5) / lv.edge
            py = (y.astype(F32) - lv.mx + 0.5) / lv.edge
            self.fx.append(jnp.where(ax == 1, px, 1.0 - px))
            self.fy.append(jnp.where(ay == 1, py, 1.0 - py))
            xs = [s * o + i for o in range(SUBS)]

            def ranged(value, low, high):
                if all(low <= v <= high for v in xs):
                    return None
                return ((value >= low) & (value <= high)).astype(F32)

            self.inx.append((ranged(x, 1, lv.width - 2), ranged(x, lv.mx, lv.mx + lv.edge - 1)))
            self.iny.append((ranged(y, 1, lv.width - 2), ranged(y, lv.mx, lv.mx + lv.edge - 1)))
            cut = (lv.mx - 1, lv.mx + lv.edge - 1)
            self.facex.append(((x != cut[0]) & (x != cut[1])).astype(F32) if any(v in cut for v in xs) else None)
            self.facey.append(((y != cut[0]) & (y != cut[1])).astype(F32) if any(v in cut for v in xs) else None)
        sx = jnp.where(ax == 1, -1.0 / lv.edge, 1.0 / lv.edge).astype(F32)
        sy = jnp.where(ay == 1, -1.0 / lv.edge, 1.0 / lv.edge).astype(F32)
        self.along_x = [sx * f for f in self.fy]
        self.along_y = [sy * f for f in self.fx]

    def fz(self, plane):
        place = (jnp.asarray(plane, jnp.int32).astype(F32) - self.lv.mz + 0.5) / self.lv.edz
        return 1.0 - place, place

    def masked(self, value, i, j, kind):
        for table, index in ((self.inx, i), (self.iny, j)):
            factor = table[index][kind]
            if factor is not None:
                value = value * factor
        return value


def tree(values):
    values = list(values)
    while len(values) > 1:
        values = [a + b for a, b in zip(values[::2], values[1::2])] + (
            [values[-1]] if len(values) % 2 else []
        )
    return values[0]


def xor_lane(value, bit):
    return jnp.where(lane_iota(value.shape) // bit % 2 == 1, turn(value, bit), turn(value, -bit))


def problem_sum(value):
    for shift in (4, 2, 1):
        value = value + turn(value, shift, 0)
    for bit in (1, 2, 4):
        value = value + xor_lane(value, bit)
    return value


def spread_weights(lv, k_ref, high_refs, low_refs, w_refs):
    s = lv.seg
    wide = (SUBS, LANES)
    pos = lane_iota(wide)
    yo = sub_iota(wide)
    first = pos < 40
    third = pos >= 80
    second = (pos >= 40) & (pos < 80)
    edge_x = first & (pos >= (lv.width - 1) * lv.step)

    def one(z, i, c):
        part = slice(c * LANES, (c + 1) * LANES)
        k = k_ref[z, i, :, part]
        nbx = turn(k, -lv.step)
        nby = k_ref[z, i + 1, :, part] if i < s - 1 else turn(k_ref[z, 0, :, part], -1, 0)
        nbz = k_ref[z + 1, i, :, part]
        nb = jnp.where(first, nbx, jnp.where(second, nby, nbz))
        w = (2.0 * lv.spacing) * k * nb / (k + nb)
        bad = edge_x | (second & (yo * s + i >= lv.width - 1))
        return jnp.where(bad, 0.0, w)

    def planes(t, _):
        units = [(2 * t + n, i) for n in range(2) for i in range(s)]
        for e in range(EZ):
            made = []
            for plane, i in units:
                z = jnp.clip(e * lv.edz + plane + 1 - lv.mz, 0, lv.levels - 1)
                w0, w1 = one(z, i, 0), one(z, i, 1)
                near, wrap = turn(w1, 40), turn(w1, 48)
                made.append((jnp.where(first, w0, near), jnp.where(third, near, w0), jnp.where(third, w0, wrap)))
            for p in range(s):
                for m in range(3):
                    both = jnp.concatenate([made[2 * p][m], made[2 * p + 1][m]], axis=0)
                    high = both.astype(BF16)
                    part = slice(e * LANES, (e + 1) * LANES)
                    high_refs[m][t * s + p, :, part] = high
                    low_refs[m][t * s + p, :, part] = (both - high.astype(F32)).astype(BF16)
        return 0

    lax.fori_loop(0, lv.planes // 2, planes, 0)
    rows = lv.planes * s * SUBS
    row = lax.broadcasted_iota(jnp.int32, (2 * LANES, 2 * LANES), 0)
    lane = lax.broadcasted_iota(jnp.int32, (1, 2 * LANES), 1)
    upper = lane // LANES
    for q in range(-(-s // 2)):
        x = lane % 8 * s + 2 * q + upper
        valid = (x < lv.width) & (2 * q + upper < s)
        for m in range(3):
            segment = jnp.where(lane // 8 % 2 == 0, m, (m + 1) % 3)
            source = jnp.where(valid, lane // 16 % 2 * LANES + segment * 40 + lv.step * x, -1)
            pick = (row == source).astype(F32).astype(BF16)
            out = jnp.dot(high_refs[m][...].reshape(rows, 2 * LANES), pick, preferred_element_type=F32)
            out = out + jnp.dot(low_refs[m][...].reshape(rows, 2 * LANES), pick, preferred_element_type=F32)
            for half in range(min(2, s - 2 * q)):
                part = out[:, half * LANES : (half + 1) * LANES]
                w_refs[m][2 * q + half] = part.reshape(lv.planes * s, SUBS, LANES)


class Case:
    def __init__(self, lv, w_refs, fields, planes):
        self.lv, self.cs, self.w_refs = lv, Consts(lv), w_refs
        self.d, self.q, self.r = fields[:3], fields[3], fields[4]
        (self.fz,) = planes

    def weights(self, plane):
        s = self.lv.seg
        return lambda m, i, j: self.w_refs[m][i, plane * s + j]


HALVES = (0, 1)
CHUNK = 640


def plane_rows(lv):
    return lv.tiles * SUBS


def field_rows(lv):
    return lv.edz * plane_rows(lv)


def padded_rows(lv):
    return -(-field_rows(lv) // CHUNK) * CHUNK


def turned_tiles(lv):
    return lv.edge * EZ * lv.edz // LANES


def looped(count, group, sums, step):
    def body(t, sums):
        return tuple(a + b for a, b in zip(sums, step(t * group)))

    start = tuple(jnp.zeros((SUBS, LANES), F32) for _ in range(sums))
    return list(lax.fori_loop(0, count // group, body, start))


def start_residual(case, group):
    lv, cs, s = case.lv, case.cs, case.lv.seg

    def step(z0):
        total = [[], []]
        for z in [z0 + n for n in range(group)]:
            get, below = case.weights(z + 1), case.weights(z)
            gz = cs.fz(z + 1)
            last = [get(1, i, s - 1) * cs.along_y[i] for i in range(s)]
            before = [turn(v, 1, 0) for v in last]
            for j in range(s):
                flux_y = last if j == s - 1 else [get(1, i, j) * cs.along_y[i] for i in range(s)]
                flux_x = [get(0, i, j) * cs.along_x[j] for i in range(s)]
                squares = [[], []]
                for i in range(s):
                    k = i * s + j
                    prev_x = flux_x[i - 1] if i else turn(flux_x[s - 1], 1)
                    flat = (prev_x - flux_x[i]) + (before[i] - flux_y[i])
                    flat = cs.masked(flat, i, j, 0)
                    tall = (cs.fx[i] * cs.fy[j]) * (1.0 / lv.edz) * (below(2, i, j) - get(2, i, j))
                    tall = cs.masked(tall, i, j, 0)
                    for h, value in enumerate((flat * gz[0] + tall, flat * gz[1] - tall)):
                        case.d[0][z, h * lv.tiles + k] = value
                        squares[h].append(value * value)
                for h in HALVES:
                    total[h].append(tree(squares[h]))
                before = flux_y
        return [tree(t) for t in total]

    return looped(lv.inner, group, 2, step)


def plane_rows_of(get, s):
    return lambda j: [get(i, j) for i in range(s)]


def x_jumps(row, s):
    return [row[i] - (row[i + 1] if i < s - 1 else turn(row[0], -1)) for i in range(s)]


def apply(case, number, betas):
    lv, cs, s = case.lv, case.cs, case.lv.seg
    keep = number < 2
    n = lv.tiles

    def fresh(z, h, k):
        at = h * n + k
        if number == 0:
            return case.d[0][z, at]
        value = case.r[z, at] + betas[h] * case.d[number - 1][z, at]
        case.d[number][z, at] = value
        return value

    firsts = []
    get = case.weights(0)
    for h in HALVES:
        terms = []
        for k in range(n):
            value = fresh(0, h, k)
            flux = -get(2, k // s, k % s) * value
            if keep:
                case.fz[h * n + k] = flux
            else:
                terms.append(-flux * value)
        firsts.append(tree(terms) if terms else 0.0)

    def step(z):
        total = [[], []]
        get = case.weights(z + 1)
        rows = [
            plane_rows_of(lambda i, j, h=h: case.d[number][z, h * n + i * s + j], s) for h in HALVES
        ]
        now = [rows[h](0) for h in HALVES]
        if keep:
            ends = [rows[h](s - 1) for h in HALVES]
            wy = [get(1, i, s - 1) for i in range(s)]
            last = [[wy[i] * (ends[h][i] - turn(now[h][i], -1, 0)) for i in range(s)] for h in HALVES]
            before = [[turn(v, 1, 0) for v in last[h]] for h in HALVES]
        for j in range(s):
            wx = [get(0, i, j) for i in range(s)]
            wy = [get(1, i, j) for i in range(s)]
            wz = [get(2, i, j) for i in range(s)]
            for h in HALVES:
                u = now[h]
                jump_x = x_jumps(u, s)
                flux_x = [w * v for w, v in zip(wx, jump_x)]
                if j < s - 1:
                    now[h] = rows[h](j + 1)
                    jump_y = [a - b for a, b in zip(u, now[h])]
                    flux_y = [w * v for w, v in zip(wy, jump_y)]
                elif keep:
                    flux_y = last[h]
                else:
                    jump_y = [a - turn(b, -1, 0) for a, b in zip(u, rows[h](0))]
                    flux_y = [w * v for w, v in zip(wy, jump_y)]
                terms = []
                for i in range(s):
                    k = i * s + j
                    jump = u[i] - fresh(z + 1, h, k)
                    flux = wz[i] * jump
                    if keep:
                        prev_x = flux_x[i - 1] if i else turn(flux_x[s - 1], 1)
                        value = (flux_x[i] - prev_x) + (flux_y[i] - before[h][i]) + (flux - case.fz[h * n + k])
                        case.fz[h * n + k] = flux
                        value = cs.masked(value, i, j, 0)
                        case.q[z, h * n + k] = value
                        terms.append(u[i] * value)
                    else:
                        terms.append((flux * jump + flux_x[i] * jump_x[i]) + flux_y[i] * jump_y[i])
                total[h].append(tree(terms))
                if keep:
                    before[h] = flux_y
        return [tree(t) for t in total]

    return [a + b for a, b in zip(looped(lv.inner, 1, 2, step), firsts)]


def reduce_residual(case, group, number, alphas):
    lv = case.lv

    def step(z0):
        total = [[], []]
        source = case.d[0] if number == 0 else case.r
        for z in [z0 + n for n in range(group)]:
            for h in HALVES:
                squares = []
                for k in range(lv.tiles):
                    at = h * lv.tiles + k
                    value = source[z, at] - alphas[h] * case.q[z, at]
                    case.r[z, at] = value
                    squares.append(value * value)
                total[h].append(tree(squares))
        return [tree(t) for t in total]

    return looped(lv.inner, group, 2, step)


def finish(case, alphas, refs, send):
    lv, cs, s = case.lv, case.cs, case.lv.seg
    n = lv.tiles
    f_ref, p_ref, y_ref = refs
    lower = lane_parts()[1] == 0

    def at(z, k):
        return pl.ds(pl.multiple_of(z * plane_rows(lv) + k * SUBS, SUBS), SUBS)

    def fresh(z, i, j, gz):
        k = i * s + j
        inner = z + lv.mz - 1
        both = cs.fx[i] * cs.fy[j]
        values = []
        for h in HALVES:
            value = both * gz[h]
            for alpha, d_ref in zip(alphas[h], case.d):
                value = value + alpha * d_ref[inner, h * n + k]
            values.append(cs.masked(value, i, j, 1))
        chosen = jnp.where(lower, values[1], values[0])
        f_ref[at(z, k), :] = chosen
        p_ref[at(z, k), :] = values[0]
        return chosen

    gz = cs.fz(lv.mz)
    for i in range(s):
        for j in range(s):
            fresh(0, i, j, gz)
            case.fz[i * s + j] = jnp.zeros((SUBS, LANES), F32)
    rest = padded_rows(lv) - field_rows(lv)
    if rest:
        for ref in refs:
            ref[field_rows(lv) :, :] = jnp.zeros((rest, LANES), F32)

    def cut(values, table):
        return [v if f is None else v * f for v, f in zip(values, table)]

    def body(z, _):
        get = case.weights(z + lv.mz)
        up = jnp.minimum(z + 1, lv.edz - 1)
        gz = cs.fz(up + lv.mz)
        rows = plane_rows_of(lambda i, j: f_ref[at(z, i * s + j), :], s)
        now = rows(0)
        last = [get(1, i, s - 1) * (v - turn(now[i], -1, 0)) for i, v in enumerate(rows(s - 1))]
        last = cut(last, [cs.facey[s - 1]] * s)
        before = [turn(v, 1, 0) for v in last]
        for j in range(s):
            u = now
            flux_x = cut([get(0, i, j) * v for i, v in enumerate(x_jumps(u, s))], cs.facex)
            flux_y = last
            if j < s - 1:
                now = rows(j + 1)
                flux_y = cut([get(1, i, j) * (u[i] - now[i]) for i in range(s)], [cs.facey[j]] * s)
            for i in range(s):
                k = i * s + j
                flux = get(2, i, j) * (u[i] - fresh(up, i, j, gz))
                prev_x = flux_x[i - 1] if i else turn(flux_x[s - 1], 1)
                y_ref[at(z, k), :] = (flux_x[i] - prev_x) + (flux_y[i] - before[i]) + (flux - case.fz[k])
                case.fz[k] = flux
            before = flux_y
        for h in HALVES:
            send(h, z).start()
        return 0

    lax.fori_loop(0, lv.edz, body, 0)
    pairs = jnp.zeros((2 * LANES, LANES), F32)
    for start in range(0, padded_rows(lv), CHUNK):
        part = slice(start, start + CHUNK)
        left = jnp.concatenate([f_ref[part, :].T, p_ref[part, :].T], axis=0)
        right = y_ref[part, :]
        left_high, right_high = left.astype(BF16), right.astype(BF16)
        left_low = (left - left_high.astype(F32)).astype(BF16)
        right_low = (right - right_high.astype(F32)).astype(BF16)
        for a, b in ((left_high, right_high), (left_low, right_high), (left_high, right_low)):
            pairs = pairs + jnp.dot(a, b, preferred_element_type=F32)
    shape = (LANES, LANES)
    row, lane = sub_iota(shape), lane_iota(shape)
    sums = [jnp.where(row == (lane + 32 * k) % LANES, pairs[:LANES], 0.0) for k in range(3)]
    sums.append(jnp.where(row % 32 == lane % 32, pairs[LANES:], 0.0))
    out = []
    for value in sums:
        value = tree([value[r : r + SUBS] for r in range(0, LANES, SUBS)])
        out.append(value)
    return out


GROUPS = {FINE: 1, TWIN: 4}


def place_kernel(center, out_ref):
    nx = center.shape[1]
    out_ref[...] = jnp.ones(out_ref.shape, F32)
    for m in range(3):
        off = m * (nx + 2 * MX) + MX
        out_ref[off : off + nx, :] = center[m]


def solve_kernel(
    inside, x_low, x_high, y_low, y_high,
    phi, message,
    flat, sides, rows, pairs, twin_rows, *refs,
):
    lanes = inside.shape[1]
    rim = y_low.shape[2]
    wide = y_low.shape[1]
    for m in range(3):
        off = m * wide
        flat[off : off + MX, :] = x_low[m]
        flat[off + wide - MX : off + wide, :] = x_high[m]
        sides[off : off + wide, :rim] = y_low[m]
        sides[off : off + wide, rim:] = y_high[m]
    sides[3 * wide :, :] = jnp.ones((LANES - 3 * wide, sides.shape[1]), F32)
    row = sub_iota((LANES, LANES))
    place = row % wide
    outer = (row < 3 * wide) & ((place < MX) | (place >= wide - MX))
    for t in range(rim // LANES):
        low, high = slice(t * LANES, (t + 1) * LANES), slice(rim + t * LANES, rim + (t + 1) * LANES)
        rows[low, :] = sides[:, low].T
        rows[lanes + rim + t * LANES : lanes + rim + (t + 1) * LANES, :] = sides[:, high].T
    for t in range(lanes // LANES):
        part = slice(t * LANES, (t + 1) * LANES)
        rows[rim + t * LANES : rim + (t + 1) * LANES, :] = jnp.where(outer, flat[:, part], inside[:, part]).T

    nz = EZ * ELZ
    twin_y = rows.shape[0] // nz // 2
    for y in range(twin_y):
        both = rows[2 * y * nz : (2 * y + 1) * nz, :] + rows[(2 * y + 1) * nz : (2 * y + 2) * nz, :]
        both = both + turn(both, -1)
        at = y * nz
        pairs[at : at + nz, :] = both
        twin_rows[at : at + 8, :] = jnp.broadcast_to(0.25 * both[0:1], (8, LANES))
        twin_rows[at + 8 + nz // 2 : at + nz, :] = jnp.broadcast_to(0.25 * both[nz - 1 : nz], (8, LANES))
    for y in range(twin_y):
        at = y * nz
        middle = pairs[pl.ds(at, nz // 2, stride=2), :] + pairs[pl.ds(at + 1, nz // 2, stride=2), :]
        twin_rows[at + 8 : at + 8 + nz // 2, :] = 0.125 * middle
    twin_rows[twin_y * nz :, :] = jnp.ones((twin_rows.shape[0] - twin_y * nz, LANES), F32)

    refs = list(refs)

    def take(count):
        got = refs[:count]
        del refs[:count]
        return got

    cases = []
    for lv, source in zip(LEVELS, (rows, twin_rows)):
        (k_ref,) = take(1)
        high_refs, low_refs, w_refs = take(3), take(3), take(3)
        for z in range(lv.levels + 1):
            cell = min(max(z - 1, 0), nz - 1) if lv is FINE else min(z, lv.levels - 1) + 7
            for i in range(lv.seg):
                for c in range(COLUMNS):
                    start = (lv.edge * c + i) * nz + cell
                    k_ref[z, i, :, c * LANES : (c + 1) * LANES] = source[pl.ds(start, SUBS, stride=lv.seg * nz), :]
        spread_weights(lv, k_ref, high_refs, low_refs, w_refs)
        case = Case(lv, w_refs, take(5), take(1))
        for k in range(2 * lv.tiles):
            case.d[0][lv.inner, k] = jnp.zeros((SUBS, LANES), F32)
            case.r[lv.inner, k] = jnp.zeros((SUBS, LANES), F32)
        cases.append(case)

    def both_levels(work):
        sums = [work(n, case, GROUPS[case.lv]) for n, case in enumerate(cases)]
        return [[problem_sum(v) for v in part] for part in sums]

    rr = both_levels(lambda n, case, group: start_residual(case, group))
    alphas = [[[], []] for _ in LEVELS]
    betas = [None] * len(LEVELS)
    for step in range(3):
        dots = both_levels(lambda n, case, group: apply(case, step, betas[n]))
        now = [[a / b for a, b in zip(rr[n], dots[n])] for n in range(len(LEVELS))]
        for n in range(len(LEVELS)):
            for h in HALVES:
                alphas[n][h].append(now[n][h])
        if step < 2:
            new = both_levels(lambda n, case, group: reduce_residual(case, group, step, now[n]))
            betas = [[a / b for a, b in zip(new[n], rr[n])] for n in range(len(LEVELS))]
            rr = new

    results = [take(3), take(3)]
    sems = take(2)

    def send(n, h, z):
        lv = LEVELS[n]
        size = plane_rows(lv)
        first = sum(2 * field_rows(v) for v in LEVELS[:n]) + h * field_rows(lv)
        return pltpu.make_async_copy(
            results[n][h].at[pl.ds(pl.multiple_of(z * size, SUBS), size)],
            phi.at[pl.ds(pl.multiple_of(first + z * size, SUBS), size)],
            sems[n].at[h * lv.edz + z],
        )

    totals = both_levels(
        lambda n, case, group: finish(case, alphas[n], results[n], functools.partial(send, n))
    )
    _, element, _, slot = lane_parts()
    packed = []
    for level in totals:
        parts = [v + xor_lane(v, 16) for v in level[:3]]
        parts.append(jnp.where(element == 0, level[3], turn(level[3], 16)))
        packed.append(
            jnp.where(slot == 0, parts[0], jnp.where(slot == 1, parts[1], jnp.where(slot == 2, parts[2], parts[3])))
        )
    row = jnp.where(element == 0, packed[0], packed[1])
    for r in range(0, message.shape[0], SUBS):
        message[r : r + SUBS, :] = row
    for n, lv in enumerate(LEVELS):
        for h in HALVES:
            for z in range(lv.edz):
                send(n, h, z).wait()


def coarse_nodes(gathered, gy_count, me):
    total_rows = gathered.shape[0]
    shape = gathered.shape
    lane = lane_iota(shape)
    row = sub_iota(shape)
    corner = lane // 32
    column = lane // 8 % 2
    last = row % gy_count == gy_count - 1
    start = row % gy_count == 0
    one = gathered
    two = turn(gathered, -1)
    four = turn(gathered, -2)
    rhs = turn(gathered, -3)
    two_back = turn(two, 32)

    def next_x(u):
        return turn(u, -gy_count, 0)

    def prev_x(u):
        return turn(u, gy_count, 0)

    def next_y(u):
        ahead = jnp.where(last, turn(u, gy_count - 1, 0), turn(u, -1, 0))
        return jnp.where(column == 0, turn(u, -8), turn(ahead, 8))

    def prev_y(u):
        behind = jnp.where(start, turn(u, 1 - gy_count, 0), turn(u, 1, 0))
        return jnp.where(column == 1, turn(u, 8), turn(behind, -8))

    def by_corner(a, b, c, d):
        return jnp.where(corner == 0, a, jnp.where(corner == 1, b, jnp.where(corner == 2, c, d)))

    def corners(u):
        ux = next_x(u)
        return by_corner(u, next_y(u), ux, next_y(ux))

    def assemble(v):
        vx = prev_x(v)
        w = by_corner(v, prev_y(v), vx, prev_y(vx))
        w = w + turn(w, 64)
        return w + turn(w, 32)

    def operate(u):
        c = corners(u)
        return assemble(one * c + two * turn(c, -32) + two_back * turn(c, 32) + four * turn(c, 64))

    def total(a, b):
        v = a * b
        v = tree([v[r : r + SUBS] for r in range(0, total_rows, SUBS)])
        for shift in (4, 2, 1):
            v = v + turn(v, shift, 0)
        v = v + xor_lane(v, 8)
        return v[0:1]

    residual = -assemble(rhs)
    direction = residual
    update = jnp.zeros_like(residual)
    now = total(residual, residual)
    for step in range(2):
        image = operate(direction)
        alpha = now / total(direction, image)
        update = update + alpha * direction
        if step == 0:
            residual = residual - alpha * image
            new = total(residual, residual)
            direction = residual + new / now * direction
            now = new
    mine = jnp.where(row == me, corners(update), 0.0)
    mine = jnp.sum(mine, axis=0, keepdims=True)
    return jnp.broadcast_to(mine, (SUBS, LANES))


def turn_kernel(phi, out_ref):
    start_row, number = 0, 0
    for lv in LEVELS:
        s = lv.seg
        nz = EZ * lv.edz
        per = LANES // nz
        for i in range(s):
            for t in range(turned_tiles(lv)):
                parts = []
                for n in range(per):
                    yo, j = divmod(lv.mx + t * per + n, s)
                    start = start_row + (i * s + j) * SUBS + yo
                    chosen, bottom = [
                        phi[pl.ds(start + h * field_rows(lv), lv.edz, stride=plane_rows(lv)), :] for h in HALVES
                    ]
                    lower = lane_iota(chosen.shape) // 16 % 2 == 0
                    parts.append(jnp.where(lower, chosen, turn(bottom, 16)))
                    parts.append(jnp.where(lower, turn(chosen, -16), 0.0))
                out_ref[number] = jnp.concatenate(parts, axis=0).T
                number += 1
        start_row += 2 * field_rows(lv)


def pressure_kernel(gy_count, me_ref, gathered, turned, fine_out, twin_out, fine_all, twin_all):
    mine = coarse_nodes(gathered[...], gy_count, me_ref[0])
    first = 0
    for n, (lv, out_ref, all_ref) in enumerate(((FINE, fine_out, fine_all), (TWIN, twin_out, twin_all))):
        s = lv.seg
        tiles = turned_tiles(lv)
        nodes = {}
        for c in range(COLUMNS):
            for p in range(4):
                at = p * 32 + n * 16 + c * 8
                nodes[p, c] = jnp.broadcast_to(mine[:, at : at + 1], (SUBS, LANES))
        for c in range(COLUMNS):
            for t in range(tiles):
                at = (c * tiles + t) * LANES
                for i in range(s):
                    def part(group):
                        return turned[first + i * tiles + t, group * 16 + c * 8 : group * 16 + c * 8 + 8, :]

                    value = tree([part(2 * p) * nodes[p, c] + part(2 * p + 1) for p in range(4)])
                    all_ref[c * tiles + t, pl.ds(i, SUBS, stride=s), :] = value
                out_ref[:, at : at + LANES] = all_ref[c * tiles + t, lv.mx : lv.mx + lv.edge, :]
        first += s * tiles


def vmem(shape, dtype=F32):
    return pltpu.VMEM(shape, dtype)


def shards(permeability):
    nz = EZ * ELZ
    rows = permeability.shape[1]
    lanes = permeability.shape[2]
    assert rows == EL and lanes == COLUMNS * EL * nz
    rim = MX * nz
    gx, gy = lax.axis_size("gx"), lax.axis_size("gy")

    def sent(value, axis, shift):
        count = lax.axis_size(axis)
        return lax.ppermute(value, axis, [(i, (i + shift) % count) for i in range(count)])

    x_low = sent(permeability[:, rows - MX :], "gx", 1)
    x_high = sent(permeability[:, :MX], "gx", -1)

    def strip(part):
        return jnp.concatenate([x_low[:, :, part], permeability[:, :, part], x_high[:, :, part]], axis=1)

    y_low = sent(strip(slice(lanes - rim, lanes)), "gy", 1)
    y_high = sent(strip(slice(0, rim)), "gy", -1)
    halos = [x_low, x_high, y_low, y_high]
    flat_lanes = lanes + 2 * rim
    scratch = [
        vmem((LANES, lanes)),
        vmem((LANES, 2 * rim)),
        vmem((flat_lanes, LANES)),
        vmem((flat_lanes // 2, LANES)),
        vmem((SUBS * (TWIN.seg + 2) * nz, LANES)),
    ]
    for lv in LEVELS:
        scratch.append(vmem((lv.levels + 1, lv.seg, SUBS, 2 * LANES)))
        scratch += [vmem((lv.planes * lv.seg // 2, 2 * SUBS, 2 * LANES), BF16)] * 6
        scratch += [vmem((lv.seg, lv.planes * lv.seg, SUBS, LANES))] * 3
        scratch += [vmem((lv.inner + 1, 2 * lv.tiles, SUBS, LANES))] * 5
        scratch.append(vmem((2 * lv.tiles, SUBS, LANES)))
    for lv in LEVELS:
        scratch += [vmem((padded_rows(lv), LANES))] * 3
    scratch += [pltpu.SemaphoreType.DMA((2 * lv.edz,)) for lv in LEVELS]
    full = pl.BlockSpec(memory_space=pltpu.VMEM)
    inside = pl.pallas_call(
        place_kernel,
        out_shape=vmem((LANES, lanes)),
        in_specs=[full],
        out_specs=full,
        compiler_params=pltpu.CompilerParams(vmem_limit_bytes=8 * 1024 * 1024),
        cost_estimate=pl.CostEstimate(flops=1000000, bytes_accessed=4000000, transcendentals=0),
        name="place",
    )(permeability)
    phi, message = pl.pallas_call(
        solve_kernel,
        out_shape=[
            pltpu.HBM((sum(2 * field_rows(lv) for lv in LEVELS), LANES), F32),
            jax.ShapeDtypeStruct((gx * gy, LANES), F32),
        ],
        in_specs=[full] * 5,
        out_specs=[pl.BlockSpec(memory_space=pltpu.HBM), full],
        scratch_shapes=scratch,
        compiler_params=pltpu.CompilerParams(vmem_limit_bytes=50 * 1024 * 1024),
        name="solve",
    )(inside, *halos)
    gathered = lax.all_to_all(message, ("gx", "gy"), 0, 0, tiled=True)
    tiles = sum(lv.seg * turned_tiles(lv) for lv in LEVELS)
    turned = pl.pallas_call(
        turn_kernel,
        out_shape=vmem((tiles, LANES, LANES)),
        in_specs=[full],
        out_specs=full,
        compiler_params=pltpu.CompilerParams(vmem_limit_bytes=16 * 1024 * 1024),
        cost_estimate=pl.CostEstimate(flops=4000000, bytes_accessed=8000000, transcendentals=0),
        name="turned",
    )(phi)
    me = (lax.axis_index("gx") * gy + lax.axis_index("gy")).astype(jnp.int32).reshape(1)
    return tuple(
        pl.pallas_call(
            functools.partial(pressure_kernel, gy),
            out_shape=[
                jax.ShapeDtypeStruct((lv.edge, COLUMNS * lv.edge * EZ * lv.edz), F32) for lv in LEVELS
            ],
            in_specs=[pl.BlockSpec(memory_space=pltpu.SMEM), full, full],
            out_specs=[full] * 2,
            scratch_shapes=[vmem((COLUMNS * turned_tiles(lv), SUBS * lv.seg, LANES)) for lv in LEVELS],
            compiler_params=pltpu.CompilerParams(vmem_limit_bytes=16 * 1024 * 1024),
            name="pressure",
        )(me, gathered, turned)
    )


def solution(mesh):
    return jax.shard_map(
        shards,
        mesh=mesh,
        in_specs=(P(None, "gx", "gy"),),
        out_specs=(P("gx", "gy"), P("gx", "gy")),
        check_vma=False,
    )
```

```python
import functools
import typing

import jax
import jax.numpy as jnp
from jax import lax
from jax.experimental import pallas as pl
from jax.experimental.pallas import tpu as pltpu
from jax.sharding import PartitionSpec as P

EL = 32
ELZ = 16
MX = 4
MZ = 2
EZ = 2
LANES = 128
SUBS = 8
COLUMNS = 2
F32 = jnp.float32
BF16 = jnp.bfloat16


class Level(typing.NamedTuple):
    edge: int
    edz: int
    mx: int
    mz: int
    spacing: float
    step: int

    @property
    def width(self):
        return self.edge + 2 * self.mx

    @property
    def inner(self):
        return self.edz + 2 * self.mz - 2

    @property
    def seg(self):
        return -(-self.width // SUBS)

    @property
    def tiles(self):
        return self.seg * self.seg

    @property
    def levels(self):
        return EZ * self.edz + 2

    @property
    def planes(self):
        return -(-(self.inner + 1) // 2) * 2


FINE = Level(EL, ELZ, MX, MZ, 1.0, 1)
TWIN = Level(EL // 2, ELZ // 2, MX // 2, MZ // 2, 2.0, 2)
LEVELS = (FINE, TWIN)


def lane_iota(shape=(SUBS, LANES)):
    return lax.broadcasted_iota(jnp.int32, shape, len(shape) - 1)


def sub_iota(shape=(SUBS, LANES)):
    return lax.broadcasted_iota(jnp.int32, shape, len(shape) - 2)


def turn(value, shift, axis=1):
    return pltpu.roll(value, shift % value.shape[axis], axis)


def lane_parts():
    lane = lane_iota()
    return lane // 32, lane // 16 % 2, lane // 8 % 2, lane % 8


class Consts:
    def __init__(self, lv):
        corner, _, _, xo = lane_parts()
        yo = sub_iota()
        ax, ay = corner // 2, corner % 2
        self.lv = lv
        s = lv.seg
        self.fx, self.fy = [], []
        self.inx, self.iny, self.facex, self.facey = [], [], [], []
        for i in range(s):
            x = xo * s + i
            y = yo * s + i
            px = (x.astype(F32) - lv.mx + 0.5) / lv.edge
            py = (y.astype(F32) - lv.mx + 0.5) / lv.edge
            self.fx.append(jnp.where(ax == 1, px, 1.0 - px))
            self.fy.append(jnp.where(ay == 1, py, 1.0 - py))
            xs = [s * o + i for o in range(SUBS)]

            def ranged(value, low, high):
                if all(low <= v <= high for v in xs):
                    return None
                return ((value >= low) & (value <= high)).astype(F32)

            self.inx.append((ranged(x, 1, lv.width - 2), ranged(x, lv.mx, lv.mx + lv.edge - 1)))
            self.iny.append((ranged(y, 1, lv.width - 2), ranged(y, lv.mx, lv.mx + lv.edge - 1)))
            cut = (lv.mx - 1, lv.mx + lv.edge - 1)
            self.facex.append(((x != cut[0]) & (x != cut[1])).astype(F32) if any(v in cut for v in xs) else None)
            self.facey.append(((y != cut[0]) & (y != cut[1])).astype(F32) if any(v in cut for v in xs) else None)
        sx = jnp.where(ax == 1, -1.0 / lv.edge, 1.0 / lv.edge).astype(F32)
        sy = jnp.where(ay == 1, -1.0 / lv.edge, 1.0 / lv.edge).astype(F32)
        self.along_x = [sx * f for f in self.fy]
        self.along_y = [sy * f for f in self.fx]

    def fz(self, plane):
        place = (jnp.asarray(plane, jnp.int32).astype(F32) - self.lv.mz + 0.5) / self.lv.edz
        return 1.0 - place, place

    def masked(self, value, i, j, kind):
        for table, index in ((self.inx, i), (self.iny, j)):
            factor = table[index][kind]
            if factor is not None:
                value = value * factor
        return value


def tree(values):
    values = list(values)
    while len(values) > 1:
        values = [a + b for a, b in zip(values[::2], values[1::2])] + (
            [values[-1]] if len(values) % 2 else []
        )
    return values[0]


def xor_lane(value, bit):
    return jnp.where(lane_iota(value.shape) // bit % 2 == 1, turn(value, bit), turn(value, -bit))


def problem_sum(value):
    for shift in (4, 2, 1):
        value = value + turn(value, shift, 0)
    for bit in (1, 2, 4):
        value = value + xor_lane(value, bit)
    return value


def spread_weights(lv, k_ref, high_refs, low_refs, w_refs):
    s = lv.seg
    wide = (SUBS, LANES)
    pos = lane_iota(wide)
    yo = sub_iota(wide)
    first = pos < 40
    third = pos >= 80
    second = (pos >= 40) & (pos < 80)
    edge_x = first & (pos >= (lv.width - 1) * lv.step)

    def one(z, i, c):
        part = slice(c * LANES, (c + 1) * LANES)
        k = k_ref[z, i, :, part]
        nbx = turn(k, -lv.step)
        nby = k_ref[z, i + 1, :, part] if i < s - 1 else turn(k_ref[z, 0, :, part], -1, 0)
        nbz = k_ref[z + 1, i, :, part]
        nb = jnp.where(first, nbx, jnp.where(second, nby, nbz))
        w = (2.0 * lv.spacing) * k * nb / (k + nb)
        bad = edge_x | (second & (yo * s + i >= lv.width - 1))
        return jnp.where(bad, 0.0, w)

    def planes(t, _):
        units = [(2 * t + n, i) for n in range(2) for i in range(s)]
        for e in range(EZ):
            made = []
            for plane, i in units:
                z = jnp.clip(e * lv.edz + plane + 1 - lv.mz, 0, lv.levels - 1)
                w0, w1 = one(z, i, 0), one(z, i, 1)
                near, wrap = turn(w1, 40), turn(w1, 48)
                made.append((jnp.where(first, w0, near), jnp.where(third, near, w0), jnp.where(third, w0, wrap)))
            for p in range(s):
                for m in range(3):
                    both = jnp.concatenate([made[2 * p][m], made[2 * p + 1][m]], axis=0)
                    high = both.astype(BF16)
                    part = slice(e * LANES, (e + 1) * LANES)
                    high_refs[m][t * s + p, :, part] = high
                    low_refs[m][t * s + p, :, part] = (both - high.astype(F32)).astype(BF16)
        return 0

    lax.fori_loop(0, lv.planes // 2, planes, 0)
    rows = lv.planes * s * SUBS
    row = lax.broadcasted_iota(jnp.int32, (2 * LANES, 2 * LANES), 0)
    lane = lax.broadcasted_iota(jnp.int32, (1, 2 * LANES), 1)
    upper = lane // LANES
    for q in range(-(-s // 2)):
        x = lane % 8 * s + 2 * q + upper
        valid = (x < lv.width) & (2 * q + upper < s)
        for m in range(3):
            segment = jnp.where(lane // 8 % 2 == 0, m, (m + 1) % 3)
            source = jnp.where(valid, lane // 16 % 2 * LANES + segment * 40 + lv.step * x, -1)
            pick = (row == source).astype(F32).astype(BF16)
            out = jnp.dot(high_refs[m][...].reshape(rows, 2 * LANES), pick, preferred_element_type=F32)
            out = out + jnp.dot(low_refs[m][...].reshape(rows, 2 * LANES), pick, preferred_element_type=F32)
            for half in range(min(2, s - 2 * q)):
                part = out[:, half * LANES : (half + 1) * LANES]
                w_refs[m][2 * q + half] = part.reshape(lv.planes * s, SUBS, LANES)


class Case:
    def __init__(self, lv, w_refs, fields, planes):
        self.lv, self.cs, self.w_refs = lv, Consts(lv), w_refs
        self.d, self.q, self.r = fields[:3], fields[3], fields[4]
        (self.fz,) = planes

    def weights(self, plane):
        s = self.lv.seg
        return lambda m, i, j: self.w_refs[m][i, plane * s + j]


HALVES = (0, 1)
CHUNK = 640


def plane_rows(lv):
    return lv.tiles * SUBS


def field_rows(lv):
    return lv.edz * plane_rows(lv)


def padded_rows(lv):
    return -(-field_rows(lv) // CHUNK) * CHUNK


def turned_tiles(lv):
    return lv.edge * EZ * lv.edz // LANES


def looped(count, group, sums, step):
    def body(t, sums):
        return tuple(a + b for a, b in zip(sums, step(t * group)))

    start = tuple(jnp.zeros((SUBS, LANES), F32) for _ in range(sums))
    return list(lax.fori_loop(0, count // group, body, start))


def start_residual(case, group):
    lv, cs, s = case.lv, case.cs, case.lv.seg

    def step(z0):
        total = [[], []]
        stores = []
        for z in [z0 + n for n in range(group)]:
            get, below = case.weights(z + 1), case.weights(z)
            gz = cs.fz(z + 1)
            last = [get(1, i, s - 1) * cs.along_y[i] for i in range(s)]
            before = [turn(v, 1, 0) for v in last]
            for j in range(s):
                flux_y = last if j == s - 1 else [get(1, i, j) * cs.along_y[i] for i in range(s)]
                flux_x = [get(0, i, j) * cs.along_x[j] for i in range(s)]
                tops = [below(2, i, j) - get(2, i, j) for i in range(s)]
                for index, value in stores:
                    case.d[0][index] = value
                del stores[:]
                squares = [[], []]
                for i in range(s):
                    k = i * s + j
                    prev_x = flux_x[i - 1] if i else turn(flux_x[s - 1], 1)
                    flat = (prev_x - flux_x[i]) + (before[i] - flux_y[i])
                    flat = cs.masked(flat, i, j, 0)
                    tall = (cs.fx[i] * cs.fy[j]) * (1.0 / lv.edz) * tops[i]
                    tall = cs.masked(tall, i, j, 0)
                    for h, value in enumerate((flat * gz[0] + tall, flat * gz[1] - tall)):
                        stores.append(((z, h * lv.tiles + k), value))
                        squares[h].append(value * value)
                for h in HALVES:
                    total[h].append(tree(squares[h]))
                before = flux_y
        for index, value in stores:
            case.d[0][index] = value
        return [tree(t) for t in total]

    return looped(lv.inner, group, 2, step)


def x_jumps(row, s):
    return [row[i] - (row[i + 1] if i < s - 1 else turn(row[0], -1)) for i in range(s)]


def apply(case, number, betas):
    lv, cs, s = case.lv, case.cs, case.lv.seg
    keep = number < 2
    n = lv.tiles

    def fresh(z, h, k):
        at = h * n + k
        if number == 0:
            return case.d[0][z, at]
        value = case.r[z, at] + betas[h] * case.d[number - 1][z, at]
        case.d[number][z, at] = value
        return value

    firsts = []
    get = case.weights(0)
    for h in HALVES:
        terms = []
        for k in range(n):
            value = fresh(0, h, k)
            flux = -get(2, k // s, k % s) * value
            if keep:
                case.fz[h * n + k] = flux
            else:
                terms.append(-flux * value)
        firsts.append(tree(terms) if terms else 0.0)

    def step(z):
        total = [[], []]
        get = case.weights(z + 1)

        def load(j):
            cells = [i * s + j for i in range(s)]
            out = {"u": [[case.d[number][z, h * n + k] for k in cells] for h in HALVES]}
            out["w"] = [[get(m, i, j) for i in range(s)] for m in range(3)]
            if keep:
                out["fz"] = [[case.fz[h * n + k] for k in cells] for h in HALVES]
            if number == 0:
                out["up"] = [[case.d[0][z + 1, h * n + k] for k in cells] for h in HALVES]
            else:
                old = case.d[number - 1]
                out["up"] = [
                    [(case.r[z + 1, h * n + k], old[z + 1, h * n + k]) for k in cells] for h in HALVES
                ]
            return out

        row = load(0)
        if keep:
            wy = [get(1, i, s - 1) for i in range(s)]
            ends = [[case.d[number][z, h * n + i * s + s - 1] for i in range(s)] for h in HALVES]
        heads = [[turn(v, -1, 0) for v in row["u"][h]] for h in HALVES]
        if keep:
            last = [[wy[i] * (ends[h][i] - heads[h][i]) for i in range(s)] for h in HALVES]
            before = [[turn(v, 1, 0) for v in last[h]] for h in HALVES]
        stores = []

        def flush():
            for ref, index, value in stores:
                ref[index] = value
            del stores[:]

        for j in range(s):
            now, row = row, (load(j + 1) if j < s - 1 else None)
            flush()
            wx, wy, wz = now["w"]
            for h in HALVES:
                u = now["u"][h]
                jump_x = x_jumps(u, s)
                flux_x = [w * v for w, v in zip(wx, jump_x)]
                if keep and j == s - 1:
                    flux_y = last[h]
                else:
                    jump_y = [a - b for a, b in zip(u, row["u"][h] if j < s - 1 else heads[h])]
                    flux_y = [w * v for w, v in zip(wy, jump_y)]
                terms = []
                for i in range(s):
                    k = i * s + j
                    after = now["up"][h][i]
                    if number:
                        after = after[0] + betas[h] * after[1]
                        stores.append((case.d[number], (z + 1, h * n + k), after))
                    jump = u[i] - after
                    flux = wz[i] * jump
                    if keep:
                        prev_x = flux_x[i - 1] if i else turn(flux_x[s - 1], 1)
                        value = (flux_x[i] - prev_x) + (flux_y[i] - before[h][i]) + (flux - now["fz"][h][i])
                        stores.append((case.fz, h * n + k, flux))
                        value = cs.masked(value, i, j, 0)
                        stores.append((case.q, (z, h * n + k), value))
                        terms.append(u[i] * value)
                    else:
                        terms.append((flux * jump + flux_x[i] * jump_x[i]) + flux_y[i] * jump_y[i])
                total[h].append(tree(terms))
                if keep:
                    before[h] = flux_y
        flush()
        return [tree(t) for t in total]

    return [a + b for a, b in zip(looped(lv.inner, 1, 2, step), firsts)]


def reduce_residual(case, group, number, alphas):
    lv = case.lv

    def step(z0):
        total = [[], []]
        source = case.d[0] if number == 0 else case.r
        for z in [z0 + n for n in range(group)]:
            for h in HALVES:
                cells = range(h * lv.tiles, (h + 1) * lv.tiles)
                values = [source[z, at] - alphas[h] * case.q[z, at] for at in cells]
                for at, value in zip(cells, values):
                    case.r[z, at] = value
                total[h].append(tree([v * v for v in values]))
        return [tree(t) for t in total]

    return looped(lv.inner, group, 2, step)


def finish(case, alphas, refs, send):
    lv, cs, s = case.lv, case.cs, case.lv.seg
    n = lv.tiles
    f_ref, p_ref, y_ref = refs
    lower = lane_parts()[1] == 0

    def at(z, k):
        return pl.ds(pl.multiple_of(z * plane_rows(lv) + k * SUBS, SUBS), SUBS)

    def parts(z, k):
        return [[d_ref[z + lv.mz - 1, h * n + k] for d_ref in case.d] for h in HALVES]

    def fresh(i, j, gz, fields):
        both = cs.fx[i] * cs.fy[j]
        values = []
        for h in HALVES:
            value = both * gz[h]
            for alpha, d in zip(alphas[h], fields[h]):
                value = value + alpha * d
            values.append(cs.masked(value, i, j, 1))
        return jnp.where(lower, values[1], values[0]), values[0]

    gz = cs.fz(lv.mz)
    for i in range(s):
        for j in range(s):
            k = i * s + j
            f_ref[at(0, k), :], p_ref[at(0, k), :] = fresh(i, j, gz, parts(0, k))
            case.fz[k] = jnp.zeros((SUBS, LANES), F32)
    rest = padded_rows(lv) - field_rows(lv)
    if rest:
        for ref in refs:
            ref[field_rows(lv) :, :] = jnp.zeros((rest, LANES), F32)

    def cut(values, table):
        return [v if f is None else v * f for v, f in zip(values, table)]

    def body(z, _):
        get = case.weights(z + lv.mz)
        up = jnp.minimum(z + 1, lv.edz - 1)
        gz = cs.fz(up + lv.mz)

        def load(j):
            cells = [i * s + j for i in range(s)]
            return {
                "u": [f_ref[at(z, k), :] for k in cells],
                "w": [[get(m, i, j) for i in range(s)] for m in range(3)],
                "fz": [case.fz[k] for k in cells],
                "up": [parts(up, k) for k in cells],
            }

        row = load(0)
        wy = [get(1, i, s - 1) for i in range(s)]
        ends = [f_ref[at(z, i * s + s - 1), :] for i in range(s)]
        last = [wy[i] * (ends[i] - turn(row["u"][i], -1, 0)) for i in range(s)]
        last = cut(last, [cs.facey[s - 1]] * s)
        before = [turn(v, 1, 0) for v in last]
        stores = []

        def flush():
            for ref, index, value in stores:
                ref[index] = value
            del stores[:]

        for j in range(s):
            now, row = row, (load(j + 1) if j < s - 1 else None)
            flush()
            u = now["u"]
            wx, wy, wz = now["w"]
            flux_x = cut([w * v for w, v in zip(wx, x_jumps(u, s))], cs.facex)
            flux_y = last
            if j < s - 1:
                flux_y = cut([w * (a - b) for w, a, b in zip(wy, u, row["u"])], [cs.facey[j]] * s)
            for i in range(s):
                k = i * s + j
                chosen, bottom = fresh(i, j, gz, now["up"][i])
                flux = wz[i] * (u[i] - chosen)
                prev_x = flux_x[i - 1] if i else turn(flux_x[s - 1], 1)
                value = (flux_x[i] - prev_x) + (flux_y[i] - before[i]) + (flux - now["fz"][i])
                stores.append((f_ref, (at(up, k), slice(None)), chosen))
                stores.append((p_ref, (at(up, k), slice(None)), bottom))
                stores.append((y_ref, (at(z, k), slice(None)), value))
                stores.append((case.fz, k, flux))
            before = flux_y
        flush()
        for h in HALVES:
            send(h, z).start()
        return 0

    lax.fori_loop(0, lv.edz, body, 0)
    pairs = jnp.zeros((2 * LANES, LANES), F32)
    for start in range(0, padded_rows(lv), CHUNK):
        part = slice(start, start + CHUNK)
        left = jnp.concatenate([f_ref[part, :].T, p_ref[part, :].T], axis=0)
        right = y_ref[part, :]
        left_high, right_high = left.astype(BF16), right.astype(BF16)
        left_low = (left - left_high.astype(F32)).astype(BF16)
        right_low = (right - right_high.astype(F32)).astype(BF16)
        for a, b in ((left_high, right_high), (left_low, right_high), (left_high, right_low)):
            pairs = pairs + jnp.dot(a, b, preferred_element_type=F32)
    shape = (LANES, LANES)
    row, lane = sub_iota(shape), lane_iota(shape)
    sums = [jnp.where(row == (lane + 32 * k) % LANES, pairs[:LANES], 0.0) for k in range(3)]
    sums.append(jnp.where(row % 32 == lane % 32, pairs[LANES:], 0.0))
    out = []
    for value in sums:
        value = tree([value[r : r + SUBS] for r in range(0, LANES, SUBS)])
        out.append(value)
    return out


GROUPS = {FINE: 1, TWIN: 4}


def place_kernel(center, out_ref):
    nx = center.shape[1]
    out_ref[...] = jnp.ones(out_ref.shape, F32)
    for m in range(3):
        off = m * (nx + 2 * MX) + MX
        out_ref[off : off + nx, :] = center[m]


def solve_kernel(
    inside, x_low, x_high, y_low, y_high,
    phi, message,
    flat, sides, rows, pairs, twin_rows, *refs,
):
    lanes = inside.shape[1]
    rim = y_low.shape[2]
    wide = y_low.shape[1]
    for m in range(3):
        off = m * wide
        flat[off : off + MX, :] = x_low[m]
        flat[off + wide - MX : off + wide, :] = x_high[m]
        sides[off : off + wide, :rim] = y_low[m]
        sides[off : off + wide, rim:] = y_high[m]
    sides[3 * wide :, :] = jnp.ones((LANES - 3 * wide, sides.shape[1]), F32)
    row = sub_iota((LANES, LANES))
    place = row % wide
    outer = (row < 3 * wide) & ((place < MX) | (place >= wide - MX))
    for t in range(rim // LANES):
        low, high = slice(t * LANES, (t + 1) * LANES), slice(rim + t * LANES, rim + (t + 1) * LANES)
        rows[low, :] = sides[:, low].T
        rows[lanes + rim + t * LANES : lanes + rim + (t + 1) * LANES, :] = sides[:, high].T
    for t in range(lanes // LANES):
        part = slice(t * LANES, (t + 1) * LANES)
        rows[rim + t * LANES : rim + (t + 1) * LANES, :] = jnp.where(outer, flat[:, part], inside[:, part]).T

    nz = EZ * ELZ
    twin_y = rows.shape[0] // nz // 2
    for y in range(twin_y):
        both = rows[2 * y * nz : (2 * y + 1) * nz, :] + rows[(2 * y + 1) * nz : (2 * y + 2) * nz, :]
        both = both + turn(both, -1)
        at = y * nz
        pairs[at : at + nz, :] = both
        twin_rows[at : at + 8, :] = jnp.broadcast_to(0.25 * both[0:1], (8, LANES))
        twin_rows[at + 8 + nz // 2 : at + nz, :] = jnp.broadcast_to(0.25 * both[nz - 1 : nz], (8, LANES))
    for y in range(twin_y):
        at = y * nz
        middle = pairs[pl.ds(at, nz // 2, stride=2), :] + pairs[pl.ds(at + 1, nz // 2, stride=2), :]
        twin_rows[at + 8 : at + 8 + nz // 2, :] = 0.125 * middle
    twin_rows[twin_y * nz :, :] = jnp.ones((twin_rows.shape[0] - twin_y * nz, LANES), F32)

    refs = list(refs)

    def take(count):
        got = refs[:count]
        del refs[:count]
        return got

    cases = []
    for lv, source in zip(LEVELS, (rows, twin_rows)):
        (k_ref,) = take(1)
        high_refs, low_refs, w_refs = take(3), take(3), take(3)
        for z in range(lv.levels + 1):
            cell = min(max(z - 1, 0), nz - 1) if lv is FINE else min(z, lv.levels - 1) + 7
            for i in range(lv.seg):
                for c in range(COLUMNS):
                    start = (lv.edge * c + i) * nz + cell
                    k_ref[z, i, :, c * LANES : (c + 1) * LANES] = source[pl.ds(start, SUBS, stride=lv.seg * nz), :]
        spread_weights(lv, k_ref, high_refs, low_refs, w_refs)
        case = Case(lv, w_refs, take(5), take(1))
        for k in range(2 * lv.tiles):
            case.d[0][lv.inner, k] = jnp.zeros((SUBS, LANES), F32)
            case.r[lv.inner, k] = jnp.zeros((SUBS, LANES), F32)
        cases.append(case)

    def both_levels(work):
        sums = [work(n, case, GROUPS[case.lv]) for n, case in enumerate(cases)]
        return [[problem_sum(v) for v in part] for part in sums]

    rr = both_levels(lambda n, case, group: start_residual(case, group))
    alphas = [[[], []] for _ in LEVELS]
    betas = [None] * len(LEVELS)
    for step in range(3):
        dots = both_levels(lambda n, case, group: apply(case, step, betas[n]))
        now = [[a / b for a, b in zip(rr[n], dots[n])] for n in range(len(LEVELS))]
        for n in range(len(LEVELS)):
            for h in HALVES:
                alphas[n][h].append(now[n][h])
        if step < 2:
            new = both_levels(lambda n, case, group: reduce_residual(case, group, step, now[n]))
            betas = [[a / b for a, b in zip(new[n], rr[n])] for n in range(len(LEVELS))]
            rr = new

    results = [take(3), take(3)]
    sems = take(2)

    def send(n, h, z):
        lv = LEVELS[n]
        size = plane_rows(lv)
        first = sum(2 * field_rows(v) for v in LEVELS[:n]) + h * field_rows(lv)
        return pltpu.make_async_copy(
            results[n][h].at[pl.ds(pl.multiple_of(z * size, SUBS), size)],
            phi.at[pl.ds(pl.multiple_of(first + z * size, SUBS), size)],
            sems[n].at[h * lv.edz + z],
        )

    totals = both_levels(
        lambda n, case, group: finish(case, alphas[n], results[n], functools.partial(send, n))
    )
    _, element, _, slot = lane_parts()
    packed = []
    for level in totals:
        parts = [v + xor_lane(v, 16) for v in level[:3]]
        parts.append(jnp.where(element == 0, level[3], turn(level[3], 16)))
        packed.append(
            jnp.where(slot == 0, parts[0], jnp.where(slot == 1, parts[1], jnp.where(slot == 2, parts[2], parts[3])))
        )
    row = jnp.where(element == 0, packed[0], packed[1])
    for r in range(0, message.shape[0], SUBS):
        message[r : r + SUBS, :] = row
    for n, lv in enumerate(LEVELS):
        for h in HALVES:
            for z in range(lv.edz):
                send(n, h, z).wait()


def coarse_nodes(gathered, gy_count, me):
    total_rows = gathered.shape[0]
    shape = gathered.shape
    lane = lane_iota(shape)
    row = sub_iota(shape)
    corner = lane // 32
    column = lane // 8 % 2
    last = row % gy_count == gy_count - 1
    start = row % gy_count == 0
    one = gathered
    two = turn(gathered, -1)
    four = turn(gathered, -2)
    rhs = turn(gathered, -3)
    two_back = turn(two, 32)

    def next_x(u):
        return turn(u, -gy_count, 0)

    def prev_x(u):
        return turn(u, gy_count, 0)

    def next_y(u):
        ahead = jnp.where(last, turn(u, gy_count - 1, 0), turn(u, -1, 0))
        return jnp.where(column == 0, turn(u, -8), turn(ahead, 8))

    def prev_y(u):
        behind = jnp.where(start, turn(u, 1 - gy_count, 0), turn(u, 1, 0))
        return jnp.where(column == 1, turn(u, 8), turn(behind, -8))

    def by_corner(a, b, c, d):
        return jnp.where(corner == 0, a, jnp.where(corner == 1, b, jnp.where(corner == 2, c, d)))

    def corners(u):
        ux = next_x(u)
        return by_corner(u, next_y(u), ux, next_y(ux))

    def assemble(v):
        vx = prev_x(v)
        w = by_corner(v, prev_y(v), vx, prev_y(vx))
        w = w + turn(w, 64)
        return w + turn(w, 32)

    def operate(u):
        c = corners(u)
        return assemble(one * c + two * turn(c, -32) + two_back * turn(c, 32) + four * turn(c, 64))

    def total(a, b):
        v = a * b
        v = tree([v[r : r + SUBS] for r in range(0, total_rows, SUBS)])
        for shift in (4, 2, 1):
            v = v + turn(v, shift, 0)
        v = v + xor_lane(v, 8)
        return v[0:1]

    residual = -assemble(rhs)
    direction = residual
    update = jnp.zeros_like(residual)
    now = total(residual, residual)
    for step in range(2):
        image = operate(direction)
        alpha = now / total(direction, image)
        update = update + alpha * direction
        if step == 0:
            residual = residual - alpha * image
            new = total(residual, residual)
            direction = residual + new / now * direction
            now = new
    mine = jnp.where(row == me, corners(update), 0.0)
    mine = jnp.sum(mine, axis=0, keepdims=True)
    return jnp.broadcast_to(mine, (SUBS, LANES))


def turn_kernel(phi, out_ref):
    start_row, number = 0, 0
    for lv in LEVELS:
        s = lv.seg
        nz = EZ * lv.edz
        per = LANES // nz
        for i in range(s):
            for t in range(turned_tiles(lv)):
                parts = []
                for n in range(per):
                    yo, j = divmod(lv.mx + t * per + n, s)
                    start = start_row + (i * s + j) * SUBS + yo
                    chosen, bottom = [
                        phi[pl.ds(start + h * field_rows(lv), lv.edz, stride=plane_rows(lv)), :] for h in HALVES
                    ]
                    lower = lane_iota(chosen.shape) // 16 % 2 == 0
                    parts.append(jnp.where(lower, chosen, turn(bottom, 16)))
                    parts.append(jnp.where(lower, turn(chosen, -16), 0.0))
                out_ref[number] = jnp.concatenate(parts, axis=0).T
                number += 1
        start_row += 2 * field_rows(lv)


def pressure_kernel(gy_count, me_ref, gathered, turned, fine_out, twin_out, fine_all, twin_all):
    mine = coarse_nodes(gathered[...], gy_count, me_ref[0])
    first = 0
    for n, (lv, out_ref, all_ref) in enumerate(((FINE, fine_out, fine_all), (TWIN, twin_out, twin_all))):
        s = lv.seg
        tiles = turned_tiles(lv)
        nodes = {}
        for c in range(COLUMNS):
            for p in range(4):
                at = p * 32 + n * 16 + c * 8
                nodes[p, c] = jnp.broadcast_to(mine[:, at : at + 1], (SUBS, LANES))
        for c in range(COLUMNS):
            for t in range(tiles):
                at = (c * tiles + t) * LANES
                for i in range(s):
                    def part(group):
                        return turned[first + i * tiles + t, group * 16 + c * 8 : group * 16 + c * 8 + 8, :]

                    value = tree([part(2 * p) * nodes[p, c] + part(2 * p + 1) for p in range(4)])
                    all_ref[c * tiles + t, pl.ds(i, SUBS, stride=s), :] = value
                out_ref[:, at : at + LANES] = all_ref[c * tiles + t, lv.mx : lv.mx + lv.edge, :]
        first += s * tiles


def vmem(shape, dtype=F32):
    return pltpu.VMEM(shape, dtype)


def shards(permeability):
    nz = EZ * ELZ
    rows = permeability.shape[1]
    lanes = permeability.shape[2]
    assert rows == EL and lanes == COLUMNS * EL * nz
    rim = MX * nz
    gx, gy = lax.axis_size("gx"), lax.axis_size("gy")

    def sent(value, axis, shift):
        count = lax.axis_size(axis)
        return lax.ppermute(value, axis, [(i, (i + shift) % count) for i in range(count)])

    x_low = sent(permeability[:, rows - MX :], "gx", 1)
    x_high = sent(permeability[:, :MX], "gx", -1)

    def strip(part):
        return jnp.concatenate([x_low[:, :, part], permeability[:, :, part], x_high[:, :, part]], axis=1)

    y_low = sent(strip(slice(lanes - rim, lanes)), "gy", 1)
    y_high = sent(strip(slice(0, rim)), "gy", -1)
    halos = [x_low, x_high, y_low, y_high]
    flat_lanes = lanes + 2 * rim
    scratch = [
        vmem((LANES, lanes)),
        vmem((LANES, 2 * rim)),
        vmem((flat_lanes, LANES)),
        vmem((flat_lanes // 2, LANES)),
        vmem((SUBS * (TWIN.seg + 2) * nz, LANES)),
    ]
    for lv in LEVELS:
        scratch.append(vmem((lv.levels + 1, lv.seg, SUBS, 2 * LANES)))
        scratch += [vmem((lv.planes * lv.seg // 2, 2 * SUBS, 2 * LANES), BF16)] * 6
        scratch += [vmem((lv.seg, lv.planes * lv.seg, SUBS, LANES))] * 3
        scratch += [vmem((lv.inner + 1, 2 * lv.tiles, SUBS, LANES))] * 5
        scratch.append(vmem((2 * lv.tiles, SUBS, LANES)))
    for lv in LEVELS:
        scratch += [vmem((padded_rows(lv), LANES))] * 3
    scratch += [pltpu.SemaphoreType.DMA((2 * lv.edz,)) for lv in LEVELS]
    full = pl.BlockSpec(memory_space=pltpu.VMEM)
    inside = pl.pallas_call(
        place_kernel,
        out_shape=vmem((LANES, lanes)),
        in_specs=[full],
        out_specs=full,
        compiler_params=pltpu.CompilerParams(vmem_limit_bytes=8 * 1024 * 1024),
        cost_estimate=pl.CostEstimate(flops=1000000, bytes_accessed=4000000, transcendentals=0),
        name="place",
    )(permeability)
    phi, message = pl.pallas_call(
        solve_kernel,
        out_shape=[
            pltpu.HBM((sum(2 * field_rows(lv) for lv in LEVELS), LANES), F32),
            jax.ShapeDtypeStruct((gx * gy, LANES), F32),
        ],
        in_specs=[full] * 5,
        out_specs=[pl.BlockSpec(memory_space=pltpu.HBM), full],
        scratch_shapes=scratch,
        compiler_params=pltpu.CompilerParams(vmem_limit_bytes=50 * 1024 * 1024),
        name="solve",
    )(inside, *halos)
    gathered = lax.all_to_all(message, ("gx", "gy"), 0, 0, tiled=True)
    tiles = sum(lv.seg * turned_tiles(lv) for lv in LEVELS)
    turned = pl.pallas_call(
        turn_kernel,
        out_shape=vmem((tiles, LANES, LANES)),
        in_specs=[full],
        out_specs=full,
        compiler_params=pltpu.CompilerParams(vmem_limit_bytes=16 * 1024 * 1024),
        cost_estimate=pl.CostEstimate(flops=4000000, bytes_accessed=8000000, transcendentals=0),
        name="turned",
    )(phi)
    me = (lax.axis_index("gx") * gy + lax.axis_index("gy")).astype(jnp.int32).reshape(1)
    return tuple(
        pl.pallas_call(
            functools.partial(pressure_kernel, gy),
            out_shape=[
                jax.ShapeDtypeStruct((lv.edge, COLUMNS * lv.edge * EZ * lv.edz), F32) for lv in LEVELS
            ],
            in_specs=[pl.BlockSpec(memory_space=pltpu.SMEM), full, full],
            out_specs=[full] * 2,
            scratch_shapes=[vmem((COLUMNS * turned_tiles(lv), SUBS * lv.seg, LANES)) for lv in LEVELS],
            compiler_params=pltpu.CompilerParams(vmem_limit_bytes=16 * 1024 * 1024),
            name="pressure",
        )(me, gathered, turned)
    )


def solution(mesh):
    return jax.shard_map(
        shards,
        mesh=mesh,
        in_specs=(P(None, "gx", "gy"),),
        out_specs=(P("gx", "gy"), P("gx", "gy")),
        check_vma=False,
    )
```

```python
import functools
import typing

import jax
import jax.numpy as jnp
from jax import lax
from jax.experimental import pallas as pl
from jax.experimental.pallas import tpu as pltpu
from jax.sharding import PartitionSpec as P

EL = 32
ELZ = 16
MX = 4
MZ = 2
EZ = 2
LANES = 128
SUBS = 8
COLUMNS = 2
F32 = jnp.float32
BF16 = jnp.bfloat16


class Level(typing.NamedTuple):
    edge: int
    edz: int
    mx: int
    mz: int
    spacing: float
    step: int

    @property
    def width(self):
        return self.edge + 2 * self.mx

    @property
    def inner(self):
        return self.edz + 2 * self.mz - 2

    @property
    def seg(self):
        return -(-self.width // SUBS)

    @property
    def tiles(self):
        return self.seg * self.seg

    @property
    def levels(self):
        return EZ * self.edz + 2

    @property
    def planes(self):
        return -(-(self.inner + 1) // 2) * 2


FINE = Level(EL, ELZ, MX, MZ, 1.0, 1)
TWIN = Level(EL // 2, ELZ // 2, MX // 2, MZ // 2, 2.0, 2)
LEVELS = (FINE, TWIN)


def lane_iota(shape=(SUBS, LANES)):
    return lax.broadcasted_iota(jnp.int32, shape, len(shape) - 1)


def sub_iota(shape=(SUBS, LANES)):
    return lax.broadcasted_iota(jnp.int32, shape, len(shape) - 2)


def turn(value, shift, axis=1):
    return pltpu.roll(value, shift % value.shape[axis], axis)


def lane_parts():
    lane = lane_iota()
    return lane // 32, lane // 16 % 2, lane // 8 % 2, lane % 8


class Consts:
    def __init__(self, lv):
        corner, _, _, xo = lane_parts()
        yo = sub_iota()
        ax, ay = corner // 2, corner % 2
        self.lv = lv
        s = lv.seg
        self.fx, self.fy = [], []
        self.inx, self.iny, self.facex, self.facey = [], [], [], []
        for i in range(s):
            x = xo * s + i
            y = yo * s + i
            px = (x.astype(F32) - lv.mx + 0.5) / lv.edge
            py = (y.astype(F32) - lv.mx + 0.5) / lv.edge
            self.fx.append(jnp.where(ax == 1, px, 1.0 - px))
            self.fy.append(jnp.where(ay == 1, py, 1.0 - py))
            xs = [s * o + i for o in range(SUBS)]

            def ranged(value, low, high):
                if all(low <= v <= high for v in xs):
                    return None
                return ((value >= low) & (value <= high)).astype(F32)

            self.inx.append((ranged(x, 1, lv.width - 2), ranged(x, lv.mx, lv.mx + lv.edge - 1)))
            self.iny.append((ranged(y, 1, lv.width - 2), ranged(y, lv.mx, lv.mx + lv.edge - 1)))
            cut = (lv.mx - 1, lv.mx + lv.edge - 1)
            self.facex.append(((x != cut[0]) & (x != cut[1])).astype(F32) if any(v in cut for v in xs) else None)
            self.facey.append(((y != cut[0]) & (y != cut[1])).astype(F32) if any(v in cut for v in xs) else None)
        sx = jnp.where(ax == 1, -1.0 / lv.edge, 1.0 / lv.edge).astype(F32)
        sy = jnp.where(ay == 1, -1.0 / lv.edge, 1.0 / lv.edge).astype(F32)
        self.along_x = [sx * f for f in self.fy]
        self.along_y = [sy * f for f in self.fx]

    def fz(self, plane):
        place = (jnp.asarray(plane, jnp.int32).astype(F32) - self.lv.mz + 0.5) / self.lv.edz
        return 1.0 - place, place

    def masked(self, value, i, j, kind):
        for table, index in ((self.inx, i), (self.iny, j)):
            factor = table[index][kind]
            if factor is not None:
                value = value * factor
        return value


def tree(values):
    values = list(values)
    while len(values) > 1:
        values = [a + b for a, b in zip(values[::2], values[1::2])] + (
            [values[-1]] if len(values) % 2 else []
        )
    return values[0]


def xor_lane(value, bit):
    return jnp.where(lane_iota(value.shape) // bit % 2 == 1, turn(value, bit), turn(value, -bit))


def problem_sum(value):
    for shift in (4, 2, 1):
        value = value + turn(value, shift, 0)
    for bit in (1, 2, 4):
        value = value + xor_lane(value, bit)
    return value


def spread_weights(lv, k_ref, high_refs, low_refs, w_refs):
    s = lv.seg
    wide = (SUBS, LANES)
    pos = lane_iota(wide)
    yo = sub_iota(wide)
    first = pos < 40
    third = pos >= 80
    second = (pos >= 40) & (pos < 80)
    edge_x = first & (pos >= (lv.width - 1) * lv.step)

    def one(z, i, c):
        part = slice(c * LANES, (c + 1) * LANES)
        k = k_ref[z, i, :, part]
        nbx = turn(k, -lv.step)
        nby = k_ref[z, i + 1, :, part] if i < s - 1 else turn(k_ref[z, 0, :, part], -1, 0)
        nbz = k_ref[z + 1, i, :, part]
        nb = jnp.where(first, nbx, jnp.where(second, nby, nbz))
        w = (2.0 * lv.spacing) * k * nb / (k + nb)
        bad = edge_x | (second & (yo * s + i >= lv.width - 1))
        return jnp.where(bad, 0.0, w)

    def planes(t, _):
        units = [(2 * t + n, i) for n in range(2) for i in range(s)]
        for e in range(EZ):
            made = []
            for plane, i in units:
                z = jnp.clip(e * lv.edz + plane + 1 - lv.mz, 0, lv.levels - 1)
                w0, w1 = one(z, i, 0), one(z, i, 1)
                near, wrap = turn(w1, 40), turn(w1, 48)
                made.append((jnp.where(first, w0, near), jnp.where(third, near, w0), jnp.where(third, w0, wrap)))
            for p in range(s):
                for m in range(3):
                    both = jnp.concatenate([made[2 * p][m], made[2 * p + 1][m]], axis=0)
                    high = both.astype(BF16)
                    part = slice(e * LANES, (e + 1) * LANES)
                    high_refs[m][t * s + p, :, part] = high
                    low_refs[m][t * s + p, :, part] = (both - high.astype(F32)).astype(BF16)
        return 0

    lax.fori_loop(0, lv.planes // 2, planes, 0)
    rows = lv.planes * s * SUBS
    row = lax.broadcasted_iota(jnp.int32, (2 * LANES, 2 * LANES), 0)
    lane = lax.broadcasted_iota(jnp.int32, (1, 2 * LANES), 1)
    upper = lane // LANES
    for q in range(-(-s // 2)):
        x = lane % 8 * s + 2 * q + upper
        valid = (x < lv.width) & (2 * q + upper < s)
        for m in range(3):
            segment = jnp.where(lane // 8 % 2 == 0, m, (m + 1) % 3)
            source = jnp.where(valid, lane // 16 % 2 * LANES + segment * 40 + lv.step * x, -1)
            pick = (row == source).astype(F32).astype(BF16)
            out = jnp.dot(high_refs[m][...].reshape(rows, 2 * LANES), pick, preferred_element_type=F32)
            out = out + jnp.dot(low_refs[m][...].reshape(rows, 2 * LANES), pick, preferred_element_type=F32)
            for half in range(min(2, s - 2 * q)):
                part = out[:, half * LANES : (half + 1) * LANES]
                w_refs[m][2 * q + half] = part.reshape(lv.planes * s, SUBS, LANES)


class Case:
    def __init__(self, lv, w_refs, fields, planes):
        self.lv, self.cs, self.w_refs = lv, Consts(lv), w_refs
        self.d, self.q, self.r = fields[:3], fields[3], fields[4]
        (self.fz,) = planes

    def weights(self, plane):
        s = self.lv.seg
        return lambda m, i, j: self.w_refs[m][i, plane * s + j]


HALVES = (0, 1)
CHUNK = 640


def plane_rows(lv):
    return lv.tiles * SUBS


def field_rows(lv):
    return lv.edz * plane_rows(lv)


def padded_rows(lv):
    return -(-field_rows(lv) // CHUNK) * CHUNK


def turned_tiles(lv):
    return lv.edge * EZ * lv.edz // LANES


def together(works):
    zero = jnp.zeros((SUBS, LANES), F32)
    sums = [tuple(zero for _ in range(number)) for _, number, _, _ in works]
    done = 0
    for stop in sorted({count for count, _, _, _ in works}):
        active = [n for n, work in enumerate(works) if work[0] > done]

        def body(z, carry, active=active):
            return tuple(
                tuple(a + b for a, b in zip(old, works[n][2](z))) for n, old in zip(active, carry)
            )

        got = lax.fori_loop(done, stop, body, tuple(sums[n] for n in active))
        for n, part in zip(active, got):
            sums[n] = part
        done = stop
    return [work[3](list(part)) for work, part in zip(works, sums)]


def start_residual(case):
    lv, cs, s = case.lv, case.cs, case.lv.seg

    def step(z0):
        total = [[], []]
        for z in [z0]:
            get, below = case.weights(z + 1), case.weights(z)
            gz = cs.fz(z + 1)
            last = [get(1, i, s - 1) * cs.along_y[i] for i in range(s)]
            before = [turn(v, 1, 0) for v in last]
            for j in range(s):
                flux_y = last if j == s - 1 else [get(1, i, j) * cs.along_y[i] for i in range(s)]
                flux_x = [get(0, i, j) * cs.along_x[j] for i in range(s)]
                squares = [[], []]
                for i in range(s):
                    k = i * s + j
                    prev_x = flux_x[i - 1] if i else turn(flux_x[s - 1], 1)
                    flat = (prev_x - flux_x[i]) + (before[i] - flux_y[i])
                    flat = cs.masked(flat, i, j, 0)
                    tall = (cs.fx[i] * cs.fy[j]) * (1.0 / lv.edz) * (below(2, i, j) - get(2, i, j))
                    tall = cs.masked(tall, i, j, 0)
                    for h, value in enumerate((flat * gz[0] + tall, flat * gz[1] - tall)):
                        case.d[0][z, h * lv.tiles + k] = value
                        squares[h].append(value * value)
                for h in HALVES:
                    total[h].append(tree(squares[h]))
                before = flux_y
        return [tree(t) for t in total]

    return lv.inner, 2, step, lambda sums: sums


def row_jumps(u, s, j):
    jump_x = [u[i * s + j] - (u[(i + 1) * s + j] if i < s - 1 else turn(u[j], -1)) for i in range(s)]
    jump_y = [u[i * s + j] - (u[i * s + j + 1] if j < s - 1 else turn(u[i * s], -1, 0)) for i in range(s)]
    return jump_x, jump_y


def apply(case, number, betas):
    lv, cs, s = case.lv, case.cs, case.lv.seg
    keep = number < 2
    n = lv.tiles

    def fresh(z, h, k):
        at = h * n + k
        if number == 0:
            return case.d[0][z, at]
        value = case.r[z, at] + betas[h] * case.d[number - 1][z, at]
        case.d[number][z, at] = value
        return value

    firsts = []
    get = case.weights(0)
    for h in HALVES:
        terms = []
        for k in range(n):
            value = fresh(0, h, k)
            flux = -get(2, k // s, k % s) * value
            if keep:
                case.fz[h * n + k] = flux
            else:
                terms.append(-flux * value)
        firsts.append(tree(terms) if terms else 0.0)

    def step(z0):
        total = [[], []]
        u = [[case.d[number][z0, h * n + k] for k in range(n)] for h in HALVES]
        flux_z = [[case.fz[h * n + k] for k in range(n)] for h in HALVES] if keep else None
        for z in [z0]:
            get = case.weights(z + 1)
            after = [[None] * n for _ in HALVES]
            if keep:
                wy = [get(1, i, s - 1) for i in range(s)]
                last = [[wy[i] * (u[h][i * s + s - 1] - turn(u[h][i * s], -1, 0)) for i in range(s)] for h in HALVES]
                before = [[turn(v, 1, 0) for v in last[h]] for h in HALVES]
            for j in range(s):
                wx = [get(0, i, j) for i in range(s)]
                wy = [get(1, i, j) for i in range(s)]
                wz = [get(2, i, j) for i in range(s)]
                for h in HALVES:
                    jump_x, jump_y = row_jumps(u[h], s, j)
                    flux_x = [w * v for w, v in zip(wx, jump_x)]
                    flux_y = last[h] if keep and j == s - 1 else [w * v for w, v in zip(wy, jump_y)]
                    terms = []
                    for i in range(s):
                        k = i * s + j
                        after[h][k] = fresh(z + 1, h, k)
                        jump = u[h][k] - after[h][k]
                        flux = wz[i] * jump
                        if keep:
                            prev_x = flux_x[i - 1] if i else turn(flux_x[s - 1], 1)
                            value = (flux_x[i] - prev_x) + (flux_y[i] - before[h][i]) + (flux - flux_z[h][k])
                            flux_z[h][k] = flux
                            value = cs.masked(value, i, j, 0)
                            case.q[z, h * n + k] = value
                            terms.append(u[h][k] * value)
                        else:
                            terms.append((flux * jump + flux_x[i] * jump_x[i]) + flux_y[i] * jump_y[i])
                    total[h].append(tree(terms))
                    if keep:
                        before[h] = flux_y
            u = after
        if keep:
            for h in HALVES:
                for k in range(n):
                    case.fz[h * n + k] = flux_z[h][k]
        return [tree(t) for t in total]

    return lv.inner, 2, step, lambda sums: [a + b for a, b in zip(sums, firsts)]


def reduce_residual(case, number, alphas):
    lv = case.lv

    def step(z0):
        total = [[], []]
        source = case.d[0] if number == 0 else case.r
        for z in [z0]:
            for h in HALVES:
                squares = []
                for k in range(lv.tiles):
                    at = h * lv.tiles + k
                    value = source[z, at] - alphas[h] * case.q[z, at]
                    case.r[z, at] = value
                    squares.append(value * value)
                total[h].append(tree(squares))
        return [tree(t) for t in total]

    return lv.inner, 2, step, lambda sums: sums


def finish(case, alphas, refs, send):
    lv, cs, s = case.lv, case.cs, case.lv.seg
    n = lv.tiles
    f_ref, p_ref, y_ref = refs
    lower = lane_parts()[1] == 0

    def at(z, k):
        return pl.ds(pl.multiple_of(z * plane_rows(lv) + k * SUBS, SUBS), SUBS)

    def fresh(z, i, j, gz):
        k = i * s + j
        inner = z + lv.mz - 1
        both = cs.fx[i] * cs.fy[j]
        values = []
        for h in HALVES:
            value = both * gz[h]
            for alpha, d_ref in zip(alphas[h], case.d):
                value = value + alpha * d_ref[inner, h * n + k]
            values.append(cs.masked(value, i, j, 1))
        chosen = jnp.where(lower, values[1], values[0])
        f_ref[at(z, k), :] = chosen
        p_ref[at(z, k), :] = values[0]
        return chosen

    gz = cs.fz(lv.mz)
    for i in range(s):
        for j in range(s):
            fresh(0, i, j, gz)
            case.fz[i * s + j] = jnp.zeros((SUBS, LANES), F32)
    rest = padded_rows(lv) - field_rows(lv)
    if rest:
        for ref in refs:
            ref[field_rows(lv) :, :] = jnp.zeros((rest, LANES), F32)

    def cut(values, table):
        return [v if f is None else v * f for v, f in zip(values, table)]

    def step(z0):
        u = [f_ref[at(z0, k), :] for k in range(n)]
        flux_z = [case.fz[k] for k in range(n)]
        for z in [z0]:
            get = case.weights(z + lv.mz)
            up = jnp.minimum(z + 1, lv.edz - 1)
            gz = cs.fz(up + lv.mz)
            after = [None] * n
            last = [get(1, i, s - 1) * (u[i * s + s - 1] - turn(u[i * s], -1, 0)) for i in range(s)]
            last = cut(last, [cs.facey[s - 1]] * s)
            before = [turn(v, 1, 0) for v in last]
            for j in range(s):
                jump_x, jump_y = row_jumps(u, s, j)
                flux_x = cut([get(0, i, j) * jump_x[i] for i in range(s)], cs.facex)
                flux_y = last
                if j < s - 1:
                    flux_y = cut([get(1, i, j) * jump_y[i] for i in range(s)], [cs.facey[j]] * s)
                for i in range(s):
                    k = i * s + j
                    after[k] = fresh(up, i, j, gz)
                    flux = get(2, i, j) * (u[k] - after[k])
                    prev_x = flux_x[i - 1] if i else turn(flux_x[s - 1], 1)
                    y_ref[at(z, k), :] = (flux_x[i] - prev_x) + (flux_y[i] - before[i]) + (flux - flux_z[k])
                    flux_z[k] = flux
                before = flux_y
            u = after
        for k in range(n):
            case.fz[k] = flux_z[k]
        for z in [z0]:
            for h in HALVES:
                send(h, z).start()
        return ()

    return lv.edz, 0, step, lambda _: corner_pairs(lv, refs)


def corner_pairs(lv, refs):
    f_ref, p_ref, y_ref = refs
    pairs = jnp.zeros((2 * LANES, LANES), F32)
    for start in range(0, padded_rows(lv), CHUNK):
        part = slice(start, start + CHUNK)
        left = jnp.concatenate([f_ref[part, :].T, p_ref[part, :].T], axis=0)
        right = y_ref[part, :]
        left_high, right_high = left.astype(BF16), right.astype(BF16)
        left_low = (left - left_high.astype(F32)).astype(BF16)
        right_low = (right - right_high.astype(F32)).astype(BF16)
        for a, b in ((left_high, right_high), (left_low, right_high), (left_high, right_low)):
            pairs = pairs + jnp.dot(a, b, preferred_element_type=F32)
    shape = (LANES, LANES)
    row, lane = sub_iota(shape), lane_iota(shape)
    sums = [jnp.where(row == (lane + 32 * k) % LANES, pairs[:LANES], 0.0) for k in range(3)]
    sums.append(jnp.where(row % 32 == lane % 32, pairs[LANES:], 0.0))
    out = []
    for value in sums:
        value = tree([value[r : r + SUBS] for r in range(0, LANES, SUBS)])
        out.append(value)
    return out


def place_kernel(center, out_ref):
    nx = center.shape[1]
    out_ref[...] = jnp.ones(out_ref.shape, F32)
    for m in range(3):
        off = m * (nx + 2 * MX) + MX
        out_ref[off : off + nx, :] = center[m]


def solve_kernel(
    inside, x_low, x_high, y_low, y_high,
    phi, message,
    flat, sides, rows, pairs, twin_rows, *refs,
):
    lanes = inside.shape[1]
    rim = y_low.shape[2]
    wide = y_low.shape[1]
    for m in range(3):
        off = m * wide
        flat[off : off + MX, :] = x_low[m]
        flat[off + wide - MX : off + wide, :] = x_high[m]
        sides[off : off + wide, :rim] = y_low[m]
        sides[off : off + wide, rim:] = y_high[m]
    sides[3 * wide :, :] = jnp.ones((LANES - 3 * wide, sides.shape[1]), F32)
    row = sub_iota((LANES, LANES))
    place = row % wide
    outer = (row < 3 * wide) & ((place < MX) | (place >= wide - MX))
    for t in range(rim // LANES):
        low, high = slice(t * LANES, (t + 1) * LANES), slice(rim + t * LANES, rim + (t + 1) * LANES)
        rows[low, :] = sides[:, low].T
        rows[lanes + rim + t * LANES : lanes + rim + (t + 1) * LANES, :] = sides[:, high].T
    for t in range(lanes // LANES):
        part = slice(t * LANES, (t + 1) * LANES)
        rows[rim + t * LANES : rim + (t + 1) * LANES, :] = jnp.where(outer, flat[:, part], inside[:, part]).T

    nz = EZ * ELZ
    twin_y = rows.shape[0] // nz // 2
    for y in range(twin_y):
        both = rows[2 * y * nz : (2 * y + 1) * nz, :] + rows[(2 * y + 1) * nz : (2 * y + 2) * nz, :]
        both = both + turn(both, -1)
        at = y * nz
        pairs[at : at + nz, :] = both
        twin_rows[at : at + 8, :] = jnp.broadcast_to(0.25 * both[0:1], (8, LANES))
        twin_rows[at + 8 + nz // 2 : at + nz, :] = jnp.broadcast_to(0.25 * both[nz - 1 : nz], (8, LANES))
    for y in range(twin_y):
        at = y * nz
        middle = pairs[pl.ds(at, nz // 2, stride=2), :] + pairs[pl.ds(at + 1, nz // 2, stride=2), :]
        twin_rows[at + 8 : at + 8 + nz // 2, :] = 0.125 * middle
    twin_rows[twin_y * nz :, :] = jnp.ones((twin_rows.shape[0] - twin_y * nz, LANES), F32)

    refs = list(refs)

    def take(count):
        got = refs[:count]
        del refs[:count]
        return got

    cases = []
    for lv, source in zip(LEVELS, (rows, twin_rows)):
        (k_ref,) = take(1)
        high_refs, low_refs, w_refs = take(3), take(3), take(3)
        for z in range(lv.levels + 1):
            cell = min(max(z - 1, 0), nz - 1) if lv is FINE else min(z, lv.levels - 1) + 7
            for i in range(lv.seg):
                for c in range(COLUMNS):
                    start = (lv.edge * c + i) * nz + cell
                    k_ref[z, i, :, c * LANES : (c + 1) * LANES] = source[pl.ds(start, SUBS, stride=lv.seg * nz), :]
        spread_weights(lv, k_ref, high_refs, low_refs, w_refs)
        case = Case(lv, w_refs, take(5), take(1))
        for k in range(2 * lv.tiles):
            case.d[0][lv.inner, k] = jnp.zeros((SUBS, LANES), F32)
            case.r[lv.inner, k] = jnp.zeros((SUBS, LANES), F32)
        cases.append(case)

    def both_levels(work):
        return [[problem_sum(v) for v in part] for part in together([work(n, case) for n, case in enumerate(cases)])]

    rr = both_levels(lambda n, case: start_residual(case))
    alphas = [[[], []] for _ in LEVELS]
    betas = [None] * len(LEVELS)
    for step in range(3):
        dots = both_levels(lambda n, case: apply(case, step, betas[n]))
        now = [[a / b for a, b in zip(rr[n], dots[n])] for n in range(len(LEVELS))]
        for n in range(len(LEVELS)):
            for h in HALVES:
                alphas[n][h].append(now[n][h])
        if step < 2:
            new = both_levels(lambda n, case: reduce_residual(case, step, now[n]))
            betas = [[a / b for a, b in zip(new[n], rr[n])] for n in range(len(LEVELS))]
            rr = new

    results = [take(3), take(3)]
    sems = take(2)

    def send(n, h, z):
        lv = LEVELS[n]
        size = plane_rows(lv)
        first = sum(2 * field_rows(v) for v in LEVELS[:n]) + h * field_rows(lv)
        return pltpu.make_async_copy(
            results[n][h].at[pl.ds(pl.multiple_of(z * size, SUBS), size)],
            phi.at[pl.ds(pl.multiple_of(first + z * size, SUBS), size)],
            sems[n].at[h * lv.edz + z],
        )

    totals = both_levels(
        lambda n, case: finish(case, alphas[n], results[n], functools.partial(send, n))
    )
    _, element, _, slot = lane_parts()
    packed = []
    for level in totals:
        parts = [v + xor_lane(v, 16) for v in level[:3]]
        parts.append(jnp.where(element == 0, level[3], turn(level[3], 16)))
        packed.append(
            jnp.where(slot == 0, parts[0], jnp.where(slot == 1, parts[1], jnp.where(slot == 2, parts[2], parts[3])))
        )
    row = jnp.where(element == 0, packed[0], packed[1])
    for r in range(0, message.shape[0], SUBS):
        message[r : r + SUBS, :] = row
    for n, lv in enumerate(LEVELS):
        for h in HALVES:
            for z in range(lv.edz):
                send(n, h, z).wait()


def coarse_nodes(gathered, gy_count, me):
    total_rows = gathered.shape[0]
    shape = gathered.shape
    lane = lane_iota(shape)
    row = sub_iota(shape)
    corner = lane // 32
    column = lane // 8 % 2
    last = row % gy_count == gy_count - 1
    start = row % gy_count == 0
    one = gathered
    two = turn(gathered, -1)
    four = turn(gathered, -2)
    rhs = turn(gathered, -3)
    two_back = turn(two, 32)

    def next_x(u):
        return turn(u, -gy_count, 0)

    def prev_x(u):
        return turn(u, gy_count, 0)

    def next_y(u):
        ahead = jnp.where(last, turn(u, gy_count - 1, 0), turn(u, -1, 0))
        return jnp.where(column == 0, turn(u, -8), turn(ahead, 8))

    def prev_y(u):
        behind = jnp.where(start, turn(u, 1 - gy_count, 0), turn(u, 1, 0))
        return jnp.where(column == 1, turn(u, 8), turn(behind, -8))

    def by_corner(a, b, c, d):
        return jnp.where(corner == 0, a, jnp.where(corner == 1, b, jnp.where(corner == 2, c, d)))

    def corners(u):
        ux = next_x(u)
        return by_corner(u, next_y(u), ux, next_y(ux))

    def assemble(v):
        vx = prev_x(v)
        w = by_corner(v, prev_y(v), vx, prev_y(vx))
        w = w + turn(w, 64)
        return w + turn(w, 32)

    def operate(u):
        c = corners(u)
        return assemble(one * c + two * turn(c, -32) + two_back * turn(c, 32) + four * turn(c, 64))

    def total(a, b):
        v = a * b
        v = tree([v[r : r + SUBS] for r in range(0, total_rows, SUBS)])
        for shift in (4, 2, 1):
            v = v + turn(v, shift, 0)
        v = v + xor_lane(v, 8)
        return v[0:1]

    residual = -assemble(rhs)
    direction = residual
    update = jnp.zeros_like(residual)
    now = total(residual, residual)
    for step in range(2):
        image = operate(direction)
        alpha = now / total(direction, image)
        update = update + alpha * direction
        if step == 0:
            residual = residual - alpha * image
            new = total(residual, residual)
            direction = residual + new / now * direction
            now = new
    mine = jnp.where(row == me, corners(update), 0.0)
    mine = jnp.sum(mine, axis=0, keepdims=True)
    return jnp.broadcast_to(mine, (SUBS, LANES))


def turn_kernel(phi, out_ref):
    start_row, number = 0, 0
    for lv in LEVELS:
        s = lv.seg
        nz = EZ * lv.edz
        per = LANES // nz
        for i in range(s):
            for t in range(turned_tiles(lv)):
                parts = []
                for n in range(per):
                    yo, j = divmod(lv.mx + t * per + n, s)
                    start = start_row + (i * s + j) * SUBS + yo
                    chosen, bottom = [
                        phi[pl.ds(start + h * field_rows(lv), lv.edz, stride=plane_rows(lv)), :] for h in HALVES
                    ]
                    lower = lane_iota(chosen.shape) // 16 % 2 == 0
                    parts.append(jnp.where(lower, chosen, turn(bottom, 16)))
                    parts.append(jnp.where(lower, turn(chosen, -16), 0.0))
                out_ref[number] = jnp.concatenate(parts, axis=0).T
                number += 1
        start_row += 2 * field_rows(lv)


def pressure_kernel(gy_count, me_ref, gathered, turned, fine_out, twin_out, fine_all, twin_all):
    mine = coarse_nodes(gathered[...], gy_count, me_ref[0])
    first = 0
    for n, (lv, out_ref, all_ref) in enumerate(((FINE, fine_out, fine_all), (TWIN, twin_out, twin_all))):
        s = lv.seg
        tiles = turned_tiles(lv)
        nodes = {}
        for c in range(COLUMNS):
            for p in range(4):
                at = p * 32 + n * 16 + c * 8
                nodes[p, c] = jnp.broadcast_to(mine[:, at : at + 1], (SUBS, LANES))
        for c in range(COLUMNS):
            for t in range(tiles):
                at = (c * tiles + t) * LANES
                for i in range(s):
                    def part(group):
                        return turned[first + i * tiles + t, group * 16 + c * 8 : group * 16 + c * 8 + 8, :]

                    value = tree([part(2 * p) * nodes[p, c] + part(2 * p + 1) for p in range(4)])
                    all_ref[c * tiles + t, pl.ds(i, SUBS, stride=s), :] = value
                out_ref[:, at : at + LANES] = all_ref[c * tiles + t, lv.mx : lv.mx + lv.edge, :]
        first += s * tiles


def vmem(shape, dtype=F32):
    return pltpu.VMEM(shape, dtype)


def shards(permeability):
    nz = EZ * ELZ
    rows = permeability.shape[1]
    lanes = permeability.shape[2]
    assert rows == EL and lanes == COLUMNS * EL * nz
    rim = MX * nz
    gx, gy = lax.axis_size("gx"), lax.axis_size("gy")

    def sent(value, axis, shift):
        count = lax.axis_size(axis)
        return lax.ppermute(value, axis, [(i, (i + shift) % count) for i in range(count)])

    x_low = sent(permeability[:, rows - MX :], "gx", 1)
    x_high = sent(permeability[:, :MX], "gx", -1)

    def strip(part):
        return jnp.concatenate([x_low[:, :, part], permeability[:, :, part], x_high[:, :, part]], axis=1)

    y_low = sent(strip(slice(lanes - rim, lanes)), "gy", 1)
    y_high = sent(strip(slice(0, rim)), "gy", -1)
    halos = [x_low, x_high, y_low, y_high]
    flat_lanes = lanes + 2 * rim
    scratch = [
        vmem((LANES, lanes)),
        vmem((LANES, 2 * rim)),
        vmem((flat_lanes, LANES)),
        vmem((flat_lanes // 2, LANES)),
        vmem((SUBS * (TWIN.seg + 2) * nz, LANES)),
    ]
    for lv in LEVELS:
        scratch.append(vmem((lv.levels + 1, lv.seg, SUBS, 2 * LANES)))
        scratch += [vmem((lv.planes * lv.seg // 2, 2 * SUBS, 2 * LANES), BF16)] * 6
        scratch += [vmem((lv.seg, lv.planes * lv.seg, SUBS, LANES))] * 3
        scratch += [vmem((lv.inner + 1, 2 * lv.tiles, SUBS, LANES))] * 5
        scratch.append(vmem((2 * lv.tiles, SUBS, LANES)))
    for lv in LEVELS:
        scratch += [vmem((padded_rows(lv), LANES))] * 3
    scratch += [pltpu.SemaphoreType.DMA((2 * lv.edz,)) for lv in LEVELS]
    full = pl.BlockSpec(memory_space=pltpu.VMEM)
    inside = pl.pallas_call(
        place_kernel,
        out_shape=vmem((LANES, lanes)),
        in_specs=[full],
        out_specs=full,
        compiler_params=pltpu.CompilerParams(vmem_limit_bytes=8 * 1024 * 1024),
        cost_estimate=pl.CostEstimate(flops=1000000, bytes_accessed=4000000, transcendentals=0),
        name="place",
    )(permeability)
    phi, message = pl.pallas_call(
        solve_kernel,
        out_shape=[
            pltpu.HBM((sum(2 * field_rows(lv) for lv in LEVELS), LANES), F32),
            jax.ShapeDtypeStruct((gx * gy, LANES), F32),
        ],
        in_specs=[full] * 5,
        out_specs=[pl.BlockSpec(memory_space=pltpu.HBM), full],
        scratch_shapes=scratch,
        compiler_params=pltpu.CompilerParams(vmem_limit_bytes=50 * 1024 * 1024),
        name="solve",
    )(inside, *halos)
    gathered = lax.all_to_all(message, ("gx", "gy"), 0, 0, tiled=True)
    tiles = sum(lv.seg * turned_tiles(lv) for lv in LEVELS)
    turned = pl.pallas_call(
        turn_kernel,
        out_shape=vmem((tiles, LANES, LANES)),
        in_specs=[full],
        out_specs=full,
        compiler_params=pltpu.CompilerParams(vmem_limit_bytes=16 * 1024 * 1024),
        cost_estimate=pl.CostEstimate(flops=4000000, bytes_accessed=8000000, transcendentals=0),
        name="turned",
    )(phi)
    me = (lax.axis_index("gx") * gy + lax.axis_index("gy")).astype(jnp.int32).reshape(1)
    return tuple(
        pl.pallas_call(
            functools.partial(pressure_kernel, gy),
            out_shape=[
                jax.ShapeDtypeStruct((lv.edge, COLUMNS * lv.edge * EZ * lv.edz), F32) for lv in LEVELS
            ],
            in_specs=[pl.BlockSpec(memory_space=pltpu.SMEM), full, full],
            out_specs=[full] * 2,
            scratch_shapes=[vmem((COLUMNS * turned_tiles(lv), SUBS * lv.seg, LANES)) for lv in LEVELS],
            compiler_params=pltpu.CompilerParams(vmem_limit_bytes=16 * 1024 * 1024),
            name="pressure",
        )(me, gathered, turned)
    )


def solution(mesh):
    return jax.shard_map(
        shards,
        mesh=mesh,
        in_specs=(P(None, "gx", "gy"),),
        out_specs=(P("gx", "gy"), P("gx", "gy")),
        check_vma=False,
    )
```

```python
import functools
import typing

import jax
import jax.numpy as jnp
from jax import lax
from jax.experimental import pallas as pl
from jax.experimental.pallas import tpu as pltpu
from jax.sharding import PartitionSpec as P

EL = 32
ELZ = 16
MX = 4
MZ = 2
EZ = 2
LANES = 128
SUBS = 8
COLUMNS = 2
F32 = jnp.float32
BF16 = jnp.bfloat16


class Level(typing.NamedTuple):
    edge: int
    edz: int
    mx: int
    mz: int
    spacing: float
    step: int

    @property
    def width(self):
        return self.edge + 2 * self.mx

    @property
    def inner(self):
        return self.edz + 2 * self.mz - 2

    @property
    def seg(self):
        return -(-self.width // SUBS)

    @property
    def tiles(self):
        return self.seg * self.seg

    @property
    def levels(self):
        return EZ * self.edz + 2

    @property
    def planes(self):
        return -(-(self.inner + 1) // 2) * 2


FINE = Level(EL, ELZ, MX, MZ, 1.0, 1)
TWIN = Level(EL // 2, ELZ // 2, MX // 2, MZ // 2, 2.0, 2)
LEVELS = (FINE, TWIN)


def lane_iota(shape=(SUBS, LANES)):
    return lax.broadcasted_iota(jnp.int32, shape, len(shape) - 1)


def sub_iota(shape=(SUBS, LANES)):
    return lax.broadcasted_iota(jnp.int32, shape, len(shape) - 2)


def turn(value, shift, axis=1):
    return pltpu.roll(value, shift % value.shape[axis], axis)


def lane_parts():
    lane = lane_iota()
    return lane // 32, lane // 16 % 2, lane // 8 % 2, lane % 8


class Consts:
    def __init__(self, lv):
        corner, _, _, xo = lane_parts()
        yo = sub_iota()
        ax, ay = corner // 2, corner % 2
        self.lv = lv
        s = lv.seg
        self.fx, self.fy = [], []
        self.inx, self.iny, self.facex, self.facey = [], [], [], []
        for i in range(s):
            x = xo * s + i
            y = yo * s + i
            px = (x.astype(F32) - lv.mx + 0.5) / lv.edge
            py = (y.astype(F32) - lv.mx + 0.5) / lv.edge
            self.fx.append(jnp.where(ax == 1, px, 1.0 - px))
            self.fy.append(jnp.where(ay == 1, py, 1.0 - py))
            xs = [s * o + i for o in range(SUBS)]

            def ranged(value, low, high):
                if all(low <= v <= high for v in xs):
                    return None
                return ((value >= low) & (value <= high)).astype(F32)

            self.inx.append((ranged(x, 1, lv.width - 2), ranged(x, lv.mx, lv.mx + lv.edge - 1)))
            self.iny.append((ranged(y, 1, lv.width - 2), ranged(y, lv.mx, lv.mx + lv.edge - 1)))
            cut = (lv.mx - 1, lv.mx + lv.edge - 1)
            self.facex.append(((x != cut[0]) & (x != cut[1])).astype(F32) if any(v in cut for v in xs) else None)
            self.facey.append(((y != cut[0]) & (y != cut[1])).astype(F32) if any(v in cut for v in xs) else None)
        sx = jnp.where(ax == 1, -1.0 / lv.edge, 1.0 / lv.edge).astype(F32)
        sy = jnp.where(ay == 1, -1.0 / lv.edge, 1.0 / lv.edge).astype(F32)
        self.along_x = [sx * f for f in self.fy]
        self.along_y = [sy * f for f in self.fx]

    def fz(self, plane):
        place = (jnp.asarray(plane, jnp.int32).astype(F32) - self.lv.mz + 0.5) / self.lv.edz
        return 1.0 - place, place

    def masked(self, value, i, j, kind):
        for table, index in ((self.inx, i), (self.iny, j)):
            factor = table[index][kind]
            if factor is not None:
                value = value * factor
        return value


def tree(values):
    values = list(values)
    while len(values) > 1:
        values = [a + b for a, b in zip(values[::2], values[1::2])] + (
            [values[-1]] if len(values) % 2 else []
        )
    return values[0]


def xor_lane(value, bit):
    return jnp.where(lane_iota(value.shape) // bit % 2 == 1, turn(value, bit), turn(value, -bit))


def problem_sum(value):
    for shift in (4, 2, 1):
        value = value + turn(value, shift, 0)
    for bit in (1, 2, 4):
        value = value + xor_lane(value, bit)
    return value


def spread_weights(lv, k_ref, high_refs, low_refs, w_refs):
    s = lv.seg
    wide = (SUBS, LANES)
    pos = lane_iota(wide)
    yo = sub_iota(wide)
    first = pos < 40
    third = pos >= 80
    second = (pos >= 40) & (pos < 80)
    edge_x = first & (pos >= (lv.width - 1) * lv.step)

    def one(z, i, c):
        part = slice(c * LANES, (c + 1) * LANES)
        k = k_ref[z, i, :, part]
        nbx = turn(k, -lv.step)
        nby = k_ref[z, i + 1, :, part] if i < s - 1 else turn(k_ref[z, 0, :, part], -1, 0)
        nbz = k_ref[z + 1, i, :, part]
        nb = jnp.where(first, nbx, jnp.where(second, nby, nbz))
        w = (2.0 * lv.spacing) * k * nb / (k + nb)
        bad = edge_x | (second & (yo * s + i >= lv.width - 1))
        return jnp.where(bad, 0.0, w)

    def planes(t, _):
        units = [(2 * t + n, i) for n in range(2) for i in range(s)]
        for e in range(EZ):
            made = []
            for plane, i in units:
                z = jnp.clip(e * lv.edz + plane + 1 - lv.mz, 0, lv.levels - 1)
                w0, w1 = one(z, i, 0), one(z, i, 1)
                near, wrap = turn(w1, 40), turn(w1, 48)
                made.append((jnp.where(first, w0, near), jnp.where(third, near, w0), jnp.where(third, w0, wrap)))
            for p in range(s):
                for m in range(3):
                    both = jnp.concatenate([made[2 * p][m], made[2 * p + 1][m]], axis=0)
                    high = both.astype(BF16)
                    part = slice(e * LANES, (e + 1) * LANES)
                    high_refs[m][t * s + p, :, part] = high
                    low_refs[m][t * s + p, :, part] = (both - high.astype(F32)).astype(BF16)
        return 0

    lax.fori_loop(0, lv.planes // 2, planes, 0)
    rows = lv.planes * s * SUBS
    row = lax.broadcasted_iota(jnp.int32, (2 * LANES, 2 * LANES), 0)
    lane = lax.broadcasted_iota(jnp.int32, (1, 2 * LANES), 1)
    upper = lane // LANES
    for q in range(-(-s // 2)):
        x = lane % 8 * s + 2 * q + upper
        valid = (x < lv.width) & (2 * q + upper < s)
        for m in range(3):
            segment = jnp.where(lane // 8 % 2 == 0, m, (m + 1) % 3)
            source = jnp.where(valid, lane // 16 % 2 * LANES + segment * 40 + lv.step * x, -1)
            pick = (row == source).astype(F32).astype(BF16)
            out = jnp.dot(high_refs[m][...].reshape(rows, 2 * LANES), pick, preferred_element_type=F32)
            out = out + jnp.dot(low_refs[m][...].reshape(rows, 2 * LANES), pick, preferred_element_type=F32)
            for half in range(min(2, s - 2 * q)):
                part = out[:, half * LANES : (half + 1) * LANES]
                w_refs[m][2 * q + half] = part.reshape(lv.planes * s, SUBS, LANES)


class Case:
    def __init__(self, lv, w_refs, fields, planes):
        self.lv, self.cs, self.w_refs = lv, Consts(lv), w_refs
        self.d, self.q, self.r = fields[:3], fields[3], fields[4]
        (self.fz,) = planes

    def weights(self, plane):
        s = self.lv.seg
        return lambda m, i, j: self.w_refs[m][i, plane * s + j]


HALVES = (0, 1)
CHUNK = 640


def plane_rows(lv):
    return lv.tiles * SUBS


def field_rows(lv):
    return lv.edz * plane_rows(lv)


def padded_rows(lv):
    return -(-field_rows(lv) // CHUNK) * CHUNK


def turned_tiles(lv):
    return lv.edge * EZ * lv.edz // LANES


def together(works):
    zero = jnp.zeros((SUBS, LANES), F32)
    sums = [tuple(zero for _ in range(number)) for _, number, _, _ in works]
    done = 0
    for stop in sorted({count for count, _, _, _ in works}):
        active = [n for n, work in enumerate(works) if work[0] > done]

        def body(z, carry, active=active):
            return tuple(
                tuple(a + b for a, b in zip(old, works[n][2](z))) for n, old in zip(active, carry)
            )

        got = lax.fori_loop(done, stop, body, tuple(sums[n] for n in active))
        for n, part in zip(active, got):
            sums[n] = part
        done = stop
    return [work[3](list(part)) for work, part in zip(works, sums)]


def start_residual(case):
    lv, cs, s = case.lv, case.cs, case.lv.seg

    def step(z0):
        total = [[], []]
        stores = []
        for z in [z0]:
            get, below = case.weights(z + 1), case.weights(z)
            gz = cs.fz(z + 1)
            last = [get(1, i, s - 1) * cs.along_y[i] for i in range(s)]
            before = [turn(v, 1, 0) for v in last]
            for j in range(s):
                flux_y = last if j == s - 1 else [get(1, i, j) * cs.along_y[i] for i in range(s)]
                flux_x = [get(0, i, j) * cs.along_x[j] for i in range(s)]
                tops = [below(2, i, j) - get(2, i, j) for i in range(s)]
                for index, value in stores:
                    case.d[0][index] = value
                del stores[:]
                squares = [[], []]
                for i in range(s):
                    k = i * s + j
                    prev_x = flux_x[i - 1] if i else turn(flux_x[s - 1], 1)
                    flat = (prev_x - flux_x[i]) + (before[i] - flux_y[i])
                    flat = cs.masked(flat, i, j, 0)
                    tall = (cs.fx[i] * cs.fy[j]) * (1.0 / lv.edz) * tops[i]
                    tall = cs.masked(tall, i, j, 0)
                    for h, value in enumerate((flat * gz[0] + tall, flat * gz[1] - tall)):
                        stores.append(((z, h * lv.tiles + k), value))
                        squares[h].append(value * value)
                for h in HALVES:
                    total[h].append(tree(squares[h]))
                before = flux_y
        for index, value in stores:
            case.d[0][index] = value
        return [tree(t) for t in total]

    return lv.inner, 2, step, lambda sums: sums


def x_jumps(row, s):
    return [row[i] - (row[i + 1] if i < s - 1 else turn(row[0], -1)) for i in range(s)]


def apply(case, number, betas):
    lv, cs, s = case.lv, case.cs, case.lv.seg
    keep = number < 2
    n = lv.tiles

    def fresh(z, h, k):
        at = h * n + k
        if number == 0:
            return case.d[0][z, at]
        value = case.r[z, at] + betas[h] * case.d[number - 1][z, at]
        case.d[number][z, at] = value
        return value

    firsts = []
    get = case.weights(0)
    for h in HALVES:
        terms = []
        for k in range(n):
            value = fresh(0, h, k)
            flux = -get(2, k // s, k % s) * value
            if keep:
                case.fz[h * n + k] = flux
            else:
                terms.append(-flux * value)
        firsts.append(tree(terms) if terms else 0.0)

    def step(z):
        total = [[], []]
        get = case.weights(z + 1)

        def load(j):
            cells = [i * s + j for i in range(s)]
            out = {"u": [[case.d[number][z, h * n + k] for k in cells] for h in HALVES]}
            out["w"] = [[get(m, i, j) for i in range(s)] for m in range(3)]
            if keep:
                out["fz"] = [[case.fz[h * n + k] for k in cells] for h in HALVES]
            if number == 0:
                out["up"] = [[case.d[0][z + 1, h * n + k] for k in cells] for h in HALVES]
            else:
                old = case.d[number - 1]
                out["up"] = [
                    [(case.r[z + 1, h * n + k], old[z + 1, h * n + k]) for k in cells] for h in HALVES
                ]
            return out

        row = load(0)
        if keep:
            wy = [get(1, i, s - 1) for i in range(s)]
            ends = [[case.d[number][z, h * n + i * s + s - 1] for i in range(s)] for h in HALVES]
        heads = [[turn(v, -1, 0) for v in row["u"][h]] for h in HALVES]
        if keep:
            last = [[wy[i] * (ends[h][i] - heads[h][i]) for i in range(s)] for h in HALVES]
            before = [[turn(v, 1, 0) for v in last[h]] for h in HALVES]
        stores = []

        def flush():
            for ref, index, value in stores:
                ref[index] = value
            del stores[:]

        for j in range(s):
            now, row = row, (load(j + 1) if j < s - 1 else None)
            flush()
            wx, wy, wz = now["w"]
            for h in HALVES:
                u = now["u"][h]
                jump_x = x_jumps(u, s)
                flux_x = [w * v for w, v in zip(wx, jump_x)]
                if keep and j == s - 1:
                    flux_y = last[h]
                else:
                    jump_y = [a - b for a, b in zip(u, row["u"][h] if j < s - 1 else heads[h])]
                    flux_y = [w * v for w, v in zip(wy, jump_y)]
                terms = []
                for i in range(s):
                    k = i * s + j
                    after = now["up"][h][i]
                    if number:
                        after = after[0] + betas[h] * after[1]
                        stores.append((case.d[number], (z + 1, h * n + k), after))
                    jump = u[i] - after
                    flux = wz[i] * jump
                    if keep:
                        prev_x = flux_x[i - 1] if i else turn(flux_x[s - 1], 1)
                        value = (flux_x[i] - prev_x) + (flux_y[i] - before[h][i]) + (flux - now["fz"][h][i])
                        stores.append((case.fz, h * n + k, flux))
                        value = cs.masked(value, i, j, 0)
                        stores.append((case.q, (z, h * n + k), value))
                        terms.append(u[i] * value)
                    else:
                        terms.append((flux * jump + flux_x[i] * jump_x[i]) + flux_y[i] * jump_y[i])
                total[h].append(tree(terms))
                if keep:
                    before[h] = flux_y
        flush()
        return [tree(t) for t in total]

    return lv.inner, 2, step, lambda sums: [a + b for a, b in zip(sums, firsts)]


def reduce_residual(case, number, alphas):
    lv = case.lv

    def step(z0):
        total = [[], []]
        source = case.d[0] if number == 0 else case.r
        for z in [z0]:
            for h in HALVES:
                cells = range(h * lv.tiles, (h + 1) * lv.tiles)
                values = [source[z, at] - alphas[h] * case.q[z, at] for at in cells]
                for at, value in zip(cells, values):
                    case.r[z, at] = value
                total[h].append(tree([v * v for v in values]))
        return [tree(t) for t in total]

    return lv.inner, 2, step, lambda sums: sums


def finish(case, alphas, refs, send):
    lv, cs, s = case.lv, case.cs, case.lv.seg
    n = lv.tiles
    f_ref, p_ref, y_ref = refs
    lower = lane_parts()[1] == 0

    def at(z, k):
        return pl.ds(pl.multiple_of(z * plane_rows(lv) + k * SUBS, SUBS), SUBS)

    def parts(z, k):
        return [[d_ref[z + lv.mz - 1, h * n + k] for d_ref in case.d] for h in HALVES]

    def fresh(i, j, gz, fields):
        both = cs.fx[i] * cs.fy[j]
        values = []
        for h in HALVES:
            value = both * gz[h]
            for alpha, d in zip(alphas[h], fields[h]):
                value = value + alpha * d
            values.append(cs.masked(value, i, j, 1))
        return jnp.where(lower, values[1], values[0]), values[0]

    gz = cs.fz(lv.mz)
    for i in range(s):
        for j in range(s):
            k = i * s + j
            f_ref[at(0, k), :], p_ref[at(0, k), :] = fresh(i, j, gz, parts(0, k))
            case.fz[k] = jnp.zeros((SUBS, LANES), F32)
    rest = padded_rows(lv) - field_rows(lv)
    if rest:
        for ref in refs:
            ref[field_rows(lv) :, :] = jnp.zeros((rest, LANES), F32)

    def cut(values, table):
        return [v if f is None else v * f for v, f in zip(values, table)]

    def step(z):
        get = case.weights(z + lv.mz)
        up = jnp.minimum(z + 1, lv.edz - 1)
        gz = cs.fz(up + lv.mz)

        def load(j):
            cells = [i * s + j for i in range(s)]
            return {
                "u": [f_ref[at(z, k), :] for k in cells],
                "w": [[get(m, i, j) for i in range(s)] for m in range(3)],
                "fz": [case.fz[k] for k in cells],
                "up": [parts(up, k) for k in cells],
            }

        row = load(0)
        wy = [get(1, i, s - 1) for i in range(s)]
        ends = [f_ref[at(z, i * s + s - 1), :] for i in range(s)]
        last = [wy[i] * (ends[i] - turn(row["u"][i], -1, 0)) for i in range(s)]
        last = cut(last, [cs.facey[s - 1]] * s)
        before = [turn(v, 1, 0) for v in last]
        stores = []

        def flush():
            for ref, index, value in stores:
                ref[index] = value
            del stores[:]

        for j in range(s):
            now, row = row, (load(j + 1) if j < s - 1 else None)
            flush()
            u = now["u"]
            wx, wy, wz = now["w"]
            flux_x = cut([w * v for w, v in zip(wx, x_jumps(u, s))], cs.facex)
            flux_y = last
            if j < s - 1:
                flux_y = cut([w * (a - b) for w, a, b in zip(wy, u, row["u"])], [cs.facey[j]] * s)
            for i in range(s):
                k = i * s + j
                chosen, bottom = fresh(i, j, gz, now["up"][i])
                flux = wz[i] * (u[i] - chosen)
                prev_x = flux_x[i - 1] if i else turn(flux_x[s - 1], 1)
                value = (flux_x[i] - prev_x) + (flux_y[i] - before[i]) + (flux - now["fz"][i])
                stores.append((f_ref, (at(up, k), slice(None)), chosen))
                stores.append((p_ref, (at(up, k), slice(None)), bottom))
                stores.append((y_ref, (at(z, k), slice(None)), value))
                stores.append((case.fz, k, flux))
            before = flux_y
        flush()
        for h in HALVES:
            send(h, z).start()
        return ()

    return lv.edz, 0, step, lambda _: corner_pairs(lv, refs)


def corner_pairs(lv, refs):
    f_ref, p_ref, y_ref = refs
    pairs = jnp.zeros((2 * LANES, LANES), F32)
    for start in range(0, padded_rows(lv), CHUNK):
        part = slice(start, start + CHUNK)
        left = jnp.concatenate([f_ref[part, :].T, p_ref[part, :].T], axis=0)
        right = y_ref[part, :]
        left_high, right_high = left.astype(BF16), right.astype(BF16)
        left_low = (left - left_high.astype(F32)).astype(BF16)
        right_low = (right - right_high.astype(F32)).astype(BF16)
        for a, b in ((left_high, right_high), (left_low, right_high), (left_high, right_low)):
            pairs = pairs + jnp.dot(a, b, preferred_element_type=F32)
    shape = (LANES, LANES)
    row, lane = sub_iota(shape), lane_iota(shape)
    sums = [jnp.where(row == (lane + 32 * k) % LANES, pairs[:LANES], 0.0) for k in range(3)]
    sums.append(jnp.where(row % 32 == lane % 32, pairs[LANES:], 0.0))
    out = []
    for value in sums:
        value = tree([value[r : r + SUBS] for r in range(0, LANES, SUBS)])
        out.append(value)
    return out


def place_kernel(center, out_ref):
    nx = center.shape[1]
    out_ref[...] = jnp.ones(out_ref.shape, F32)
    for m in range(3):
        off = m * (nx + 2 * MX) + MX
        out_ref[off : off + nx, :] = center[m]


def solve_kernel(
    inside, x_low, x_high, y_low, y_high,
    phi, message,
    flat, sides, rows, pairs, twin_rows, *refs,
):
    lanes = inside.shape[1]
    rim = y_low.shape[2]
    wide = y_low.shape[1]
    for m in range(3):
        off = m * wide
        flat[off : off + MX, :] = x_low[m]
        flat[off + wide - MX : off + wide, :] = x_high[m]
        sides[off : off + wide, :rim] = y_low[m]
        sides[off : off + wide, rim:] = y_high[m]
    sides[3 * wide :, :] = jnp.ones((LANES - 3 * wide, sides.shape[1]), F32)
    row = sub_iota((LANES, LANES))
    place = row % wide
    outer = (row < 3 * wide) & ((place < MX) | (place >= wide - MX))
    for t in range(rim // LANES):
        low, high = slice(t * LANES, (t + 1) * LANES), slice(rim + t * LANES, rim + (t + 1) * LANES)
        rows[low, :] = sides[:, low].T
        rows[lanes + rim + t * LANES : lanes + rim + (t + 1) * LANES, :] = sides[:, high].T
    for t in range(lanes // LANES):
        part = slice(t * LANES, (t + 1) * LANES)
        rows[rim + t * LANES : rim + (t + 1) * LANES, :] = jnp.where(outer, flat[:, part], inside[:, part]).T

    nz = EZ * ELZ
    twin_y = rows.shape[0] // nz // 2
    for y in range(twin_y):
        both = rows[2 * y * nz : (2 * y + 1) * nz, :] + rows[(2 * y + 1) * nz : (2 * y + 2) * nz, :]
        both = both + turn(both, -1)
        at = y * nz
        pairs[at : at + nz, :] = both
        twin_rows[at : at + 8, :] = jnp.broadcast_to(0.25 * both[0:1], (8, LANES))
        twin_rows[at + 8 + nz // 2 : at + nz, :] = jnp.broadcast_to(0.25 * both[nz - 1 : nz], (8, LANES))
    for y in range(twin_y):
        at = y * nz
        middle = pairs[pl.ds(at, nz // 2, stride=2), :] + pairs[pl.ds(at + 1, nz // 2, stride=2), :]
        twin_rows[at + 8 : at + 8 + nz // 2, :] = 0.125 * middle
    twin_rows[twin_y * nz :, :] = jnp.ones((twin_rows.shape[0] - twin_y * nz, LANES), F32)

    refs = list(refs)

    def take(count):
        got = refs[:count]
        del refs[:count]
        return got

    cases = []
    for lv, source in zip(LEVELS, (rows, twin_rows)):
        (k_ref,) = take(1)
        high_refs, low_refs, w_refs = take(3), take(3), take(3)
        for z in range(lv.levels + 1):
            cell = min(max(z - 1, 0), nz - 1) if lv is FINE else min(z, lv.levels - 1) + 7
            for i in range(lv.seg):
                for c in range(COLUMNS):
                    start = (lv.edge * c + i) * nz + cell
                    k_ref[z, i, :, c * LANES : (c + 1) * LANES] = source[pl.ds(start, SUBS, stride=lv.seg * nz), :]
        spread_weights(lv, k_ref, high_refs, low_refs, w_refs)
        case = Case(lv, w_refs, take(5), take(1))
        for k in range(2 * lv.tiles):
            case.d[0][lv.inner, k] = jnp.zeros((SUBS, LANES), F32)
            case.r[lv.inner, k] = jnp.zeros((SUBS, LANES), F32)
        cases.append(case)

    def both_levels(work):
        return [[problem_sum(v) for v in part] for part in together([work(n, case) for n, case in enumerate(cases)])]

    rr = both_levels(lambda n, case: start_residual(case))
    alphas = [[[], []] for _ in LEVELS]
    betas = [None] * len(LEVELS)
    for step in range(3):
        dots = both_levels(lambda n, case: apply(case, step, betas[n]))
        now = [[a / b for a, b in zip(rr[n], dots[n])] for n in range(len(LEVELS))]
        for n in range(len(LEVELS)):
            for h in HALVES:
                alphas[n][h].append(now[n][h])
        if step < 2:
            new = both_levels(lambda n, case: reduce_residual(case, step, now[n]))
            betas = [[a / b for a, b in zip(new[n], rr[n])] for n in range(len(LEVELS))]
            rr = new

    results = [take(3), take(3)]
    sems = take(2)

    def send(n, h, z):
        lv = LEVELS[n]
        size = plane_rows(lv)
        first = sum(2 * field_rows(v) for v in LEVELS[:n]) + h * field_rows(lv)
        return pltpu.make_async_copy(
            results[n][h].at[pl.ds(pl.multiple_of(z * size, SUBS), size)],
            phi.at[pl.ds(pl.multiple_of(first + z * size, SUBS), size)],
            sems[n].at[h * lv.edz + z],
        )

    totals = both_levels(
        lambda n, case: finish(case, alphas[n], results[n], functools.partial(send, n))
    )
    _, element, _, slot = lane_parts()
    packed = []
    for level in totals:
        parts = [v + xor_lane(v, 16) for v in level[:3]]
        parts.append(jnp.where(element == 0, level[3], turn(level[3], 16)))
        packed.append(
            jnp.where(slot == 0, parts[0], jnp.where(slot == 1, parts[1], jnp.where(slot == 2, parts[2], parts[3])))
        )
    row = jnp.where(element == 0, packed[0], packed[1])
    for r in range(0, message.shape[0], SUBS):
        message[r : r + SUBS, :] = row
    for n, lv in enumerate(LEVELS):
        for h in HALVES:
            for z in range(lv.edz):
                send(n, h, z).wait()


def coarse_nodes(gathered, gy_count, me):
    total_rows = gathered.shape[0]
    shape = gathered.shape
    lane = lane_iota(shape)
    row = sub_iota(shape)
    corner = lane // 32
    column = lane // 8 % 2
    last = row % gy_count == gy_count - 1
    start = row % gy_count == 0
    one = gathered
    two = turn(gathered, -1)
    four = turn(gathered, -2)
    rhs = turn(gathered, -3)
    two_back = turn(two, 32)

    def next_x(u):
        return turn(u, -gy_count, 0)

    def prev_x(u):
        return turn(u, gy_count, 0)

    def next_y(u):
        ahead = jnp.where(last, turn(u, gy_count - 1, 0), turn(u, -1, 0))
        return jnp.where(column == 0, turn(u, -8), turn(ahead, 8))

    def prev_y(u):
        behind = jnp.where(start, turn(u, 1 - gy_count, 0), turn(u, 1, 0))
        return jnp.where(column == 1, turn(u, 8), turn(behind, -8))

    def by_corner(a, b, c, d):
        return jnp.where(corner == 0, a, jnp.where(corner == 1, b, jnp.where(corner == 2, c, d)))

    def corners(u):
        ux = next_x(u)
        return by_corner(u, next_y(u), ux, next_y(ux))

    def assemble(v):
        vx = prev_x(v)
        w = by_corner(v, prev_y(v), vx, prev_y(vx))
        w = w + turn(w, 64)
        return w + turn(w, 32)

    def operate(u):
        c = corners(u)
        return assemble(one * c + two * turn(c, -32) + two_back * turn(c, 32) + four * turn(c, 64))

    def total(a, b):
        v = a * b
        v = tree([v[r : r + SUBS] for r in range(0, total_rows, SUBS)])
        for shift in (4, 2, 1):
            v = v + turn(v, shift, 0)
        v = v + xor_lane(v, 8)
        return v[0:1]

    residual = -assemble(rhs)
    direction = residual
    update = jnp.zeros_like(residual)
    now = total(residual, residual)
    for step in range(2):
        image = operate(direction)
        alpha = now / total(direction, image)
        update = update + alpha * direction
        if step == 0:
            residual = residual - alpha * image
            new = total(residual, residual)
            direction = residual + new / now * direction
            now = new
    mine = jnp.where(row == me, corners(update), 0.0)
    mine = jnp.sum(mine, axis=0, keepdims=True)
    return jnp.broadcast_to(mine, (SUBS, LANES))


def turn_kernel(phi, out_ref):
    start_row, number = 0, 0
    for lv in LEVELS:
        s = lv.seg
        nz = EZ * lv.edz
        per = LANES // nz
        for i in range(s):
            for t in range(turned_tiles(lv)):
                parts = []
                for n in range(per):
                    yo, j = divmod(lv.mx + t * per + n, s)
                    start = start_row + (i * s + j) * SUBS + yo
                    chosen, bottom = [
                        phi[pl.ds(start + h * field_rows(lv), lv.edz, stride=plane_rows(lv)), :] for h in HALVES
                    ]
                    lower = lane_iota(chosen.shape) // 16 % 2 == 0
                    parts.append(jnp.where(lower, chosen, turn(bottom, 16)))
                    parts.append(jnp.where(lower, turn(chosen, -16), 0.0))
                out_ref[number] = jnp.concatenate(parts, axis=0).T
                number += 1
        start_row += 2 * field_rows(lv)


def pressure_kernel(gy_count, me_ref, gathered, turned, fine_out, twin_out, fine_all, twin_all):
    mine = coarse_nodes(gathered[...], gy_count, me_ref[0])
    first = 0
    for n, (lv, out_ref, all_ref) in enumerate(((FINE, fine_out, fine_all), (TWIN, twin_out, twin_all))):
        s = lv.seg
        tiles = turned_tiles(lv)
        nodes = {}
        for c in range(COLUMNS):
            for p in range(4):
                at = p * 32 + n * 16 + c * 8
                nodes[p, c] = jnp.broadcast_to(mine[:, at : at + 1], (SUBS, LANES))
        for c in range(COLUMNS):
            for t in range(tiles):
                at = (c * tiles + t) * LANES
                for i in range(s):
                    def part(group):
                        return turned[first + i * tiles + t, group * 16 + c * 8 : group * 16 + c * 8 + 8, :]

                    value = tree([part(2 * p) * nodes[p, c] + part(2 * p + 1) for p in range(4)])
                    all_ref[c * tiles + t, pl.ds(i, SUBS, stride=s), :] = value
                out_ref[:, at : at + LANES] = all_ref[c * tiles + t, lv.mx : lv.mx + lv.edge, :]
        first += s * tiles


def vmem(shape, dtype=F32):
    return pltpu.VMEM(shape, dtype)


def shards(permeability):
    nz = EZ * ELZ
    rows = permeability.shape[1]
    lanes = permeability.shape[2]
    assert rows == EL and lanes == COLUMNS * EL * nz
    rim = MX * nz
    gx, gy = lax.axis_size("gx"), lax.axis_size("gy")

    def sent(value, axis, shift):
        count = lax.axis_size(axis)
        return lax.ppermute(value, axis, [(i, (i + shift) % count) for i in range(count)])

    x_low = sent(permeability[:, rows - MX :], "gx", 1)
    x_high = sent(permeability[:, :MX], "gx", -1)

    def strip(part):
        return jnp.concatenate([x_low[:, :, part], permeability[:, :, part], x_high[:, :, part]], axis=1)

    y_low = sent(strip(slice(lanes - rim, lanes)), "gy", 1)
    y_high = sent(strip(slice(0, rim)), "gy", -1)
    halos = [x_low, x_high, y_low, y_high]
    flat_lanes = lanes + 2 * rim
    scratch = [
        vmem((LANES, lanes)),
        vmem((LANES, 2 * rim)),
        vmem((flat_lanes, LANES)),
        vmem((flat_lanes // 2, LANES)),
        vmem((SUBS * (TWIN.seg + 2) * nz, LANES)),
    ]
    for lv in LEVELS:
        scratch.append(vmem((lv.levels + 1, lv.seg, SUBS, 2 * LANES)))
        scratch += [vmem((lv.planes * lv.seg // 2, 2 * SUBS, 2 * LANES), BF16)] * 6
        scratch += [vmem((lv.seg, lv.planes * lv.seg, SUBS, LANES))] * 3
        scratch += [vmem((lv.inner + 1, 2 * lv.tiles, SUBS, LANES))] * 5
        scratch.append(vmem((2 * lv.tiles, SUBS, LANES)))
    for lv in LEVELS:
        scratch += [vmem((padded_rows(lv), LANES))] * 3
    scratch += [pltpu.SemaphoreType.DMA((2 * lv.edz,)) for lv in LEVELS]
    full = pl.BlockSpec(memory_space=pltpu.VMEM)
    inside = pl.pallas_call(
        place_kernel,
        out_shape=vmem((LANES, lanes)),
        in_specs=[full],
        out_specs=full,
        compiler_params=pltpu.CompilerParams(vmem_limit_bytes=8 * 1024 * 1024),
        cost_estimate=pl.CostEstimate(flops=1000000, bytes_accessed=4000000, transcendentals=0),
        name="place",
    )(permeability)
    phi, message = pl.pallas_call(
        solve_kernel,
        out_shape=[
            pltpu.HBM((sum(2 * field_rows(lv) for lv in LEVELS), LANES), F32),
            jax.ShapeDtypeStruct((gx * gy, LANES), F32),
        ],
        in_specs=[full] * 5,
        out_specs=[pl.BlockSpec(memory_space=pltpu.HBM), full],
        scratch_shapes=scratch,
        compiler_params=pltpu.CompilerParams(vmem_limit_bytes=50 * 1024 * 1024),
        name="solve",
    )(inside, *halos)
    gathered = lax.all_to_all(message, ("gx", "gy"), 0, 0, tiled=True)
    tiles = sum(lv.seg * turned_tiles(lv) for lv in LEVELS)
    turned = pl.pallas_call(
        turn_kernel,
        out_shape=vmem((tiles, LANES, LANES)),
        in_specs=[full],
        out_specs=full,
        compiler_params=pltpu.CompilerParams(vmem_limit_bytes=16 * 1024 * 1024),
        cost_estimate=pl.CostEstimate(flops=4000000, bytes_accessed=8000000, transcendentals=0),
        name="turned",
    )(phi)
    me = (lax.axis_index("gx") * gy + lax.axis_index("gy")).astype(jnp.int32).reshape(1)
    return tuple(
        pl.pallas_call(
            functools.partial(pressure_kernel, gy),
            out_shape=[
                jax.ShapeDtypeStruct((lv.edge, COLUMNS * lv.edge * EZ * lv.edz), F32) for lv in LEVELS
            ],
            in_specs=[pl.BlockSpec(memory_space=pltpu.SMEM), full, full],
            out_specs=[full] * 2,
            scratch_shapes=[vmem((COLUMNS * turned_tiles(lv), SUBS * lv.seg, LANES)) for lv in LEVELS],
            compiler_params=pltpu.CompilerParams(vmem_limit_bytes=16 * 1024 * 1024),
            name="pressure",
        )(me, gathered, turned)
    )


def solution(mesh):
    return jax.shard_map(
        shards,
        mesh=mesh,
        in_specs=(P(None, "gx", "gy"),),
        out_specs=(P("gx", "gy"), P("gx", "gy")),
        check_vma=False,
    )
```

```python
import functools
import typing

import jax
import jax.numpy as jnp
from jax import lax
from jax.experimental import pallas as pl
from jax.experimental.pallas import tpu as pltpu
from jax.sharding import PartitionSpec as P

EL = 32
ELZ = 16
MX = 4
MZ = 2
EZ = 2
LANES = 128
SUBS = 8
COLUMNS = 2
F32 = jnp.float32
BF16 = jnp.bfloat16


class Level(typing.NamedTuple):
    edge: int
    edz: int
    mx: int
    mz: int
    spacing: float
    step: int

    @property
    def width(self):
        return self.edge + 2 * self.mx

    @property
    def inner(self):
        return self.edz + 2 * self.mz - 2

    @property
    def seg(self):
        return -(-self.width // SUBS)

    @property
    def tiles(self):
        return self.seg * self.seg

    @property
    def levels(self):
        return EZ * self.edz + 2

    @property
    def planes(self):
        return -(-(self.inner + 1) // 2) * 2


FINE = Level(EL, ELZ, MX, MZ, 1.0, 1)
TWIN = Level(EL // 2, ELZ // 2, MX // 2, MZ // 2, 2.0, 2)
LEVELS = (FINE, TWIN)


def lane_iota(shape=(SUBS, LANES)):
    return lax.broadcasted_iota(jnp.int32, shape, len(shape) - 1)


def sub_iota(shape=(SUBS, LANES)):
    return lax.broadcasted_iota(jnp.int32, shape, len(shape) - 2)


def turn(value, shift, axis=1):
    return pltpu.roll(value, shift % value.shape[axis], axis)


def lane_parts():
    lane = lane_iota()
    return lane // 32, lane // 16 % 2, lane // 8 % 2, lane % 8


class Consts:
    def __init__(self, lv):
        corner, _, _, xo = lane_parts()
        yo = sub_iota()
        ax, ay = corner // 2, corner % 2
        self.lv = lv
        s = lv.seg
        self.fx, self.fy = [], []
        self.inx, self.iny, self.facex, self.facey = [], [], [], []
        for i in range(s):
            x = xo * s + i
            y = yo * s + i
            px = (x.astype(F32) - lv.mx + 0.5) / lv.edge
            py = (y.astype(F32) - lv.mx + 0.5) / lv.edge
            self.fx.append(jnp.where(ax == 1, px, 1.0 - px))
            self.fy.append(jnp.where(ay == 1, py, 1.0 - py))
            xs = [s * o + i for o in range(SUBS)]

            def ranged(value, low, high):
                if all(low <= v <= high for v in xs):
                    return None
                return ((value >= low) & (value <= high)).astype(F32)

            self.inx.append((ranged(x, 1, lv.width - 2), ranged(x, lv.mx, lv.mx + lv.edge - 1)))
            self.iny.append((ranged(y, 1, lv.width - 2), ranged(y, lv.mx, lv.mx + lv.edge - 1)))
            cut = (lv.mx - 1, lv.mx + lv.edge - 1)
            self.facex.append(((x != cut[0]) & (x != cut[1])).astype(F32) if any(v in cut for v in xs) else None)
            self.facey.append(((y != cut[0]) & (y != cut[1])).astype(F32) if any(v in cut for v in xs) else None)
        sx = jnp.where(ax == 1, -1.0 / lv.edge, 1.0 / lv.edge).astype(F32)
        sy = jnp.where(ay == 1, -1.0 / lv.edge, 1.0 / lv.edge).astype(F32)
        self.along_x = [sx * f for f in self.fy]
        self.along_y = [sy * f for f in self.fx]

    def fz(self, plane):
        place = (jnp.asarray(plane, jnp.int32).astype(F32) - self.lv.mz + 0.5) / self.lv.edz
        return 1.0 - place, place

    def masked(self, value, i, j, kind):
        for table, index in ((self.inx, i), (self.iny, j)):
            factor = table[index][kind]
            if factor is not None:
                value = value * factor
        return value


def tree(values):
    values = list(values)
    while len(values) > 1:
        values = [a + b for a, b in zip(values[::2], values[1::2])] + (
            [values[-1]] if len(values) % 2 else []
        )
    return values[0]


def xor_lane(value, bit):
    return jnp.where(lane_iota(value.shape) // bit % 2 == 1, turn(value, bit), turn(value, -bit))


def problem_sum(value):
    for shift in (4, 2, 1):
        value = value + turn(value, shift, 0)
    for bit in (1, 2, 4):
        value = value + xor_lane(value, bit)
    return value


def split_weights(lv, k_ref, high_refs, low_refs):
    s = lv.seg
    wide = (SUBS, LANES)
    pos = lane_iota(wide)
    yo = sub_iota(wide)
    first = pos < 40
    third = pos >= 80
    second = (pos >= 40) & (pos < 80)
    edge_x = first & (pos >= (lv.width - 1) * lv.step)

    def one(z, i, c):
        part = slice(c * LANES, (c + 1) * LANES)
        k = k_ref[z, i, :, part]
        nbx = turn(k, -lv.step)
        nby = k_ref[z, i + 1, :, part] if i < s - 1 else turn(k_ref[z, 0, :, part], -1, 0)
        nbz = k_ref[z + 1, i, :, part]
        nb = jnp.where(first, nbx, jnp.where(second, nby, nbz))
        w = (2.0 * lv.spacing) * k * nb / (k + nb)
        bad = edge_x | (second & (yo * s + i >= lv.width - 1))
        return jnp.where(bad, 0.0, w)

    def planes(t, _):
        units = [(2 * t + n, i) for n in range(2) for i in range(s)]
        for e in range(EZ):
            made = []
            for plane, i in units:
                z = jnp.clip(e * lv.edz + plane + 1 - lv.mz, 0, lv.levels - 1)
                w0, w1 = one(z, i, 0), one(z, i, 1)
                near, wrap = turn(w1, 40), turn(w1, 48)
                made.append((jnp.where(first, w0, near), jnp.where(third, near, w0), jnp.where(third, w0, wrap)))
            for p in range(s):
                for m in range(3):
                    both = jnp.concatenate([made[2 * p][m], made[2 * p + 1][m]], axis=0)
                    high = both.astype(BF16)
                    part = slice(e * LANES, (e + 1) * LANES)
                    high_refs[m][t * s + p, :, part] = high
                    low_refs[m][t * s + p, :, part] = (both - high.astype(F32)).astype(BF16)
        return 0

    return planes


def place_weights(lv, high_refs, low_refs, w_refs):
    s = lv.seg
    rows = lv.planes * s * SUBS
    row = lax.broadcasted_iota(jnp.int32, (2 * LANES, 2 * LANES), 0)
    lane = lax.broadcasted_iota(jnp.int32, (1, 2 * LANES), 1)
    upper = lane // LANES
    for q in range(-(-s // 2)):
        x = lane % 8 * s + 2 * q + upper
        valid = (x < lv.width) & (2 * q + upper < s)
        for m in range(3):
            segment = jnp.where(lane // 8 % 2 == 0, m, (m + 1) % 3)
            source = jnp.where(valid, lane // 16 % 2 * LANES + segment * 40 + lv.step * x, -1)
            pick = (row == source).astype(F32).astype(BF16)
            out = jnp.dot(high_refs[m][...].reshape(rows, 2 * LANES), pick, preferred_element_type=F32)
            out = out + jnp.dot(low_refs[m][...].reshape(rows, 2 * LANES), pick, preferred_element_type=F32)
            for half in range(min(2, s - 2 * q)):
                part = out[:, half * LANES : (half + 1) * LANES]
                w_refs[m][2 * q + half] = part.reshape(lv.planes * s, SUBS, LANES)


class Case:
    def __init__(self, lv, w_refs, fields, planes):
        self.lv, self.cs, self.w_refs = lv, Consts(lv), w_refs
        self.d, self.q, self.r = fields[:3], fields[3], fields[4]
        (self.fz,) = planes

    def weights(self, plane):
        s = self.lv.seg
        return lambda m, i, j: self.w_refs[m][i, plane * s + j]


HALVES = (0, 1)
CHUNK = 640


def plane_rows(lv):
    return lv.tiles * SUBS


def field_rows(lv):
    return lv.edz * plane_rows(lv)


def padded_rows(lv):
    return -(-field_rows(lv) // CHUNK) * CHUNK


def turned_tiles(lv):
    return lv.edge * EZ * lv.edz // LANES


def together(works):
    zero = jnp.zeros((SUBS, LANES), F32)
    sums = [tuple(zero for _ in range(number)) for _, number, _, _ in works]
    done = 0
    for stop in sorted({count for count, _, _, _ in works}):
        active = [n for n, work in enumerate(works) if work[0] > done]

        def body(z, carry, active=active):
            return tuple(
                tuple(a + b for a, b in zip(old, works[n][2](z))) for n, old in zip(active, carry)
            )

        got = lax.fori_loop(done, stop, body, tuple(sums[n] for n in active))
        for n, part in zip(active, got):
            sums[n] = part
        done = stop
    return [work[3](list(part)) for work, part in zip(works, sums)]


def start_residual(case):
    lv, cs, s = case.lv, case.cs, case.lv.seg

    def step(z0):
        total = [[], []]
        for z in [z0]:
            get, below = case.weights(z + 1), case.weights(z)
            gz = cs.fz(z + 1)
            last = [get(1, i, s - 1) * cs.along_y[i] for i in range(s)]
            before = [turn(v, 1, 0) for v in last]
            for j in range(s):
                flux_y = last if j == s - 1 else [get(1, i, j) * cs.along_y[i] for i in range(s)]
                flux_x = [get(0, i, j) * cs.along_x[j] for i in range(s)]
                squares = [[], []]
                for i in range(s):
                    k = i * s + j
                    prev_x = flux_x[i - 1] if i else turn(flux_x[s - 1], 1)
                    flat = (prev_x - flux_x[i]) + (before[i] - flux_y[i])
                    flat = cs.masked(flat, i, j, 0)
                    tall = (cs.fx[i] * cs.fy[j]) * (1.0 / lv.edz) * (below(2, i, j) - get(2, i, j))
                    tall = cs.masked(tall, i, j, 0)
                    for h, value in enumerate((flat * gz[0] + tall, flat * gz[1] - tall)):
                        case.d[0][z, h * lv.tiles + k] = value
                        squares[h].append(value * value)
                for h in HALVES:
                    total[h].append(tree(squares[h]))
                before = flux_y
        return [tree(t) for t in total]

    return lv.inner, 2, step, lambda sums: sums


def row_jumps(u, s, j):
    jump_x = [u[i * s + j] - (u[(i + 1) * s + j] if i < s - 1 else turn(u[j], -1)) for i in range(s)]
    jump_y = [u[i * s + j] - (u[i * s + j + 1] if j < s - 1 else turn(u[i * s], -1, 0)) for i in range(s)]
    return jump_x, jump_y


def apply(case, number, betas):
    lv, cs, s = case.lv, case.cs, case.lv.seg
    keep = number < 2
    n = lv.tiles

    def fresh(z, h, k):
        at = h * n + k
        if number == 0:
            return case.d[0][z, at]
        value = case.r[z, at] + betas[h] * case.d[number - 1][z, at]
        case.d[number][z, at] = value
        return value

    firsts = []
    get = case.weights(0)
    for h in HALVES:
        terms = []
        for k in range(n):
            value = fresh(0, h, k)
            flux = -get(2, k // s, k % s) * value
            if keep:
                case.fz[h * n + k] = flux
            else:
                terms.append(-flux * value)
        firsts.append(tree(terms) if terms else 0.0)

    def step(z0):
        total = [[], []]
        u = [[case.d[number][z0, h * n + k] for k in range(n)] for h in HALVES]
        flux_z = [[case.fz[h * n + k] for k in range(n)] for h in HALVES] if keep else None
        for z in [z0]:
            get = case.weights(z + 1)
            after = [[None] * n for _ in HALVES]
            if keep:
                wy = [get(1, i, s - 1) for i in range(s)]
                last = [[wy[i] * (u[h][i * s + s - 1] - turn(u[h][i * s], -1, 0)) for i in range(s)] for h in HALVES]
                before = [[turn(v, 1, 0) for v in last[h]] for h in HALVES]
            for j in range(s):
                wx = [get(0, i, j) for i in range(s)]
                wy = [get(1, i, j) for i in range(s)]
                wz = [get(2, i, j) for i in range(s)]
                for h in HALVES:
                    jump_x, jump_y = row_jumps(u[h], s, j)
                    flux_x = [w * v for w, v in zip(wx, jump_x)]
                    flux_y = last[h] if keep and j == s - 1 else [w * v for w, v in zip(wy, jump_y)]
                    terms = []
                    for i in range(s):
                        k = i * s + j
                        after[h][k] = fresh(z + 1, h, k)
                        jump = u[h][k] - after[h][k]
                        flux = wz[i] * jump
                        if keep:
                            prev_x = flux_x[i - 1] if i else turn(flux_x[s - 1], 1)
                            value = (flux_x[i] - prev_x) + (flux_y[i] - before[h][i]) + (flux - flux_z[h][k])
                            flux_z[h][k] = flux
                            value = cs.masked(value, i, j, 0)
                            case.q[z, h * n + k] = value
                            terms.append(u[h][k] * value)
                        else:
                            terms.append((flux * jump + flux_x[i] * jump_x[i]) + flux_y[i] * jump_y[i])
                    total[h].append(tree(terms))
                    if keep:
                        before[h] = flux_y
            u = after
        if keep:
            for h in HALVES:
                for k in range(n):
                    case.fz[h * n + k] = flux_z[h][k]
        return [tree(t) for t in total]

    return lv.inner, 2, step, lambda sums: [a + b for a, b in zip(sums, firsts)]


def reduce_residual(case, number, alphas):
    lv = case.lv

    def step(z0):
        total = [[], []]
        source = case.d[0] if number == 0 else case.r
        for z in [z0]:
            for h in HALVES:
                squares = []
                for k in range(lv.tiles):
                    at = h * lv.tiles + k
                    value = source[z, at] - alphas[h] * case.q[z, at]
                    case.r[z, at] = value
                    squares.append(value * value)
                total[h].append(tree(squares))
        return [tree(t) for t in total]

    return lv.inner, 2, step, lambda sums: sums


def finish(case, alphas, refs, send):
    lv, cs, s = case.lv, case.cs, case.lv.seg
    n = lv.tiles
    f_ref, p_ref, y_ref = refs
    lower = lane_parts()[1] == 0

    def at(z, k):
        return pl.ds(pl.multiple_of(z * plane_rows(lv) + k * SUBS, SUBS), SUBS)

    def fresh(z, i, j, gz):
        k = i * s + j
        inner = z + lv.mz - 1
        both = cs.fx[i] * cs.fy[j]
        values = []
        for h in HALVES:
            value = both * gz[h]
            for alpha, d_ref in zip(alphas[h], case.d):
                value = value + alpha * d_ref[inner, h * n + k]
            values.append(cs.masked(value, i, j, 1))
        chosen = jnp.where(lower, values[1], values[0])
        f_ref[at(z, k), :] = chosen
        p_ref[at(z, k), :] = values[0]
        return chosen

    gz = cs.fz(lv.mz)
    for i in range(s):
        for j in range(s):
            fresh(0, i, j, gz)
            case.fz[i * s + j] = jnp.zeros((SUBS, LANES), F32)
    rest = padded_rows(lv) - field_rows(lv)
    if rest:
        for ref in refs:
            ref[field_rows(lv) :, :] = jnp.zeros((rest, LANES), F32)

    def cut(values, table):
        return [v if f is None else v * f for v, f in zip(values, table)]

    def step(z0):
        u = [f_ref[at(z0, k), :] for k in range(n)]
        flux_z = [case.fz[k] for k in range(n)]
        for z in [z0]:
            get = case.weights(z + lv.mz)
            up = jnp.minimum(z + 1, lv.edz - 1)
            gz = cs.fz(up + lv.mz)
            after = [None] * n
            last = [get(1, i, s - 1) * (u[i * s + s - 1] - turn(u[i * s], -1, 0)) for i in range(s)]
            last = cut(last, [cs.facey[s - 1]] * s)
            before = [turn(v, 1, 0) for v in last]
            for j in range(s):
                jump_x, jump_y = row_jumps(u, s, j)
                flux_x = cut([get(0, i, j) * jump_x[i] for i in range(s)], cs.facex)
                flux_y = last
                if j < s - 1:
                    flux_y = cut([get(1, i, j) * jump_y[i] for i in range(s)], [cs.facey[j]] * s)
                for i in range(s):
                    k = i * s + j
                    after[k] = fresh(up, i, j, gz)
                    flux = get(2, i, j) * (u[k] - after[k])
                    prev_x = flux_x[i - 1] if i else turn(flux_x[s - 1], 1)
                    y_ref[at(z, k), :] = (flux_x[i] - prev_x) + (flux_y[i] - before[i]) + (flux - flux_z[k])
                    flux_z[k] = flux
                before = flux_y
            u = after
        for k in range(n):
            case.fz[k] = flux_z[k]
        for z in [z0]:
            for h in HALVES:
                send(h, z).start()
        return ()

    return lv.edz, 0, step, lambda _: corner_pairs(lv, refs)


def corner_pairs(lv, refs):
    f_ref, p_ref, y_ref = refs
    pairs = jnp.zeros((2 * LANES, LANES), F32)
    for start in range(0, padded_rows(lv), CHUNK):
        part = slice(start, start + CHUNK)
        left = jnp.concatenate([f_ref[part, :].T, p_ref[part, :].T], axis=0)
        right = y_ref[part, :]
        left_high, right_high = left.astype(BF16), right.astype(BF16)
        left_low = (left - left_high.astype(F32)).astype(BF16)
        right_low = (right - right_high.astype(F32)).astype(BF16)
        for a, b in ((left_high, right_high), (left_low, right_high), (left_high, right_low)):
            pairs = pairs + jnp.dot(a, b, preferred_element_type=F32)
    shape = (LANES, LANES)
    row, lane = sub_iota(shape), lane_iota(shape)
    sums = [jnp.where(row == (lane + 32 * k) % LANES, pairs[:LANES], 0.0) for k in range(3)]
    sums.append(jnp.where(row % 32 == lane % 32, pairs[LANES:], 0.0))
    out = []
    for value in sums:
        value = tree([value[r : r + SUBS] for r in range(0, LANES, SUBS)])
        out.append(value)
    return out


def place_kernel(center, out_ref):
    nx = center.shape[1]
    out_ref[...] = jnp.ones(out_ref.shape, F32)
    for m in range(3):
        off = m * (nx + 2 * MX) + MX
        out_ref[off : off + nx, :] = center[m]


def solve_kernel(
    inside, x_low, x_high, y_low, y_high,
    phi, message,
    flat, sides, rows, pairs, twin_rows, *refs,
):
    lanes = inside.shape[1]
    rim = y_low.shape[2]
    wide = y_low.shape[1]
    for m in range(3):
        off = m * wide
        flat[off : off + MX, :] = x_low[m]
        flat[off + wide - MX : off + wide, :] = x_high[m]
        sides[off : off + wide, :rim] = y_low[m]
        sides[off : off + wide, rim:] = y_high[m]
    sides[3 * wide :, :] = jnp.ones((LANES - 3 * wide, sides.shape[1]), F32)
    row = sub_iota((LANES, LANES))
    place = row % wide
    outer = (row < 3 * wide) & ((place < MX) | (place >= wide - MX))
    for t in range(rim // LANES):
        low, high = slice(t * LANES, (t + 1) * LANES), slice(rim + t * LANES, rim + (t + 1) * LANES)
        rows[low, :] = sides[:, low].T
        rows[lanes + rim + t * LANES : lanes + rim + (t + 1) * LANES, :] = sides[:, high].T
    for t in range(lanes // LANES):
        part = slice(t * LANES, (t + 1) * LANES)
        rows[rim + t * LANES : rim + (t + 1) * LANES, :] = jnp.where(outer, flat[:, part], inside[:, part]).T

    nz = EZ * ELZ
    twin_y = rows.shape[0] // nz // 2
    for y in range(twin_y):
        both = rows[2 * y * nz : (2 * y + 1) * nz, :] + rows[(2 * y + 1) * nz : (2 * y + 2) * nz, :]
        both = both + turn(both, -1)
        at = y * nz
        pairs[at : at + nz, :] = both
        twin_rows[at : at + 8, :] = jnp.broadcast_to(0.25 * both[0:1], (8, LANES))
        twin_rows[at + 8 + nz // 2 : at + nz, :] = jnp.broadcast_to(0.25 * both[nz - 1 : nz], (8, LANES))
    for y in range(twin_y):
        at = y * nz
        middle = pairs[pl.ds(at, nz // 2, stride=2), :] + pairs[pl.ds(at + 1, nz // 2, stride=2), :]
        twin_rows[at + 8 : at + 8 + nz // 2, :] = 0.125 * middle
    twin_rows[twin_y * nz :, :] = jnp.ones((twin_rows.shape[0] - twin_y * nz, LANES), F32)

    refs = list(refs)

    def take(count):
        got = refs[:count]
        del refs[:count]
        return got

    cases, splits, places = [], [], []
    for lv, source in zip(LEVELS, (rows, twin_rows)):
        (k_ref,) = take(1)
        high_refs, low_refs, w_refs = take(3), take(3), take(3)
        for z in range(lv.levels + 1):
            cell = min(max(z - 1, 0), nz - 1) if lv is FINE else min(z, lv.levels - 1) + 7
            for i in range(lv.seg):
                for c in range(COLUMNS):
                    start = (lv.edge * c + i) * nz + cell
                    k_ref[z, i, :, c * LANES : (c + 1) * LANES] = source[pl.ds(start, SUBS, stride=lv.seg * nz), :]
        splits.append(split_weights(lv, k_ref, high_refs, low_refs))
        places.append(functools.partial(place_weights, lv, high_refs, low_refs, w_refs))
        case = Case(lv, w_refs, take(5), take(1))
        for k in range(2 * lv.tiles):
            case.d[0][lv.inner, k] = jnp.zeros((SUBS, LANES), F32)
            case.r[lv.inner, k] = jnp.zeros((SUBS, LANES), F32)
        cases.append(case)

    def split(t, _):
        for step in splits:
            step(t, 0)
        return 0

    both = TWIN.planes // 2
    lax.fori_loop(0, both, split, 0)
    lax.fori_loop(both, FINE.planes // 2, splits[0], 0)
    for work in places:
        work()

    def both_levels(work):
        return [[problem_sum(v) for v in part] for part in together([work(n, case) for n, case in enumerate(cases)])]

    rr = both_levels(lambda n, case: start_residual(case))
    alphas = [[[], []] for _ in LEVELS]
    betas = [None] * len(LEVELS)
    for step in range(3):
        dots = both_levels(lambda n, case: apply(case, step, betas[n]))
        now = [[a / b for a, b in zip(rr[n], dots[n])] for n in range(len(LEVELS))]
        for n in range(len(LEVELS)):
            for h in HALVES:
                alphas[n][h].append(now[n][h])
        if step < 2:
            new = both_levels(lambda n, case: reduce_residual(case, step, now[n]))
            betas = [[a / b for a, b in zip(new[n], rr[n])] for n in range(len(LEVELS))]
            rr = new

    results = [take(3), take(3)]
    sems = take(2)

    def send(n, h, z):
        lv = LEVELS[n]
        size = plane_rows(lv)
        first = sum(2 * field_rows(v) for v in LEVELS[:n]) + h * field_rows(lv)
        return pltpu.make_async_copy(
            results[n][h].at[pl.ds(pl.multiple_of(z * size, SUBS), size)],
            phi.at[pl.ds(pl.multiple_of(first + z * size, SUBS), size)],
            sems[n].at[h * lv.edz + z],
        )

    totals = both_levels(
        lambda n, case: finish(case, alphas[n], results[n], functools.partial(send, n))
    )
    _, element, _, slot = lane_parts()
    packed = []
    for level in totals:
        parts = [v + xor_lane(v, 16) for v in level[:3]]
        parts.append(jnp.where(element == 0, level[3], turn(level[3], 16)))
        packed.append(
            jnp.where(slot == 0, parts[0], jnp.where(slot == 1, parts[1], jnp.where(slot == 2, parts[2], parts[3])))
        )
    row = jnp.where(element == 0, packed[0], packed[1])
    for r in range(0, message.shape[0], SUBS):
        message[r : r + SUBS, :] = row
    for n, lv in enumerate(LEVELS):
        for h in HALVES:
            for z in range(lv.edz):
                send(n, h, z).wait()


def coarse_nodes(gathered, gy_count, me):
    total_rows = gathered.shape[0]
    shape = gathered.shape
    lane = lane_iota(shape)
    row = sub_iota(shape)
    corner = lane // 32
    column = lane // 8 % 2
    last = row % gy_count == gy_count - 1
    start = row % gy_count == 0
    one = gathered
    two = turn(gathered, -1)
    four = turn(gathered, -2)
    rhs = turn(gathered, -3)
    two_back = turn(two, 32)

    def next_x(u):
        return turn(u, -gy_count, 0)

    def prev_x(u):
        return turn(u, gy_count, 0)

    def next_y(u):
        ahead = jnp.where(last, turn(u, gy_count - 1, 0), turn(u, -1, 0))
        return jnp.where(column == 0, turn(u, -8), turn(ahead, 8))

    def prev_y(u):
        behind = jnp.where(start, turn(u, 1 - gy_count, 0), turn(u, 1, 0))
        return jnp.where(column == 1, turn(u, 8), turn(behind, -8))

    def by_corner(a, b, c, d):
        return jnp.where(corner == 0, a, jnp.where(corner == 1, b, jnp.where(corner == 2, c, d)))

    def corners(u):
        ux = next_x(u)
        return by_corner(u, next_y(u), ux, next_y(ux))

    def assemble(v):
        vx = prev_x(v)
        w = by_corner(v, prev_y(v), vx, prev_y(vx))
        w = w + turn(w, 64)
        return w + turn(w, 32)

    def operate(u):
        c = corners(u)
        return assemble(one * c + two * turn(c, -32) + two_back * turn(c, 32) + four * turn(c, 64))

    def total(a, b):
        v = a * b
        v = tree([v[r : r + SUBS] for r in range(0, total_rows, SUBS)])
        for shift in (4, 2, 1):
            v = v + turn(v, shift, 0)
        v = v + xor_lane(v, 8)
        return v[0:1]

    residual = -assemble(rhs)
    direction = residual
    update = jnp.zeros_like(residual)
    now = total(residual, residual)
    for step in range(2):
        image = operate(direction)
        alpha = now / total(direction, image)
        update = update + alpha * direction
        if step == 0:
            residual = residual - alpha * image
            new = total(residual, residual)
            direction = residual + new / now * direction
            now = new
    mine = jnp.where(row == me, corners(update), 0.0)
    mine = jnp.sum(mine, axis=0, keepdims=True)
    return jnp.broadcast_to(mine, (SUBS, LANES))


def turn_kernel(phi, out_ref):
    start_row, number = 0, 0
    for lv in LEVELS:
        s = lv.seg
        nz = EZ * lv.edz
        per = LANES // nz
        for i in range(s):
            for t in range(turned_tiles(lv)):
                parts = []
                for n in range(per):
                    yo, j = divmod(lv.mx + t * per + n, s)
                    start = start_row + (i * s + j) * SUBS + yo
                    chosen, bottom = [
                        phi[pl.ds(start + h * field_rows(lv), lv.edz, stride=plane_rows(lv)), :] for h in HALVES
                    ]
                    lower = lane_iota(chosen.shape) // 16 % 2 == 0
                    parts.append(jnp.where(lower, chosen, turn(bottom, 16)))
                    parts.append(jnp.where(lower, turn(chosen, -16), 0.0))
                out_ref[number] = jnp.concatenate(parts, axis=0).T
                number += 1
        start_row += 2 * field_rows(lv)


def pressure_kernel(gy_count, me_ref, gathered, turned, fine_out, twin_out, fine_all, twin_all):
    mine = coarse_nodes(gathered[...], gy_count, me_ref[0])
    first = 0
    for n, (lv, out_ref, all_ref) in enumerate(((FINE, fine_out, fine_all), (TWIN, twin_out, twin_all))):
        s = lv.seg
        tiles = turned_tiles(lv)
        nodes = {}
        for c in range(COLUMNS):
            for p in range(4):
                at = p * 32 + n * 16 + c * 8
                nodes[p, c] = jnp.broadcast_to(mine[:, at : at + 1], (SUBS, LANES))
        for c in range(COLUMNS):
            for t in range(tiles):
                at = (c * tiles + t) * LANES
                for i in range(s):
                    def part(group):
                        return turned[first + i * tiles + t, group * 16 + c * 8 : group * 16 + c * 8 + 8, :]

                    value = tree([part(2 * p) * nodes[p, c] + part(2 * p + 1) for p in range(4)])
                    all_ref[c * tiles + t, pl.ds(i, SUBS, stride=s), :] = value
                out_ref[:, at : at + LANES] = all_ref[c * tiles + t, lv.mx : lv.mx + lv.edge, :]
        first += s * tiles


def vmem(shape, dtype=F32):
    return pltpu.VMEM(shape, dtype)


def shards(permeability):
    nz = EZ * ELZ
    rows = permeability.shape[1]
    lanes = permeability.shape[2]
    assert rows == EL and lanes == COLUMNS * EL * nz
    rim = MX * nz
    gx, gy = lax.axis_size("gx"), lax.axis_size("gy")

    def sent(value, axis, shift):
        count = lax.axis_size(axis)
        return lax.ppermute(value, axis, [(i, (i + shift) % count) for i in range(count)])

    x_low = sent(permeability[:, rows - MX :], "gx", 1)
    x_high = sent(permeability[:, :MX], "gx", -1)

    def strip(part):
        return jnp.concatenate([x_low[:, :, part], permeability[:, :, part], x_high[:, :, part]], axis=1)

    y_low = sent(strip(slice(lanes - rim, lanes)), "gy", 1)
    y_high = sent(strip(slice(0, rim)), "gy", -1)
    halos = [x_low, x_high, y_low, y_high]
    flat_lanes = lanes + 2 * rim
    scratch = [
        vmem((LANES, lanes)),
        vmem((LANES, 2 * rim)),
        vmem((flat_lanes, LANES)),
        vmem((flat_lanes // 2, LANES)),
        vmem((SUBS * (TWIN.seg + 2) * nz, LANES)),
    ]
    for lv in LEVELS:
        scratch.append(vmem((lv.levels + 1, lv.seg, SUBS, 2 * LANES)))
        scratch += [vmem((lv.planes * lv.seg // 2, 2 * SUBS, 2 * LANES), BF16)] * 6
        scratch += [vmem((lv.seg, lv.planes * lv.seg, SUBS, LANES))] * 3
        scratch += [vmem((lv.inner + 1, 2 * lv.tiles, SUBS, LANES))] * 5
        scratch.append(vmem((2 * lv.tiles, SUBS, LANES)))
    for lv in LEVELS:
        scratch += [vmem((padded_rows(lv), LANES))] * 3
    scratch += [pltpu.SemaphoreType.DMA((2 * lv.edz,)) for lv in LEVELS]
    full = pl.BlockSpec(memory_space=pltpu.VMEM)
    inside = pl.pallas_call(
        place_kernel,
        out_shape=vmem((LANES, lanes)),
        in_specs=[full],
        out_specs=full,
        compiler_params=pltpu.CompilerParams(vmem_limit_bytes=8 * 1024 * 1024),
        cost_estimate=pl.CostEstimate(flops=1000000, bytes_accessed=4000000, transcendentals=0),
        name="place",
    )(permeability)
    phi, message = pl.pallas_call(
        solve_kernel,
        out_shape=[
            pltpu.HBM((sum(2 * field_rows(lv) for lv in LEVELS), LANES), F32),
            jax.ShapeDtypeStruct((gx * gy, LANES), F32),
        ],
        in_specs=[full] * 5,
        out_specs=[pl.BlockSpec(memory_space=pltpu.HBM), full],
        scratch_shapes=scratch,
        compiler_params=pltpu.CompilerParams(vmem_limit_bytes=50 * 1024 * 1024),
        name="solve",
    )(inside, *halos)
    gathered = lax.all_to_all(message, ("gx", "gy"), 0, 0, tiled=True)
    tiles = sum(lv.seg * turned_tiles(lv) for lv in LEVELS)
    turned = pl.pallas_call(
        turn_kernel,
        out_shape=vmem((tiles, LANES, LANES)),
        in_specs=[full],
        out_specs=full,
        compiler_params=pltpu.CompilerParams(vmem_limit_bytes=16 * 1024 * 1024),
        cost_estimate=pl.CostEstimate(flops=4000000, bytes_accessed=8000000, transcendentals=0),
        name="turned",
    )(phi)
    me = (lax.axis_index("gx") * gy + lax.axis_index("gy")).astype(jnp.int32).reshape(1)
    return tuple(
        pl.pallas_call(
            functools.partial(pressure_kernel, gy),
            out_shape=[
                jax.ShapeDtypeStruct((lv.edge, COLUMNS * lv.edge * EZ * lv.edz), F32) for lv in LEVELS
            ],
            in_specs=[pl.BlockSpec(memory_space=pltpu.SMEM), full, full],
            out_specs=[full] * 2,
            scratch_shapes=[vmem((COLUMNS * turned_tiles(lv), SUBS * lv.seg, LANES)) for lv in LEVELS],
            compiler_params=pltpu.CompilerParams(vmem_limit_bytes=16 * 1024 * 1024),
            name="pressure",
        )(me, gathered, turned)
    )


def solution(mesh):
    return jax.shard_map(
        shards,
        mesh=mesh,
        in_specs=(P(None, "gx", "gy"),),
        out_specs=(P("gx", "gy"), P("gx", "gy")),
        check_vma=False,
    )
```
